32 devices in a mesh: pass: 4 (over z), dp: 8 (over y, x, core).
Axes of the slice: x: 2, y: 2, z: 4, core: 2. Of those that a mesh axis runs over, the one named last changes fastest.
Arguments:
- decoder_in: bfloat16 [4, 8, 256, 512], P('pass', 'dp'), may hold values from -6 to 6
- decoder_segments: int32 [4, 8, 256], P('pass', 'dp'), may hold values from 0 to 2, never falling along the last dimension, each value on 1 to 128 neighbouring positions
- edit_target: int32 [4, 8, 256], P('pass', 'dp'), may hold values from 0 to 32767
- loss_mask: int32 [4, 8, 256], P('pass', 'dp'), may hold values 0 or 1
- source_out: bfloat16 [8, 512, 512], P('dp', 'pass'), may hold values from -6 to 6
- source_segments: int32 [8, 512], P('dp', 'pass'), may hold values from 0 to 2, never falling along the last dimension, each value on 1 to 256 neighbouring positions
- norm_gain: bfloat16 [4, 512], replicated, may hold values from 0.5 to 1.5
- norm_bias: bfloat16 [4, 512], replicated, may hold values from -1.5 to 1.5
- self_qkv: bfloat16 [512, 1536], replicated, may hold values from -0.25 to 0.25
- self_out: bfloat16 [512, 512], replicated, may hold values from -1 to 1
- cross_query: bfloat16 [512, 512], replicated, may hold values from -0.25 to 0.25
- cross_kv: bfloat16 [512, 1024], replicated, may hold values from -0.25 to 0.25
- cross_out: bfloat16 [512, 512], replicated, may hold values from -1 to 1
- ffn_in: bfloat16 [512, 2048], replicated, may hold values from -0.25 to 0.25
- ffn_out: bfloat16 [2048, 512], replicated, may hold values from -0.125 to 0.125
- delete_head: bfloat16 [512, 2], replicated, may hold values from -0.25 to 0.25
- insert_head: bfloat16 [1024, 256], replicated, may hold values from -0.1875 to 0.1875
- token_head: bfloat16 [32768, 512], P(('pass', 'dp')), may hold values from -0.25 to 0.25
Outputs:
- layer_out: bfloat16 [4, 8, 256, 512], P('pass', 'dp')
- row_loss: float32 [4, 8], P('pass', 'dp')
- input_grad: float32 [4, 8, 256, 512], P('pass', 'dp')
- source_grad: float32 [8, 512, 512], P('dp', 'pass')
- gain_grad: float32 [4, 512], P(None, 'dp')
- bias_grad: float32 [4, 512], P(None, 'dp')
- self_qkv_grad: float32 [512, 1536], P('dp')
- self_out_grad: float32 [512, 512], P('dp')
- cross_query_grad: float32 [512, 512], P('dp')
- cross_kv_grad: float32 [512, 1024], P('dp')
- cross_out_grad: float32 [512, 512], P('dp')
- ffn_in_grad: float32 [512, 2048], P('dp')
- ffn_out_grad: float32 [2048, 512], P('dp')
- delete_grad: float32 [512, 2], P('dp')
- insert_grad: float32 [1024, 256], P('dp')
- token_grad: float32 [32768, 512], P(('pass', 'dp'))
The draws below stay inside these ranges and needn't reach their ends.
All inputs are finite; a program needn't handle non-finite values. No bound on the sum of `loss_mask` on one device may be relied on, other than what follows from the above.
Results may differ from the reference program's by a relative error of at most 0.015.
Values may be sent and summed in bfloat16 or wider, within the bound.
No kernel may reach another device: no remote copies, remote signals or barrier semaphores. Data moves between devices by JAX's collectives and lax.ppermute only.
A program may use at most 320 MiB of HBM per device.

```python
import math
import jax
import jax.numpy as jnp
import numpy as np
from jax import lax

D = 512
HEADS = 8
FF = 2048
V = 32768
INS = 256
TOK_DEV = 256
SEGS = 3
SRC = 512
N_PASS = 4
N_DP = 8


def set_ends(result, key, least, top_value):
    shape = result.shape
    place = [jax.random.randint(jax.random.fold_in(key, axis), (), 0, shape[axis]) for axis in range(len(shape))]
    result = result.at[tuple(place)].set(least)
    longest = shape.index(max(shape))
    place[longest] = (place[longest] + 1) % shape[longest]
    return result.at[tuple(place)].set(top_value)


def block_scale(rng, extent, cuts, low, high):
    level = 1.0
    for position, shards_of in cuts:
        heights = jax.random.uniform(jax.random.fold_in(jax.random.fold_in(rng, 6), position), (shards_of,), jnp.float32, low / len(cuts), high / len(cuts))
        level = level * jnp.repeat(jnp.exp(heights), extent[position] // shards_of).reshape((-1,) + (1,) * (len(extent) - 1 - position))
    return level


def split_up(number_of, total, bound, skew):
    weights = [(1 << 20) // math.isqrt(rank ** skew) + 1 for rank in range(2, number_of + 1)]
    spare, given = total - bound - (number_of - 1), [1] * (number_of - 1)
    while spare > 0:
        free = [i for i in range(number_of - 1) if given[i] < bound]
        mass, left = sum([weights[i] for i in free]), spare
        for i in free:
            more = min(bound - given[i], max(1, left * weights[i] // mass), spare)
            given[i] = given[i] + more
            spare = spare - more
    return np.array([bound] + given)


def uneven(stream_key, count, total, limit, lean):
    if count == 2:
        one = jax.random.randint(stream_key, (), max(1, total - limit), min(limit, total - 1) + 1)
        return jnp.stack([one, total - one])
    tallies = jnp.asarray(split_up(count, total, limit, lean), jnp.int32)
    couples = (count - 1) // 2
    source_of, receiver = tallies[1:1 + 2 * couples:2], tallies[2:2 + 2 * couples:2]
    margin = jnp.minimum(source_of - 1, limit - receiver)
    passed = jax.random.randint(jax.random.fold_in(stream_key, 1), (couples,), 0, 1 << 20) % (margin + 1)
    tallies = tallies.at[1:1 + 2 * couples:2].set(source_of - passed).at[2:2 + 2 * couples:2].set(receiver + passed)
    return tallies[jax.random.permutation(jax.random.fold_in(stream_key, 2), count)]


def gaussian(rng, shape, scale, most, cuts=(), kind=jnp.bfloat16):
    drawn = scale * jax.random.normal(rng, shape, jnp.float32)
    if cuts:
        drawn = drawn * block_scale(rng, shape, cuts, -0.22, 0.18)
    return jnp.clip(drawn, -most, most).astype(kind)


def setup_inputs(seed: int = 0) -> dict:
    arg_keys = jax.random.split(jax.random.key(seed), 19)
    return {
        "decoder_in": gaussian(arg_keys[0], (N_PASS, N_DP, TOK_DEV, D), 1.0, 6.0, ((0, 4), (1, 8))),
        "decoder_segments": jax.vmap(lambda own: jnp.searchsorted(jnp.cumsum(uneven(own, SEGS, TOK_DEV, TOK_DEV // 2, 1)), jnp.arange(TOK_DEV), side="right"))(jax.random.split(arg_keys[1], N_PASS * N_DP)).reshape((N_PASS, N_DP, TOK_DEV)).astype(jnp.int32),
        "edit_target": set_ends(jax.random.randint(arg_keys[2], (N_PASS, N_DP, TOK_DEV), 0, V), jax.random.fold_in(arg_keys[2], 1), 0, V - 1).astype(jnp.int32),
        "loss_mask": set_ends((jax.random.randint(arg_keys[3], (N_PASS, N_DP, TOK_DEV), 0, 2) < 1).astype(jnp.int32), jax.random.fold_in(arg_keys[3], 1), 0, 1),
        "source_out": gaussian(arg_keys[4], (N_DP, SRC, D), 1.0, 6.0, ((0, 8), (1, 4))),
        "source_segments": jax.vmap(lambda own: jnp.searchsorted(jnp.cumsum(uneven(own, SEGS, SRC, SRC // 2, 1)), jnp.arange(SRC), side="right"))(jax.random.split(arg_keys[5], N_DP)).reshape((N_DP, SRC)).astype(jnp.int32),
        "norm_gain": jnp.clip(1.0 + 0.1 * jax.random.normal(arg_keys[6], (4, D), jnp.float32), 0.5, 1.5).astype(jnp.bfloat16),
        "norm_bias": gaussian(arg_keys[7], (4, D), 0.3, 1.5),
        "self_qkv": gaussian(arg_keys[8], (D, 3 * D), D ** -0.5, 0.25),
        "self_out": gaussian(arg_keys[9], (D, D), (D // 16) ** -0.5, 1.0),
        "cross_query": gaussian(arg_keys[10], (D, D), D ** -0.5, 0.25),
        "cross_kv": gaussian(arg_keys[11], (D, 2 * D), D ** -0.5, 0.25),
        "cross_out": gaussian(arg_keys[12], (D, D), (D // 16) ** -0.5, 1.0),
        "ffn_in": gaussian(arg_keys[13], (D, FF), D ** -0.5, 0.25),
        "ffn_out": gaussian(arg_keys[14], (FF, D), FF ** -0.5, 0.125),
        "delete_head": gaussian(arg_keys[15], (D, 2), D ** -0.5, 0.25),
        "insert_head": gaussian(arg_keys[16], (2 * D, INS), (2 * D) ** -0.5, 0.1875),
        "token_head": gaussian(arg_keys[17], (V, D), D ** -0.5, 0.25, ((0, 32),)),
    }


@jax.custom_vjp
def low(v):
    return lax.optimization_barrier(v.astype(jnp.bfloat16)).astype(jnp.float32)

@jax.custom_vjp
def low_back(v):
    return v

def low_keep(v):
    return (low(v), None)

def low_pass(kept, grad):
    return (grad,)

def back_keep(v):
    return (v, None)

def back_low(kept, grad):
    return (low(grad),)
low.defvjp(low_keep, low_pass)
low_back.defvjp(back_keep, back_low)

def matmul(left, right):
    return jnp.dot(left, right, precision=lax.Precision.HIGHEST)

def norm_rows(values, gain, shift):
    center = values - lax.optimization_barrier(jnp.mean(values, axis=-1, keepdims=True))
    spread = lax.optimization_barrier(jnp.mean(center * center, axis=-1, keepdims=True))
    return center * lax.rsqrt(spread + 1e-05) * gain + shift

def attend(query, keys, values, allowed):
    rows, width = query.shape
    size = width // HEADS
    qh = query.reshape(rows, HEADS, size)
    kh = keys.reshape(keys.shape[0], HEADS, size)
    vh = values.reshape(values.shape[0], HEADS, size)
    scores = jnp.einsum('qhd,khd->hqk', qh, kh, precision=lax.Precision.HIGHEST) * size ** (-0.5)
    scores = jnp.where(allowed[None], scores, -1000000000.0)
    top = lax.optimization_barrier(jnp.max(scores, axis=-1, keepdims=True))
    expo = jnp.exp(scores - top)
    probs = low(expo / lax.optimization_barrier(jnp.sum(expo, axis=-1, keepdims=True)))
    context = jnp.einsum('hqk,khd->qhd', probs, vh, precision=lax.Precision.HIGHEST)
    return low(low_back(context.reshape(rows, width)))

def trunk(params, rows, segs, source, source_segs):
    gains, shifts, w_qkv, w_self, w_query, w_kv, w_cross, w_in, w_out = params[:9]
    width = rows.shape[1]
    normed = low(norm_rows(rows, gains[0], shifts[0]))
    qkv = low(low_back(matmul(normed, w_qkv)))
    same = segs[:, None] == segs[None, :]
    context = attend(qkv[:, :width], qkv[:, width:2 * width], qkv[:, 2 * width:], same)
    first = rows + matmul(context, w_self)
    normed = low(norm_rows(first, gains[1], shifts[1]))
    query = low(low_back(matmul(normed, w_query)))
    keyval = low(low_back(matmul(source, w_kv)))
    linked = segs[:, None] == source_segs[None, :]
    context = attend(query, keyval[:, :width], keyval[:, width:], linked)
    second = first + matmul(context, w_cross)
    normed = low(norm_rows(second, gains[2], shifts[2]))
    hidden = low(low_back(jax.nn.gelu(matmul(normed, w_in), approximate=False)))
    third = second + matmul(hidden, w_out)
    final = low(norm_rows(third, gains[3], shifts[3]))
    return (third, final)

def pairs(final, segs):
    after = jnp.concatenate([final[1:], jnp.zeros((1, final.shape[1]), jnp.float32)], axis=0)
    joined = jnp.concatenate([segs[1:] == segs[:-1], jnp.zeros((1,), bool)], axis=0)
    after = jnp.where(joined[:, None], after, 0.0)
    return jnp.concatenate([final, after], axis=1)

def entropy(logits, labels, weight):
    top = lax.optimization_barrier(jnp.max(logits, axis=-1, keepdims=True))
    total = top[:, 0] + jnp.log(lax.optimization_barrier(jnp.sum(jnp.exp(logits - top), axis=-1)))
    picked = jnp.take_along_axis(logits, labels[:, None].astype(jnp.int32), axis=1)[:, 0]
    return jnp.sum(weight * (total - picked))

def group_loss(params, vocab, rows, segs, source, source_segs, labels, weight, section):
    third, final = trunk(params, rows, segs, source, source_segs)
    if section == 0:
        logits = low_back(matmul(final, params[9]))
        loss = entropy(logits, labels % 2, weight)
    elif section == 1:
        logits = low_back(matmul(pairs(final, segs), params[10]))
        loss = entropy(logits, labels % INS, weight)
    else:
        logits = low_back(jnp.dot(final, vocab.T, precision=lax.Precision.HIGHEST))
        loss = entropy(logits, labels, weight)
    return (loss, third)

def reference(decoder_in, decoder_segments, edit_target, loss_mask, source_out, source_segments, norm_gain, norm_bias, self_qkv, self_out, cross_query, cross_kv, cross_out, ffn_in, ffn_out, delete_head, insert_head, token_head):
    params = tuple((w.astype(jnp.float32) for w in (norm_gain, norm_bias, self_qkv, self_out, cross_query, cross_kv, cross_out, ffn_in, ffn_out, delete_head, insert_head)))

    def total(params, inputs, source, vocab):
        losses = []
        outputs = []
        for section in range(N_PASS):

            def one(item, section=section):
                rows, segs, src, src_segs, labels, weight = item

                def inner(params, vocab, rows, src):
                    return group_loss(params, vocab, rows, segs, src, src_segs, labels, weight.astype(jnp.float32), section)
                return jax.checkpoint(inner)(params, vocab, rows, src)
            loss_part, out_part = lax.map(one, (inputs[section], decoder_segments[section], source, source_segments, edit_target[section], loss_mask[section]))
            losses.append(loss_part)
            outputs.append(out_part)
        losses = jnp.stack(losses)
        return (jnp.sum(losses), (losses, jnp.stack(outputs)))
    inputs = decoder_in.astype(jnp.float32)
    source = source_out.astype(jnp.float32)
    vocab = token_head.astype(jnp.float32)
    value, pull, extra = jax.vjp(total, params, inputs, source, vocab, has_aux=True)
    grads, input_grad, source_grad, token_grad = pull(jnp.ones((), jnp.float32))
    return (extra[1].astype(jnp.bfloat16), extra[0], input_grad, source_grad, grads[0], grads[1], grads[2], grads[3], grads[4], grads[5], grads[6], grads[7], grads[8], grads[9], grads[10], token_grad)
```

```python
import jax
import jax.numpy as jnp
from jax import lax
from jax.sharding import PartitionSpec as P

HEADS = 8
INS = 256
EPS = 1e-05
BF = jnp.bfloat16
F32 = jnp.float32


def dot(left, right, dims):
    return lax.dot_general(left.astype(BF), right.astype(BF), (dims, ((), ())), preferred_element_type=F32)


def nn(left, right):
    return dot(left, right, ((1,), (0,)))


def nt(left, right):
    return dot(left, right, ((1,), (1,)))


def tn(left, right):
    return dot(left, right, ((0,), (0,)))


def norm_fwd(values, gain, shift):
    center = values - jnp.mean(values, axis=-1, keepdims=True)
    rstd = lax.rsqrt(jnp.mean(center * center, axis=-1, keepdims=True) + EPS)
    unit = center * rstd
    return (unit * gain + shift).astype(BF), unit, rstd


def norm_bwd(grad, unit, rstd, gain):
    scaled = grad * gain
    back = rstd * (
        scaled
        - jnp.mean(scaled, axis=-1, keepdims=True)
        - unit * jnp.mean(scaled * unit, axis=-1, keepdims=True)
    )
    return back, jnp.sum(grad * unit, axis=0), jnp.sum(grad, axis=0)


def heads_of(values):
    return values.reshape(values.shape[0], HEADS, -1)


def attend(query, keys, values, allowed):
    qh, kh, vh = heads_of(query), heads_of(keys), heads_of(values)
    scores = jnp.einsum("qhd,khd->hqk", qh, kh, preferred_element_type=F32) * qh.shape[2] ** (-0.5)
    scores = jnp.where(allowed[None], scores, -1000000000.0)
    expo = jnp.exp(scores - jnp.max(scores, axis=-1, keepdims=True))
    probs = expo / jnp.sum(expo, axis=-1, keepdims=True)
    context = jnp.einsum("hqk,khd->qhd", probs.astype(BF), vh, preferred_element_type=F32)
    return context.reshape(query.shape).astype(BF), probs


def attend_bwd(grad, query, keys, values, probs):
    gh, qh, kh, vh = heads_of(grad), heads_of(query), heads_of(keys), heads_of(values)
    dprobs = jnp.einsum("qhd,khd->hqk", gh, vh, preferred_element_type=F32)
    dvalues = jnp.einsum("hqk,qhd->khd", probs.astype(BF), gh, preferred_element_type=F32)
    dscores = probs * (dprobs - jnp.sum(dprobs * probs, axis=-1, keepdims=True)) * qh.shape[2] ** (-0.5)
    dscores = dscores.astype(BF)
    dquery = jnp.einsum("hqk,khd->qhd", dscores, kh, preferred_element_type=F32)
    dkeys = jnp.einsum("hqk,qhd->khd", dscores, qh, preferred_element_type=F32)
    return (
        dquery.reshape(query.shape).astype(BF),
        dkeys.reshape(keys.shape).astype(BF),
        dvalues.reshape(values.shape).astype(BF),
    )


def gelu_parts(inner):
    cdf = 0.5 * (1.0 + lax.erf(inner * 0.7071067811865476))
    return cdf, inner * cdf


def entropy(logits, labels, weight):
    top = jnp.max(logits, axis=-1, keepdims=True)
    expo = jnp.exp(logits - top)
    total = jnp.sum(expo, axis=-1, keepdims=True)
    hit = lax.broadcasted_iota(jnp.int32, logits.shape, 1) == labels[:, None]
    picked = jnp.sum(jnp.where(hit, logits, 0.0), axis=1)
    loss = jnp.sum(weight * (top[:, 0] + jnp.log(total[:, 0]) - picked))
    grad = weight[:, None] * (expo / total - hit.astype(F32))
    return loss, grad.astype(BF)


def solution(mesh):
    n_pass, n_dp = mesh.shape["pass"], mesh.shape["dp"]
    bits = [1 << i for i in range(n_dp.bit_length() - 1)]
    core_bit, chip_bits = bits[0], bits[1:]
    orders = (chip_bits, chip_bits[1::-1] + chip_bits[2:])

    def swap_core(x):
        return lax.ppermute(x, "dp", [(i, i ^ core_bit) for i in range(n_dp)])

    def swap_chip(x, step):
        return lax.ppermute(x, "dp", [(i, i ^ orders[i & 1][step]) for i in range(n_dp)])

    def swap_pass(x, bit):
        return lax.ppermute(x, "pass", [(i, i ^ bit) for i in range(n_pass)])

    def spread(index, flip):
        result = 0
        for step in range(len(chip_bits)):
            a, b = orders[0][step], orders[1][step]
            bit = jnp.where(flip == 0, a, b)
            result = result + ((index >> (len(chip_bits) - 1 - step)) & 1) * bit
        return result

    def reduce_dp(packed):
        me = lax.axis_index("dp")
        core = me & 1
        half = n_dp // 2
        keep, send = [], []
        for slot in range(half):
            keep.append(lax.dynamic_index_in_dim(packed, me ^ spread(slot, core), 0, keepdims=False))
            send.append(
                lax.dynamic_index_in_dim(packed, me ^ 1 ^ spread(slot, 1 - core), 0, keepdims=False)
            )
        keep = jnp.stack(keep) + swap_core(jnp.stack(send).astype(BF)).astype(F32)
        for step in range(len(chip_bits)):
            half = half // 2
            keep = keep[:half] + swap_chip(keep[half:].astype(BF), step).astype(F32)
        return keep[0]

    def reduce_pass(values):
        pair = values + swap_pass(values.astype(BF), 1).astype(F32)
        return pair + swap_pass(pair.astype(BF), 2).astype(F32)

    def body(
        decoder_in,
        decoder_segments,
        edit_target,
        loss_mask,
        source_out,
        source_segments,
        norm_gain,
        norm_bias,
        self_qkv,
        self_out,
        cross_query,
        cross_kv,
        cross_out,
        ffn_in,
        ffn_out,
        delete_head,
        insert_head,
        token_head,
    ):
        section = lax.axis_index("pass")
        segs = decoder_segments[0, 0]
        labels = edit_target[0, 0]
        weight = loss_mask[0, 0].astype(F32)
        gains, shifts = norm_gain.astype(F32), norm_bias.astype(F32)
        rows = decoder_in[0, 0].astype(F32)
        count, width = rows.shape
        shard = token_head.shape[0]

        part = source_out.shape[1]
        note = jnp.zeros((16, width), BF).at[0, :part].set(source_segments[0].astype(BF))
        mine = jnp.concatenate([source_out[0], note], axis=0)
        parts = [mine] + [swap_pass(mine, bit) for bit in (1, 2, 3)]
        source = jnp.concatenate([p[:part] for p in parts], axis=0)
        source_segs = jnp.concatenate([p[part, :part] for p in parts], axis=0).astype(jnp.int32)

        pair = jnp.concatenate([token_head, swap_pass(token_head, 1)], axis=0)
        vocab = jnp.concatenate([pair, swap_core(pair)], axis=0)
        dp_me = lax.axis_index("dp")
        bases = []
        for core_off, pass_off in ((0, 0), (0, 1), (1, 0), (1, 1)):
            bases.append(((section ^ pass_off) * n_dp + (dp_me ^ core_off)) * shard)
        vocab_ids = jnp.concatenate([b + jnp.arange(shard, dtype=jnp.int32) for b in bases])

        def to_token(x):
            moved = lax.ppermute(x, "pass", [(2, 0), (3, 1)])
            return jnp.where(section >= 2, x, moved)

        def gather_chips(x):
            for step in reversed(range(len(chip_bits))):
                x = jnp.concatenate([x, swap_chip(x, step)], axis=0)
            return x

        marks = jnp.concatenate([labels[None], loss_mask[0, 0][None]], axis=0)[None]
        marks = gather_chips(to_token(marks))
        t_labels, t_weight = marks[:, 0].reshape(-1), marks[:, 1].reshape(-1).astype(F32)

        a1, unit0, rstd0 = norm_fwd(rows, gains[0], shifts[0])
        qkv = nn(a1, self_qkv).astype(BF)
        q1, k1, v1 = qkv[:, :width], qkv[:, width : 2 * width], qkv[:, 2 * width :]
        same = segs[:, None] == segs[None, :]
        ctx1, probs1 = attend(q1, k1, v1, same)
        first = rows + nn(ctx1, self_out)
        a2, unit1, rstd1 = norm_fwd(first, gains[1], shifts[1])
        q2 = nn(a2, cross_query).astype(BF)
        keyval = nn(source, cross_kv).astype(BF)
        k2, v2 = keyval[:, :width], keyval[:, width:]
        linked = segs[:, None] == source_segs[None, :]
        ctx2, probs2 = attend(q2, k2, v2, linked)
        second = first + nn(ctx2, cross_out)
        a3, unit2, rstd2 = norm_fwd(second, gains[2], shifts[2])
        inner = nn(a3, ffn_in)
        cdf, hidden = gelu_parts(inner)
        hidden = hidden.astype(BF)
        third = second + nn(hidden, ffn_out)
        final, unit3, rstd3 = norm_fwd(third, gains[3], shifts[3])

        tokens = gather_chips(to_token(final))
        logits = nt(tokens, vocab)
        top = jnp.max(logits, axis=1)
        hit = vocab_ids[None, :] == t_labels[:, None]
        rest = jnp.sum(jnp.where(hit, 0.0, jnp.exp(logits - top[:, None])), axis=1)
        picked = jnp.sum(jnp.where(hit, logits, 0.0), axis=1)
        stats = jnp.stack([top, rest, picked])

        def merge(a, b):
            peak = jnp.maximum(a[0], b[0])
            total = a[1] * jnp.exp(a[0] - peak) + b[1] * jnp.exp(b[0] - peak)
            return jnp.stack([peak, total, a[2] + b[2]])

        for step in range(len(chip_bits)):
            other = swap_chip(stats, step).reshape(3, 1 << step, 2, -1)[:, :, ::-1].reshape(3, -1)
            stats = merge(stats, other)
        stats = merge(stats, swap_pass(stats, 2))
        peak, rest, picked = stats[0], stats[1], stats[2]
        mine_hit = jnp.exp(picked - peak)
        lse = peak + jnp.log(rest + mine_hit)
        missing = rest / (rest + mine_hit)
        dlogits = jnp.where(hit, -missing[:, None], jnp.exp(logits - lse[:, None])) * t_weight[:, None]
        dlogits = dlogits.astype(BF)
        dtokens = nn(dlogits, vocab)
        for step in range(len(chip_bits)):
            half = dtokens.shape[0] // 2
            dtokens = dtokens[:half] + swap_chip(dtokens[half:].astype(BF), step).astype(F32)
        back = lax.ppermute(dtokens.astype(BF), "pass", [(0, 2), (1, 3)]).astype(F32)
        token_live = (section >= 2).astype(F32)
        token_final = (dtokens + back) * token_live
        token_loss = jnp.sum(token_live * weight * (lse - picked)[:count])

        dvocab = tn(dlogits, tokens)
        half = 2 * shard
        dpair = dvocab[:half] + swap_core(dvocab[half:].astype(BF)).astype(F32)
        token_grad = dpair[:shard] + swap_pass(dpair[shard:].astype(BF), 1).astype(F32)

        joined = jnp.concatenate([segs[1:] == segs[:-1], jnp.zeros((1,), bool)], axis=0)[:, None]
        after = jnp.concatenate([final[1:], jnp.zeros((1, width), BF)], axis=0)
        after = jnp.where(joined, after, jnp.zeros((), BF))
        both = jnp.concatenate([final, after], axis=1)
        delete_loss, ddelete = entropy(
            nn(final, delete_head), labels % 2, weight * (section == 0).astype(F32)
        )
        insert_loss, dinsert = entropy(
            nn(both, insert_head), labels % INS, weight * (section == 1).astype(F32)
        )
        g_delete = tn(final, ddelete)
        g_insert = tn(both, dinsert)
        dboth = nt(dinsert, insert_head)
        dafter = jnp.where(joined, dboth[:, width:], 0.0)
        dafter = jnp.concatenate([jnp.zeros((1, width), F32), dafter[:-1]], axis=0)
        dfinal = token_final + nt(ddelete, delete_head) + dboth[:, :width] + dafter
        row_loss = (token_loss + delete_loss + insert_loss).reshape(1, 1)

        dthird, g_gain3, g_bias3 = norm_bwd(dfinal, unit3, rstd3, gains[3])
        g_out = tn(hidden, dthird)
        dhidden = nt(dthird, ffn_out).astype(BF).astype(F32)
        slope = cdf + inner * jnp.exp(-0.5 * inner * inner) * 0.3989422804014327
        dinner = (dhidden * slope).astype(BF)
        g_in = tn(a3, dinner)
        back2, g_gain2, g_bias2 = norm_bwd(nt(dinner, ffn_in), unit2, rstd2, gains[2])
        dsecond = dthird + back2
        g_cross = tn(ctx2, dsecond)
        dq2, dk2, dv2 = attend_bwd(nt(dsecond, cross_out).astype(BF), q2, k2, v2, probs2)
        dkeyval = jnp.concatenate([dk2, dv2], axis=1)
        g_kv = tn(source, dkeyval)
        dsource = nt(dkeyval, cross_kv)
        g_query = tn(a2, dq2)
        back1, g_gain1, g_bias1 = norm_bwd(nt(dq2, cross_query), unit1, rstd1, gains[1])
        dfirst = dsecond + back1
        g_self = tn(ctx1, dfirst)
        dq1, dk1, dv1 = attend_bwd(nt(dfirst, self_out).astype(BF), q1, k1, v1, probs1)
        dqkv = jnp.concatenate([dq1, dk1, dv1], axis=1)
        g_qkv = tn(a1, dqkv)
        back0, g_gain0, g_bias0 = norm_bwd(nt(dqkv, self_qkv), unit0, rstd0, gains[0])
        input_grad = dfirst + back0

        dparts = dsource.reshape(n_pass, part, width)
        source_grad = dparts[0]
        for bit in (1, 2, 3):
            source_grad = source_grad + swap_pass(dparts[bit].astype(BF), bit).astype(F32)

        def by_owner(values):
            return values.reshape(n_dp, -1, width)

        def reduced(group):
            packed = [by_owner(v) for v in group]
            total = reduce_pass(reduce_dp(jnp.concatenate(packed, axis=1)))
            out, at = [], 0
            for v, p in zip(group, packed):
                out.append(total[at : at + p.shape[1]].reshape(v.shape[0] // n_dp, v.shape[1]))
                at += p.shape[1]
            return out

        p_in, p_out, p_insert = reduced([g_in, g_out, g_insert])
        p_cross, p_kv, p_query = reduced([g_cross, g_kv, g_query])
        small = jnp.stack(
            [g_gain0, g_gain1, g_gain2, g_gain3, g_bias0, g_bias1, g_bias2, g_bias3], axis=1
        )
        small = jnp.concatenate([small, g_delete], axis=1)
        small = jnp.pad(small, ((0, 0), (0, 16 * width * n_dp // width - small.shape[1])))
        p_qkv, p_self, p_small = reduced([g_qkv, g_self, small])
        p_gain, p_bias, p_delete = p_small[:, :4].T, p_small[:, 4:8].T, p_small[:, 8:10]
        return (
            third.astype(BF)[None, None],
            row_loss,
            input_grad[None, None],
            source_grad[None],
            p_gain,
            p_bias,
            p_qkv,
            p_self,
            p_query,
            p_kv,
            p_cross,
            p_in,
            p_out,
            p_delete,
            p_insert,
            token_grad,
        )

    full = ("pass", "dp")
    rows_at, row_at = P("pass", "dp", None, None), P("pass", "dp", None)
    weight_at = P("dp", None)
    return jax.shard_map(
        body,
        mesh=mesh,
        in_specs=(rows_at, row_at, row_at, row_at, P("dp", "pass", None), P("dp", "pass"))
        + (P(),) * 11
        + (P(full, None),),
        out_specs=(rows_at, P("pass", "dp"), rows_at, P("dp", "pass", None), P(None, "dp"), P(None, "dp"))
        + (weight_at,) * 9
        + (P(full, None),),
        check_vma=False,
    )
```

```python
import functools

import jax
import jax.numpy as jnp
from jax import lax
from jax.experimental import pallas as pl
from jax.experimental.pallas import tpu as pltpu
from jax.sharding import PartitionSpec as P

HEADS = 8
INS = 256
EPS = 1e-05
LANES = 128
EXTRA = 16
BF = jnp.bfloat16
F32 = jnp.float32
MIB = 1 << 20


def dot(left, right, dims):
    return lax.dot_general(left, right, (dims, ((), ())), preferred_element_type=F32)


def nn(left, right):
    return dot(left, right, ((1,), (0,)))


def nt(left, right):
    return dot(left, right, ((1,), (1,)))


def flip(values):
    return values.astype(F32).T.astype(BF)


def run(kernel, outs, ins, flops, limit, scratch=(), name=None):
    whole = pl.BlockSpec(memory_space=pltpu.VMEM)
    moved = sum(x.size * x.dtype.itemsize for x in list(ins) + list(outs))
    return pl.pallas_call(
        kernel,
        out_shape=outs,
        in_specs=[whole] * len(ins),
        out_specs=[whole] * len(outs),
        scratch_shapes=scratch,
        compiler_params=pltpu.CompilerParams(vmem_limit_bytes=limit * MIB),
        cost_estimate=pl.CostEstimate(flops=int(flops), bytes_accessed=moved, transcendentals=0),
        name=name,
    )(*ins)


def like(shape, dtype):
    return jax.ShapeDtypeStruct(shape, dtype)


def norm_parts(values):
    center = values - jnp.mean(values, axis=-1, keepdims=True)
    rstd = lax.rsqrt(jnp.mean(center * center, axis=-1, keepdims=True) + EPS)
    return center * rstd, rstd


def norm_out(unit, gain, shift, index):
    return (unit * gain[index : index + 1] + shift[index : index + 1]).astype(BF)


def norm_bwd(grad, unit, rstd, gain):
    scaled = grad * gain
    back = rstd * (
        scaled
        - jnp.mean(scaled, axis=-1, keepdims=True)
        - unit * jnp.mean(scaled * unit, axis=-1, keepdims=True)
    )
    return back, jnp.sum(grad * unit, axis=0, keepdims=True), jnp.sum(grad, axis=0, keepdims=True)


def column(row, count):
    return jnp.broadcast_to(row, (count, row.shape[1])).T


def lane_half(values, half):
    lane = lax.broadcasted_iota(jnp.int32, values.shape, 1)
    picked = (lane >= LANES // 2) if half else (lane < LANES // 2)
    return jnp.where(picked, values, jnp.zeros_like(values))


def attend(query, keys, values, bias_ref, probs_ref, out_ref, scale):
    half_size = LANES // 2
    for tile in range(out_ref.shape[1] // LANES):
        q = query(tile).astype(F32) * scale
        k, v_t = keys(tile), flip(values(tile))
        parts = []
        for half in range(2):
            scores = nt(k, lane_half(q, half).astype(BF)) + bias_ref[...]
            expo = jnp.exp(scores - jnp.max(scores, axis=0, keepdims=True))
            probs = (expo * (1.0 / jnp.sum(expo, axis=0, keepdims=True))).astype(BF)
            probs_ref[2 * tile + half] = probs
            parts.append(nn(v_t[half * half_size : (half + 1) * half_size], probs))
        out_ref[:, tile * LANES : (tile + 1) * LANES] = jnp.concatenate(parts, axis=0).T.astype(BF)


def attend_bwd(grad, query, keys, values, probs_ref, put_query, put_keys, put_values, scale, tiles):
    half_size = LANES // 2
    for tile in range(tiles):
        g, q, k, v = grad(tile), query(tile), keys(tile), values(tile)
        k_t = flip(k)
        dq, dk, dv = [], [], []
        for half in range(2):
            probs = probs_ref[2 * tile + half]
            full = probs.astype(F32)
            dprobs = nt(v, lane_half(g, half))
            delta = jnp.sum(dprobs * full, axis=0, keepdims=True)
            dscores = (full * ((dprobs - delta) * scale)).astype(BF)
            dv.append(nn(probs, g))
            dk.append(nn(dscores, q))
            dq.append(nn(k_t[half * half_size : (half + 1) * half_size], dscores))
        lane = lax.broadcasted_iota(jnp.int32, dk[0].shape, 1) < half_size
        put_query(tile, jnp.concatenate(dq, axis=0).T.astype(BF))
        put_keys(tile, jnp.where(lane, dk[0], dk[1]).astype(BF))
        put_values(tile, jnp.where(lane, dv[0], dv[1]).astype(BF))


def tile_of(ref, start):
    return lambda tile: ref[:, start + tile * LANES : start + (tile + 1) * LANES]


def put_in(ref, start):
    def put(tile, value):
        ref[:, start + tile * LANES : start + (tile + 1) * LANES] = value

    return put


def solution(mesh):
    n_pass, n_dp = mesh.shape["pass"], mesh.shape["dp"]
    bits = [1 << i for i in range(n_dp.bit_length() - 1)]
    core_bit, chip_bits = bits[0], bits[1:]
    orders = (chip_bits, chip_bits[1::-1] + chip_bits[2:])
    n_steps = len(chip_bits)
    n_half = n_dp // 2

    def swap_core(x):
        return lax.ppermute(x, "dp", [(i, i ^ core_bit) for i in range(n_dp)])

    def swap_chip(x, step):
        return lax.ppermute(x, "dp", [(i, i ^ orders[i & 1][step]) for i in range(n_dp)])

    def swap_pass(x, bit):
        return lax.ppermute(x, "pass", [(i, i ^ bit) for i in range(n_pass)])

    def owners():
        me = lax.axis_index("dp")
        core = me & 1
        result = []
        for slot in range(n_dp):
            own_half = slot < n_half
            turn = core if own_half else 1 - core
            owner = me if own_half else me ^ 1
            for step in range(n_steps):
                if (slot >> (n_steps - 1 - step)) & 1:
                    owner = owner ^ jnp.where(turn == 0, orders[0][step], orders[1][step])
            result.append(owner)
        return result

    def small_dtype(rows):
        return BF if rows % 16 == 0 else F32

    def turn_rows(values, turned_ref, sorted_ref, owner_list):
        block = values.shape[1] // n_dp
        turned_ref[...] = values.astype(F32).T.astype(turned_ref.dtype)
        for slot, owner in enumerate(owner_list):
            start = pl.multiple_of(owner * block, block)
            sorted_ref[slot * block : (slot + 1) * block] = turned_ref[pl.ds(start, block)]
        return sorted_ref[...].astype(BF)

    def turn_scratch(features, count):
        dtype = small_dtype(features // n_dp)
        return [pltpu.VMEM((features, count), dtype)] * 2

    def pack(keep_ref, send_ref, at, left_t, right):
        width = keep_ref.shape[2]
        block = left_t.shape[0] // n_dp
        for col in range(right.shape[1] // width):
            grad = nn(left_t, right[:, col * width : (col + 1) * width]).astype(keep_ref.dtype)
            for slot in range(n_dp):
                ref, index = (keep_ref, slot) if slot < n_half else (send_ref, slot - n_half)
                ref[index, at : at + block] = grad[slot * block : (slot + 1) * block]
            at += block
        return at


    def self_kernel(x, seg, gain, shift, w_qkv, w_out, w_query, first, qkv, probs, ctx, query, bias):
        width = x.shape[1]
        gains, shifts = gain[...].astype(F32), shift[...].astype(F32)
        rows = x[...].astype(F32)
        unit, _ = norm_parts(rows)
        qkv[...] = nn(norm_out(unit, gains, shifts, 0), w_qkv[...]).astype(BF)
        seg_row = seg[...].astype(F32)
        bias[...] = jnp.where(column(seg_row, seg_row.shape[1]) == seg_row, 0.0, -1000000000.0)
        attend(
            tile_of(qkv, 0), tile_of(qkv, width), tile_of(qkv, 2 * width), bias, probs, ctx, (width // HEADS) ** -0.5
        )
        after = rows + nn(ctx[...], w_out[...])
        first[...] = after
        unit, _ = norm_parts(after)
        query[...] = nn(norm_out(unit, gains, shifts, 1), w_query[...]).astype(BF)

    def cross_kernel(
        first, query, seg, labels, mask, part0, part1, part2, part3, gain, shift, w_kv, w_out, w_in, w_ffn,
        second, keyval, probs, ctx, hidden, slope, third, layer, final, bias,
    ):
        width = first.shape[1]
        count = first.shape[0]
        gains, shifts = gain[...].astype(F32), shift[...].astype(F32)
        seg_row = seg[...].astype(F32)
        size = part0.shape[0] - EXTRA
        for index, part in enumerate((part0, part1, part2, part3)):
            span = slice(index * size, (index + 1) * size)
            keyval[span] = nn(part[:size], w_kv[...]).astype(BF)
            source_seg = part[size : size + EXTRA, :size].astype(F32)[0:1]
            bias[span] = jnp.where(column(source_seg, count) == seg_row, 0.0, -1000000000.0)
        attend(
            tile_of(query, 0), tile_of(keyval, 0), tile_of(keyval, width), bias, probs, ctx, (width // HEADS) ** -0.5
        )
        after = first[...] + nn(ctx[...], w_out[...])
        second[...] = after
        unit, _ = norm_parts(after)
        normed = norm_out(unit, gains, shifts, 2)
        for col in range(w_in.shape[1] // width):
            span = slice(col * width, (col + 1) * width)
            inner = nn(normed, w_in[:, span])
            cdf = 0.5 * (1.0 + lax.erf(inner * 0.7071067811865476))
            hidden[:, span] = (inner * cdf).astype(BF)
            slope[:, span] = (cdf + inner * jnp.exp(-0.5 * inner * inner) * 0.3989422804014327).astype(BF)
        after = after + nn(hidden[...], w_ffn[...])
        third[...] = after
        layer[...] = after.astype(BF)
        unit, _ = norm_parts(after)
        final[:count] = norm_out(unit, gains, shifts, 3)
        label = labels[...]
        line = lax.broadcasted_iota(jnp.int32, (EXTRA, count), 0)
        high = lax.shift_right_logical(label, 8).astype(F32)
        marks = jnp.where(line == 0, high, 0.0)
        marks = jnp.where(line == 1, (label & 255).astype(F32), marks)
        marks = jnp.where(line == 2, mask[...].astype(F32), marks)
        final[count:] = jnp.concatenate([marks, jnp.zeros((EXTRA, width - count), F32)], axis=1).astype(BF)

    def head_kernel(
        final, seg, labels, mask, w_delete, w_insert,
        dfinal, keep, send, d_delete, loss, turned, ordered,
    ):
        section = lax.axis_index("pass")
        count = seg.shape[1]
        width = final.shape[1]
        h = final[:count]
        h32 = h.astype(F32)
        seg_col = column(seg[...].astype(F32), LANES)
        row_id = lax.broadcasted_iota(jnp.int32, (count, LANES), 0)
        linked = (pltpu.roll(seg_col, count - 1, 0) == seg_col) & (row_id < count - 1)
        linked = jnp.concatenate([linked.astype(F32)] * (width // LANES), axis=1)
        after = (pltpu.roll(h32, count - 1, 0) * linked).astype(BF)
        weight = column(mask[...].astype(F32), LANES)

        def entropy(logits, label, live):
            top = jnp.max(logits, axis=-1, keepdims=True)
            expo = jnp.exp(logits - top)
            total = jnp.sum(expo, axis=-1, keepdims=True)
            lane = lax.broadcasted_iota(jnp.int32, logits.shape, 1)
            target = column(label.astype(F32), logits.shape[1])
            hit = lane.astype(F32) == target
            picked = jnp.sum(jnp.where(hit, logits, 0.0), axis=1, keepdims=True)
            w = weight[:, :1] * live
            rest = jnp.sum(jnp.where(hit, 0.0, expo), axis=1, keepdims=True)
            grad = jnp.where(hit, -rest, expo) * (w / total)
            return jnp.sum(w * (top + jnp.log(total) - picked)), grad.astype(BF)

        label = labels[...]
        logits = nn(h, w_delete[...])
        lane = lax.broadcasted_iota(jnp.int32, logits.shape, 1)
        logits = jnp.where(lane < 2, logits, -1e30)
        loss_d, grad_d = entropy(logits, lax.rem(label, 2), (section == 0).astype(F32))
        logits = nn(h, w_insert[:width]) + nn(after, w_insert[width:])
        loss_i, grad_i = entropy(logits, lax.rem(label, INS), (section == 1).astype(F32))
        loss[...] = jnp.full(loss.shape, loss_d + loss_i)
        d_after = nt(grad_i, w_insert[width:]) * linked
        dfinal[...] = nt(grad_d, w_delete[...]) + nt(grad_i, w_insert[:width]) + pltpu.roll(d_after, 1, 0)
        d_delete[...] = nn(flip(grad_d)[:EXTRA], h)[: d_delete.shape[0]]
        both_t = turn_rows(jnp.concatenate([h, after], axis=1), turned, ordered, owners())
        grad = nn(both_t, grad_i).astype(keep.dtype)
        block = both_t.shape[0] // n_dp
        half = block // 2
        for slot in range(n_dp):
            ref, index = (keep, slot) if slot < n_half else (send, slot - n_half)
            ref[index, :, :INS] = grad[slot * block : slot * block + half]
            ref[index, :, INS:] = grad[slot * block + half : (slot + 1) * block]


    def shard_base(chunk, shard):
        section, me = lax.axis_index("pass"), lax.axis_index("dp")
        return ((section ^ (chunk & 1)) * n_dp + (me ^ (chunk >> 1))) * shard

    def hits(base, start, shape, label):
        ids = lax.broadcasted_iota(jnp.int32, shape, 0) + (base + start)
        return ids == label

    def logit_kernel(shard, n_prev, tokens, own, near, pair, *rest):
        prev, (stats, expo, logits) = rest[:-3], rest[-3:]
        count = tokens.shape[1] - EXTRA
        index = pl.program_id(0)
        if n_prev:

            @pl.when(index == 0)
            def _():
                stats[:, : n_prev * count] = prev[0][...]

        h = tokens[0, :count]
        marks = tokens[0, count:].astype(F32)
        label_f = marks[0:1, :count] * 256.0 + marks[1:2, :count]
        label = label_f.astype(jnp.int32)
        weight = marks[2:3, :count]
        step = min(shard, 256)
        peak = jnp.full((8, count), -jnp.inf, F32)
        for chunk, (ref, at) in enumerate(((own, 0), (near, 0), (pair, 0), (pair, shard))):
            for start in range(0, shard, step):
                value = nt(ref[at + start : at + start + step], h)
                logits[chunk * shard + start : chunk * shard + start + step] = value
                peak = jnp.maximum(peak, jnp.max(value.reshape(step // 8, 8, count), axis=0))
        peak = jnp.max(peak, axis=0, keepdims=True)
        total = jnp.zeros((8, count), F32)
        chosen = jnp.zeros((8, count), F32)
        sub = min(shard, 128)
        for chunk in range(4):
            base = shard_base(chunk, shard)

            def part(i, carry, chunk=chunk, base=base):
                total, chosen = carry
                at = pl.multiple_of(chunk * shard + i * sub, sub)
                value = logits[pl.ds(at, sub)]
                hit = hits(base, i * sub, (sub, count), label)
                weight_of = jnp.where(hit, 0.0, jnp.exp(value - peak))
                expo[0, pl.ds(at, sub)] = weight_of.astype(BF)
                total = total + jnp.sum(weight_of.reshape(sub // 8, 8, count), axis=0)
                picked = jnp.where(hit, value, 0.0)
                return total, chosen + jnp.sum(picked.reshape(sub // 8, 8, count), axis=0)

            total, chosen = lax.fori_loop(0, shard // sub, part, (total, chosen))
        total = jnp.sum(total, axis=0, keepdims=True)
        chosen = jnp.sum(chosen, axis=0, keepdims=True)
        line = lax.broadcasted_iota(jnp.int32, (8, count), 0)
        block = jnp.zeros((8, count), F32)
        for at, value in enumerate((peak, total, chosen, label_f, weight)):
            block = jnp.where(line == at, value, block)
        stats[:, pl.ds(pl.multiple_of((n_prev + index) * count, count), count)] = block

    def logit_call(tokens, vocab, prev):
        n, height, width = tokens.shape
        count = height - EXTRA
        shard = vocab[0].shape[0]
        n_prev = prev[0].shape[1] // count if prev else 0
        fixed = [pl.BlockSpec(v.shape, lambda t: (0, 0)) for v in tuple(vocab) + tuple(prev)]
        total = (n_prev + n) * count
        return pl.pallas_call(
            functools.partial(logit_kernel, shard, n_prev),
            grid=(n,),
            in_specs=[pl.BlockSpec((1, height, width), lambda t: (t, 0, 0))] + fixed,
            out_specs=[
                pl.BlockSpec((8, total), lambda t: (0, 0)),
                pl.BlockSpec((1, 4 * shard, count), lambda t: (t, 0, 0)),
            ],
            out_shape=[like((8, total), F32), like((n, 4 * shard, count), BF)],
            scratch_shapes=[pltpu.VMEM((4 * shard, count), F32)],
            compiler_params=pltpu.CompilerParams(vmem_limit_bytes=32 * MIB),
            cost_estimate=pl.CostEstimate(
                flops=n * 8 * shard * count * width * 2, bytes_accessed=12 * shard * width, transcendentals=0
            ),
            name="token_logits",
        )(tokens, *vocab, *prev)

    def merged(own, other):
        peak = jnp.maximum(own[0:1], other[0:1])
        total = own[1:2] * jnp.exp(own[0:1] - peak) + other[1:2] * jnp.exp(other[0:1] - peak)
        return peak, total, own[2:3] + other[2:3]

    def merge_kernel(step, own, other, out):
        size = own.shape[1] >> (step + 1)
        blocks = [other[:, i * size : (i + 1) * size] for i in range(2 << step)]
        swapped = jnp.concatenate([blocks[i ^ 1] for i in range(2 << step)], axis=1)
        mine = own[...]
        peak, total, chosen = merged(mine, swapped)
        line = lax.broadcasted_iota(jnp.int32, mine.shape, 0)
        out[...] = jnp.where(
            line == 0, peak, jnp.where(line == 1, total, jnp.where(line == 2, chosen, mine))
        )

    def closing(local, merged_ref, other):
        peak, total, chosen = merged(merged_ref[...], other[...])
        hit = jnp.exp(chosen - peak)
        full = total + hit
        lse = peak + jnp.log(full)
        weight = local[4:5]
        factor = weight * jnp.exp(local[0:1] - lse)
        return lse, chosen, factor, -weight * (total / full)

    def dlogits_into(ref, at, cols, expo, start, base, shape, label, factor, at_label):
        sub = min(shape[0], 128)

        def part(i, _):
            row = pl.multiple_of(i * sub, sub)
            hit = hits(base, i * sub, (sub, shape[1]), label)
            value = expo[pl.ds(pl.multiple_of(start + row, sub), sub)].astype(F32) * factor
            ref[pl.ds(pl.multiple_of(at + row, sub), sub), cols] = jnp.where(hit, at_label, value).astype(BF)
            return 0

        lax.fori_loop(0, shape[0] // sub, part, 0)

    def dtoken_kernel(shard, expo, local, merged_ref, other, vocab_t, out, dlogits):
        _, _, factor, at_label = closing(local, merged_ref, other)
        label = local[3:4].astype(jnp.int32)
        count = local.shape[1]
        for chunk in range(4):
            dlogits_into(
                dlogits, chunk * shard, slice(None), expo.at[0], chunk * shard, shard_base(chunk, shard),
                (shard, count), label, factor, at_label,
            )
        out[0] = nn(vocab_t[...], dlogits[...]).T.astype(out.dtype)

    def dtoken_call(expo, first, local, merged_ref, other, vocab_t, dtype):
        n, rows, count = expo.shape
        width = vocab_t.shape[0]
        line = pl.BlockSpec((8, count), lambda t: (0, first + t))
        return pl.pallas_call(
            functools.partial(dtoken_kernel, rows // 4),
            grid=(n,),
            in_specs=[pl.BlockSpec((1, rows, count), lambda t: (t, 0, 0)), line, line, line]
            + [pl.BlockSpec(vocab_t.shape, lambda t: (0, 0))],
            out_specs=pl.BlockSpec((1, count, width), lambda t: (t, 0, 0)),
            out_shape=like((n, count, width), dtype),
            scratch_shapes=[pltpu.VMEM((rows, count), BF)],
            compiler_params=pltpu.CompilerParams(vmem_limit_bytes=24 * MIB),
            cost_estimate=pl.CostEstimate(
                flops=n * 2 * rows * count * width, bytes_accessed=rows * (n * count + width) * 2, transcendentals=0
            ),
            name="token_dfinal",
        )(expo, local, merged_ref, other, vocab_t)

    def dvocab_kernel(shard, chunk0, n_pieces, *refs):
        expos, tokens = refs[:n_pieces], refs[n_pieces : 2 * n_pieces]
        local, merged_ref, other, out, dlogits, held = refs[2 * n_pieces :]
        index = pl.program_id(0)
        _, _, factor, at_label = closing(local, merged_ref, other)
        label = local[3:4].astype(jnp.int32)
        count = tokens[0].shape[1] - EXTRA
        section, me = lax.axis_index("pass"), lax.axis_index("dp")
        chunk = chunk0 + index
        base = ((section ^ (chunk & 1)) * n_dp + (me ^ (chunk >> 1))) * shard
        at = 0
        for expo, token in zip(expos, tokens):
            for i in range(token.shape[0]):
                cols = slice(at, at + count)
                held[cols] = token[i, :count]
                dlogits_into(
                    dlogits, 0, cols, expo.at[i], 0, base, (shard, count), label[:, cols], factor[:, cols],
                    at_label[:, cols],
                )
                at += count
        out[...] = nn(dlogits[...], held[...]).astype(out.dtype)

    def dvocab_call(expos, tokens, local, merged_ref, other, chunk0, dtype):
        shard = expos[0].shape[1] // 4
        count = expos[0].shape[2]
        width = tokens[0].shape[2]
        total = local.shape[1]
        fixed2 = pl.BlockSpec(local.shape, lambda c: (0, 0))
        return pl.pallas_call(
            functools.partial(dvocab_kernel, shard, chunk0, len(expos)),
            grid=(2,),
            in_specs=[pl.BlockSpec((e.shape[0], shard, count), lambda c: (0, chunk0 + c, 0)) for e in expos]
            + [pl.BlockSpec(t.shape, lambda c: (0, 0, 0)) for t in tokens]
            + [fixed2] * 3,
            out_specs=pl.BlockSpec((shard, width), lambda c: (c, 0)),
            out_shape=like((2 * shard, width), dtype),
            scratch_shapes=[pltpu.VMEM((shard, total), BF), pltpu.VMEM((total, width), BF)],
            compiler_params=pltpu.CompilerParams(vmem_limit_bytes=32 * MIB),
            cost_estimate=pl.CostEstimate(
                flops=4 * shard * total * width, bytes_accessed=4 * shard * total, transcendentals=0
            ),
            name="token_dvocab",
        )(*expos, *tokens, local, merged_ref, other)

    def turn_kernel(own, near, pair, out):
        shard = own.shape[0]
        out[:, :shard] = flip(own[...])
        out[:, shard : 2 * shard] = flip(near[...])
        out[:, 2 * shard :] = flip(pair[...])


    def ffn_back_kernel(
        third, second, kept, moved, dhead, head_loss, local, merged_ref, other, gain, shift, hidden, slope, w_in, w_ffn,
        ins_keep, ins_send,
        dthird, dsecond, keep, send, vecs, loss, wide_t, wide_s, thin_t, thin_s, dinner,
    ):
        width = third.shape[1]
        count = third.shape[0]
        gains, shifts = gain[...].astype(F32), shift[...].astype(F32)
        live = (lax.axis_index("pass") >= 2).astype(F32)
        lse, chosen, _, _ = closing(local, merged_ref, other)
        token_loss = jnp.sum(local[4:5] * (lse - chosen)) * live
        loss[...] = head_loss[...] + token_loss
        owner_list = owners()
        hidden_t = turn_rows(hidden[...], wide_t, wide_s, owner_list)
        unit2, rstd2 = norm_parts(second[...])
        normed_t = turn_rows(norm_out(unit2, gains, shifts, 2), thin_t, thin_s, owner_list)
        dfinal = dhead[...] + live * (kept[...] + moved[...].astype(F32))
        unit3, rstd3 = norm_parts(third[...])
        back, g_gain3, g_bias3 = norm_bwd(dfinal, unit3, rstd3, gains[3:4])
        dthird[...] = back
        low = back.astype(BF)
        at = pack(keep, send, 0, hidden_t, low)
        for col in range(w_in.shape[1] // width):
            span = slice(col * width, (col + 1) * width)
            part = nt(low, w_ffn[span]).astype(BF).astype(F32) * slope[:, span].astype(F32)
            dinner[:, span] = part.astype(BF)
        at = pack(keep, send, at, normed_t, dinner[...])
        keep[:, at:] = ins_keep[...]
        send[:, at:] = ins_send[...]
        dnormed = nt(dinner[...], w_in[...])
        back, g_gain2, g_bias2 = norm_bwd(dnormed, unit2, rstd2, gains[2:3])
        dsecond[...] = dthird[...] + back
        line = lax.broadcasted_iota(jnp.int32, (8, width), 0)
        block = jnp.zeros((8, width), F32)
        for at, value in enumerate((g_gain3, g_gain2, g_bias3, g_bias2)):
            block = jnp.where(line == at, value, block)
        vecs[...] = block

    def cross_back_kernel(
        dsecond, first, query, keyval, probs, ctx, part0, part1, part2, part3, gain, shift, w_out, w_kv, w_query,
        dfirst, keep, send, vecs, dsrc0, dsrc1, dsrc2, dsrc3, thin_t, thin_s, src_t, src_s, dquery, dkeyval, dctx,
    ):
        width = first.shape[1]
        gains, shifts = gain[...].astype(F32), shift[...].astype(F32)
        owner_list = owners()
        low = dsecond[...].astype(BF)
        dctx[...] = nt(low, w_out[...]).astype(BF)
        at = pack(keep, send, 0, turn_rows(ctx[...], thin_t, thin_s, owner_list), low)
        attend_bwd(
            tile_of(dctx, 0), tile_of(query, 0), tile_of(keyval, 0), tile_of(keyval, width), probs,
            put_in(dquery, 0), put_in(dkeyval, 0), put_in(dkeyval, width), (width // HEADS) ** -0.5, width // LANES,
        )
        size = part0.shape[0] - EXTRA
        source = jnp.concatenate([p[:size] for p in (part0, part1, part2, part3)], axis=0)
        at = pack(keep, send, at, turn_rows(source, src_t, src_s, owner_list), dkeyval[...])
        for index, ref in enumerate((dsrc0, dsrc1, dsrc2, dsrc3)):
            ref[...] = nt(dkeyval[index * size : (index + 1) * size], w_kv[...]).astype(ref.dtype)
        unit, rstd = norm_parts(first[...])
        normed_t = turn_rows(norm_out(unit, gains, shifts, 1), thin_t, thin_s, owner_list)
        pack(keep, send, at, normed_t, dquery[...])
        back, g_gain, g_bias = norm_bwd(nt(dquery[...], w_query[...]), unit, rstd, gains[1:2])
        dfirst[...] = dsecond[...] + back
        line = lax.broadcasted_iota(jnp.int32, (8, width), 0)
        vecs[...] = jnp.where(line == 0, g_gain, jnp.where(line == 1, g_bias, 0.0))

    def self_back_kernel(
        dfirst, x, qkv, probs, ctx, gain, shift, w_qkv, w_out, vec_ffn, vec_cross, d_delete,
        dx, keep, send, thin_t, thin_s, dqkv, dctx,
    ):
        width = x.shape[1]
        gains, shifts = gain[...].astype(F32), shift[...].astype(F32)
        owner_list = owners()
        low = dfirst[...].astype(BF)
        dctx[...] = nt(low, w_out[...]).astype(BF)
        at = pack(keep, send, 0, turn_rows(ctx[...], thin_t, thin_s, owner_list), low)
        attend_bwd(
            tile_of(dctx, 0), tile_of(qkv, 0), tile_of(qkv, width), tile_of(qkv, 2 * width), probs,
            put_in(dqkv, 0), put_in(dqkv, width), put_in(dqkv, 2 * width), (width // HEADS) ** -0.5, width // LANES,
        )
        unit, rstd = norm_parts(x[...].astype(F32))
        normed_t = turn_rows(norm_out(unit, gains, shifts, 0), thin_t, thin_s, owner_list)
        at = pack(keep, send, at, normed_t, dqkv[...])
        back, g_gain, g_bias = norm_bwd(nt(dqkv[...], w_qkv[...]), unit, rstd, gains[0:1])
        dx[...] = dfirst[...] + back
        line = lax.broadcasted_iota(jnp.int32, (EXTRA, width), 0)
        block = jnp.zeros((EXTRA, width), F32)
        lines = (
            (0, d_delete[0:1]), (1, d_delete[1:2]),
            (8, g_gain), (9, vec_cross[0:1]), (10, vec_ffn[1:2]), (11, vec_ffn[0:1]),
            (12, g_bias), (13, vec_cross[1:2]), (14, vec_ffn[3:4]), (15, vec_ffn[2:3]),
        )
        for row, value in lines:
            block = jnp.where(line == row, value, block)
        block = block.astype(keep.dtype)
        for slot in range(n_half):
            keep[slot, at:] = block
            send[slot, at:] = block


    def spread_out(total, at, ref):
        rows, width = ref.shape[0], total.shape[1]
        for col in range(max(1, ref.shape[1] // width)):
            ref[:, col * width : (col + 1) * width] = total[at : at + rows]
            at += rows
        return at

    def ffn_end_kernel(own, other, p_out, p_in, p_insert):
        total = own[...].astype(F32) + other[...].astype(F32)
        at = spread_out(total, 0, p_out)
        at = spread_out(total, at, p_in)
        half = p_insert.shape[0] // 2
        p_insert[:half] = total[at : at + half, :INS]
        p_insert[half:] = total[at : at + half, INS:]

    def cross_end_kernel(own, other, p_out, p_kv, p_query):
        total = own[...].astype(F32) + other[...].astype(F32)
        at = spread_out(total, 0, p_out)
        at = spread_out(total, at, p_kv)
        spread_out(total, at, p_query)

    def self_end_kernel(own, other, p_out, p_qkv, p_gain, p_bias, p_delete):
        total = own[...].astype(F32) + other[...].astype(F32)
        at = spread_out(total, 0, p_out)
        at = spread_out(total, at, p_qkv)
        width = total.shape[1]
        size = p_gain.shape[1]
        me = lax.axis_index("dp")
        mine = pltpu.roll(total[at : at + EXTRA], lax.rem(width - me * size, width), 1)
        p_gain[...] = mine[8:12, :size]
        p_bias[...] = mine[12:16, :size]
        p_delete[...] = mine[:, :LANES].T[:size, :2]

    def reduce_dp(keep, send):
        half = n_half
        keep = keep.astype(F32) + swap_core(send.astype(BF)).astype(F32)
        for step in range(n_steps):
            half = half // 2
            keep = keep[:half] + swap_chip(keep[half:].astype(BF), step).astype(F32)
        return keep[0]

    def reduce_pass(values):
        pair = values + swap_pass(values.astype(BF), 1).astype(F32)
        pair = pair.astype(BF)
        return pair, swap_pass(pair, 2)

    def body(
        decoder_in,
        decoder_segments,
        edit_target,
        loss_mask,
        source_out,
        source_segments,
        norm_gain,
        norm_bias,
        self_qkv,
        self_out,
        cross_query,
        cross_kv,
        cross_out,
        ffn_in,
        ffn_out,
        delete_head,
        insert_head,
        token_head,
    ):
        section = lax.axis_index("pass")
        segs, labels, mask = decoder_segments[0], edit_target[0], loss_mask[0]
        rows = decoder_in[0, 0]
        count, width = rows.shape
        shard = token_head.shape[0]
        part = source_out.shape[1]
        src = n_pass * part
        hid = ffn_in.shape[1]
        unit = width // n_dp
        wire = small_dtype(unit)
        macs = count * width * width

        note = jnp.pad(source_segments.astype(BF), ((0, EXTRA - 1), (0, width - part)))
        mine = jnp.concatenate([source_out[0], note], axis=0)
        parts = [mine] + [swap_pass(mine, bit) for bit in (1, 2, 3)]

        first, qkv, probs1, ctx1, query = run(
            self_kernel,
            [
                like((count, width), F32),
                like((count, 3 * width), BF),
                like((HEADS, count, count), BF),
                like((count, width), BF),
                like((count, width), BF),
            ],
            [rows, segs, norm_gain, norm_bias, self_qkv, self_out, cross_query],
            14 * macs,
            24,
            [pltpu.VMEM((count, count), F32)],
            "self_forward",
        )
        second, keyval, probs2, ctx2, hidden, slope, third, layer, final = run(
            cross_kernel,
            [
                like((count, width), F32),
                like((src, 2 * width), BF),
                like((HEADS, src, count), BF),
                like((count, width), BF),
                like((count, hid), BF),
                like((count, hid), BF),
                like((count, width), F32),
                like((count, width), BF),
                like((count + EXTRA, width), BF),
            ],
            [first, query, segs, labels, mask, *parts, norm_gain, norm_bias, cross_kv, cross_out, ffn_in, ffn_out],
            40 * macs,
            40,
            [pltpu.VMEM((src, count), F32)],
            "cross_forward",
        )

        near = swap_pass(token_head, 1)
        pair = swap_core(jnp.concatenate([token_head, near], axis=0))
        vocab = (token_head, near, pair)
        (vocab_t,) = run(turn_kernel, [like((width, 4 * shard), BF)], vocab, macs, 24, name="vocab_turn")

        moved = lax.ppermute(final, "pass", [(2, 0), (3, 1)])
        group = jnp.where(section >= 2, final, moved)[None]
        pieces, expos, stats = [], [], ()
        for step in reversed(range(n_steps + 1)):
            tokens = group if step == n_steps else swap_chip(group, step)
            if step < n_steps:
                group = jnp.concatenate([group, tokens], axis=0) if step else None
            pieces.append(tokens)
            stats, expo = logit_call(tokens, vocab, stats)
            stats = (stats,)
            expos.append(expo)
        local = stats[0]
        whole = local
        for step in range(n_steps):
            (whole,) = run(
                functools.partial(merge_kernel, step), [like(local.shape, F32)], [whole, swap_chip(whole, step)],
                macs // 64, 8, name="stats_merge",
            )
        other = swap_pass(whole, 2)

        delete_wide = jnp.pad(delete_head, ((0, 0), (0, LANES - delete_head.shape[1])))
        ins_rows = 2 * width // n_dp // 2
        dhead, ins_keep, ins_send, d_delete, head_loss = run(
            head_kernel,
            [
                like((count, width), F32),
                like((n_half, ins_rows, 2 * INS), wire),
                like((n_half, ins_rows, 2 * INS), wire),
                like((8, width), F32),
                like((8, LANES), F32),
            ],
            [final, segs, labels, mask, delete_wide, insert_head],
            10 * macs,
            24,
            turn_scratch(2 * width, count),
            "small_heads",
        )

        firsts = [0]
        for piece in pieces:
            firsts.append(firsts[-1] + piece.shape[0])
        parts_back = [None] * len(pieces)
        for index in reversed(range(len(pieces))):
            dtype = BF if index == len(pieces) - 1 else F32
            parts_back[index] = dtoken_call(expos[index], firsts[index], local, whole, other, vocab_t, dtype)
        for step in range(n_steps):
            got = swap_chip(parts_back.pop().astype(BF), step)
            for index in range(len(parts_back)):
                span = slice(firsts[index], firsts[index + 1])
                parts_back[index] = parts_back[index] + got[span].astype(F32)
        kept = parts_back[0][0]
        back = lax.ppermute(kept.astype(BF), "pass", [(0, 2), (1, 3)])

        dvocab_send = dvocab_call(expos, pieces, local, whole, other, 2, BF)
        dvocab_keep = dvocab_call(expos, pieces, local, whole, other, 0, F32)
        dpair = dvocab_keep + swap_core(dvocab_send).astype(F32)
        token_grad = dpair[:shard] + swap_pass(dpair[shard:].astype(BF), 1).astype(F32)

        rows_ffn = hid // n_dp + unit * (hid // width) + ins_rows
        dthird, dsecond, keep_ffn, send_ffn, vec_ffn, loss = run(
            ffn_back_kernel,
            [
                like((count, width), F32),
                like((count, width), F32),
                like((n_half, rows_ffn, width), wire),
                like((n_half, rows_ffn, width), wire),
                like((8, width), F32),
                like((8, LANES), F32),
            ],
            [third, second, kept, back, dhead, head_loss, local[:, :count], whole[:, :count], other[:, :count]]
            + [norm_gain, norm_bias, hidden, slope, ffn_in, ffn_out, ins_keep, ins_send],
            32 * macs,
            48,
            turn_scratch(hid, count) + turn_scratch(width, count) + [pltpu.VMEM((count, hid), BF)],
            "ffn_backward",
        )
        rows_cross = 4 * unit
        dfirst, keep_cross, send_cross, vec_cross, *dsources = run(
            cross_back_kernel,
            [
                like((count, width), F32),
                like((n_half, rows_cross, width), wire),
                like((n_half, rows_cross, width), wire),
                like((8, width), F32),
                like((part, width), F32),
                like((part, width), BF),
                like((part, width), BF),
                like((part, width), BF),
            ],
            [dsecond, first, query, keyval, probs2, ctx2, *parts, norm_gain, norm_bias, cross_out, cross_kv]
            + [cross_query],
            40 * macs,
            40,
            turn_scratch(width, count)
            + turn_scratch(width, src)
            + [pltpu.VMEM((count, width), BF), pltpu.VMEM((src, 2 * width), BF), pltpu.VMEM((count, width), BF)],
            "cross_backward",
        )
        rows_self = 4 * unit + EXTRA
        input_grad, keep_self, send_self = run(
            self_back_kernel,
            [
                like((count, width), F32),
                like((n_half, rows_self, width), wire),
                like((n_half, rows_self, width), wire),
            ],
            [dfirst, rows, qkv, probs1, ctx1, norm_gain, norm_bias, self_qkv, self_out, vec_ffn, vec_cross, d_delete],
            36 * macs,
            40,
            turn_scratch(width, count) + [pltpu.VMEM((count, 3 * width), BF), pltpu.VMEM((count, width), BF)],
            "self_backward",
        )

        source_grad = dsources[0]
        for bit in (1, 2, 3):
            source_grad = source_grad + swap_pass(dsources[bit], bit).astype(F32)

        p_out, p_in, p_insert = run(
            ffn_end_kernel,
            [like((hid // n_dp, width), F32), like((unit, hid), F32), like((2 * unit, INS), F32)],
            reduce_pass(reduce_dp(keep_ffn, send_ffn)),
            macs // 16,
            16,
            name="ffn_sums",
        )
        p_cross, p_kv, p_query = run(
            cross_end_kernel,
            [like((unit, width), F32), like((unit, 2 * width), F32), like((unit, width), F32)],
            reduce_pass(reduce_dp(keep_cross, send_cross)),
            macs // 16,
            16,
            name="cross_sums",
        )
        p_self, p_qkv, p_gain, p_bias, p_delete = run(
            self_end_kernel,
            [like((unit, width), F32), like((unit, 3 * width), F32), like((4, unit), F32), like((4, unit), F32)]
            + [like((unit, 2), F32)],
            reduce_pass(reduce_dp(keep_self, send_self)),
            macs // 16,
            16,
            name="self_sums",
        )
        return (
            layer[None, None],
            loss[:1, :1],
            input_grad[None, None],
            source_grad[None],
            p_gain,
            p_bias,
            p_qkv,
            p_self,
            p_query,
            p_kv,
            p_cross,
            p_in,
            p_out,
            p_delete,
            p_insert,
            token_grad,
        )

    full = ("pass", "dp")
    rows_at, row_at = P("pass", "dp", None, None), P("pass", "dp", None)
    weight_at = P("dp", None)
    return jax.shard_map(
        body,
        mesh=mesh,
        in_specs=(rows_at, row_at, row_at, row_at, P("dp", "pass", None), P("dp", "pass"))
        + (P(),) * 11
        + (P(full, None),),
        out_specs=(rows_at, P("pass", "dp"), rows_at, P("dp", "pass", None), P(None, "dp"), P(None, "dp"))
        + (weight_at,) * 9
        + (P(full, None),),
        check_vma=False,
    )
```

```python
import functools

import jax
import jax.numpy as jnp
from jax import lax
from jax.experimental import pallas as pl
from jax.experimental.pallas import tpu as pltpu
from jax.sharding import PartitionSpec as P

HEADS = 8
INS = 256
EPS = 1e-05
LANES = 128
EXTRA = 16
BF = jnp.bfloat16
F32 = jnp.float32
MIB = 1 << 20


def cost(us):
    return pl.CostEstimate(flops=int(us * 0.3e9), bytes_accessed=1, transcendentals=0)


def dot(left, right, dims):
    return lax.dot_general(left, right, (dims, ((), ())), preferred_element_type=F32)


def nn(left, right):
    return dot(left, right, ((1,), (0,)))


def nt(left, right):
    return dot(left, right, ((1,), (1,)))


def flip(values):
    return values.astype(F32).T.astype(BF)


class Far:
    def __init__(self, value):
        self.value = value


class Fetched:
    def __init__(self, source, buffer, sem):
        self.buffer, self.shape, self.dtype = buffer, buffer.shape, buffer.dtype
        self.copy = pltpu.make_async_copy(source, buffer, sem)
        self.copy.start()
        self.waiting = True

    def wait(self):
        if self.waiting:
            self.copy.wait()
            self.waiting = False

    def __getitem__(self, index):
        self.wait()
        return self.buffer[index]


class Stored:
    def __init__(self, target, buffer, sem):
        self.buffer, self.shape, self.dtype = buffer, buffer.shape, buffer.dtype
        self.copy = pltpu.make_async_copy(buffer, target, sem)
        self.sent = False

    def __getitem__(self, index):
        return self.buffer[index]

    def __setitem__(self, index, value):
        self.buffer[index] = value

    def send(self):
        self.copy.start()
        self.sent = True


def run(kernel, outs, ins, us, limit, scratch=(), name=None):
    far_in = [isinstance(x, Far) for x in ins]
    far_out = [isinstance(x, Far) for x in outs]
    ins = [x.value if f else x for x, f in zip(ins, far_in)]
    outs = [x.value if f else x for x, f in zip(outs, far_out)]
    ins = [pltpu.with_memory_space_constraint(x, pltpu.HBM) if f else x for x, f in zip(ins, far_in)]
    buffers = [pltpu.VMEM(x.shape, x.dtype) for x, f in zip(ins + outs, far_in + far_out) if f]
    n_in, n_out = len(ins), len(outs)

    def wrapped(*refs):
        if buffers:
            sems = refs[-1]
            held = list(refs[-1 - len(buffers) : -1])
            rest = refs[n_in + n_out : len(refs) - 1 - len(buffers)]
        else:
            held, rest = [], refs[n_in + n_out :]
        given, made, count = [], [], 0
        for ref, far in zip(refs[:n_in], far_in):
            given.append(Fetched(ref, held[count], sems.at[count]) if far else ref)
            count += far
        for ref, far in zip(refs[n_in : n_in + n_out], far_out):
            made.append(Stored(ref, held[count], sems.at[count]) if far else ref)
            count += far
        kernel(*given, *made, *rest)
        for x in given:
            if isinstance(x, Fetched):
                x.wait()
        for x in made:
            if isinstance(x, Stored) and not x.sent:
                x.send()
        for x in made:
            if isinstance(x, Stored):
                x.copy.wait()

    def place(far):
        return pl.BlockSpec(memory_space=pltpu.HBM if far else pltpu.VMEM)

    return pl.pallas_call(
        wrapped,
        out_shape=[pltpu.HBM(x.shape, x.dtype) if f else x for x, f in zip(outs, far_out)],
        in_specs=[place(f) for f in far_in],
        out_specs=[place(f) for f in far_out],
        scratch_shapes=list(scratch) + buffers + ([pltpu.SemaphoreType.DMA((len(buffers),))] if buffers else []),
        compiler_params=pltpu.CompilerParams(vmem_limit_bytes=limit * MIB),
        cost_estimate=cost(us),
        name=name,
    )(*ins)


def after(value, *done):
    return lax.optimization_barrier((value, *done))[0]


def after_all(values, *done):
    return list(lax.optimization_barrier((*values, *done))[: len(values)])


def like(shape, dtype):
    return jax.ShapeDtypeStruct(shape, dtype)


def norm_parts(values):
    center = values - jnp.mean(values, axis=-1, keepdims=True)
    rstd = lax.rsqrt(jnp.mean(center * center, axis=-1, keepdims=True) + EPS)
    return center * rstd, rstd


def norm_out(unit, gain, shift, index):
    return (unit * gain[index : index + 1] + shift[index : index + 1]).astype(BF)


def norm_bwd(grad, unit, rstd, gain):
    scaled = grad * gain
    back = rstd * (
        scaled
        - jnp.mean(scaled, axis=-1, keepdims=True)
        - unit * jnp.mean(scaled * unit, axis=-1, keepdims=True)
    )
    return back, jnp.sum(grad * unit, axis=0, keepdims=True), jnp.sum(grad, axis=0, keepdims=True)


def column(row, count):
    return jnp.broadcast_to(row, (count, row.shape[1])).T


def lane_half(values, half):
    lane = lax.broadcasted_iota(jnp.int32, values.shape, 1)
    picked = (lane >= LANES // 2) if half else (lane < LANES // 2)
    return jnp.where(picked, values, jnp.zeros_like(values))


def attend(query, keys, values, bias_ref, probs_ref, out_ref, scale):
    half_size = LANES // 2
    for tile in range(out_ref.shape[1] // LANES):
        q = query(tile).astype(F32) * scale
        k, v_t = keys(tile), flip(values(tile))
        parts = []
        for half in range(2):
            scores = nt(k, lane_half(q, half).astype(BF)) + bias_ref[...]
            expo = jnp.exp(scores - jnp.max(scores, axis=0, keepdims=True))
            probs = (expo * (1.0 / jnp.sum(expo, axis=0, keepdims=True))).astype(BF)
            probs_ref[2 * tile + half] = probs
            parts.append(nn(v_t[half * half_size : (half + 1) * half_size], probs))
        out_ref[:, tile * LANES : (tile + 1) * LANES] = jnp.concatenate(parts, axis=0).T.astype(BF)


def attend_bwd(grad, query, keys, values, probs_ref, put_query, put_keys, put_values, scale, tiles):
    half_size = LANES // 2
    for tile in range(tiles):
        g, q, k, v = grad(tile), query(tile), keys(tile), values(tile)
        k_t = flip(k)
        dq, dk, dv = [], [], []
        for half in range(2):
            probs = probs_ref[2 * tile + half]
            full = probs.astype(F32)
            dprobs = nt(v, lane_half(g, half))
            delta = jnp.sum(dprobs * full, axis=0, keepdims=True)
            dscores = (full * ((dprobs - delta) * scale)).astype(BF)
            dv.append(nn(probs, g))
            dk.append(nn(dscores, q))
            dq.append(nn(k_t[half * half_size : (half + 1) * half_size], dscores))
        lane = lax.broadcasted_iota(jnp.int32, dk[0].shape, 1) < half_size
        put_query(tile, jnp.concatenate(dq, axis=0).T.astype(BF))
        put_keys(tile, jnp.where(lane, dk[0], dk[1]).astype(BF))
        put_values(tile, jnp.where(lane, dv[0], dv[1]).astype(BF))


def tile_of(ref, start):
    return lambda tile: ref[:, start + tile * LANES : start + (tile + 1) * LANES]


def put_in(ref, start):
    def put(tile, value):
        ref[:, start + tile * LANES : start + (tile + 1) * LANES] = value

    return put


def solution(mesh):
    n_pass, n_dp = mesh.shape["pass"], mesh.shape["dp"]
    bits = [1 << i for i in range(n_dp.bit_length() - 1)]
    core_bit, chip_bits = bits[0], bits[1:]
    orders = (chip_bits, chip_bits[1::-1] + chip_bits[2:])
    n_steps = len(chip_bits)
    n_half = n_dp // 2

    def swap_core(x):
        return lax.ppermute(x, "dp", [(i, i ^ core_bit) for i in range(n_dp)])

    def swap_chip(x, step):
        return lax.ppermute(x, "dp", [(i, i ^ orders[i & 1][step]) for i in range(n_dp)])

    def swap_pass(x, bit):
        return lax.ppermute(x, "pass", [(i, i ^ bit) for i in range(n_pass)])

    def owners():
        me = lax.axis_index("dp")
        core = me & 1
        result = []
        for slot in range(n_dp):
            own_half = slot < n_half
            turn = core if own_half else 1 - core
            owner = me if own_half else me ^ 1
            for step in range(n_steps):
                if (slot >> (n_steps - 1 - step)) & 1:
                    owner = owner ^ jnp.where(turn == 0, orders[0][step], orders[1][step])
            result.append(owner)
        return result

    def small_dtype(rows):
        return BF if rows % 16 == 0 else F32

    def turn_rows(values, turned_ref, sorted_ref, owner_list):
        block = values.shape[1] // n_dp
        turned_ref[...] = values.astype(F32).T.astype(turned_ref.dtype)
        for slot, owner in enumerate(owner_list):
            start = pl.multiple_of(owner * block, block)
            sorted_ref[slot * block : (slot + 1) * block] = turned_ref[pl.ds(start, block)]
        return sorted_ref[...].astype(BF)

    def turn_scratch(features, count):
        dtype = small_dtype(features // n_dp)
        return [pltpu.VMEM((features, count), dtype)] * 2

    def pack(keep_ref, send_ref, base, first, left_t, right):
        width = keep_ref.shape[2]
        section = lax.axis_index("pass")
        unit = width // n_dp
        block = left_t.shape[0] // n_dp
        quarter = first
        for col in range(right.shape[1] // width):
            grad = nn(left_t, right[:, col * width : (col + 1) * width]).astype(keep_ref.dtype)
            for piece in range(block // unit):
                place = pl.ds(pl.multiple_of(base + (quarter ^ section) * unit, unit), unit)
                for slot in range(n_dp):
                    ref, index = (keep_ref, slot) if slot < n_half else (send_ref, slot - n_half)
                    start = slot * block + piece * unit
                    ref[index, place] = grad[start : start + unit]
                quarter += 1
        return quarter


    def self_kernel(x, gain, shift, w_qkv, seg, w_out, w_query, first, query, first_far, query_far, qkv, probs, ctx, bias):
        width = x.shape[1]
        gains, shifts = gain[...].astype(F32), shift[...].astype(F32)
        rows = x[...].astype(F32)
        unit, _ = norm_parts(rows)
        qkv[...] = nn(norm_out(unit, gains, shifts, 0), w_qkv[...]).astype(BF)
        seg_row = seg[...].astype(F32)
        bias[...] = jnp.where(column(seg_row, seg_row.shape[1]) == seg_row, 0.0, -1000000000.0)
        attend(
            tile_of(qkv, 0), tile_of(qkv, width), tile_of(qkv, 2 * width), bias, probs, ctx, (width // HEADS) ** -0.5
        )
        for ref in (qkv, probs, ctx):
            ref.send()
        added = rows + nn(ctx[...], w_out[...])
        first[...] = added
        first_far[...] = added
        first_far.send()
        unit, _ = norm_parts(added)
        value = nn(norm_out(unit, gains, shifts, 1), w_query[...]).astype(BF)
        query[...] = value
        query_far[...] = value

    def cross_kernel(
        first, query, w_kv, seg, part0, part1, part2, part3, w_out, gain, shift, w_in, w_ffn, labels, mask,
        second, keyval, probs, ctx, hidden, slope, third, layer, final, bias,
    ):
        width = first.shape[1]
        count = first.shape[0]
        seg_row = seg[...].astype(F32)
        size = part0.shape[0] - EXTRA
        for index, part in enumerate((part0, part1, part2, part3)):
            span = slice(index * size, (index + 1) * size)
            keyval[span] = nn(part[:size], w_kv[...]).astype(BF)
            source_seg = part[size : size + EXTRA, :size].astype(F32)[0:1]
            bias[span] = jnp.where(column(source_seg, count) == seg_row, 0.0, -1000000000.0)
        attend(
            tile_of(query, 0), tile_of(keyval, 0), tile_of(keyval, width), bias, probs, ctx, (width // HEADS) ** -0.5
        )
        for ref in (keyval, probs, ctx):
            ref.send()
        added = first[...] + nn(ctx[...], w_out[...])
        second[...] = added
        second.send()
        gains, shifts = gain[...].astype(F32), shift[...].astype(F32)
        unit, _ = norm_parts(added)
        normed = norm_out(unit, gains, shifts, 2)
        for col in range(w_in.shape[1] // width):
            span = slice(col * width, (col + 1) * width)
            inner = nn(normed, w_in[:, span])
            cdf = 0.5 * (1.0 + lax.erf(inner * 0.7071067811865476))
            hidden[:, span] = (inner * cdf).astype(BF)
            slope[:, span] = (cdf + inner * jnp.exp(-0.5 * inner * inner) * 0.3989422804014327).astype(BF)
        hidden.send()
        slope.send()
        added = added + nn(hidden[...], w_ffn[...])
        third[...] = added
        layer[...] = added.astype(BF)
        third.send()
        layer.send()
        unit, _ = norm_parts(added)
        final[:count] = norm_out(unit, gains, shifts, 3)
        label = labels[...]
        line = lax.broadcasted_iota(jnp.int32, (EXTRA, count), 0)
        high = lax.shift_right_logical(label, 8).astype(F32)
        marks = jnp.where(line == 0, high, 0.0)
        marks = jnp.where(line == 1, (label & 255).astype(F32), marks)
        marks = jnp.where(line == 2, mask[...].astype(F32), marks)
        final[count:] = jnp.concatenate([marks, jnp.zeros((EXTRA, width - count), F32)], axis=1).astype(BF)

    def head_kernel(
        final, seg, labels, mask, w_delete, w_insert,
        dfinal, keep, send, d_delete, loss, turned, ordered,
    ):
        section = lax.axis_index("pass")
        count = seg.shape[1]
        width = final.shape[1]
        h = final[:count]
        h32 = h.astype(F32)
        seg_col = column(seg[...].astype(F32), LANES)
        row_id = lax.broadcasted_iota(jnp.int32, (count, LANES), 0)
        linked = (pltpu.roll(seg_col, count - 1, 0) == seg_col) & (row_id < count - 1)
        linked = jnp.concatenate([linked.astype(F32)] * (width // LANES), axis=1)
        after = (pltpu.roll(h32, count - 1, 0) * linked).astype(BF)
        weight = column(mask[...].astype(F32), LANES)

        def entropy(logits, label, live):
            top = jnp.max(logits, axis=-1, keepdims=True)
            expo = jnp.exp(logits - top)
            total = jnp.sum(expo, axis=-1, keepdims=True)
            lane = lax.broadcasted_iota(jnp.int32, logits.shape, 1)
            target = column(label.astype(F32), logits.shape[1])
            hit = lane.astype(F32) == target
            picked = jnp.sum(jnp.where(hit, logits, 0.0), axis=1, keepdims=True)
            w = weight[:, :1] * live
            rest = jnp.sum(jnp.where(hit, 0.0, expo), axis=1, keepdims=True)
            grad = jnp.where(hit, -rest, expo) * (w / total)
            return jnp.sum(w * (top + jnp.log(total) - picked)), grad.astype(BF)

        label = labels[...]
        logits = nn(h, w_delete[...])
        lane = lax.broadcasted_iota(jnp.int32, logits.shape, 1)
        logits = jnp.where(lane < 2, logits, -1e30)
        loss_d, grad_d = entropy(logits, lax.rem(label, 2), (section == 0).astype(F32))
        logits = nn(h, w_insert[:width]) + nn(after, w_insert[width:])
        loss_i, grad_i = entropy(logits, lax.rem(label, INS), (section == 1).astype(F32))
        loss[...] = jnp.full(loss.shape, loss_d + loss_i)
        d_after = nt(grad_i, w_insert[width:]) * linked
        dfinal[...] = nt(grad_d, w_delete[...]) + nt(grad_i, w_insert[:width]) + pltpu.roll(d_after, 1, 0)
        d_delete[...] = nn(flip(grad_d)[:EXTRA], h)[: d_delete.shape[0]]
        both_t = turn_rows(jnp.concatenate([h, after], axis=1), turned, ordered, owners())
        grad = nn(both_t, grad_i).astype(keep.dtype)
        block = both_t.shape[0] // n_dp
        half = block // 2
        for slot in range(n_dp):
            ref, index = (keep, slot) if slot < n_half else (send, slot - n_half)
            ref[index, :, :INS] = grad[slot * block : slot * block + half]
            ref[index, :, INS:] = grad[slot * block + half : (slot + 1) * block]


    def shard_base(chunk, shard):
        section, me = lax.axis_index("pass"), lax.axis_index("dp")
        return ((section ^ (chunk & 1)) * n_dp + (me ^ (chunk >> 1))) * shard

    def hits(base, start, shape, label):
        ids = lax.broadcasted_iota(jnp.int32, shape, 0) + (base + start)
        return ids == label

    def logit_kernel(shard, n_prev, n_vocab, tokens, *rest):
        vocab, prev, (stats, expo, logits) = rest[:n_vocab], rest[n_vocab:-3], rest[-3:]
        count = tokens.shape[1] - EXTRA
        index = pl.program_id(0)
        if n_prev:

            @pl.when(index == 0)
            def _():
                stats[:, : n_prev * count] = prev[0][...]

        h = tokens[0, :count]
        marks = tokens[0, count:].astype(F32)
        label_f = marks[0:1, :count] * 256.0 + marks[1:2, :count]
        label = label_f.astype(jnp.int32)
        weight = marks[2:3, :count]
        peak = jnp.full((8, count), -jnp.inf, F32)
        at = 0
        for ref in vocab:
            for start in range(0, ref.shape[0], 256):
                step = min(256, ref.shape[0] - start)
                value = nt(ref[start : start + step], h)
                logits[at : at + step] = value
                peak = jnp.maximum(peak, jnp.max(value.reshape(step // 8, 8, count), axis=0))
                at += step
        peak = jnp.max(peak, axis=0, keepdims=True)
        total = jnp.zeros((8, count), F32)
        chosen = jnp.zeros((8, count), F32)
        sub = min(shard, 128)
        for chunk in range(4):
            base = shard_base(chunk, shard)

            def part(i, carry, chunk=chunk, base=base):
                total, chosen = carry
                at = pl.multiple_of(chunk * shard + i * sub, sub)
                value = logits[pl.ds(at, sub)]
                hit = hits(base, i * sub, (sub, count), label)
                weight_of = jnp.where(hit, 0.0, jnp.exp(value - peak))
                expo[0, pl.ds(at, sub)] = weight_of.astype(BF)
                total = total + jnp.sum(weight_of.reshape(sub // 8, 8, count), axis=0)
                picked = jnp.where(hit, value, 0.0)
                return total, chosen + jnp.sum(picked.reshape(sub // 8, 8, count), axis=0)

            total, chosen = lax.fori_loop(0, shard // sub, part, (total, chosen))
        total = jnp.sum(total, axis=0, keepdims=True)
        chosen = jnp.sum(chosen, axis=0, keepdims=True)
        line = lax.broadcasted_iota(jnp.int32, (8, count), 0)
        block = jnp.zeros((8, count), F32)
        for at, value in enumerate((peak, total, chosen, label_f, weight)):
            block = jnp.where(line == at, value, block)
        stats[:, pl.ds(pl.multiple_of((n_prev + index) * count, count), count)] = block

    def logit_call(tokens, vocab, prev):
        n, height, width = tokens.shape
        count = height - EXTRA
        shard = sum(v.shape[0] for v in vocab) // 4
        n_prev = prev[0].shape[1] // count if prev else 0
        fixed = [pl.BlockSpec(v.shape, lambda t: (0, 0)) for v in tuple(vocab) + tuple(prev)]
        total = (n_prev + n) * count
        return pl.pallas_call(
            functools.partial(logit_kernel, shard, n_prev, len(vocab)),
            grid=(n,),
            in_specs=[pl.BlockSpec((1, height, width), lambda t: (t, 0, 0))] + fixed,
            out_specs=[
                pl.BlockSpec((8, total), lambda t: (0, 0)),
                pl.BlockSpec((1, 4 * shard, count), lambda t: (t, 0, 0)),
            ],
            out_shape=[like((8, total), F32), like((n, 4 * shard, count), BF)],
            scratch_shapes=[pltpu.VMEM((4 * shard, count), F32)],
            compiler_params=pltpu.CompilerParams(vmem_limit_bytes=20 * MIB),
            cost_estimate=cost(2.8 * n),
            name="token_logits",
        )(tokens, *vocab, *prev)

    def merged(own, other):
        peak = jnp.maximum(own[0:1], other[0:1])
        total = own[1:2] * jnp.exp(own[0:1] - peak) + other[1:2] * jnp.exp(other[0:1] - peak)
        return peak, total, own[2:3] + other[2:3]

    def merge_kernel(step, own, other, out):
        size = own.shape[1] >> (step + 1)
        blocks = [other[:, i * size : (i + 1) * size] for i in range(2 << step)]
        swapped = jnp.concatenate([blocks[i ^ 1] for i in range(2 << step)], axis=1)
        mine = own[...]
        peak, total, chosen = merged(mine, swapped)
        line = lax.broadcasted_iota(jnp.int32, mine.shape, 0)
        out[...] = jnp.where(
            line == 0, peak, jnp.where(line == 1, total, jnp.where(line == 2, chosen, mine))
        )

    def closing(local, merged_ref, other):
        peak, total, chosen = merged(merged_ref, other)
        hit = jnp.exp(chosen - peak)
        full = total + hit
        lse = peak + jnp.log(full)
        weight = local[4:5]
        factor = weight * jnp.exp(local[0:1] - lse)
        return lse, chosen, factor, -weight * (total / full)

    def dlogits_into(ref, at, cols, expo, start, base, shape, label, factor, at_label):
        sub = min(shape[0], 128)

        def part(i, _):
            row = pl.multiple_of(i * sub, sub)
            hit = hits(base, i * sub, (sub, shape[1]), label)
            value = expo[pl.ds(pl.multiple_of(start + row, sub), sub)].astype(F32) * factor
            ref[pl.ds(pl.multiple_of(at + row, sub), sub), cols] = jnp.where(hit, at_label, value).astype(BF)
            return 0

        lax.fori_loop(0, shape[0] // sub, part, 0)

    def dtoken_kernel(shard, expo, local, merged_ref, other, vocab_t, out, dlogits):
        _, _, factor, at_label = closing(local[...], merged_ref[...], other[...])
        label = local[3:4].astype(jnp.int32)
        count = local.shape[1]
        for chunk in range(4):
            dlogits_into(
                dlogits, chunk * shard, slice(None), expo.at[0], chunk * shard, shard_base(chunk, shard),
                (shard, count), label, factor, at_label,
            )
        out[0] = nn(vocab_t[...], dlogits[...]).T.astype(out.dtype)

    def dtoken_call(expo, first, local, merged_ref, other, vocab_t, dtype):
        n, rows, count = expo.shape
        width = vocab_t.shape[0]
        line = pl.BlockSpec((8, count), lambda t: (0, first + t))
        return pl.pallas_call(
            functools.partial(dtoken_kernel, rows // 4),
            grid=(n,),
            in_specs=[pl.BlockSpec((1, rows, count), lambda t: (t, 0, 0)), line, line, line]
            + [pl.BlockSpec(vocab_t.shape, lambda t: (0, 0))],
            out_specs=pl.BlockSpec((1, count, width), lambda t: (t, 0, 0)),
            out_shape=like((n, count, width), dtype),
            scratch_shapes=[pltpu.VMEM((rows, count), BF)],
            compiler_params=pltpu.CompilerParams(vmem_limit_bytes=20 * MIB),
            cost_estimate=cost(2.2 * n),
            name="token_dfinal",
        )(expo, local, merged_ref, other, vocab_t)

    def dvocab_kernel(shard, chunk0, n_pieces, *refs):
        expos, tokens = refs[:n_pieces], refs[n_pieces : 2 * n_pieces]
        local, merged_ref, other, out, dlogits, held = refs[2 * n_pieces :]
        index = pl.program_id(0)
        _, _, factor, at_label = closing(local[...], merged_ref[...], other[...])
        label = local[3:4].astype(jnp.int32)
        count = tokens[0].shape[1] - EXTRA
        section, me = lax.axis_index("pass"), lax.axis_index("dp")
        chunk = chunk0 + index
        base = ((section ^ (chunk & 1)) * n_dp + (me ^ (chunk >> 1))) * shard
        at = 0
        for expo, token in zip(expos, tokens):
            for i in range(token.shape[0]):
                cols = slice(at, at + count)
                held[cols] = token[i, :count]
                dlogits_into(
                    dlogits, 0, cols, expo.at[i], 0, base, (shard, count), label[:, cols], factor[:, cols],
                    at_label[:, cols],
                )
                at += count
        out[...] = nn(dlogits[...], held[...]).astype(out.dtype)

    def dvocab_call(expos, tokens, local, merged_ref, other, chunk0, dtype):
        shard = expos[0].shape[1] // 4
        count = expos[0].shape[2]
        width = tokens[0].shape[2]
        total = local.shape[1]
        fixed2 = pl.BlockSpec(local.shape, lambda c: (0, 0))
        return pl.pallas_call(
            functools.partial(dvocab_kernel, shard, chunk0, len(expos)),
            grid=(2,),
            in_specs=[pl.BlockSpec((e.shape[0], shard, count), lambda c: (0, chunk0 + c, 0)) for e in expos]
            + [pl.BlockSpec(t.shape, lambda c: (0, 0, 0)) for t in tokens]
            + [fixed2] * 3,
            out_specs=pl.BlockSpec((shard, width), lambda c: (c, 0)),
            out_shape=like((2 * shard, width), dtype),
            scratch_shapes=[pltpu.VMEM((shard, total), BF), pltpu.VMEM((total, width), BF)],
            compiler_params=pltpu.CompilerParams(vmem_limit_bytes=20 * MIB),
            cost_estimate=cost(9),
            name="token_dvocab",
        )(*expos, *tokens, local, merged_ref, other)

    def turn_kernel(*refs):
        at = 0
        for ref in refs[:-1]:
            refs[-1][:, at : at + ref.shape[0]] = flip(ref[...])
            at += ref.shape[0]


    def ffn_back_kernel(
        hidden, third, gain, w_ffn, slope, second, shift, w_in,
        kept, moved, dhead, head_loss, local, merged_ref, other, ins_keep, ins_send,
        dsecond, keep, send, vecs, loss, wide_t, wide_s, thin_t, thin_s, dinner,
    ):
        width = third.shape[1]
        count = third.shape[0]
        live = (lax.axis_index("pass") >= 2).astype(F32)
        hidden_t = turn_rows(hidden[...], wide_t, wide_s, owners())
        dfinal = dhead[...] + live * (kept[...] + moved[...].astype(F32))
        unit3, rstd3 = norm_parts(third[...])
        gains = gain[...].astype(F32)
        dthird, g_gain3, g_bias3 = norm_bwd(dfinal, unit3, rstd3, gains[3:4])
        low = dthird.astype(BF)
        pack(keep, send, 0, 0, hidden_t, low)
        for col in range(w_ffn.shape[0] // width):
            span = slice(col * width, (col + 1) * width)
            part = nt(low, w_ffn[span]).astype(BF).astype(F32) * slope[:, span].astype(F32)
            dinner[:, span] = part.astype(BF)
        unit2, rstd2 = norm_parts(second[...])
        normed_t = turn_rows(norm_out(unit2, gains, shift[...].astype(F32), 2), thin_t, thin_s, owners())
        pack(keep, send, 4 * (width // n_dp), 0, normed_t, dinner[...])
        extra = ins_keep.shape[1]
        keep[:, keep.shape[1] - extra :] = ins_keep[...]
        send[:, keep.shape[1] - extra :] = ins_send[...]
        dnormed = nt(dinner[...], w_in[...])
        back, g_gain2, g_bias2 = norm_bwd(dnormed, unit2, rstd2, gains[2:3])
        dsecond[...] = dthird + back
        lse, chosen, _, _ = closing(local[:, :count], merged_ref[:, :count], other[:, :count])
        token_loss = jnp.sum(local[4:5, :count] * (lse - chosen)) * live
        loss[...] = head_loss[...] + token_loss
        line = lax.broadcasted_iota(jnp.int32, (8, width), 0)
        block = jnp.zeros((8, width), F32)
        for at, value in enumerate((g_gain3, g_gain2, g_bias3, g_bias2)):
            block = jnp.where(line == at, value, block)
        vecs[...] = block

    def cross_back_kernel(
        dsecond, w_out, ctx, keyval, probs, query, part0, part1, part2, part3, w_kv, first, gain, shift, w_query,
        dfirst, keep, send, vecs, dsrc0, dsrc1, dsrc2, dsrc3, thin_t, thin_s, src_t, src_s, dquery, dkeyval, dctx,
    ):
        width = first.shape[1]
        owner_list = owners()
        low = dsecond[...].astype(BF)
        dctx[...] = nt(low, w_out[...]).astype(BF)
        at = pack(keep, send, 0, 0, turn_rows(ctx[...], thin_t, thin_s, owner_list), low)
        attend_bwd(
            tile_of(dctx, 0), tile_of(query, 0), tile_of(keyval, 0), tile_of(keyval, width), probs,
            put_in(dquery, 0), put_in(dkeyval, 0), put_in(dkeyval, width), (width // HEADS) ** -0.5, width // LANES,
        )
        size = part0.shape[0] - EXTRA
        source = jnp.concatenate([p[:size] for p in (part0, part1, part2, part3)], axis=0)
        at = pack(keep, send, 0, at, turn_rows(source, src_t, src_s, owner_list), dkeyval[...])
        for index, ref in enumerate((dsrc0, dsrc1, dsrc2, dsrc3)):
            ref[...] = nt(dkeyval[index * size : (index + 1) * size], w_kv[...]).astype(ref.dtype)
        gains, shifts = gain[...].astype(F32), shift[...].astype(F32)
        unit, rstd = norm_parts(first[...])
        normed_t = turn_rows(norm_out(unit, gains, shifts, 1), thin_t, thin_s, owner_list)
        pack(keep, send, 0, at, normed_t, dquery[...])
        back, g_gain, g_bias = norm_bwd(nt(dquery[...], w_query[...]), unit, rstd, gains[1:2])
        dfirst[...] = dsecond[...] + back
        line = lax.broadcasted_iota(jnp.int32, (8, width), 0)
        vecs[...] = jnp.where(line == 0, g_gain, jnp.where(line == 1, g_bias, 0.0))

    def self_back_kernel(
        dfirst, w_out, ctx, qkv, probs, x, gain, shift, w_qkv, vec_ffn, vec_cross, d_delete,
        dx, keep, send, thin_t, thin_s, dqkv, dctx,
    ):
        width = x.shape[1]
        owner_list = owners()
        low = dfirst[...].astype(BF)
        dctx[...] = nt(low, w_out[...]).astype(BF)
        at = pack(keep, send, 0, 0, turn_rows(ctx[...], thin_t, thin_s, owner_list), low)
        attend_bwd(
            tile_of(dctx, 0), tile_of(qkv, 0), tile_of(qkv, width), tile_of(qkv, 2 * width), probs,
            put_in(dqkv, 0), put_in(dqkv, width), put_in(dqkv, 2 * width), (width // HEADS) ** -0.5, width // LANES,
        )
        gains, shifts = gain[...].astype(F32), shift[...].astype(F32)
        unit, rstd = norm_parts(x[...].astype(F32))
        normed_t = turn_rows(norm_out(unit, gains, shifts, 0), thin_t, thin_s, owner_list)
        at = pack(keep, send, 0, at, normed_t, dqkv[...])
        back, g_gain, g_bias = norm_bwd(nt(dqkv[...], w_qkv[...]), unit, rstd, gains[0:1])
        dx[...] = dfirst[...] + back
        line = lax.broadcasted_iota(jnp.int32, (EXTRA, width), 0)
        block = jnp.zeros((EXTRA, width), F32)
        lines = (
            (0, d_delete[0:1]), (1, d_delete[1:2]),
            (8, g_gain), (9, vec_cross[0:1]), (10, vec_ffn[1:2]), (11, vec_ffn[0:1]),
            (12, g_bias), (13, vec_cross[1:2]), (14, vec_ffn[3:4]), (15, vec_ffn[2:3]),
        )
        for row, value in lines:
            block = jnp.where(line == row, value, block)
        block = block.astype(keep.dtype)
        at = at * (width // n_dp)
        for slot in range(n_half):
            keep[slot, at:] = block
            send[slot, at:] = block


    def add_kernel(pairs, *refs):
        ins, outs = refs[: 2 * pairs], refs[2 * pairs :]
        at = 0
        for keep, got in zip(ins[::2], ins[1::2]):
            rows = keep.shape[1]
            slot = 0
            for ref in outs:
                for i in range(ref.shape[0]):
                    value = keep[slot].astype(F32) + got[slot].astype(F32)
                    ref[i, at : at + rows] = value.astype(ref.dtype)
                    slot += 1
            at += rows

    def add_call(blocks, *counts):
        rows, width = sum(b.shape[1] for b in blocks[::2]), blocks[0].shape[2]
        outs = [like((count, rows, width), wire_of(width)) for count in counts]
        return run(functools.partial(add_kernel, len(blocks) // 2), outs, blocks, 0.8, 8, name="sum_slots")

    def wire_of(width):
        return small_dtype(width // n_dp)

    def regroup_kernel(plan, n_terms, *refs):
        value = refs[0][...].astype(F32)
        for ref in refs[1:n_terms]:
            value = value + ref[...].astype(F32)
        for spans, ref in zip(plan, refs[n_terms:]):
            at = 0
            for start, stop in spans:
                ref[at : at + stop - start] = value[start:stop].astype(ref.dtype)
                at += stop - start

    def pair_kernel(plan, n_terms, *refs):
        first = refs[0][...].astype(F32) + refs[1][...].astype(F32)
        value = first + (refs[2][...].astype(F32) + refs[3][...].astype(F32))
        for spans, ref in zip(plan, refs[n_terms:]):
            at = 0
            for start, stop in spans:
                ref[at : at + stop - start] = value[start:stop].astype(ref.dtype)
                at += stop - start

    def regroup(terms, plan, kernel=regroup_kernel, name="sum_rows"):
        width = terms[0].shape[-1]
        outs = [like((sum(b - a for a, b in spans), width), wire_of(width)) for spans in plan]
        terms = [t.reshape(t.shape[-2:]) for t in terms]
        return run(functools.partial(kernel, plan, len(terms)), outs, terms, 0.7, 8, name=name)

    def picked(pieces):
        section = lax.axis_index("pass")
        values = [p.astype(F32) for p in pieces]
        result = []
        for j in range(4):
            value = values[0]
            for b in (1, 2, 3):
                value = jnp.where((section ^ b) == j, values[b], value)
            result.append(value)
        return result

    def halves(refs):
        rows = refs[0].shape[0] // 2
        return [r[:rows] for r in refs], [r[rows:] for r in refs]

    def ffn_end_kernel(own, near, third, far, extra, p_out, p_in, p_insert):
        outs, ins = halves((own, near, third, far))
        rows, width = outs[0].shape
        for j, value in enumerate(picked(outs)):
            p_out[j * rows : (j + 1) * rows] = value
        for j, value in enumerate(picked(ins)):
            p_in[:, j * width : (j + 1) * width] = value
        half = p_insert.shape[0] // 2
        value = extra[...].astype(F32)
        p_insert[:half] = value[:, :INS]
        p_insert[half:] = value[:, INS:]

    def attention_end_kernel(
        own, near, third, far, extra, p_cross, p_kv, p_query, p_out, p_qkv, p_gain, p_bias, p_delete
    ):
        cross, own_part = halves((own, near, third, far))
        width = extra.shape[1]
        values = picked(cross)
        p_cross[...] = values[0]
        p_kv[:, :width] = values[1]
        p_kv[:, width:] = values[2]
        p_query[...] = values[3]
        values = picked(own_part)
        p_out[...] = values[0]
        for j in range(3):
            p_qkv[:, j * width : (j + 1) * width] = values[j + 1]
        size = p_gain.shape[1]
        me = lax.axis_index("dp")
        mine = pltpu.roll(extra[...].astype(F32), lax.rem(width - me * size, width), 1)
        p_gain[...] = mine[8:12, :size]
        p_bias[...] = mine[12:16, :size]
        p_delete[...] = mine[:, :LANES].T[:size, :2]

    def body(
        decoder_in,
        decoder_segments,
        edit_target,
        loss_mask,
        source_out,
        source_segments,
        norm_gain,
        norm_bias,
        self_qkv,
        self_out,
        cross_query,
        cross_kv,
        cross_out,
        ffn_in,
        ffn_out,
        delete_head,
        insert_head,
        token_head,
    ):
        section = lax.axis_index("pass")
        segs, labels, mask = decoder_segments[0], edit_target[0], loss_mask[0]
        rows = decoder_in[0, 0]
        count, width = rows.shape
        shard = token_head.shape[0]
        part = source_out.shape[1]
        src = n_pass * part
        hid = ffn_in.shape[1]
        unit = width // n_dp
        wire = small_dtype(unit)

        note = jnp.pad(source_segments.astype(BF), ((0, EXTRA - 1), (0, width - part)))
        mine = jnp.concatenate([source_out[0], note], axis=0)
        parts = [mine] + [swap_pass(mine, bit) for bit in (1, 2, 3)]

        gain, shift = Far(norm_gain), Far(norm_bias)
        first, query, first_far, query_far, qkv, probs1, ctx1 = run(
            self_kernel,
            [
                like((count, width), F32),
                like((count, width), BF),
                Far(like((count, width), F32)),
                Far(like((count, width), BF)),
                Far(like((count, 3 * width), BF)),
                Far(like((HEADS, count, count), BF)),
                Far(like((count, width), BF)),
            ],
            [Far(rows), gain, shift, Far(self_qkv), Far(segs), Far(self_out), Far(cross_query)],
            4.2,
            10,
            [pltpu.VMEM((count, count), F32)],
            "self_forward",
        )
        second, keyval, probs2, ctx2, hidden, slope, third, layer, final = run(
            cross_kernel,
            [
                Far(like((count, width), F32)),
                Far(like((src, 2 * width), BF)),
                Far(like((HEADS, src, count), BF)),
                Far(like((count, width), BF)),
                Far(like((count, hid), BF)),
                Far(like((count, hid), BF)),
                Far(like((count, width), F32)),
                Far(like((count, width), BF)),
                like((count + EXTRA, width), BF),
            ],
            [first, query, Far(cross_kv), Far(segs), *parts, Far(cross_out), gain, shift]
            + [Far(ffn_in), Far(ffn_out), Far(labels), Far(mask)],
            7.6,
            20,
            [pltpu.VMEM((src, count), F32)],
            "cross_forward",
        )

        near = swap_pass(after(token_head, parts[1]), 1)
        moved = lax.ppermute(final, "pass", [(2, 0), (3, 1)])
        group = jnp.where(section >= 2, final, moved)[None]
        pieces = [group]
        for step in reversed(range(n_steps)):
            pieces.append(swap_chip(group, step))
            if step:
                group = jnp.concatenate([group, pieces[-1]], axis=0)
        near = after(near, pieces[1])
        vocab = (token_head, near, swap_core(token_head), swap_core(near))
        expos, stats = [], ()
        for tokens in pieces:
            stats, expo = logit_call(tokens, vocab, stats)
            stats = (stats,)
            expos.append(expo)
        (vocab_t,) = run(turn_kernel, [like((width, 4 * shard), BF)], vocab, 1.3, 20, name="vocab_turn")
        local = stats[0]
        whole = local
        for step in range(n_steps):
            (whole,) = run(
                functools.partial(merge_kernel, step), [like(local.shape, F32)], [whole, swap_chip(whole, step)],
                1.0, 8, name="stats_merge",
            )
        other = swap_pass(whole, 2)

        delete_wide = jnp.pad(delete_head, ((0, 0), (0, LANES - delete_head.shape[1])))
        ins_rows = 2 * width // n_dp // 2
        dhead, ins_keep, ins_send, d_delete, head_loss = run(
            head_kernel,
            [
                like((count, width), F32),
                like((n_half, ins_rows, 2 * INS), wire),
                like((n_half, ins_rows, 2 * INS), wire),
                like((8, width), F32),
                like((8, LANES), F32),
            ],
            [after(final, whole), Far(segs), Far(labels), Far(mask), delete_wide, Far(insert_head)],
            1.4,
            10,
            turn_scratch(2 * width, count),
            "small_heads",
        )
        other = after(other, dhead)

        firsts = [0]
        for piece in pieces:
            firsts.append(firsts[-1] + piece.shape[0])
        parts_back = [None] * len(pieces)
        for index in reversed(range(len(pieces))):
            dtype = BF if index == len(pieces) - 1 else F32
            parts_back[index] = dtoken_call(expos[index], firsts[index], local, whole, other, vocab_t, dtype)
        dvocab_send = dvocab_call(expos, pieces, after(local, parts_back[-1]), whole, other, 2, BF)
        for step in range(n_steps):
            got = swap_chip(parts_back.pop().astype(BF), step)
            if step == 0:
                got = after(got, dvocab_send, *parts_back)
                dvocab_keep = dvocab_call(expos, pieces, after(local, got), whole, other, 0, BF)
            elif step == n_steps - 1:
                got = after(got, dvocab_keep)
            for index in range(len(parts_back)):
                span = slice(firsts[index], firsts[index + 1])
                parts_back[index] = parts_back[index] + got[span].astype(F32)
        kept = parts_back[0][0]
        back = lax.ppermute(kept.astype(BF), "pass", [(0, 2), (1, 3)])

        vocab_got = swap_core(dvocab_send)
        vocab_keep = dvocab_keep[:shard].astype(F32) + vocab_got[:shard].astype(F32)
        vocab_send = (dvocab_keep[shard:].astype(F32) + vocab_got[shard:].astype(F32)).astype(BF)
        back = after(back, vocab_send)
        cuts = (0, shard // 4, 5 * shard // 8, shard)
        vocab_parts = [after(vocab_send, back)[a:b] for a, b in zip(cuts, cuts[1:])]
        vocab_parts[0] = swap_pass(vocab_parts[0], 1)

        def packed(rows):
            return like((n_half, rows, width), wire)

        def sent(x):
            return x.astype(BF)

        rows_ffn = 8 * unit + ins_rows
        dsecond, keep_ffn, send_ffn, vec_ffn, loss = run(
            ffn_back_kernel,
            [like((count, width), F32), packed(rows_ffn), packed(rows_ffn), like((8, width), F32), like((8, LANES), F32)],
            [Far(hidden), Far(third), gain, Far(ffn_out), Far(slope), Far(second), shift, Far(ffn_in)]
            + [kept, back, dhead, head_loss, local, whole, other, ins_keep, ins_send],
            6.0,
            16,
            turn_scratch(hid, count) + turn_scratch(width, count) + [pltpu.VMEM((count, hid), BF)],
            "ffn_backward",
        )
        dsecond, keep_ffn, send_ffn, vec_ffn, loss = after_all(
            [dsecond, keep_ffn, send_ffn, vec_ffn, loss], vocab_parts[0]
        )
        vocab_parts[1] = swap_pass(after(vocab_parts[1], dsecond), 1)
        keep_ffn, send_ffn = add_call([keep_ffn, swap_core(sent(send_ffn))], n_half // 2, n_half // 2)
        dsecond = after(dsecond, send_ffn)
        dfirst, *chunk_cross, vec_cross, src0, src1, src2, src3 = run(
            cross_back_kernel,
            [
                like((count, width), F32),
                packed(4 * unit),
                packed(4 * unit),
                like((8, width), F32),
                like((part, width), F32),
                like((part, width), BF),
                like((part, width), BF),
                like((part, width), BF),
            ],
            [dsecond, Far(cross_out), Far(ctx2), Far(keyval), Far(probs2), Far(query_far), *parts]
            + [Far(cross_kv), Far(first_far), gain, shift, Far(cross_query)],
            8.0,
            15,
            turn_scratch(width, count)
            + turn_scratch(width, src)
            + [pltpu.VMEM((count, width), BF), pltpu.VMEM((src, 2 * width), BF), pltpu.VMEM((count, width), BF)],
            "cross_backward",
        )
        blocks_ffn = [keep_ffn, swap_chip(sent(send_ffn), 0)]
        dfirst, *chunk_cross, vec_cross, src0, src1, src2, src3 = after_all(
            [dfirst, *chunk_cross, vec_cross, src0, src1, src2, src3], vocab_parts[1]
        )
        vocab_parts[2] = swap_pass(after(vocab_parts[2], dfirst), 1)
        input_grad, *chunk_self = run(
            self_back_kernel,
            [Far(like((count, width), F32)), packed(4 * unit + EXTRA), packed(4 * unit + EXTRA)],
            [dfirst, Far(self_out), Far(ctx1), Far(qkv), Far(probs1), Far(rows), gain, shift, Far(self_qkv)]
            + [vec_ffn, vec_cross, d_delete],
            6.0,
            12,
            turn_scratch(width, count) + [pltpu.VMEM((count, 3 * width), BF), pltpu.VMEM((count, width), BF)],
            "self_backward",
        )
        def reduce_chips(blocks, step):
            while step < n_steps:
                half = n_half >> (step + 1)
                keep, send = add_call(blocks, half, half)
                blocks = [keep, swap_chip(sent(send), step)]
                step += 1
            return blocks

        def rows_at(*spots, extra=0, start=8):
            spans = [(i * unit, (i + 1) * unit) for i in spots]
            return spans + ([(start * unit, start * unit + extra)] if extra else [])

        input_grad, *chunk_self = after_all([input_grad, *chunk_self], blocks_ffn[1], vocab_parts[2])
        token_grad = vocab_keep + jnp.concatenate(vocab_parts, axis=0).astype(F32)
        blocks_ffn = reduce_chips(blocks_ffn, 1)

        got_cross = swap_core(sent(chunk_cross[1]))
        keep_self, send_self = chunk_self
        send_self = after(send_self, got_cross)
        got_self = swap_core(sent(send_self))
        keep_att, send_att = add_call([chunk_cross[0], got_cross, keep_self, got_self], n_half // 2, n_half // 2)
        source_got = [swap_pass(value, bit) for bit, value in ((1, src1), (2, src2), (3, src3))]
        source_grad = src0 + sum(got.astype(F32) for got in source_got)
        blocks_att = [keep_att, swap_chip(after(sent(send_att), blocks_ffn[1], source_got[1]), 0)]

        keep, send = regroup(
            blocks_ffn,
            [rows_at(0, 2, 4, 6, extra=ins_rows), rows_at(1, 3, 5, 7, extra=ins_rows)],
        )
        got = swap_pass(sent(send), 1)
        blocks_att[1] = after(blocks_att[1], got, source_got[0], source_got[2])
        blocks_att = reduce_chips(blocks_att, 1)
        keep, send = regroup(
            [keep, got],
            [rows_at(0, 2, extra=ins_rows, start=4), rows_at(1, 3, extra=ins_rows, start=4)],
        )
        got = swap_pass(sent(send), 2)
        blocks_att[1] = after(blocks_att[1], got)
        pieces_by_place = regroup(blocks_att, [rows_at(i, 4 + i, extra=EXTRA) for i in range(4)])
        own, ins_sum = regroup([keep, got], [rows_at(0, 1), rows_at(extra=ins_rows, start=2)])
        near, third_part = swap_pass(sent(own), 1), swap_pass(sent(own), 2)
        ffn_parts = [own, near, third_part, swap_pass(third_part, 1), ins_sum]

        gots = [swap_pass(sent(pieces_by_place[b]), b) for b in (1, 2, 3)]
        own, extra_sum = regroup(
            [pieces_by_place[0], *gots], [rows_at(0, 1), rows_at(extra=EXTRA, start=2)], pair_kernel, "sum_pass"
        )
        attention_parts = [own] + [swap_pass(sent(own), b) for b in (1, 2, 3)] + [extra_sum]

        def out(*shape):
            return Far(like(shape, F32))

        p_out, p_in, p_insert = run(
            ffn_end_kernel, [out(hid // n_dp, width), out(unit, hid), out(2 * unit, INS)], ffn_parts, 1.0, 8,
            name="ffn_sums",
        )
        p_cross, p_kv, p_query, p_self, p_qkv, p_gain, p_bias, p_delete = run(
            attention_end_kernel,
            [out(unit, width), out(unit, 2 * width), out(unit, width), out(unit, width), out(unit, 3 * width)]
            + [out(4, unit), out(4, unit), out(unit, 2)],
            attention_parts,
            1.0,
            8,
            name="attention_sums",
        )
        return (
            layer[None, None],
            loss[:1, :1],
            input_grad[None, None],
            source_grad[None],
            p_gain,
            p_bias,
            p_qkv,
            p_self,
            p_query,
            p_kv,
            p_cross,
            p_in,
            p_out,
            p_delete,
            p_insert,
            token_grad,
        )

    full = ("pass", "dp")
    rows_at, row_at = P("pass", "dp", None, None), P("pass", "dp", None)
    weight_at = P("dp", None)
    return jax.shard_map(
        body,
        mesh=mesh,
        in_specs=(rows_at, row_at, row_at, row_at, P("dp", "pass", None), P("dp", "pass"))
        + (P(),) * 11
        + (P(full, None),),
        out_specs=(rows_at, P("pass", "dp"), rows_at, P("dp", "pass", None), P(None, "dp"), P(None, "dp"))
        + (weight_at,) * 9
        + (P(full, None),),
        check_vma=False,
    )
```

```python
import functools

import jax
import jax.numpy as jnp
from jax import lax
from jax.experimental import pallas as pl
from jax.experimental.pallas import tpu as pltpu
from jax.sharding import PartitionSpec as P

HEADS = 8
INS = 256
EPS = 1e-05
LANES = 128
EXTRA = 16
BF = jnp.bfloat16
F32 = jnp.float32
MIB = 1 << 20


def cost(us):
    return pl.CostEstimate(flops=int(us * 0.3e9), bytes_accessed=1, transcendentals=0)


def dot(left, right, dims):
    return lax.dot_general(left, right, (dims, ((), ())), preferred_element_type=F32)


def nn(left, right):
    return dot(left, right, ((1,), (0,)))


def nt(left, right):
    return dot(left, right, ((1,), (1,)))


def flip(values):
    return values.astype(F32).T.astype(BF)


class Far:
    def __init__(self, value):
        self.value = value


class Raw(Far):
    pass


class Pin(Far):
    pass


class Fetched:
    def __init__(self, source, buffer, sem):
        self.buffer, self.shape, self.dtype = buffer, buffer.shape, buffer.dtype
        self.copy = pltpu.make_async_copy(source, buffer, sem)
        self.copy.start()
        self.waiting = True

    def wait(self):
        if self.waiting:
            self.copy.wait()
            self.waiting = False

    def __getitem__(self, index):
        self.wait()
        return self.buffer[index]


class Stored:
    def __init__(self, target, buffer, sem):
        self.buffer, self.shape, self.dtype = buffer, buffer.shape, buffer.dtype
        self.copy = pltpu.make_async_copy(buffer, target, sem)
        self.sent = False

    def __getitem__(self, index):
        return self.buffer[index]

    def __setitem__(self, index, value):
        self.buffer[index] = value

    def send(self):
        self.copy.start()
        self.sent = True


def run(kernel, outs, ins, us, limit, scratch=(), name=None):
    far_in, far_out = [type(x) is Far for x in ins], [type(x) is Far for x in outs]
    marks_in, marks_out = [type(x) for x in ins], [type(x) for x in outs]
    ins = [x.value if isinstance(x, Far) else x for x in ins]
    outs = [x.value if isinstance(x, Far) else x for x in outs]
    buffers = [pltpu.VMEM(x.shape, x.dtype) for x, f in zip(ins + outs, far_in + far_out) if f]
    spaces = {Far: pltpu.HBM, Raw: pltpu.HBM, Pin: pltpu.VMEM}
    ins = [pltpu.with_memory_space_constraint(x, spaces[m]) if m in spaces else x for x, m in zip(ins, marks_in)]
    outs = [spaces[m](x.shape, x.dtype) if m in spaces else x for x, m in zip(outs, marks_out)]
    n_in, n_out = len(ins), len(outs)

    def wrapped(*refs):
        if buffers:
            sems = refs[-1]
            held = list(refs[-1 - len(buffers) : -1])
            rest = refs[n_in + n_out : len(refs) - 1 - len(buffers)]
        else:
            held, rest = [], refs[n_in + n_out :]
        given, made, count = [], [], 0
        for ref, far in zip(refs[:n_in], far_in):
            given.append(Fetched(ref, held[count], sems.at[count]) if far else ref)
            count += far
        for ref, far in zip(refs[n_in : n_in + n_out], far_out):
            made.append(Stored(ref, held[count], sems.at[count]) if far else ref)
            count += far
        kernel(*given, *made, *rest)
        for x in given:
            if isinstance(x, Fetched):
                x.wait()
        for x in made:
            if isinstance(x, Stored) and not x.sent:
                x.send()
        for x in made:
            if isinstance(x, Stored):
                x.copy.wait()

    def place(mark):
        return pl.BlockSpec(memory_space=spaces.get(mark, pltpu.VMEM))

    return pl.pallas_call(
        wrapped,
        out_shape=outs,
        in_specs=[place(m) for m in marks_in],
        out_specs=[place(m) for m in marks_out],
        scratch_shapes=list(scratch) + buffers + ([pltpu.SemaphoreType.DMA((len(buffers),))] if buffers else []),
        compiler_params=pltpu.CompilerParams(vmem_limit_bytes=limit * MIB),
        cost_estimate=cost(us),
        name=name,
    )(*ins)


def after(value, *done):
    return lax.optimization_barrier((value, *done))[0]


def after_all(values, *done):
    return list(lax.optimization_barrier((*values, *done))[: len(values)])


def like(shape, dtype):
    return jax.ShapeDtypeStruct(shape, dtype)


def norm_parts(values):
    center = values - jnp.mean(values, axis=-1, keepdims=True)
    rstd = lax.rsqrt(jnp.mean(center * center, axis=-1, keepdims=True) + EPS)
    return center * rstd, rstd


def norm_out(unit, gain, shift, index):
    return (unit * gain[index : index + 1] + shift[index : index + 1]).astype(BF)


def norm_bwd(grad, unit, rstd, gain):
    scaled = grad * gain
    back = rstd * (
        scaled
        - jnp.mean(scaled, axis=-1, keepdims=True)
        - unit * jnp.mean(scaled * unit, axis=-1, keepdims=True)
    )
    return back, jnp.sum(grad * unit, axis=0, keepdims=True), jnp.sum(grad, axis=0, keepdims=True)


def column(row, count):
    return jnp.broadcast_to(row, (count, row.shape[1])).T


def lane_half(values, half):
    lane = lax.broadcasted_iota(jnp.int32, values.shape, 1)
    picked = (lane >= LANES // 2) if half else (lane < LANES // 2)
    return jnp.where(picked, values, jnp.zeros_like(values))


def attend(query, keys, values, bias_ref, probs_ref, out_ref, scale):
    half_size = LANES // 2
    for tile in range(out_ref.shape[1] // LANES):
        q = query(tile).astype(F32) * scale
        k, v_t = keys(tile), flip(values(tile))
        parts = []
        for half in range(2):
            scores = nt(k, lane_half(q, half).astype(BF)) + bias_ref[...]
            expo = jnp.exp(scores - jnp.max(scores, axis=0, keepdims=True))
            probs = (expo * (1.0 / jnp.sum(expo, axis=0, keepdims=True))).astype(BF)
            probs_ref[2 * tile + half] = probs
            parts.append(nn(v_t[half * half_size : (half + 1) * half_size], probs))
        out_ref[:, tile * LANES : (tile + 1) * LANES] = jnp.concatenate(parts, axis=0).T.astype(BF)


def attend_bwd(grad, query, keys, values, probs_ref, put_query, put_keys, put_values, scale, tiles):
    half_size = LANES // 2
    for tile in range(tiles):
        g, q, k, v = grad(tile), query(tile), keys(tile), values(tile)
        k_t = flip(k)
        dq, dk, dv = [], [], []
        for half in range(2):
            probs = probs_ref[2 * tile + half]
            full = probs.astype(F32)
            dprobs = nt(v, lane_half(g, half))
            delta = jnp.sum(dprobs * full, axis=0, keepdims=True)
            dscores = (full * ((dprobs - delta) * scale)).astype(BF)
            dv.append(nn(probs, g))
            dk.append(nn(dscores, q))
            dq.append(nn(k_t[half * half_size : (half + 1) * half_size], dscores))
        lane = lax.broadcasted_iota(jnp.int32, dk[0].shape, 1) < half_size
        put_query(tile, jnp.concatenate(dq, axis=0).T.astype(BF))
        put_keys(tile, jnp.where(lane, dk[0], dk[1]).astype(BF))
        put_values(tile, jnp.where(lane, dv[0], dv[1]).astype(BF))


def tile_of(ref, start):
    return lambda tile: ref[:, start + tile * LANES : start + (tile + 1) * LANES]


def put_in(ref, start):
    def put(tile, value):
        ref[:, start + tile * LANES : start + (tile + 1) * LANES] = value

    return put


def solution(mesh):
    n_pass, n_dp = mesh.shape["pass"], mesh.shape["dp"]
    bits = [1 << i for i in range(n_dp.bit_length() - 1)]
    core_bit, chip_bits = bits[0], bits[1:]
    orders = (chip_bits, chip_bits[1::-1] + chip_bits[2:])
    n_steps = len(chip_bits)
    n_half = n_dp // 2

    def swap_core(x):
        return lax.ppermute(x, "dp", [(i, i ^ core_bit) for i in range(n_dp)])

    def swap_chip(x, step):
        return lax.ppermute(x, "dp", [(i, i ^ orders[i & 1][step]) for i in range(n_dp)])

    def swap_pass(x, bit):
        return lax.ppermute(x, "pass", [(i, i ^ bit) for i in range(n_pass)])

    def owners():
        me = lax.axis_index("dp")
        core = me & 1
        result = []
        for slot in range(n_dp):
            own_half = slot < n_half
            turn = core if own_half else 1 - core
            owner = me if own_half else me ^ 1
            for step in range(n_steps):
                if (slot >> (n_steps - 1 - step)) & 1:
                    owner = owner ^ jnp.where(turn == 0, orders[0][step], orders[1][step])
            result.append(owner)
        return result

    def small_dtype(rows):
        return BF if rows % 16 == 0 else F32

    def turn_rows(values, turned_ref, sorted_ref, owner_list):
        block = values.shape[1] // n_dp
        turned_ref[...] = values.astype(F32).T.astype(turned_ref.dtype)
        for slot, owner in enumerate(owner_list):
            start = pl.multiple_of(owner * block, block)
            sorted_ref[slot * block : (slot + 1) * block] = turned_ref[pl.ds(start, block)]
        return sorted_ref[...].astype(BF)

    def turn_scratch(features, count):
        dtype = small_dtype(features // n_dp)
        return [pltpu.VMEM((features, count), dtype)] * 2

    def pack(keep_ref, send_ref, base, first, left_t, right):
        width = keep_ref.shape[2]
        section = lax.axis_index("pass")
        unit = width // n_dp
        block = left_t.shape[0] // n_dp
        quarter = first
        for col in range(right.shape[1] // width):
            grad = nn(left_t, right[:, col * width : (col + 1) * width]).astype(keep_ref.dtype)
            for piece in range(block // unit):
                place = pl.ds(pl.multiple_of(base + (quarter ^ section) * unit, unit), unit)
                for slot in range(n_dp):
                    ref, index = (keep_ref, slot) if slot < n_half else (send_ref, slot - n_half)
                    start = slot * block + piece * unit
                    ref[index, place] = grad[start : start + unit]
                quarter += 1
        return quarter


    def self_kernel(x, gain, shift, w_qkv, seg, w_out, w_query, first, query, first_far, query_far, qkv, probs, ctx, bias):
        width = x.shape[1]
        gains, shifts = gain[...].astype(F32), shift[...].astype(F32)
        rows = x[...].astype(F32)
        unit, _ = norm_parts(rows)
        qkv[...] = nn(norm_out(unit, gains, shifts, 0), w_qkv[...]).astype(BF)
        seg_row = seg[...].astype(F32)
        bias[...] = jnp.where(column(seg_row, seg_row.shape[1]) == seg_row, 0.0, -1000000000.0)
        attend(
            tile_of(qkv, 0), tile_of(qkv, width), tile_of(qkv, 2 * width), bias, probs, ctx, (width // HEADS) ** -0.5
        )
        for ref in (qkv, probs, ctx):
            ref.send()
        added = rows + nn(ctx[...], w_out[...])
        first[...] = added
        first_far[...] = added
        first_far.send()
        unit, _ = norm_parts(added)
        value = nn(norm_out(unit, gains, shifts, 1), w_query[...]).astype(BF)
        query[...] = value
        query_far[...] = value

    def cross_kernel(
        first, query, w_kv, seg, part0, part1, part2, part3, w_out, gain, shift, w_in, w_ffn, labels, mask,
        second, keyval, probs, ctx, hidden, slope, third, layer, final, bias,
    ):
        width = first.shape[1]
        count = first.shape[0]
        seg_row = seg[...].astype(F32)
        size = part0.shape[0] - EXTRA
        for index, part in enumerate((part0, part1, part2, part3)):
            span = slice(index * size, (index + 1) * size)
            keyval[span] = nn(part[:size], w_kv[...]).astype(BF)
            source_seg = part[size : size + EXTRA, :size].astype(F32)[0:1]
            bias[span] = jnp.where(column(source_seg, count) == seg_row, 0.0, -1000000000.0)
        attend(
            tile_of(query, 0), tile_of(keyval, 0), tile_of(keyval, width), bias, probs, ctx, (width // HEADS) ** -0.5
        )
        for ref in (keyval, probs, ctx):
            ref.send()
        added = first[...] + nn(ctx[...], w_out[...])
        second[...] = added
        second.send()
        gains, shifts = gain[...].astype(F32), shift[...].astype(F32)
        unit, _ = norm_parts(added)
        normed = norm_out(unit, gains, shifts, 2)
        for col in range(w_in.shape[1] // width):
            span = slice(col * width, (col + 1) * width)
            inner = nn(normed, w_in[:, span])
            cdf = 0.5 * (1.0 + lax.erf(inner * 0.7071067811865476))
            hidden[:, span] = (inner * cdf).astype(BF)
            slope[:, span] = (cdf + inner * jnp.exp(-0.5 * inner * inner) * 0.3989422804014327).astype(BF)
        hidden.send()
        slope.send()
        added = added + nn(hidden[...], w_ffn[...])
        third[...] = added
        layer[...] = added.astype(BF)
        third.send()
        layer.send()
        unit, _ = norm_parts(added)
        normed = norm_out(unit, gains, shifts, 3)
        size = count // 2
        for index in range(2):
            span = slice(index * size, (index + 1) * size)
            final[index, :size] = normed[span]
            label = labels[:, span]
            line = lax.broadcasted_iota(jnp.int32, (EXTRA, size), 0)
            high = lax.shift_right_logical(label, 8).astype(F32)
            marks = jnp.where(line == 0, high, 0.0)
            marks = jnp.where(line == 1, (label & 255).astype(F32), marks)
            marks = jnp.where(line == 2, mask[:, span].astype(F32), marks)
            lined = jnp.concatenate([marks, jnp.zeros((EXTRA, width - size), F32)], axis=1)
            final[index, size:] = lined.astype(BF)

    def head_kernel(
        final, seg, labels, mask, w_delete, w_insert,
        dfinal, keep, send, d_delete, loss, turned, ordered,
    ):
        section = lax.axis_index("pass")
        count = seg.shape[1]
        width = final.shape[2]
        h = jnp.concatenate([final[0, : count // 2], final[1, : count // 2]], axis=0)
        h32 = h.astype(F32)
        seg_col = column(seg[...].astype(F32), LANES)
        row_id = lax.broadcasted_iota(jnp.int32, (count, LANES), 0)
        linked = (pltpu.roll(seg_col, count - 1, 0) == seg_col) & (row_id < count - 1)
        linked = jnp.concatenate([linked.astype(F32)] * (width // LANES), axis=1)
        after = (pltpu.roll(h32, count - 1, 0) * linked).astype(BF)
        weight = column(mask[...].astype(F32), LANES)

        def entropy(logits, label, live):
            top = jnp.max(logits, axis=-1, keepdims=True)
            expo = jnp.exp(logits - top)
            total = jnp.sum(expo, axis=-1, keepdims=True)
            lane = lax.broadcasted_iota(jnp.int32, logits.shape, 1)
            target = column(label.astype(F32), logits.shape[1])
            hit = lane.astype(F32) == target
            picked = jnp.sum(jnp.where(hit, logits, 0.0), axis=1, keepdims=True)
            w = weight[:, :1] * live
            rest = jnp.sum(jnp.where(hit, 0.0, expo), axis=1, keepdims=True)
            grad = jnp.where(hit, -rest, expo) * (w / total)
            return jnp.sum(w * (top + jnp.log(total) - picked)), grad.astype(BF)

        label = labels[...]
        spot = lax.broadcasted_iota(jnp.int32, (LANES, width), 0)
        two = w_delete[...].astype(F32)
        both_rows = jnp.where(spot == 0, two[0:1], jnp.where(spot == 1, two[1:2], 0.0)).astype(BF)
        logits = nt(h, both_rows)
        lane = lax.broadcasted_iota(jnp.int32, logits.shape, 1)
        logits = jnp.where(lane < 2, logits, -1e30)
        loss_d, grad_d = entropy(logits, lax.rem(label, 2), (section == 0).astype(F32))
        logits = nn(h, w_insert[:width]) + nn(after, w_insert[width:])
        loss_i, grad_i = entropy(logits, lax.rem(label, INS), (section == 1).astype(F32))
        loss[...] = jnp.full(loss.shape, loss_d + loss_i)
        d_after = nt(grad_i, w_insert[width:]) * linked
        dfinal[...] = nn(grad_d, both_rows) + nt(grad_i, w_insert[:width]) + pltpu.roll(d_after, 1, 0)
        d_delete[...] = nn(flip(grad_d)[:EXTRA], h)[: d_delete.shape[0]]
        both_t = turn_rows(jnp.concatenate([h, after], axis=1), turned, ordered, owners())
        grad = nn(both_t, grad_i).astype(keep.dtype)
        block = both_t.shape[0] // n_dp
        half = block // 2
        for slot in range(n_dp):
            ref, index = (keep, slot) if slot < n_half else (send, slot - n_half)
            ref[index, :, :INS] = grad[slot * block : slot * block + half]
            ref[index, :, INS:] = grad[slot * block + half : (slot + 1) * block]


    def shard_base(chunk, shard):
        section, me = lax.axis_index("pass"), lax.axis_index("dp")
        return ((section ^ (chunk >> 1)) * n_dp + (me ^ (chunk & 1))) * shard

    def hits(base, start, shape, label):
        ids = lax.broadcasted_iota(jnp.int32, shape, 0) + (base + start)
        return ids == label

    def slots_of(refs):
        return [(ref, (i, half)) for half in range(2) for ref in refs for i in range(ref.shape[0])]

    def logit_kernel(n_prev, turn, n_tokens, spots, *refs):
        slots = [slots_of(refs[:n_tokens])[i] for i in spots]
        vocab, refs = refs[n_tokens : n_tokens + 4], refs[n_tokens + 4 :]
        if n_prev:
            prev, refs = refs[0], refs[1:]
        n = len(slots) // 2
        stats, expos = refs[0], refs[1 : 1 + n]
        turned = refs[1 + n] if turn else None
        h, logits = refs[-2:]
        size = slots[0][0].shape[2] - EXTRA
        count = 2 * size
        shard = vocab[0].shape[0]
        if n_prev:
            stats[:, : n_prev * count] = prev[...]
        for tile in range(n):
            both = slots[2 * tile : 2 * tile + 2]
            for index, (ref, i) in enumerate(both):
                h[index * size : (index + 1) * size] = ref[*i, :size]
            marks = jnp.concatenate([ref[*i, size:].astype(F32)[:, :size] for ref, i in both], axis=1)
            label_f = marks[0:1] * 256.0 + marks[1:2]
            label = label_f.astype(jnp.int32)
            weight = marks[2:3]
            peak = jnp.full((8, count), -jnp.inf, F32)
            for chunk, ref in enumerate(vocab):
                for start in range(0, shard, 1024):
                    step = min(1024, shard - start)
                    value = nt(ref[start : start + step], h[...])
                    at = chunk * shard + start
                    logits[at : at + step] = value
                    peak = jnp.maximum(peak, jnp.max(value.reshape(step // 8, 8, count), axis=0))
                if turn and not tile:
                    turned[:, chunk * shard : (chunk + 1) * shard] = flip(ref[...])
            peak = jnp.max(peak, axis=0, keepdims=True)
            total = jnp.zeros((8, count), F32)
            chosen = jnp.zeros((8, count), F32)
            sub = min(shard, 128)
            expo = expos[tile]
            for chunk in range(4):
                base = shard_base(chunk, shard)

                def part(i, carry, chunk=chunk, base=base, expo=expo, peak=peak, label=label):
                    total, chosen = carry
                    at = pl.multiple_of(chunk * shard + i * sub, sub)
                    value = logits[pl.ds(at, sub)]
                    hit = hits(base, i * sub, (sub, count), label)
                    weight_of = jnp.where(hit, 0.0, jnp.exp(value - peak))
                    expo[pl.ds(at, sub)] = weight_of.astype(BF)
                    total = total + jnp.sum(weight_of.reshape(sub // 8, 8, count), axis=0)
                    picked = jnp.where(hit, value, 0.0)
                    return total, chosen + jnp.sum(picked.reshape(sub // 8, 8, count), axis=0)

                total, chosen = lax.fori_loop(0, shard // sub, part, (total, chosen))
            total = jnp.sum(total, axis=0, keepdims=True)
            chosen = jnp.sum(chosen, axis=0, keepdims=True)
            line = lax.broadcasted_iota(jnp.int32, (8, count), 0)
            block = jnp.zeros((8, count), F32)
            for at, value in enumerate((peak, total, chosen, label_f, weight)):
                block = jnp.where(line == at, value, block)
            at = (n_prev + tile) * count
            stats[:, at : at + count] = block

    def logit_call(tokens, vocab, prev, turn, spots):
        height, width = tokens[0].shape[2:]
        count = 2 * (height - EXTRA)
        n = len(spots) // 2
        shard = vocab[0].shape[0]
        n_prev = prev[0].shape[1] // count if prev else 0
        outs = [like((8, (n_prev + n) * count), F32)] + [like((4 * shard, count), BF)] * n
        stats, *rest = run(
            functools.partial(logit_kernel, n_prev, turn, len(tokens), spots),
            outs + ([like((width, 4 * shard), BF)] if turn else []),
            [*tokens, *vocab, *prev],
            2.8 * n,
            12,
            [pltpu.VMEM((count, width), BF), pltpu.VMEM((4 * shard, count), F32)],
            "token_logits",
        )
        return stats, rest[:n], rest[n:]

    def merged(own, other):
        peak = jnp.maximum(own[0:1], other[0:1])
        total = own[1:2] * jnp.exp(own[0:1] - peak) + other[1:2] * jnp.exp(other[0:1] - peak)
        return peak, total, own[2:3] + other[2:3]

    def merge_kernel(step, order, own, other, out):
        size = own.shape[1] // len(order)
        blocks = [other[:, i * size : (i + 1) * size] for i in range(len(order))]
        bit = len(order) >> (step + 2)
        swapped = jnp.concatenate([blocks[order.index((half, slot ^ bit))] for half, slot in order], axis=1)
        mine = own[...]
        peak, total, chosen = merged(mine, swapped)
        line = lax.broadcasted_iota(jnp.int32, mine.shape, 0)
        out[...] = jnp.where(
            line == 0, peak, jnp.where(line == 1, total, jnp.where(line == 2, chosen, mine))
        )

    def closing(local, merged_ref, other):
        peak, total, chosen = merged(merged_ref, other)
        hit = jnp.exp(chosen - peak)
        full = total + hit
        lse = peak + jnp.log(full)
        weight = local[4:5]
        factor = weight * jnp.exp(local[0:1] - lse)
        return lse, chosen, factor, -weight * (total / full)

    def dlogits_into(ref, at, cols, expo, start, base, shape, label, factor, at_label):
        sub = min(shape[0], 128)

        def part(i, _):
            row = pl.multiple_of(i * sub, sub)
            hit = hits(base, i * sub, (sub, shape[1]), label)
            value = expo[pl.ds(pl.multiple_of(start + row, sub), sub)].astype(F32) * factor
            ref[pl.ds(pl.multiple_of(at + row, sub), sub), cols] = jnp.where(hit, at_label, value).astype(BF)
            return 0

        lax.fori_loop(0, shape[0] // sub, part, 0)

    def dtoken_kernel(tile, expo, vocab_t, local, merged_ref, other, out, dlogits):
        rows, count = expo.shape
        shard = rows // 4
        span = slice(tile * count, (tile + 1) * count)
        _, _, factor, at_label = closing(local[:, span], merged_ref[:, span], other[:, span])
        label = local[3:4, span].astype(jnp.int32)
        for chunk in range(4):
            dlogits_into(
                dlogits, chunk * shard, slice(None), expo, chunk * shard, shard_base(chunk, shard),
                (shard, count), label, factor, at_label,
            )
        total = nn(vocab_t[...], dlogits[...]).T.astype(out.dtype)
        out[0] = total[: count // 2]
        out[1] = total[count // 2 :]

    def dtoken_call(expo, tile, local, merged_ref, other, vocab_t, dtype):
        rows, count = expo.shape
        return run(
            functools.partial(dtoken_kernel, tile),
            [like((2, count // 2, vocab_t.shape[0]), dtype)],
            [expo, vocab_t, local, merged_ref, other],
            2.2,
            8,
            [pltpu.VMEM((rows, count), BF)],
            "token_dfinal",
        )[0]

    def dvocab_kernel(shard, parity, n_tiles, *refs):
        expos, tokens = refs[:n_tiles], refs[n_tiles:-6]
        local, merged_ref, other, out, dlogits, held = refs[-6:]
        index = pl.program_id(0)
        _, _, factor, at_label = closing(local[...], merged_ref[...], other[...])
        label = local[3:4].astype(jnp.int32)
        size = tokens[0].shape[2] - EXTRA
        count = 2 * size
        section, me = lax.axis_index("pass"), lax.axis_index("dp")
        chunk = 2 * index + parity
        base = ((section ^ (chunk >> 1)) * n_dp + (me ^ (chunk & 1))) * shard
        slots = slots_of(tokens[:2]) + [slot for token in tokens[2:] for slot in slots_of([token])]
        for at, (token, i) in enumerate(slots):
            held[at * size : (at + 1) * size] = token[*i, :size]
        for at, expo in enumerate(expos):
            cols = slice(at * count, (at + 1) * count)
            dlogits_into(
                dlogits, 0, cols, expo, 0, base, (shard, count), label[:, cols], factor[:, cols], at_label[:, cols]
            )
        out[...] = nn(dlogits[...], held[...]).astype(out.dtype)

    def dvocab_call(expos, tokens, local, merged_ref, other, parity, dtype):
        shard, count = expos[0].shape[0] // 4, expos[0].shape[1]
        width = tokens[0].shape[3]
        total = local.shape[1]
        fixed2 = pl.BlockSpec(local.shape, lambda c: (0, 0))
        return pl.pallas_call(
            functools.partial(dvocab_kernel, shard, parity, len(expos)),
            grid=(2,),
            in_specs=[pl.BlockSpec((shard, count), lambda c: (2 * c + parity, 0))] * len(expos)
            + [pl.BlockSpec(t.shape, lambda c: (0, 0, 0, 0)) for t in tokens]
            + [fixed2] * 3,
            out_specs=pl.BlockSpec((shard, width), lambda c: (c, 0)),
            out_shape=like((2 * shard, width), dtype),
            scratch_shapes=[pltpu.VMEM((shard, total), BF), pltpu.VMEM((total, width), BF)],
            compiler_params=pltpu.CompilerParams(vmem_limit_bytes=20 * MIB),
            cost_estimate=cost(0.1),
            name="token_dvocab",
        )(*expos, *tokens, local, merged_ref, other)


    def ffn_back_kernel(
        hidden, third, gain, w_ffn, slope, second, shift, w_in,
        kept0, kept1, moved0, moved1, dhead, head_loss, local, merged_ref, other, ins_keep, ins_send,
        dsecond, keep, send, vecs, loss, wide_t, wide_s, thin_t, thin_s, dinner,
    ):
        width = third.shape[1]
        count = third.shape[0]
        live = (lax.axis_index("pass") >= 2).astype(F32)
        hidden_t = turn_rows(hidden[...], wide_t, wide_s, owners())
        parts = [kept[...] + moved[...].astype(F32) for kept, moved in ((kept0, moved0), (kept1, moved1))]
        dfinal = dhead[...] + live * jnp.concatenate(parts, axis=0)
        unit3, rstd3 = norm_parts(third[...])
        gains = gain[...].astype(F32)
        dthird, g_gain3, g_bias3 = norm_bwd(dfinal, unit3, rstd3, gains[3:4])
        low = dthird.astype(BF)
        pack(keep, send, 0, 0, hidden_t, low)
        for col in range(w_ffn.shape[0] // width):
            span = slice(col * width, (col + 1) * width)
            part = nt(low, w_ffn[span]).astype(BF).astype(F32) * slope[:, span].astype(F32)
            dinner[:, span] = part.astype(BF)
        unit2, rstd2 = norm_parts(second[...])
        normed_t = turn_rows(norm_out(unit2, gains, shift[...].astype(F32), 2), thin_t, thin_s, owners())
        pack(keep, send, 4 * (width // n_dp), 0, normed_t, dinner[...])
        extra = ins_keep.shape[1]
        keep[:, keep.shape[1] - extra :] = ins_keep[...]
        send[:, keep.shape[1] - extra :] = ins_send[...]
        dnormed = nt(dinner[...], w_in[...])
        back, g_gain2, g_bias2 = norm_bwd(dnormed, unit2, rstd2, gains[2:3])
        dsecond[...] = dthird + back
        token_loss = 0.0
        for start in (0, count):
            span = slice(start, start + count // 2)
            lse, chosen, _, _ = closing(local[:, span], merged_ref[:, span], other[:, span])
            token_loss = token_loss + jnp.sum(local[4:5, span] * (lse - chosen))
        loss[...] = head_loss[...] + token_loss * live
        line = lax.broadcasted_iota(jnp.int32, (8, width), 0)
        block = jnp.zeros((8, width), F32)
        for at, value in enumerate((g_gain3, g_gain2, g_bias3, g_bias2)):
            block = jnp.where(line == at, value, block)
        vecs[...] = block

    def cross_back_kernel(
        dsecond, w_out, ctx, keyval, probs, query, part0, part1, part2, part3, w_kv, first, gain, shift, w_query,
        dfirst, keep, send, vecs, dsrc0, dsrc2, dsrc13, thin_t, thin_s, src_t, src_s, dquery, dkeyval, dctx,
    ):
        width = first.shape[1]
        owner_list = owners()
        low = dsecond[...].astype(BF)
        dctx[...] = nt(low, w_out[...]).astype(BF)
        at = pack(keep, send, 0, 0, turn_rows(ctx[...], thin_t, thin_s, owner_list), low)
        attend_bwd(
            tile_of(dctx, 0), tile_of(query, 0), tile_of(keyval, 0), tile_of(keyval, width), probs,
            put_in(dquery, 0), put_in(dkeyval, 0), put_in(dkeyval, width), (width // HEADS) ** -0.5, width // LANES,
        )
        size = part0.shape[0] - EXTRA
        source = jnp.concatenate([p[:size] for p in (part0, part1, part2, part3)], axis=0)
        at = pack(keep, send, 0, at, turn_rows(source, src_t, src_s, owner_list), dkeyval[...])
        for index, (ref, row) in enumerate(((dsrc0, 0), (dsrc13, 0), (dsrc2, 0), (dsrc13, size))):
            part = nt(dkeyval[index * size : (index + 1) * size], w_kv[...])
            ref[row : row + size] = part.astype(ref.dtype)
        gains, shifts = gain[...].astype(F32), shift[...].astype(F32)
        unit, rstd = norm_parts(first[...])
        normed_t = turn_rows(norm_out(unit, gains, shifts, 1), thin_t, thin_s, owner_list)
        pack(keep, send, 0, at, normed_t, dquery[...])
        back, g_gain, g_bias = norm_bwd(nt(dquery[...], w_query[...]), unit, rstd, gains[1:2])
        dfirst[...] = dsecond[...] + back
        line = lax.broadcasted_iota(jnp.int32, (8, width), 0)
        vecs[...] = jnp.where(line == 0, g_gain, jnp.where(line == 1, g_bias, 0.0))

    def self_back_kernel(
        dfirst, w_out, ctx, qkv, probs, x, gain, shift, w_qkv, vec_ffn, vec_cross, d_delete,
        dx, keep, send, thin_t, thin_s, dqkv, dctx,
    ):
        width = x.shape[1]
        owner_list = owners()
        low = dfirst[...].astype(BF)
        dctx[...] = nt(low, w_out[...]).astype(BF)
        at = pack(keep, send, 0, 0, turn_rows(ctx[...], thin_t, thin_s, owner_list), low)
        attend_bwd(
            tile_of(dctx, 0), tile_of(qkv, 0), tile_of(qkv, width), tile_of(qkv, 2 * width), probs,
            put_in(dqkv, 0), put_in(dqkv, width), put_in(dqkv, 2 * width), (width // HEADS) ** -0.5, width // LANES,
        )
        gains, shifts = gain[...].astype(F32), shift[...].astype(F32)
        unit, rstd = norm_parts(x[...].astype(F32))
        normed_t = turn_rows(norm_out(unit, gains, shifts, 0), thin_t, thin_s, owner_list)
        at = pack(keep, send, 0, at, normed_t, dqkv[...])
        back, g_gain, g_bias = norm_bwd(nt(dqkv[...], w_qkv[...]), unit, rstd, gains[0:1])
        dx[...] = dfirst[...] + back
        line = lax.broadcasted_iota(jnp.int32, (EXTRA, width), 0)
        block = jnp.zeros((EXTRA, width), F32)
        lines = (
            (0, d_delete[0:1]), (1, d_delete[1:2]),
            (8, g_gain), (9, vec_cross[0:1]), (10, vec_ffn[1:2]), (11, vec_ffn[0:1]),
            (12, g_bias), (13, vec_cross[1:2]), (14, vec_ffn[3:4]), (15, vec_ffn[2:3]),
        )
        for row, value in lines:
            block = jnp.where(line == row, value, block)
        block = block.astype(keep.dtype)
        at = at * (width // n_dp)
        for slot in range(n_half):
            keep[slot, at:] = block
            send[slot, at:] = block


    def add_kernel(pairs, *refs):
        ins, outs = refs[: 2 * pairs], refs[2 * pairs :]
        at = 0
        for keep, got in zip(ins[::2], ins[1::2]):
            rows = keep.shape[1]
            slot = 0
            for ref in outs:
                for i in range(ref.shape[0]):
                    value = keep[slot].astype(F32) + got[slot].astype(F32)
                    ref[i, at : at + rows] = value.astype(ref.dtype)
                    slot += 1
            at += rows

    def add_call(blocks, *counts):
        rows, width = sum(b.shape[1] for b in blocks[::2]), blocks[0].shape[2]
        outs = [like((count, rows, width), wire_of(width)) for count in counts]
        return run(functools.partial(add_kernel, len(blocks) // 2), outs, blocks, 0.8, 8, name="sum_slots")

    def wire_of(width):
        return small_dtype(width // n_dp)

    def regroup_kernel(plan, n_terms, *refs):
        value = refs[0][...].astype(F32)
        for ref in refs[1:n_terms]:
            value = value + ref[...].astype(F32)
        for spans, ref in zip(plan, refs[n_terms:]):
            at = 0
            for start, stop in spans:
                ref[at : at + stop - start] = value[start:stop].astype(ref.dtype)
                at += stop - start

    def pair_kernel(plan, n_terms, *refs):
        first = refs[0][...].astype(F32) + refs[1][...].astype(F32)
        value = first + (refs[2][...].astype(F32) + refs[3][...].astype(F32))
        for spans, ref in zip(plan, refs[n_terms:]):
            at = 0
            for start, stop in spans:
                ref[at : at + stop - start] = value[start:stop].astype(ref.dtype)
                at += stop - start

    def regroup(terms, plan, kernel=regroup_kernel, name="sum_rows"):
        width = terms[0].shape[-1]
        outs = [like((sum(b - a for a, b in spans), width), wire_of(width)) for spans in plan]
        terms = [t.reshape(t.shape[-2:]) for t in terms]
        return run(functools.partial(kernel, plan, len(terms)), outs, terms, 0.7, 8, name=name)

    def picked(pieces):
        section = lax.axis_index("pass")
        values = [p.astype(F32) for p in pieces]
        result = []
        for j in range(4):
            value = values[0]
            for b in (1, 2, 3):
                value = jnp.where((section ^ b) == j, values[b], value)
            result.append(value)
        return result

    def halves(refs):
        rows = refs[0].shape[0] // 2
        return [r[:rows] for r in refs], [r[rows:] for r in refs]

    def ffn_end_kernel(own, near, third, far, extra, p_out, p_in, p_insert):
        outs, ins = halves((own, near, third, far))
        rows, width = outs[0].shape
        for j, value in enumerate(picked(outs)):
            p_out[j * rows : (j + 1) * rows] = value
        for j, value in enumerate(picked(ins)):
            p_in[:, j * width : (j + 1) * width] = value
        half = p_insert.shape[0] // 2
        value = extra[...].astype(F32)
        p_insert[:half] = value[:, :INS]
        p_insert[half:] = value[:, INS:]

    def attention_end_kernel(
        own, near, third, far, extra, p_cross, p_kv, p_query, p_out, p_qkv, p_gain, p_bias, p_delete
    ):
        cross, own_part = halves((own, near, third, far))
        width = extra.shape[1]
        values = picked(cross)
        p_cross[...] = values[0]
        p_kv[:, :width] = values[1]
        p_kv[:, width:] = values[2]
        p_query[...] = values[3]
        values = picked(own_part)
        p_out[...] = values[0]
        for j in range(3):
            p_qkv[:, j * width : (j + 1) * width] = values[j + 1]
        size = p_gain.shape[1]
        me = lax.axis_index("dp")
        mine = pltpu.roll(extra[...].astype(F32), lax.rem(width - me * size, width), 1)
        p_gain[...] = mine[8:12, :size]
        p_bias[...] = mine[12:16, :size]
        p_delete[...] = mine[:2, :size]

    def body(
        decoder_in,
        decoder_segments,
        edit_target,
        loss_mask,
        source_out,
        source_segments,
        norm_gain,
        norm_bias,
        self_qkv,
        self_out,
        cross_query,
        cross_kv,
        cross_out,
        ffn_in,
        ffn_out,
        delete_head,
        insert_head,
        token_head,
    ):
        section = lax.axis_index("pass")
        segs, labels, mask = decoder_segments[0], edit_target[0], loss_mask[0]
        rows = decoder_in[0, 0]
        count, width = rows.shape
        shard = token_head.shape[0]
        part = source_out.shape[1]
        src = n_pass * part
        hid = ffn_in.shape[1]
        unit = width // n_dp
        wire = small_dtype(unit)

        note = jnp.pad(source_segments.astype(BF), ((0, EXTRA - 1), (0, width - part)))
        mine = jnp.concatenate([source_out[0], note], axis=0)
        parts = [mine] + [swap_pass(mine, bit) for bit in (1, 2, 3)]

        gain, shift = Far(norm_gain), Far(norm_bias)
        first, query, first_far, query_far, qkv, probs1, ctx1 = run(
            self_kernel,
            [
                like((count, width), F32),
                like((count, width), BF),
                Far(like((count, width), F32)),
                Far(like((count, width), BF)),
                Far(like((count, 3 * width), BF)),
                Far(like((HEADS, count, count), BF)),
                Far(like((count, width), BF)),
            ],
            [Far(rows), gain, shift, Far(self_qkv), Far(segs), Far(self_out), Far(cross_query)],
            4.2,
            10,
            [pltpu.VMEM((count, count), F32)],
            "self_forward",
        )
        second, keyval, probs2, ctx2, hidden, slope, third, layer, final = run(
            cross_kernel,
            [
                Far(like((count, width), F32)),
                Far(like((src, 2 * width), BF)),
                Far(like((HEADS, src, count), BF)),
                Far(like((count, width), BF)),
                Far(like((count, hid), BF)),
                Far(like((count, hid), BF)),
                Far(like((count, width), F32)),
                Far(like((count, width), BF)),
                like((2, count // 2 + EXTRA, width), BF),
            ],
            [first, query, Pin(cross_kv), Far(segs), *parts, Pin(cross_out), gain, shift]
            + [Pin(ffn_in), Pin(ffn_out), Far(labels), Far(mask)],
            7.6,
            20,
            [pltpu.VMEM((src, count), F32)],
            "cross_forward",
        )

        near = swap_pass(after(token_head, parts[1]), 1)
        moved = lax.ppermute(final, "pass", [(2, 0), (3, 1)])
        group = jnp.where(section >= 2, final, moved)[None]
        tokens = [group]
        for step in reversed(range(n_steps)):
            tokens.append(swap_chip(group, step))
            if step:
                group = jnp.concatenate([group, tokens[-1]], axis=0)
        near = after(near, tokens[1])
        vocab = (token_head, swap_core(token_head), near, swap_core(near))
        expos, stats, vocab_t, order = [[], []], (), None, []
        for pieces in [tokens[:2]] + [[t] for t in tokens[2:]]:
            made = []
            for tile in range(sum(p.shape[0] for p in pieces)):
                stats, new, turned = logit_call(pieces, vocab, stats, not vocab_t, (2 * tile, 2 * tile + 1))
                stats = (stats,)
                vocab_t = vocab_t or turned
                made += new
            first_slot, n_slots = len(order) // 2, sum(p.shape[0] for p in pieces)
            for half in range(2):
                spot = half * len(made) // 2
                expos[half] += [(e, len(order) // 2 + i) for i, e in enumerate(made[spot : spot + len(made) // 2])]
                order += [(half, first_slot + i) for i in range(n_slots)]
        (vocab_t,) = vocab_t
        local = stats[0]
        whole = local
        for step in range(n_steps):
            (whole,) = run(
                functools.partial(merge_kernel, step, order), [like(local.shape, F32)], [whole, swap_chip(whole, step)],
                1.0, 8, name="stats_merge",
            )
        other = swap_pass(whole, 2)

        ins_rows = 2 * width // n_dp // 2
        dhead, ins_keep, ins_send, d_delete, head_loss = run(
            head_kernel,
            [
                like((count, width), F32),
                like((n_half, ins_rows, 2 * INS), wire),
                like((n_half, ins_rows, 2 * INS), wire),
                like((8, width), F32),
                like((8, LANES), F32),
            ],
            [after(final, whole), Far(segs), Far(labels), Far(mask), Far(delete_head.T), Pin(insert_head)],
            1.4,
            10,
            turn_scratch(2 * width, count),
            "small_heads",
        )
        other = after(other, dhead)

        n_tiles = len(expos[0])
        made = [[None] * n_tiles for _ in expos]
        for tile in reversed(range(n_tiles)):
            for half in range(2):
                dtype = BF if tile >= n_tiles // 2 and n_tiles > 1 else F32
                expo, spot = expos[half][tile]
                made[half][tile] = dtoken_call(expo, spot, local, whole, other, vocab_t, dtype)
        kept = []
        for half in range(2):
            tiles = made[half]
            for step in range(n_steps):
                if len(tiles) > 1:
                    middle = len(tiles) // 2
                    sending = tiles[middle:]
                    sending = jnp.concatenate(sending, axis=0) if len(sending) > 1 else sending[0]
                    got = swap_chip(sending.astype(BF), step)
                    tiles = [t + got[2 * i : 2 * i + 2].astype(F32) for i, t in enumerate(tiles[:middle])]
                else:
                    got = swap_chip(tiles[0][1].astype(BF), step)
                    kept.append(tiles[0][0] + got.astype(F32))
        backs = [lax.ppermute(k.astype(BF), "pass", [(0, 2), (1, 3)]) for k in kept]

        flat = [e for e, _ in sorted(sum(expos, []), key=lambda pair: pair[1])]
        dvocab_send = dvocab_call(flat, tokens, after(local, *kept), whole, other, 1, BF)
        dvocab_keep = dvocab_call(flat, tokens, after(local, dvocab_send), whole, other, 0, BF)
        backs = after_all(backs, dvocab_send, dvocab_keep)
        vocab_got = swap_core(after(dvocab_send, *backs))

        def packed(rows):
            return like((n_half, rows, width), wire)

        def sent(x):
            return x.astype(BF)

        def reduce_chips(blocks, step):
            while step < n_steps:
                half = n_half >> (step + 1)
                keep, send = add_call(blocks, half, half)
                blocks = [keep, swap_chip(sent(send), step)]
                step += 1
            return blocks

        rows_ffn = 8 * unit + ins_rows
        dsecond, keep_ffn, send_ffn, vec_ffn, loss = run(
            ffn_back_kernel,
            [like((count, width), F32), packed(rows_ffn), packed(rows_ffn), like((8, width), F32), like((8, LANES), F32)],
            [Pin(hidden), Pin(third), gain, Pin(ffn_out), Pin(slope), Pin(second), shift, Pin(ffn_in)]
            + [*kept, *backs, dhead, head_loss, local, whole, other, ins_keep, ins_send],
            0.1,
            16,
            turn_scratch(hid, count) + turn_scratch(width, count) + [pltpu.VMEM((count, hid), BF)],
            "ffn_backward",
        )
        dsecond, keep_ffn, send_ffn, vec_ffn, loss = after_all(
            [dsecond, keep_ffn, send_ffn, vec_ffn, loss], vocab_got
        )
        vocab_keep = dvocab_keep[:shard].astype(F32) + vocab_got[:shard].astype(F32)
        vocab_send = (dvocab_keep[shard:].astype(F32) + vocab_got[shard:].astype(F32)).astype(BF)
        cuts = [shard * i // 64 for i in (0, 30, 42, 64)]
        vocab_parts = [vocab_send[a:b] for a, b in zip(cuts, cuts[1:])]
        vocab_parts[0] = swap_pass(vocab_parts[0], 1)
        keep_ffn, send_ffn = add_call([keep_ffn, swap_core(sent(send_ffn))], n_half // 2, n_half // 2)
        dsecond = after(dsecond, send_ffn)
        dfirst, *chunk_cross, vec_cross, src0, src2, src13 = run(
            cross_back_kernel,
            [
                like((count, width), F32),
                packed(4 * unit),
                packed(4 * unit),
                like((8, width), F32),
                like((part, width), F32),
                like((part, width), F32),
                like((2 * part, width), BF),
            ],
            [dsecond, Pin(cross_out), Pin(ctx2), Pin(keyval), Pin(probs2), Pin(query_far), *parts]
            + [Pin(cross_kv), Pin(first_far), gain, shift, Pin(cross_query)],
            0.1,
            15,
            turn_scratch(width, count)
            + turn_scratch(width, src)
            + [pltpu.VMEM((count, width), BF), pltpu.VMEM((src, 2 * width), BF), pltpu.VMEM((count, width), BF)],
            "cross_backward",
        )
        blocks_ffn = [keep_ffn, swap_chip(sent(send_ffn), 0)]
        dfirst, *chunk_cross, vec_cross, src0, src2, src13 = after_all(
            [dfirst, *chunk_cross, vec_cross, src0, src2, src13], vocab_parts[0]
        )
        vocab_parts[1] = swap_pass(after(vocab_parts[1], dfirst), 1)
        input_grad, *chunk_self = run(
            self_back_kernel,
            [Far(like((count, width), F32)), packed(4 * unit + EXTRA), packed(4 * unit + EXTRA)],
            [dfirst, Pin(self_out), Pin(ctx1), Pin(qkv), Pin(probs1), Pin(rows), gain, shift, Pin(self_qkv)]
            + [vec_ffn, vec_cross, d_delete],
            0.1,
            12,
            turn_scratch(width, count) + [pltpu.VMEM((count, 3 * width), BF), pltpu.VMEM((count, width), BF)],
            "self_backward",
        )
        def rows_at(*spots, extra=0, start=8):
            spans = [(i * unit, (i + 1) * unit) for i in spots]
            return spans + ([(start * unit, start * unit + extra)] if extra else [])

        input_grad, *chunk_self = after_all([input_grad, *chunk_self], blocks_ffn[1], vocab_parts[1])
        blocks_ffn = reduce_chips(blocks_ffn, 1)

        got_cross = swap_core(sent(chunk_cross[1]))
        keep_self, send_self = chunk_self
        send_self = after(send_self, got_cross)
        got_self = swap_core(sent(send_self))
        keep_att, send_att = add_call([chunk_cross[0], got_cross, keep_self, got_self], n_half // 2, n_half // 2)
        source_got = swap_pass(src13, 1)
        source_half = swap_pass((src2 + source_got[part:].astype(F32)).astype(BF), 2)
        source_grad = (src0 + source_got[:part].astype(F32)) + source_half.astype(F32)
        blocks_att = [keep_att, swap_chip(after(sent(send_att), blocks_ffn[1], source_got), 0)]

        keep, send = regroup(
            blocks_ffn,
            [rows_at(0, 2, 4, 6, extra=ins_rows), rows_at(1, 3, 5, 7, extra=ins_rows)],
        )
        got = swap_pass(sent(send), 1)
        got = after(got, source_half)
        blocks_att[1] = after(blocks_att[1], got)
        blocks_att = reduce_chips(blocks_att, 1)
        keep, send = regroup(
            [keep, got],
            [rows_at(0, 2, extra=ins_rows, start=4), rows_at(1, 3, extra=ins_rows, start=4)],
        )
        got = swap_pass(sent(send), 2)
        vocab_parts[2] = swap_pass(after(vocab_parts[2], send), 1)
        token_grad = vocab_keep + jnp.concatenate(vocab_parts, axis=0).astype(F32)
        got = after(got, vocab_parts[2])
        blocks_att[1] = after(blocks_att[1], got)
        pieces_by_place = regroup(blocks_att, [rows_at(i, 4 + i, extra=EXTRA) for i in range(4)])
        own, ins_sum = regroup([keep, got], [rows_at(0, 1), rows_at(extra=ins_rows, start=2)])
        near, third_part = swap_pass(sent(own), 1), swap_pass(sent(own), 2)
        ffn_parts = [own, near, third_part, swap_pass(third_part, 1), ins_sum]

        gots = [swap_pass(sent(pieces_by_place[b]), b) for b in (1, 2, 3)]
        own, extra_sum = regroup(
            [pieces_by_place[0], *gots], [rows_at(0, 1), rows_at(extra=EXTRA, start=2)], pair_kernel, "sum_pass"
        )
        attention_parts = [own] + [swap_pass(sent(own), b) for b in (1, 2, 3)] + [extra_sum]

        def out(*shape):
            return Far(like(shape, F32))

        p_out, p_in, p_insert = run(
            ffn_end_kernel, [out(hid // n_dp, width), out(unit, hid), out(2 * unit, INS)], ffn_parts, 1.0, 8,
            name="ffn_sums",
        )
        p_cross, p_kv, p_query, p_self, p_qkv, p_gain, p_bias, p_delete = run(
            attention_end_kernel,
            [out(unit, width), out(unit, 2 * width), out(unit, width), out(unit, width), out(unit, 3 * width)]
            + [out(4, unit), out(4, unit), out(2, unit)],
            attention_parts,
            1.0,
            8,
            name="attention_sums",
        )
        return (
            layer[None, None],
            loss[:1, :1],
            input_grad[None, None],
            source_grad[None],
            p_gain,
            p_bias,
            p_qkv,
            p_self,
            p_query,
            p_kv,
            p_cross,
            p_in,
            p_out,
            p_delete.T,
            p_insert,
            token_grad,
        )

    full = ("pass", "dp")
    rows_at, row_at = P("pass", "dp", None, None), P("pass", "dp", None)
    weight_at = P("dp", None)
    return jax.shard_map(
        body,
        mesh=mesh,
        in_specs=(rows_at, row_at, row_at, row_at, P("dp", "pass", None), P("dp", "pass"))
        + (P(),) * 11
        + (P(full, None),),
        out_specs=(rows_at, P("pass", "dp"), rows_at, P("dp", "pass", None), P(None, "dp"), P(None, "dp"))
        + (weight_at,) * 9
        + (P(full, None),),
        check_vma=False,
    )
```

```python
import functools

import jax
import jax.numpy as jnp
from jax import lax
from jax.experimental import pallas as pl
from jax.experimental.pallas import tpu as pltpu
from jax.sharding import PartitionSpec as P

HEADS = 8
INS = 256
EPS = 1e-05
LANES = 128
EXTRA = 16
BF = jnp.bfloat16
F32 = jnp.float32
MIB = 1 << 20


def cost(us):
    return pl.CostEstimate(flops=int(us * 0.3e9), bytes_accessed=1, transcendentals=0)


def dot(left, right, dims):
    return lax.dot_general(left, right, (dims, ((), ())), preferred_element_type=F32)


def nn(left, right):
    return dot(left, right, ((1,), (0,)))


def nt(left, right):
    return dot(left, right, ((1,), (1,)))


def flip(values):
    return values.astype(F32).T.astype(BF)


class Far:
    def __init__(self, value):
        self.value = value


class Raw(Far):
    pass


class Pin(Far):
    pass


class Fetched:
    def __init__(self, source, buffer, sem):
        self.buffer, self.shape, self.dtype = buffer, buffer.shape, buffer.dtype
        self.copy = pltpu.make_async_copy(source, buffer, sem)
        self.copy.start()
        self.waiting = True

    def wait(self):
        if self.waiting:
            self.copy.wait()
            self.waiting = False

    def __getitem__(self, index):
        self.wait()
        return self.buffer[index]


class Stored:
    def __init__(self, target, buffer, sem):
        self.buffer, self.shape, self.dtype = buffer, buffer.shape, buffer.dtype
        self.copy = pltpu.make_async_copy(buffer, target, sem)
        self.sent = False

    def __getitem__(self, index):
        return self.buffer[index]

    def __setitem__(self, index, value):
        self.buffer[index] = value

    def send(self):
        self.copy.start()
        self.sent = True


def run(kernel, outs, ins, us, limit, scratch=(), name=None):
    far_in, far_out = [type(x) is Far for x in ins], [type(x) is Far for x in outs]
    marks_in, marks_out = [type(x) for x in ins], [type(x) for x in outs]
    ins = [x.value if isinstance(x, Far) else x for x in ins]
    outs = [x.value if isinstance(x, Far) else x for x in outs]
    buffers = [pltpu.VMEM(x.shape, x.dtype) for x, f in zip(ins + outs, far_in + far_out) if f]
    spaces = {Far: pltpu.HBM, Raw: pltpu.HBM, Pin: pltpu.VMEM}
    ins = [pltpu.with_memory_space_constraint(x, spaces[m]) if m in spaces else x for x, m in zip(ins, marks_in)]
    outs = [spaces[m](x.shape, x.dtype) if m in spaces else x for x, m in zip(outs, marks_out)]
    n_in, n_out = len(ins), len(outs)

    def wrapped(*refs):
        if buffers:
            sems = refs[-1]
            held = list(refs[-1 - len(buffers) : -1])
            rest = refs[n_in + n_out : len(refs) - 1 - len(buffers)]
        else:
            held, rest = [], refs[n_in + n_out :]
        given, made, count = [], [], 0
        for ref, far in zip(refs[:n_in], far_in):
            given.append(Fetched(ref, held[count], sems.at[count]) if far else ref)
            count += far
        for ref, far in zip(refs[n_in : n_in + n_out], far_out):
            made.append(Stored(ref, held[count], sems.at[count]) if far else ref)
            count += far
        kernel(*given, *made, *rest)
        for x in given:
            if isinstance(x, Fetched):
                x.wait()
        for x in made:
            if isinstance(x, Stored) and not x.sent:
                x.send()
        for x in made:
            if isinstance(x, Stored):
                x.copy.wait()

    def place(mark):
        return pl.BlockSpec(memory_space=spaces.get(mark, pltpu.VMEM))

    return pl.pallas_call(
        wrapped,
        out_shape=outs,
        in_specs=[place(m) for m in marks_in],
        out_specs=[place(m) for m in marks_out],
        scratch_shapes=list(scratch) + buffers + ([pltpu.SemaphoreType.DMA((len(buffers),))] if buffers else []),
        compiler_params=pltpu.CompilerParams(vmem_limit_bytes=limit * MIB),
        cost_estimate=cost(us),
        name=name,
    )(*ins)


def after(value, *done):
    return lax.optimization_barrier((value, *done))[0]


def after_all(values, *done):
    return list(lax.optimization_barrier((*values, *done))[: len(values)])


def like(shape, dtype):
    return jax.ShapeDtypeStruct(shape, dtype)


def norm_parts(values):
    center = values - jnp.mean(values, axis=-1, keepdims=True)
    rstd = lax.rsqrt(jnp.mean(center * center, axis=-1, keepdims=True) + EPS)
    return center * rstd, rstd


def norm_out(unit, gain, shift, index):
    return (unit * gain[index : index + 1] + shift[index : index + 1]).astype(BF)


def norm_bwd(grad, unit, rstd, gain):
    scaled = grad * gain
    back = rstd * (
        scaled
        - jnp.mean(scaled, axis=-1, keepdims=True)
        - unit * jnp.mean(scaled * unit, axis=-1, keepdims=True)
    )
    return back, jnp.sum(grad * unit, axis=0, keepdims=True), jnp.sum(grad, axis=0, keepdims=True)


def column(row, count):
    return jnp.broadcast_to(row, (count, row.shape[1])).T


def lane_half(values, half):
    lane = lax.broadcasted_iota(jnp.int32, values.shape, 1)
    picked = (lane >= LANES // 2) if half else (lane < LANES // 2)
    return jnp.where(picked, values, jnp.zeros_like(values))


def attend(query, keys, values, bias_ref, probs_ref, out_ref, scale):
    half_size = LANES // 2
    for tile in range(out_ref.shape[1] // LANES):
        q = query(tile).astype(F32) * scale
        k, v_t = keys(tile), flip(values(tile))
        parts = []
        for half in range(2):
            scores = nt(k, lane_half(q, half).astype(BF)) + bias_ref[...]
            expo = jnp.exp(scores - jnp.max(scores, axis=0, keepdims=True))
            probs = (expo * (1.0 / jnp.sum(expo, axis=0, keepdims=True))).astype(BF)
            probs_ref[2 * tile + half] = probs
            parts.append(nn(v_t[half * half_size : (half + 1) * half_size], probs))
        out_ref[:, tile * LANES : (tile + 1) * LANES] = jnp.concatenate(parts, axis=0).T.astype(BF)


def attend_bwd(grad, query, keys, values, probs_ref, put_query, put_keys, put_values, scale, tiles):
    half_size = LANES // 2
    for tile in range(tiles):
        g, q, k, v = grad(tile), query(tile), keys(tile), values(tile)
        k_t = flip(k)
        dq, dk, dv = [], [], []
        for half in range(2):
            probs = probs_ref[2 * tile + half]
            full = probs.astype(F32)
            dprobs = nt(v, lane_half(g, half))
            delta = jnp.sum(dprobs * full, axis=0, keepdims=True)
            dscores = (full * ((dprobs - delta) * scale)).astype(BF)
            dv.append(nn(probs, g))
            dk.append(nn(dscores, q))
            dq.append(nn(k_t[half * half_size : (half + 1) * half_size], dscores))
        lane = lax.broadcasted_iota(jnp.int32, dk[0].shape, 1) < half_size
        put_query(tile, jnp.concatenate(dq, axis=0).T.astype(BF))
        put_keys(tile, jnp.where(lane, dk[0], dk[1]).astype(BF))
        put_values(tile, jnp.where(lane, dv[0], dv[1]).astype(BF))


def tile_of(ref, start):
    return lambda tile: ref[:, start + tile * LANES : start + (tile + 1) * LANES]


def put_in(ref, start):
    def put(tile, value):
        ref[:, start + tile * LANES : start + (tile + 1) * LANES] = value

    return put


def solution(mesh):
    n_pass, n_dp = mesh.shape["pass"], mesh.shape["dp"]
    bits = [1 << i for i in range(n_dp.bit_length() - 1)]
    core_bit, chip_bits = bits[0], bits[1:]
    orders = (chip_bits, chip_bits[1::-1] + chip_bits[2:])
    n_steps = len(chip_bits)
    n_half = n_dp // 2

    def swap_core(x):
        return lax.ppermute(x, "dp", [(i, i ^ core_bit) for i in range(n_dp)])

    def swap_chip(x, step):
        return lax.ppermute(x, "dp", [(i, i ^ orders[i & 1][step]) for i in range(n_dp)])

    def swap_pass(x, bit):
        return lax.ppermute(x, "pass", [(i, i ^ bit) for i in range(n_pass)])

    def owners():
        me = lax.axis_index("dp")
        core = me & 1
        result = []
        for slot in range(n_dp):
            own_half = slot < n_half
            turn = core if own_half else 1 - core
            owner = me if own_half else me ^ 1
            for step in range(n_steps):
                if (slot >> (n_steps - 1 - step)) & 1:
                    owner = owner ^ jnp.where(turn == 0, orders[0][step], orders[1][step])
            result.append(owner)
        return result

    def small_dtype(rows):
        return BF if rows % 16 == 0 else F32

    def turn_rows(values, turned_ref, sorted_ref, owner_list):
        block = values.shape[1] // n_dp
        turned_ref[...] = values.astype(F32).T.astype(turned_ref.dtype)
        for slot, owner in enumerate(owner_list):
            start = pl.multiple_of(owner * block, block)
            sorted_ref[slot * block : (slot + 1) * block] = turned_ref[pl.ds(start, block)]
        return sorted_ref[...].astype(BF)

    def turn_scratch(features, count):
        dtype = small_dtype(features // n_dp)
        return [pltpu.VMEM((features, count), dtype)] * 2

    def pack(keep_ref, send_ref, base, first, left_t, right):
        width = keep_ref.shape[2]
        section = lax.axis_index("pass")
        unit = width // n_dp
        block = left_t.shape[0] // n_dp
        quarter = first
        for col in range(right.shape[1] // width):
            grad = nn(left_t, right[:, col * width : (col + 1) * width]).astype(keep_ref.dtype)
            for piece in range(block // unit):
                place = pl.ds(pl.multiple_of(base + (quarter ^ section) * unit, unit), unit)
                for slot in range(n_dp):
                    ref, index = (keep_ref, slot) if slot < n_half else (send_ref, slot - n_half)
                    start = slot * block + piece * unit
                    ref[index, place] = grad[start : start + unit]
                quarter += 1
        return quarter


    def self_kernel(
        x, gain, shift, w_qkv, seg, w_out, w_query, w_next, first, query, held, first_far, query_far, qkv, probs, ctx,
        bias, sem,
    ):
        copy = pltpu.make_async_copy(w_next, held, sem)
        copy.start()
        width = x.shape[1]
        gains, shifts = gain[...].astype(F32), shift[...].astype(F32)
        rows = x[...].astype(F32)
        unit, _ = norm_parts(rows)
        qkv[...] = nn(norm_out(unit, gains, shifts, 0), w_qkv[...]).astype(BF)
        seg_row = seg[...].astype(F32)
        bias[...] = jnp.where(column(seg_row, seg_row.shape[1]) == seg_row, 0.0, -1000000000.0)
        attend(
            tile_of(qkv, 0), tile_of(qkv, width), tile_of(qkv, 2 * width), bias, probs, ctx, (width // HEADS) ** -0.5
        )
        for ref in (qkv, probs, ctx):
            ref.send()
        added = rows + nn(ctx[...], w_out[...])
        first[...] = added
        first_far[...] = added
        first_far.send()
        unit, _ = norm_parts(added)
        value = nn(norm_out(unit, gains, shifts, 1), w_query[...]).astype(BF)
        query[...] = value
        query_far[...] = value
        copy.wait()

    def cross_kernel(
        first, query, w_kv, seg, part0, part1, part2, part3, w_out, gain, shift, w_in, w_ffn, labels, mask,
        second, keyval, probs, ctx, hidden, slope, third, layer, final, bias,
    ):
        width = first.shape[1]
        count = first.shape[0]
        seg_row = seg[...].astype(F32)
        size = part0.shape[0] - EXTRA
        for index, part in enumerate((part0, part1, part2, part3)):
            span = slice(index * size, (index + 1) * size)
            keyval[span] = nn(part[:size], w_kv[...]).astype(BF)
            source_seg = part[size : size + EXTRA, :size].astype(F32)[0:1]
            bias[span] = jnp.where(column(source_seg, count) == seg_row, 0.0, -1000000000.0)
        attend(
            tile_of(query, 0), tile_of(keyval, 0), tile_of(keyval, width), bias, probs, ctx, (width // HEADS) ** -0.5
        )
        for ref in (keyval, probs, ctx):
            ref.send()
        added = first[...] + nn(ctx[...], w_out[...])
        second[...] = added
        second.send()
        gains, shifts = gain[...].astype(F32), shift[...].astype(F32)
        unit, _ = norm_parts(added)
        normed = norm_out(unit, gains, shifts, 2)
        for col in range(w_in.shape[1] // width):
            span = slice(col * width, (col + 1) * width)
            inner = nn(normed, w_in[:, span])
            cdf = 0.5 * (1.0 + lax.erf(inner * 0.7071067811865476))
            hidden[:, span] = (inner * cdf).astype(BF)
            slope[:, span] = (cdf + inner * jnp.exp(-0.5 * inner * inner) * 0.3989422804014327).astype(BF)
        hidden.send()
        slope.send()
        added = added + nn(hidden[...], w_ffn[...])
        third[...] = added
        layer[...] = added.astype(BF)
        third.send()
        layer.send()
        unit, _ = norm_parts(added)
        normed = norm_out(unit, gains, shifts, 3)
        final[:count] = normed
        label = labels[...]
        line = lax.broadcasted_iota(jnp.int32, (EXTRA, count), 0)
        high = lax.shift_right_logical(label, 8).astype(F32)
        marks = jnp.where(line == 0, high, 0.0)
        marks = jnp.where(line == 1, (label & 255).astype(F32), marks)
        marks = jnp.where(line == 2, mask[...].astype(F32), marks)
        final[count:] = jnp.concatenate([marks, jnp.zeros((EXTRA, width - count), F32)], axis=1).astype(BF)

    def head_kernel(
        final, seg, labels, mask, w_delete, w_insert,
        dfinal, keep, send, d_delete, loss, turned, ordered,
    ):
        section = lax.axis_index("pass")
        count = seg.shape[1]
        width = final.shape[1]
        h = final[:count]
        h32 = h.astype(F32)
        seg_col = column(seg[...].astype(F32), LANES)
        row_id = lax.broadcasted_iota(jnp.int32, (count, LANES), 0)
        linked = (pltpu.roll(seg_col, count - 1, 0) == seg_col) & (row_id < count - 1)
        linked = jnp.concatenate([linked.astype(F32)] * (width // LANES), axis=1)
        after = (pltpu.roll(h32, count - 1, 0) * linked).astype(BF)
        weight = column(mask[...].astype(F32), LANES)

        def entropy(logits, label, live):
            top = jnp.max(logits, axis=-1, keepdims=True)
            expo = jnp.exp(logits - top)
            total = jnp.sum(expo, axis=-1, keepdims=True)
            lane = lax.broadcasted_iota(jnp.int32, logits.shape, 1)
            target = column(label.astype(F32), logits.shape[1])
            hit = lane.astype(F32) == target
            picked = jnp.sum(jnp.where(hit, logits, 0.0), axis=1, keepdims=True)
            w = weight[:, :1] * live
            rest = jnp.sum(jnp.where(hit, 0.0, expo), axis=1, keepdims=True)
            grad = jnp.where(hit, -rest, expo) * (w / total)
            return jnp.sum(w * (top + jnp.log(total) - picked)), grad.astype(BF)

        label = labels[...]
        spot = lax.broadcasted_iota(jnp.int32, (LANES, width), 0)
        two = w_delete[...].astype(F32)
        both_rows = jnp.where(spot == 0, two[0:1], jnp.where(spot == 1, two[1:2], 0.0)).astype(BF)
        logits = nt(h, both_rows)
        lane = lax.broadcasted_iota(jnp.int32, logits.shape, 1)
        logits = jnp.where(lane < 2, logits, -1e30)
        loss_d, grad_d = entropy(logits, lax.rem(label, 2), (section == 0).astype(F32))
        logits = nn(h, w_insert[:width]) + nn(after, w_insert[width:])
        loss_i, grad_i = entropy(logits, lax.rem(label, INS), (section == 1).astype(F32))
        loss[...] = jnp.full(loss.shape, loss_d + loss_i)
        d_after = nt(grad_i, w_insert[width:]) * linked
        dfinal[...] = nn(grad_d, both_rows) + nt(grad_i, w_insert[:width]) + pltpu.roll(d_after, 1, 0)
        d_delete[...] = nn(flip(grad_d)[:EXTRA], h)[: d_delete.shape[0]]
        both_t = turn_rows(jnp.concatenate([h, after], axis=1), turned, ordered, owners())
        grad = nn(both_t, grad_i).astype(keep.dtype)
        block = both_t.shape[0] // n_dp
        half = block // 2
        for slot in range(n_dp):
            ref, index = (keep, slot) if slot < n_half else (send, slot - n_half)
            ref[index, :, :INS] = grad[slot * block : slot * block + half]
            ref[index, :, INS:] = grad[slot * block + half : (slot + 1) * block]


    def shard_base(chunk, shard):
        section, me = lax.axis_index("pass"), lax.axis_index("dp")
        return ((section ^ (chunk >> 1)) * n_dp + (me ^ (chunk & 1))) * shard

    def hits(base, start, shape, label):
        ids = lax.broadcasted_iota(jnp.int32, shape, 0) + (base + start)
        return ids == label

    def slots_of(refs):
        return [(ref, (i, half)) for half in range(2) for ref in refs for i in range(ref.shape[0])]

    def logit_kernel(n_prev, turn, n_tokens, spots, *refs):
        slots = [slots_of(refs[:n_tokens])[i] for i in spots]
        vocab, refs = refs[n_tokens : n_tokens + 4], refs[n_tokens + 4 :]
        if n_prev:
            prev, refs = refs[0], refs[1:]
        n = len(slots) // 2
        stats, expos = refs[0], refs[1 : 1 + n]
        turned = refs[1 + n] if turn else None
        h, logits = refs[-2:]
        size = (slots[0][0].shape[1] - EXTRA) // 2
        count = 2 * size
        shard = vocab[0].shape[0]
        if n_prev:
            stats[:, : n_prev * count] = prev[...]
        for tile in range(n):
            both = slots[2 * tile : 2 * tile + 2]
            for index, (ref, (i, half)) in enumerate(both):
                h[index * size : (index + 1) * size] = ref[i, half * size : (half + 1) * size]
            marks = jnp.concatenate(
                [ref[i, count:, half * size : (half + 1) * size].astype(F32) for ref, (i, half) in both], axis=1
            )
            label_f = marks[0:1] * 256.0 + marks[1:2]
            label = label_f.astype(jnp.int32)
            weight = marks[2:3]
            peak = jnp.full((8, count), -jnp.inf, F32)
            for chunk, ref in enumerate(vocab):
                for start in range(0, shard, 1024):
                    step = min(1024, shard - start)
                    value = nt(ref[start : start + step], h[...])
                    at = chunk * shard + start
                    logits[at : at + step] = value
                    peak = jnp.maximum(peak, jnp.max(value.reshape(step // 8, 8, count), axis=0))
                if turn and not tile:
                    turned[:, chunk * shard : (chunk + 1) * shard] = flip(ref[...])
            peak = jnp.max(peak, axis=0, keepdims=True)
            total = jnp.zeros((8, count), F32)
            chosen = jnp.zeros((8, count), F32)
            sub = min(shard, 128)
            expo = expos[tile]
            for chunk in range(4):
                base = shard_base(chunk, shard)

                def part(i, carry, chunk=chunk, base=base, expo=expo, peak=peak, label=label):
                    total, chosen = carry
                    at = pl.multiple_of(chunk * shard + i * sub, sub)
                    value = logits[pl.ds(at, sub)]
                    hit = hits(base, i * sub, (sub, count), label)
                    weight_of = jnp.where(hit, 0.0, jnp.exp(value - peak))
                    expo[pl.ds(at, sub)] = weight_of.astype(BF)
                    total = total + jnp.sum(weight_of.reshape(sub // 8, 8, count), axis=0)
                    picked = jnp.where(hit, value, 0.0)
                    return total, chosen + jnp.sum(picked.reshape(sub // 8, 8, count), axis=0)

                total, chosen = lax.fori_loop(0, shard // sub, part, (total, chosen))
            total = jnp.sum(total, axis=0, keepdims=True)
            chosen = jnp.sum(chosen, axis=0, keepdims=True)
            line = lax.broadcasted_iota(jnp.int32, (8, count), 0)
            block = jnp.zeros((8, count), F32)
            for at, value in enumerate((peak, total, chosen, label_f, weight)):
                block = jnp.where(line == at, value, block)
            at = (n_prev + tile) * count
            stats[:, at : at + count] = block

    def logit_call(tokens, vocab, prev, turn, spots):
        height, width = tokens[0].shape[1:]
        count = height - EXTRA
        n = len(spots) // 2
        shard = vocab[0].shape[0]
        n_prev = prev[0].shape[1] // count if prev else 0
        outs = [like((8, (n_prev + n) * count), F32)] + [like((4 * shard, count), BF)] * n
        stats, *rest = run(
            functools.partial(logit_kernel, n_prev, turn, len(tokens), spots),
            outs + ([like((width, 4 * shard), BF)] if turn else []),
            [*tokens, *vocab, *prev],
            2.8 * n,
            12,
            [pltpu.VMEM((count, width), BF), pltpu.VMEM((4 * shard, count), F32)],
            "token_logits",
        )
        return stats, rest[:n], rest[n:]

    def merged(own, other):
        peak = jnp.maximum(own[0:1], other[0:1])
        total = own[1:2] * jnp.exp(own[0:1] - peak) + other[1:2] * jnp.exp(other[0:1] - peak)
        return peak, total, own[2:3] + other[2:3]

    def merge_kernel(step, order, own, other, out):
        size = own.shape[1] // len(order)
        blocks = [other[:, i * size : (i + 1) * size] for i in range(len(order))]
        bit = len(order) >> (step + 2)
        swapped = jnp.concatenate([blocks[order.index((half, slot ^ bit))] for half, slot in order], axis=1)
        mine = own[...]
        peak, total, chosen = merged(mine, swapped)
        line = lax.broadcasted_iota(jnp.int32, mine.shape, 0)
        out[...] = jnp.where(
            line == 0, peak, jnp.where(line == 1, total, jnp.where(line == 2, chosen, mine))
        )

    def closing(local, merged_ref, other):
        peak, total, chosen = merged(merged_ref, other)
        hit = jnp.exp(chosen - peak)
        full = total + hit
        lse = peak + jnp.log(full)
        weight = local[4:5]
        factor = weight * jnp.exp(local[0:1] - lse)
        return lse, chosen, factor, -weight * (total / full)

    def dlogits_into(ref, at, cols, expo, start, base, shape, label, factor, at_label):
        sub = min(shape[0], 128)

        def part(i, _):
            row = pl.multiple_of(i * sub, sub)
            hit = hits(base, i * sub, (sub, shape[1]), label)
            value = expo[pl.ds(pl.multiple_of(start + row, sub), sub)].astype(F32) * factor
            ref[pl.ds(pl.multiple_of(at + row, sub), sub), cols] = jnp.where(hit, at_label, value).astype(BF)
            return 0

        lax.fori_loop(0, shape[0] // sub, part, 0)

    def dtoken_kernel(tile, expo, vocab_t, local, merged_ref, other, out, dlogits):
        rows, count = expo.shape
        shard = rows // 4
        span = slice(tile * count, (tile + 1) * count)
        _, _, factor, at_label = closing(local[:, span], merged_ref[:, span], other[:, span])
        label = local[3:4, span].astype(jnp.int32)
        for chunk in range(4):
            dlogits_into(
                dlogits, chunk * shard, slice(None), expo, chunk * shard, shard_base(chunk, shard),
                (shard, count), label, factor, at_label,
            )
        total = nn(vocab_t[...], dlogits[...]).T.astype(out.dtype)
        out[0] = total[: count // 2]
        out[1] = total[count // 2 :]

    def dtoken_call(expo, tile, local, merged_ref, other, vocab_t, dtype):
        rows, count = expo.shape
        return run(
            functools.partial(dtoken_kernel, tile),
            [like((2, count // 2, vocab_t.shape[0]), dtype)],
            [expo, vocab_t, local, merged_ref, other],
            2.2,
            8,
            [pltpu.VMEM((rows, count), BF)],
            "token_dfinal",
        )[0]

    def dvocab_kernel(shard, parity, n_tiles, *refs):
        expos, tokens = refs[:n_tiles], refs[n_tiles:-6]
        local, merged_ref, other, out, dlogits, held = refs[-6:]
        index = pl.program_id(0)
        _, _, factor, at_label = closing(local[...], merged_ref[...], other[...])
        label = local[3:4].astype(jnp.int32)
        size = (tokens[0].shape[1] - EXTRA) // 2
        count = 2 * size
        section, me = lax.axis_index("pass"), lax.axis_index("dp")
        chunk = 2 * index + parity
        base = ((section ^ (chunk >> 1)) * n_dp + (me ^ (chunk & 1))) * shard
        slots = slots_of(tokens[:2]) + [slot for token in tokens[2:] for slot in slots_of([token])]
        for at, (token, (i, half)) in enumerate(slots):
            held[at * size : (at + 1) * size] = token[i, half * size : (half + 1) * size]
        for at, expo in enumerate(expos):
            cols = slice(at * count, (at + 1) * count)
            dlogits_into(
                dlogits, 0, cols, expo, 0, base, (shard, count), label[:, cols], factor[:, cols], at_label[:, cols]
            )
        out[...] = nn(dlogits[...], held[...]).astype(out.dtype)

    def dvocab_call(expos, tokens, local, merged_ref, other, parity, dtype):
        shard, count = expos[0].shape[0] // 4, expos[0].shape[1]
        width = tokens[0].shape[2]
        total = local.shape[1]
        fixed2 = pl.BlockSpec(local.shape, lambda c: (0, 0))
        return pl.pallas_call(
            functools.partial(dvocab_kernel, shard, parity, len(expos)),
            grid=(2,),
            in_specs=[pl.BlockSpec((shard, count), lambda c: (2 * c + parity, 0))] * len(expos)
            + [pl.BlockSpec(t.shape, lambda c: (0, 0, 0)) for t in tokens]
            + [fixed2] * 3,
            out_specs=pl.BlockSpec((shard, width), lambda c: (c, 0)),
            out_shape=like((2 * shard, width), dtype),
            scratch_shapes=[pltpu.VMEM((shard, total), BF), pltpu.VMEM((total, width), BF)],
            compiler_params=pltpu.CompilerParams(vmem_limit_bytes=20 * MIB),
            cost_estimate=cost(0.1),
            name="token_dvocab",
        )(*expos, *tokens, local, merged_ref, other)


    def ffn_back_kernel(
        hidden, third, gain, w_ffn, slope, second, shift, w_in,
        kept0, kept1, moved0, moved1, dhead, head_loss, local, merged_ref, other, ins_keep, ins_send,
        dsecond, keep, send, vecs, loss, wide_t, wide_s, thin_t, thin_s, dinner,
    ):
        width = third.shape[1]
        count = third.shape[0]
        live = (lax.axis_index("pass") >= 2).astype(F32)
        hidden_t = turn_rows(hidden[...], wide_t, wide_s, owners())
        parts = [kept[...] + moved[...].astype(F32) for kept, moved in ((kept0, moved0), (kept1, moved1))]
        dfinal = dhead[...] + live * jnp.concatenate(parts, axis=0)
        unit3, rstd3 = norm_parts(third[...])
        gains = gain[...].astype(F32)
        dthird, g_gain3, g_bias3 = norm_bwd(dfinal, unit3, rstd3, gains[3:4])
        low = dthird.astype(BF)
        pack(keep, send, 0, 0, hidden_t, low)
        for col in range(w_ffn.shape[0] // width):
            span = slice(col * width, (col + 1) * width)
            part = nt(low, w_ffn[span]).astype(BF).astype(F32) * slope[:, span].astype(F32)
            dinner[:, span] = part.astype(BF)
        unit2, rstd2 = norm_parts(second[...])
        normed_t = turn_rows(norm_out(unit2, gains, shift[...].astype(F32), 2), thin_t, thin_s, owners())
        pack(keep, send, 4 * (width // n_dp), 0, normed_t, dinner[...])
        extra = ins_keep.shape[1]
        keep[:, keep.shape[1] - extra :] = ins_keep[...]
        send[:, keep.shape[1] - extra :] = ins_send[...]
        dnormed = nt(dinner[...], w_in[...])
        back, g_gain2, g_bias2 = norm_bwd(dnormed, unit2, rstd2, gains[2:3])
        dsecond[...] = dthird + back
        token_loss = 0.0
        for start in (0, count):
            span = slice(start, start + count // 2)
            lse, chosen, _, _ = closing(local[:, span], merged_ref[:, span], other[:, span])
            token_loss = token_loss + jnp.sum(local[4:5, span] * (lse - chosen))
        loss[...] = head_loss[...] + token_loss * live
        line = lax.broadcasted_iota(jnp.int32, (8, width), 0)
        block = jnp.zeros((8, width), F32)
        for at, value in enumerate((g_gain3, g_gain2, g_bias3, g_bias2)):
            block = jnp.where(line == at, value, block)
        vecs[...] = block

    def cross_back_kernel(
        dsecond, w_out, ctx, keyval, probs, query, part0, part1, part2, part3, w_kv, first, gain, shift, w_query,
        dfirst, keep, send, vecs, dsrc0, dsrc2, dsrc13, thin_t, thin_s, src_t, src_s, dquery, dkeyval, dctx,
    ):
        width = first.shape[1]
        owner_list = owners()
        low = dsecond[...].astype(BF)
        dctx[...] = nt(low, w_out[...]).astype(BF)
        at = pack(keep, send, 0, 0, turn_rows(ctx[...], thin_t, thin_s, owner_list), low)
        attend_bwd(
            tile_of(dctx, 0), tile_of(query, 0), tile_of(keyval, 0), tile_of(keyval, width), probs,
            put_in(dquery, 0), put_in(dkeyval, 0), put_in(dkeyval, width), (width // HEADS) ** -0.5, width // LANES,
        )
        size = part0.shape[0] - EXTRA
        source = jnp.concatenate([p[:size] for p in (part0, part1, part2, part3)], axis=0)
        at = pack(keep, send, 0, at, turn_rows(source, src_t, src_s, owner_list), dkeyval[...])
        for index, (ref, row) in enumerate(((dsrc0, 0), (dsrc13, 0), (dsrc2, 0), (dsrc13, size))):
            part = nt(dkeyval[index * size : (index + 1) * size], w_kv[...])
            ref[row : row + size] = part.astype(ref.dtype)
        gains, shifts = gain[...].astype(F32), shift[...].astype(F32)
        unit, rstd = norm_parts(first[...])
        normed_t = turn_rows(norm_out(unit, gains, shifts, 1), thin_t, thin_s, owner_list)
        pack(keep, send, 0, at, normed_t, dquery[...])
        back, g_gain, g_bias = norm_bwd(nt(dquery[...], w_query[...]), unit, rstd, gains[1:2])
        dfirst[...] = dsecond[...] + back
        line = lax.broadcasted_iota(jnp.int32, (8, width), 0)
        vecs[...] = jnp.where(line == 0, g_gain, jnp.where(line == 1, g_bias, 0.0))

    def self_back_kernel(
        dfirst, w_out, ctx, qkv, probs, x, gain, shift, w_qkv, vec_ffn, vec_cross, d_delete,
        dx, keep, send, thin_t, thin_s, dqkv, dctx,
    ):
        width = x.shape[1]
        owner_list = owners()
        low = dfirst[...].astype(BF)
        dctx[...] = nt(low, w_out[...]).astype(BF)
        at = pack(keep, send, 0, 0, turn_rows(ctx[...], thin_t, thin_s, owner_list), low)
        attend_bwd(
            tile_of(dctx, 0), tile_of(qkv, 0), tile_of(qkv, width), tile_of(qkv, 2 * width), probs,
            put_in(dqkv, 0), put_in(dqkv, width), put_in(dqkv, 2 * width), (width // HEADS) ** -0.5, width // LANES,
        )
        gains, shifts = gain[...].astype(F32), shift[...].astype(F32)
        unit, rstd = norm_parts(x[...].astype(F32))
        normed_t = turn_rows(norm_out(unit, gains, shifts, 0), thin_t, thin_s, owner_list)
        at = pack(keep, send, 0, at, normed_t, dqkv[...])
        back, g_gain, g_bias = norm_bwd(nt(dqkv[...], w_qkv[...]), unit, rstd, gains[0:1])
        dx[...] = dfirst[...] + back
        line = lax.broadcasted_iota(jnp.int32, (EXTRA, width), 0)
        block = jnp.zeros((EXTRA, width), F32)
        lines = (
            (0, d_delete[0:1]), (1, d_delete[1:2]),
            (8, g_gain), (9, vec_cross[0:1]), (10, vec_ffn[1:2]), (11, vec_ffn[0:1]),
            (12, g_bias), (13, vec_cross[1:2]), (14, vec_ffn[3:4]), (15, vec_ffn[2:3]),
        )
        for row, value in lines:
            block = jnp.where(line == row, value, block)
        block = block.astype(keep.dtype)
        at = at * (width // n_dp)
        for slot in range(n_half):
            keep[slot, at:] = block
            send[slot, at:] = block


    def add_kernel(pairs, *refs):
        ins, outs = refs[: 2 * pairs], refs[2 * pairs :]
        at = 0
        for keep, got in zip(ins[::2], ins[1::2]):
            rows = keep.shape[1]
            slot = 0
            for ref in outs:
                for i in range(ref.shape[0]):
                    value = keep[slot].astype(F32) + got[slot].astype(F32)
                    ref[i, at : at + rows] = value.astype(ref.dtype)
                    slot += 1
            at += rows

    def add_call(blocks, *counts):
        rows, width = sum(b.shape[1] for b in blocks[::2]), blocks[0].shape[2]
        outs = [like((count, rows, width), wire_of(width)) for count in counts]
        return run(functools.partial(add_kernel, len(blocks) // 2), outs, blocks, 0.8, 8, name="sum_slots")

    def wire_of(width):
        return small_dtype(width // n_dp)

    def regroup_kernel(plan, n_terms, *refs):
        value = refs[0][...].astype(F32)
        for ref in refs[1:n_terms]:
            value = value + ref[...].astype(F32)
        for spans, ref in zip(plan, refs[n_terms:]):
            at = 0
            for start, stop in spans:
                ref[at : at + stop - start] = value[start:stop].astype(ref.dtype)
                at += stop - start

    def pair_kernel(plan, n_terms, *refs):
        first = refs[0][...].astype(F32) + refs[1][...].astype(F32)
        value = first + (refs[2][...].astype(F32) + refs[3][...].astype(F32))
        for spans, ref in zip(plan, refs[n_terms:]):
            at = 0
            for start, stop in spans:
                ref[at : at + stop - start] = value[start:stop].astype(ref.dtype)
                at += stop - start

    def regroup(terms, plan, kernel=regroup_kernel, name="sum_rows"):
        width = terms[0].shape[-1]
        outs = [like((sum(b - a for a, b in spans), width), wire_of(width)) for spans in plan]
        terms = [t.reshape(t.shape[-2:]) for t in terms]
        return run(functools.partial(kernel, plan, len(terms)), outs, terms, 0.7, 8, name=name)

    def picked(pieces):
        section = lax.axis_index("pass")
        values = [p.astype(F32) for p in pieces]
        result = []
        for j in range(4):
            value = values[0]
            for b in (1, 2, 3):
                value = jnp.where((section ^ b) == j, values[b], value)
            result.append(value)
        return result

    def halves(refs):
        rows = refs[0].shape[0] // 2
        return [r[:rows] for r in refs], [r[rows:] for r in refs]

    def ffn_end_kernel(own, near, third, far, extra, p_out, p_in, p_insert):
        outs, ins = halves((own, near, third, far))
        rows, width = outs[0].shape
        for j, value in enumerate(picked(outs)):
            p_out[j * rows : (j + 1) * rows] = value
        for j, value in enumerate(picked(ins)):
            p_in[:, j * width : (j + 1) * width] = value
        half = p_insert.shape[0] // 2
        value = extra[...].astype(F32)
        p_insert[:half] = value[:, :INS]
        p_insert[half:] = value[:, INS:]

    def attention_end_kernel(
        own, near, third, far, extra, p_cross, p_kv, p_query, p_out, p_qkv, p_gain, p_bias, p_delete
    ):
        cross, own_part = halves((own, near, third, far))
        width = extra.shape[1]
        values = picked(cross)
        p_cross[...] = values[0]
        p_kv[:, :width] = values[1]
        p_kv[:, width:] = values[2]
        p_query[...] = values[3]
        values = picked(own_part)
        p_out[...] = values[0]
        for j in range(3):
            p_qkv[:, j * width : (j + 1) * width] = values[j + 1]
        size = p_gain.shape[1]
        me = lax.axis_index("dp")
        mine = pltpu.roll(extra[...].astype(F32), lax.rem(width - me * size, width), 1)
        p_gain[...] = mine[8:12, :size]
        p_bias[...] = mine[12:16, :size]
        p_delete[...] = mine[:2, :size]

    def body(
        decoder_in,
        decoder_segments,
        edit_target,
        loss_mask,
        source_out,
        source_segments,
        norm_gain,
        norm_bias,
        self_qkv,
        self_out,
        cross_query,
        cross_kv,
        cross_out,
        ffn_in,
        ffn_out,
        delete_head,
        insert_head,
        token_head,
    ):
        section = lax.axis_index("pass")
        segs, labels, mask = decoder_segments[0], edit_target[0], loss_mask[0]
        rows = decoder_in[0, 0]
        count, width = rows.shape
        shard = token_head.shape[0]
        part = source_out.shape[1]
        src = n_pass * part
        hid = ffn_in.shape[1]
        unit = width // n_dp
        wire = small_dtype(unit)

        note = jnp.pad(source_segments.astype(BF), ((0, EXTRA - 1), (0, width - part)))
        mine = jnp.concatenate([source_out[0], note], axis=0)
        parts = [mine] + [swap_pass(mine, bit) for bit in (1, 2, 3)]

        gain, shift = Far(norm_gain), Far(norm_bias)
        first, query, w_kv, first_far, query_far, qkv, probs1, ctx1 = run(
            self_kernel,
            [
                like((count, width), F32),
                like((count, width), BF),
                like(cross_kv.shape, BF),
                Far(like((count, width), F32)),
                Far(like((count, width), BF)),
                Far(like((count, 3 * width), BF)),
                Far(like((HEADS, count, count), BF)),
                Far(like((count, width), BF)),
            ],
            [Far(rows), gain, shift, Far(self_qkv), Far(segs), Far(self_out), Far(cross_query), Raw(cross_kv)],
            4.2,
            10,
            [pltpu.VMEM((count, count), F32), pltpu.SemaphoreType.DMA],
            "self_forward",
        )
        second, keyval, probs2, ctx2, hidden, slope, third, layer, final = run(
            cross_kernel,
            [
                Far(like((count, width), F32)),
                Far(like((src, 2 * width), BF)),
                Far(like((HEADS, src, count), BF)),
                Far(like((count, width), BF)),
                Far(like((count, hid), BF)),
                Far(like((count, hid), BF)),
                Far(like((count, width), F32)),
                Far(like((count, width), BF)),
                like((count + EXTRA, width), BF),
            ],
            [first, query, w_kv, Far(segs), *parts, Pin(cross_out), gain, shift]
            + [Pin(ffn_in), Pin(ffn_out), Far(labels), Far(mask)],
            7.6,
            20,
            [pltpu.VMEM((src, count), F32)],
            "cross_forward",
        )

        near = swap_pass(after(token_head, parts[1]), 1)
        moved = lax.ppermute(final, "pass", [(2, 0), (3, 1)])
        group = jnp.where(section >= 2, final, moved)[None]
        tokens = [group]
        for step in reversed(range(n_steps)):
            tokens.append(swap_chip(group, step))
            if step:
                group = jnp.concatenate([group, tokens[-1]], axis=0)
        near = after(near, tokens[1])
        vocab = (token_head, swap_core(token_head), near, swap_core(near))
        expos, stats, vocab_t, order = [[], []], (), None, []
        for pieces in [tokens[:2]] + [[t] for t in tokens[2:]]:
            made = []
            for tile in range(sum(p.shape[0] for p in pieces)):
                stats, new, turned = logit_call(pieces, vocab, stats, not vocab_t, (2 * tile, 2 * tile + 1))
                stats = (stats,)
                vocab_t = vocab_t or turned
                made += new
            first_slot, n_slots = len(order) // 2, sum(p.shape[0] for p in pieces)
            for half in range(2):
                spot = half * len(made) // 2
                expos[half] += [(e, len(order) // 2 + i) for i, e in enumerate(made[spot : spot + len(made) // 2])]
                order += [(half, first_slot + i) for i in range(n_slots)]
        (vocab_t,) = vocab_t
        local = stats[0]
        whole = local
        for step in range(n_steps):
            (whole,) = run(
                functools.partial(merge_kernel, step, order), [like(local.shape, F32)], [whole, swap_chip(whole, step)],
                1.0, 8, name="stats_merge",
            )
        other = swap_pass(whole, 2)

        ins_rows = 2 * width // n_dp // 2
        dhead, ins_keep, ins_send, d_delete, head_loss = run(
            head_kernel,
            [
                like((count, width), F32),
                like((n_half, ins_rows, 2 * INS), wire),
                like((n_half, ins_rows, 2 * INS), wire),
                like((8, width), F32),
                like((8, LANES), F32),
            ],
            [after(final, whole), Far(segs), Far(labels), Far(mask), Far(delete_head.T), Pin(insert_head)],
            1.4,
            10,
            turn_scratch(2 * width, count),
            "small_heads",
        )
        other = after(other, dhead)

        n_tiles = len(expos[0])
        made = [[None] * n_tiles for _ in expos]
        for tile in reversed(range(n_tiles)):
            for half in range(2):
                dtype = BF if tile >= n_tiles // 2 and n_tiles > 1 else F32
                expo, spot = expos[half][tile]
                made[half][tile] = dtoken_call(expo, spot, local, whole, other, vocab_t, dtype)
        kept = []
        for half in range(2):
            tiles = made[half]
            for step in range(n_steps):
                if len(tiles) > 1:
                    middle = len(tiles) // 2
                    sending = tiles[middle:]
                    sending = jnp.concatenate(sending, axis=0) if len(sending) > 1 else sending[0]
                    got = swap_chip(sending.astype(BF), step)
                    tiles = [t + got[2 * i : 2 * i + 2].astype(F32) for i, t in enumerate(tiles[:middle])]
                else:
                    got = swap_chip(tiles[0][1].astype(BF), step)
                    kept.append(tiles[0][0] + got.astype(F32))
        backs = [lax.ppermute(k.astype(BF), "pass", [(0, 2), (1, 3)]) for k in kept]

        flat = [e for e, _ in sorted(sum(expos, []), key=lambda pair: pair[1])]
        dvocab_send = dvocab_call(flat, tokens, after(local, *kept), whole, other, 1, BF)
        dvocab_keep = dvocab_call(flat, tokens, after(local, dvocab_send), whole, other, 0, BF)
        backs = after_all(backs, dvocab_send, dvocab_keep)
        vocab_got = swap_core(after(dvocab_send, *backs))

        def packed(rows):
            return like((n_half, rows, width), wire)

        def sent(x):
            return x.astype(BF)

        def reduce_chips(blocks, step):
            while step < n_steps:
                half = n_half >> (step + 1)
                keep, send = add_call(blocks, half, half)
                blocks = [keep, swap_chip(sent(send), step)]
                step += 1
            return blocks

        rows_ffn = 8 * unit + ins_rows
        dsecond, keep_ffn, send_ffn, vec_ffn, loss = run(
            ffn_back_kernel,
            [like((count, width), F32), packed(rows_ffn), packed(rows_ffn), like((8, width), F32), like((8, LANES), F32)],
            [Pin(hidden), Pin(third), gain, Pin(ffn_out), Pin(slope), Pin(second), shift, Pin(ffn_in)]
            + [*kept, *backs, dhead, head_loss, local, whole, other, ins_keep, ins_send],
            0.1,
            16,
            turn_scratch(hid, count) + turn_scratch(width, count) + [pltpu.VMEM((count, hid), BF)],
            "ffn_backward",
        )
        dsecond, keep_ffn, send_ffn, vec_ffn, loss = after_all(
            [dsecond, keep_ffn, send_ffn, vec_ffn, loss], vocab_got
        )
        vocab_keep = dvocab_keep[:shard].astype(F32) + vocab_got[:shard].astype(F32)
        vocab_send = (dvocab_keep[shard:].astype(F32) + vocab_got[shard:].astype(F32)).astype(BF)
        cuts = [shard * i // 64 for i in (0, 30, 42, 64)]
        vocab_parts = [vocab_send[a:b] for a, b in zip(cuts, cuts[1:])]
        vocab_parts[0] = swap_pass(vocab_parts[0], 1)
        keep_ffn, send_ffn = add_call([keep_ffn, swap_core(sent(send_ffn))], n_half // 2, n_half // 2)
        dsecond = after(dsecond, send_ffn)
        dfirst, *chunk_cross, vec_cross, src0, src2, src13 = run(
            cross_back_kernel,
            [
                like((count, width), F32),
                packed(4 * unit),
                packed(4 * unit),
                like((8, width), F32),
                like((part, width), F32),
                like((part, width), F32),
                like((2 * part, width), BF),
            ],
            [dsecond, Pin(cross_out), Pin(ctx2), Pin(keyval), Pin(probs2), Pin(query_far), *parts]
            + [Pin(cross_kv), Pin(first_far), gain, shift, Pin(cross_query)],
            0.1,
            15,
            turn_scratch(width, count)
            + turn_scratch(width, src)
            + [pltpu.VMEM((count, width), BF), pltpu.VMEM((src, 2 * width), BF), pltpu.VMEM((count, width), BF)],
            "cross_backward",
        )
        blocks_ffn = [keep_ffn, swap_chip(sent(send_ffn), 0)]
        dfirst, *chunk_cross, vec_cross, src0, src2, src13 = after_all(
            [dfirst, *chunk_cross, vec_cross, src0, src2, src13], vocab_parts[0]
        )
        vocab_parts[1] = swap_pass(after(vocab_parts[1], dfirst), 1)
        input_grad, *chunk_self = run(
            self_back_kernel,
            [Far(like((count, width), F32)), packed(4 * unit + EXTRA), packed(4 * unit + EXTRA)],
            [dfirst, Pin(self_out), Pin(ctx1), Pin(qkv), Pin(probs1), Pin(rows), gain, shift, Pin(self_qkv)]
            + [vec_ffn, vec_cross, d_delete],
            0.1,
            12,
            turn_scratch(width, count) + [pltpu.VMEM((count, 3 * width), BF), pltpu.VMEM((count, width), BF)],
            "self_backward",
        )
        def rows_at(*spots, extra=0, start=8):
            spans = [(i * unit, (i + 1) * unit) for i in spots]
            return spans + ([(start * unit, start * unit + extra)] if extra else [])

        input_grad, *chunk_self = after_all([input_grad, *chunk_self], blocks_ffn[1], vocab_parts[1])
        blocks_ffn = reduce_chips(blocks_ffn, 1)

        got_cross = swap_core(sent(chunk_cross[1]))
        keep_self, send_self = chunk_self
        send_self = after(send_self, got_cross)
        got_self = swap_core(sent(send_self))
        keep_att, send_att = add_call([chunk_cross[0], got_cross, keep_self, got_self], n_half // 2, n_half // 2)
        source_got = swap_pass(src13, 1)
        source_half = swap_pass((src2 + source_got[part:].astype(F32)).astype(BF), 2)
        source_grad = (src0 + source_got[:part].astype(F32)) + source_half.astype(F32)
        blocks_att = [keep_att, swap_chip(after(sent(send_att), blocks_ffn[1], source_got), 0)]

        keep, send = regroup(
            blocks_ffn,
            [rows_at(0, 2, 4, 6, extra=ins_rows), rows_at(1, 3, 5, 7, extra=ins_rows)],
        )
        got = swap_pass(sent(send), 1)
        got = after(got, source_half)
        blocks_att[1] = after(blocks_att[1], got)
        blocks_att = reduce_chips(blocks_att, 1)
        keep, send = regroup(
            [keep, got],
            [rows_at(0, 2, extra=ins_rows, start=4), rows_at(1, 3, extra=ins_rows, start=4)],
        )
        got = swap_pass(sent(send), 2)
        vocab_parts[2] = swap_pass(after(vocab_parts[2], send), 1)
        token_grad = vocab_keep + jnp.concatenate(vocab_parts, axis=0).astype(F32)
        blocks_att[1] = after(blocks_att[1], got)
        pieces_by_place = regroup(blocks_att, [rows_at(i, 4 + i, extra=EXTRA) for i in range(4)])
        own, ins_sum = regroup([keep, got], [rows_at(0, 1), rows_at(extra=ins_rows, start=2)])
        near, third_part = swap_pass(sent(own), 1), swap_pass(sent(own), 2)
        ffn_parts = [own, near, third_part, swap_pass(third_part, 1), ins_sum]

        gots = [swap_pass(sent(pieces_by_place[b]), b) for b in (1, 2, 3)]
        own, extra_sum = regroup(
            [pieces_by_place[0], *gots], [rows_at(0, 1), rows_at(extra=EXTRA, start=2)], pair_kernel, "sum_pass"
        )
        attention_parts = [own] + [swap_pass(sent(own), b) for b in (1, 2, 3)] + [extra_sum]

        def out(*shape):
            return Far(like(shape, F32))

        p_out, p_in, p_insert = run(
            ffn_end_kernel, [out(hid // n_dp, width), out(unit, hid), out(2 * unit, INS)], ffn_parts, 1.0, 8,
            name="ffn_sums",
        )
        p_cross, p_kv, p_query, p_self, p_qkv, p_gain, p_bias, p_delete = run(
            attention_end_kernel,
            [out(unit, width), out(unit, 2 * width), out(unit, width), out(unit, width), out(unit, 3 * width)]
            + [out(4, unit), out(4, unit), out(2, unit)],
            attention_parts,
            1.0,
            8,
            name="attention_sums",
        )
        return (
            layer[None, None],
            loss[:1, :1],
            input_grad[None, None],
            source_grad[None],
            p_gain,
            p_bias,
            p_qkv,
            p_self,
            p_query,
            p_kv,
            p_cross,
            p_in,
            p_out,
            p_delete.T,
            p_insert,
            token_grad,
        )

    full = ("pass", "dp")
    rows_at, row_at = P("pass", "dp", None, None), P("pass", "dp", None)
    weight_at = P("dp", None)
    return jax.shard_map(
        body,
        mesh=mesh,
        in_specs=(rows_at, row_at, row_at, row_at, P("dp", "pass", None), P("dp", "pass"))
        + (P(),) * 11
        + (P(full, None),),
        out_specs=(rows_at, P("pass", "dp"), rows_at, P("dp", "pass", None), P(None, "dp"), P(None, "dp"))
        + (weight_at,) * 9
        + (P(full, None),),
        check_vma=False,
    )
```

```python
import functools

import jax
import jax.numpy as jnp
from jax import lax
from jax.experimental import pallas as pl
from jax.experimental.pallas import tpu as pltpu
from jax.sharding import PartitionSpec as P

HEADS = 8
INS = 256
EPS = 1e-05
LANES = 128
EXTRA = 16
BF = jnp.bfloat16
F32 = jnp.float32
MIB = 1 << 20


def cost(us):
    return pl.CostEstimate(flops=int(us * 0.3e9), bytes_accessed=1, transcendentals=0)


def dot(left, right, dims):
    return lax.dot_general(left, right, (dims, ((), ())), preferred_element_type=F32)


def nn(left, right):
    return dot(left, right, ((1,), (0,)))


def nt(left, right):
    return dot(left, right, ((1,), (1,)))


def flip(values):
    return values.astype(F32).T.astype(BF)


class Far:
    def __init__(self, value):
        self.value = value


class Raw(Far):
    pass


class Pin(Far):
    pass


class Fetched:
    def __init__(self, source, buffer, sem):
        self.buffer, self.shape, self.dtype = buffer, buffer.shape, buffer.dtype
        self.copy = pltpu.make_async_copy(source, buffer, sem)
        self.copy.start()
        self.waiting = True

    def wait(self):
        if self.waiting:
            self.copy.wait()
            self.waiting = False

    def __getitem__(self, index):
        self.wait()
        return self.buffer[index]


class Stored:
    def __init__(self, target, buffer, sem):
        self.buffer, self.shape, self.dtype = buffer, buffer.shape, buffer.dtype
        self.copy = pltpu.make_async_copy(buffer, target, sem)
        self.sent = False

    def __getitem__(self, index):
        return self.buffer[index]

    def __setitem__(self, index, value):
        self.buffer[index] = value

    def send(self):
        self.copy.start()
        self.sent = True


def run(kernel, outs, ins, us, limit, scratch=(), name=None):
    far_in, far_out = [type(x) is Far for x in ins], [type(x) is Far for x in outs]
    marks_in, marks_out = [type(x) for x in ins], [type(x) for x in outs]
    ins = [x.value if isinstance(x, Far) else x for x in ins]
    outs = [x.value if isinstance(x, Far) else x for x in outs]
    buffers = [pltpu.VMEM(x.shape, x.dtype) for x, f in zip(ins + outs, far_in + far_out) if f]
    spaces = {Far: pltpu.HBM, Raw: pltpu.HBM, Pin: pltpu.VMEM}
    ins = [pltpu.with_memory_space_constraint(x, spaces[m]) if m in spaces else x for x, m in zip(ins, marks_in)]
    outs = [spaces[m](x.shape, x.dtype) if m in spaces else x for x, m in zip(outs, marks_out)]
    n_in, n_out = len(ins), len(outs)

    def wrapped(*refs):
        if buffers:
            sems = refs[-1]
            held = list(refs[-1 - len(buffers) : -1])
            rest = refs[n_in + n_out : len(refs) - 1 - len(buffers)]
        else:
            held, rest = [], refs[n_in + n_out :]
        given, made, count = [], [], 0
        for ref, far in zip(refs[:n_in], far_in):
            given.append(Fetched(ref, held[count], sems.at[count]) if far else ref)
            count += far
        for ref, far in zip(refs[n_in : n_in + n_out], far_out):
            made.append(Stored(ref, held[count], sems.at[count]) if far else ref)
            count += far
        kernel(*given, *made, *rest)
        for x in given:
            if isinstance(x, Fetched):
                x.wait()
        for x in made:
            if isinstance(x, Stored) and not x.sent:
                x.send()
        for x in made:
            if isinstance(x, Stored):
                x.copy.wait()

    def place(mark):
        return pl.BlockSpec(memory_space=spaces.get(mark, pltpu.VMEM))

    return pl.pallas_call(
        wrapped,
        out_shape=outs,
        in_specs=[place(m) for m in marks_in],
        out_specs=[place(m) for m in marks_out],
        scratch_shapes=list(scratch) + buffers + ([pltpu.SemaphoreType.DMA((len(buffers),))] if buffers else []),
        compiler_params=pltpu.CompilerParams(vmem_limit_bytes=limit * MIB),
        cost_estimate=cost(us),
        name=name,
    )(*ins)


def after(value, *done):
    return lax.optimization_barrier((value, *done))[0]


def after_all(values, *done):
    return list(lax.optimization_barrier((*values, *done))[: len(values)])


def like(shape, dtype):
    return jax.ShapeDtypeStruct(shape, dtype)


def norm_parts(values):
    center = values - jnp.mean(values, axis=-1, keepdims=True)
    rstd = lax.rsqrt(jnp.mean(center * center, axis=-1, keepdims=True) + EPS)
    return center * rstd, rstd


def norm_out(unit, gain, shift, index):
    return (unit * gain[index : index + 1] + shift[index : index + 1]).astype(BF)


def norm_bwd(grad, unit, rstd, gain):
    scaled = grad * gain
    back = rstd * (
        scaled
        - jnp.mean(scaled, axis=-1, keepdims=True)
        - unit * jnp.mean(scaled * unit, axis=-1, keepdims=True)
    )
    return back, jnp.sum(grad * unit, axis=0, keepdims=True), jnp.sum(grad, axis=0, keepdims=True)


def column(row, count):
    return jnp.broadcast_to(row, (count, row.shape[1])).T


def lane_half(values, half):
    lane = lax.broadcasted_iota(jnp.int32, values.shape, 1)
    picked = (lane >= LANES // 2) if half else (lane < LANES // 2)
    return jnp.where(picked, values, jnp.zeros_like(values))


def attend(query, keys, values, bias_ref, probs_ref, out_ref, scale):
    half_size = LANES // 2
    for tile in range(out_ref.shape[1] // LANES):
        q = query(tile).astype(F32) * scale
        k, v_t = keys(tile), flip(values(tile))
        parts = []
        for half in range(2):
            scores = nt(k, lane_half(q, half).astype(BF)) + bias_ref[...]
            expo = jnp.exp(scores - jnp.max(scores, axis=0, keepdims=True))
            probs = (expo * (1.0 / jnp.sum(expo, axis=0, keepdims=True))).astype(BF)
            probs_ref[2 * tile + half] = probs
            parts.append(nn(v_t[half * half_size : (half + 1) * half_size], probs))
        out_ref[:, tile * LANES : (tile + 1) * LANES] = jnp.concatenate(parts, axis=0).T.astype(BF)


def attend_bwd(grad, query, keys, values, probs_ref, put_query, put_keys, put_values, scale, tiles):
    half_size = LANES // 2
    for tile in range(tiles):
        g, q, k, v = grad(tile), query(tile), keys(tile), values(tile)
        k_t = flip(k)
        dq, dk, dv = [], [], []
        for half in range(2):
            probs = probs_ref[2 * tile + half]
            full = probs.astype(F32)
            dprobs = nt(v, lane_half(g, half))
            delta = jnp.sum(dprobs * full, axis=0, keepdims=True)
            dscores = (full * ((dprobs - delta) * scale)).astype(BF)
            dv.append(nn(probs, g))
            dk.append(nn(dscores, q))
            dq.append(nn(k_t[half * half_size : (half + 1) * half_size], dscores))
        lane = lax.broadcasted_iota(jnp.int32, dk[0].shape, 1) < half_size
        put_query(tile, jnp.concatenate(dq, axis=0).T.astype(BF))
        put_keys(tile, jnp.where(lane, dk[0], dk[1]).astype(BF))
        put_values(tile, jnp.where(lane, dv[0], dv[1]).astype(BF))


def tile_of(ref, start):
    return lambda tile: ref[:, start + tile * LANES : start + (tile + 1) * LANES]


def put_in(ref, start):
    def put(tile, value):
        ref[:, start + tile * LANES : start + (tile + 1) * LANES] = value

    return put


def solution(mesh):
    n_pass, n_dp = mesh.shape["pass"], mesh.shape["dp"]
    bits = [1 << i for i in range(n_dp.bit_length() - 1)]
    core_bit, chip_bits = bits[0], bits[1:]
    orders = (chip_bits, chip_bits[1::-1] + chip_bits[2:])
    n_steps = len(chip_bits)
    n_half = n_dp // 2

    def swap_core(x):
        return lax.ppermute(x, "dp", [(i, i ^ core_bit) for i in range(n_dp)])

    def swap_chip(x, step):
        return lax.ppermute(x, "dp", [(i, i ^ orders[i & 1][step]) for i in range(n_dp)])

    def swap_pass(x, bit):
        return lax.ppermute(x, "pass", [(i, i ^ bit) for i in range(n_pass)])

    def owners():
        me = lax.axis_index("dp")
        core = me & 1
        result = []
        for slot in range(n_dp):
            own_half = slot < n_half
            turn = core if own_half else 1 - core
            owner = me if own_half else me ^ 1
            for step in range(n_steps):
                if (slot >> (n_steps - 1 - step)) & 1:
                    owner = owner ^ jnp.where(turn == 0, orders[0][step], orders[1][step])
            result.append(owner)
        return result

    def small_dtype(rows):
        return BF if rows % 16 == 0 else F32

    def turn_rows(values, turned_ref, sorted_ref, owner_list):
        block = values.shape[1] // n_dp
        turned_ref[...] = values.astype(F32).T.astype(turned_ref.dtype)
        for slot, owner in enumerate(owner_list):
            start = pl.multiple_of(owner * block, block)
            sorted_ref[slot * block : (slot + 1) * block] = turned_ref[pl.ds(start, block)]
        return sorted_ref[...].astype(BF)

    def turn_scratch(features, count):
        dtype = small_dtype(features // n_dp)
        return [pltpu.VMEM((features, count), dtype)] * 2

    def pack(keep_ref, send_ref, base, first, left_t, right):
        width = keep_ref.shape[2]
        section = lax.axis_index("pass")
        unit = width // n_dp
        block = left_t.shape[0] // n_dp
        quarter = first
        for col in range(right.shape[1] // width):
            grad = nn(left_t, right[:, col * width : (col + 1) * width]).astype(keep_ref.dtype)
            for piece in range(block // unit):
                place = pl.ds(pl.multiple_of(base + (quarter ^ section) * unit, unit), unit)
                for slot in range(n_dp):
                    ref, index = (keep_ref, slot) if slot < n_half else (send_ref, slot - n_half)
                    start = slot * block + piece * unit
                    ref[index, place] = grad[start : start + unit]
                quarter += 1
        return quarter


    def self_kernel(
        x, gain, shift, w_qkv, seg, w_out, w_query, w_next, first, query, held, first_far, query_far, qkv, probs, ctx,
        bias, sem,
    ):
        copy = pltpu.make_async_copy(w_next, held, sem)
        copy.start()
        width = x.shape[1]
        gains, shifts = gain[...].astype(F32), shift[...].astype(F32)
        rows = x[...].astype(F32)
        unit, _ = norm_parts(rows)
        qkv[...] = nn(norm_out(unit, gains, shifts, 0), w_qkv[...]).astype(BF)
        seg_row = seg[...].astype(F32)
        bias[...] = jnp.where(column(seg_row, seg_row.shape[1]) == seg_row, 0.0, -1000000000.0)
        attend(
            tile_of(qkv, 0), tile_of(qkv, width), tile_of(qkv, 2 * width), bias, probs, ctx, (width // HEADS) ** -0.5
        )
        for ref in (qkv, probs, ctx):
            ref.send()
        added = rows + nn(ctx[...], w_out[...])
        first[...] = added
        first_far[...] = added
        first_far.send()
        unit, _ = norm_parts(added)
        value = nn(norm_out(unit, gains, shifts, 1), w_query[...]).astype(BF)
        query[...] = value
        query_far[...] = value
        copy.wait()

    def cross_kernel(
        first, query, w_kv, seg, part0, part1, part2, part3, w_out, gain, shift, w_in, w_ffn, labels, mask,
        second, keyval, probs, ctx, hidden, slope, third, layer, final, bias,
    ):
        width = first.shape[1]
        count = first.shape[0]
        seg_row = seg[...].astype(F32)
        size = part0.shape[0] - EXTRA
        for index, part in enumerate((part0, part1, part2, part3)):
            span = slice(index * size, (index + 1) * size)
            keyval[span] = nn(part[:size], w_kv[...]).astype(BF)
            source_seg = part[size : size + EXTRA, :size].astype(F32)[0:1]
            bias[span] = jnp.where(column(source_seg, count) == seg_row, 0.0, -1000000000.0)
        attend(
            tile_of(query, 0), tile_of(keyval, 0), tile_of(keyval, width), bias, probs, ctx, (width // HEADS) ** -0.5
        )
        for ref in (keyval, probs, ctx):
            ref.send()
        added = first[...] + nn(ctx[...], w_out[...])
        second[...] = added
        second.send()
        gains, shifts = gain[...].astype(F32), shift[...].astype(F32)
        unit, _ = norm_parts(added)
        normed = norm_out(unit, gains, shifts, 2)
        for col in range(w_in.shape[1] // width):
            span = slice(col * width, (col + 1) * width)
            inner = nn(normed, w_in[:, span])
            cdf = 0.5 * (1.0 + lax.erf(inner * 0.7071067811865476))
            hidden[:, span] = (inner * cdf).astype(BF)
            slope[:, span] = (cdf + inner * jnp.exp(-0.5 * inner * inner) * 0.3989422804014327).astype(BF)
        hidden.send()
        slope.send()
        added = added + nn(hidden[...], w_ffn[...])
        third[...] = added
        layer[...] = added.astype(BF)
        third.send()
        layer.send()
        unit, _ = norm_parts(added)
        normed = norm_out(unit, gains, shifts, 3)
        final[:count] = normed
        label = labels[...]
        line = lax.broadcasted_iota(jnp.int32, (EXTRA, count), 0)
        high = lax.shift_right_logical(label, 8).astype(F32)
        marks = jnp.where(line == 0, high, 0.0)
        marks = jnp.where(line == 1, (label & 255).astype(F32), marks)
        marks = jnp.where(line == 2, mask[...].astype(F32), marks)
        final[count:] = jnp.concatenate([marks, jnp.zeros((EXTRA, width - count), F32)], axis=1).astype(BF)

    def head_kernel(
        final, seg, labels, mask, w_delete, w_insert,
        dfinal, keep, send, d_delete, loss, turned, ordered,
    ):
        section = lax.axis_index("pass")
        count = seg.shape[1]
        width = final.shape[1]
        h = final[:count]
        h32 = h.astype(F32)
        seg_col = column(seg[...].astype(F32), LANES)
        row_id = lax.broadcasted_iota(jnp.int32, (count, LANES), 0)
        linked = (pltpu.roll(seg_col, count - 1, 0) == seg_col) & (row_id < count - 1)
        linked = jnp.concatenate([linked.astype(F32)] * (width // LANES), axis=1)
        after = (pltpu.roll(h32, count - 1, 0) * linked).astype(BF)
        weight = column(mask[...].astype(F32), LANES)

        def entropy(logits, label, live):
            top = jnp.max(logits, axis=-1, keepdims=True)
            expo = jnp.exp(logits - top)
            total = jnp.sum(expo, axis=-1, keepdims=True)
            lane = lax.broadcasted_iota(jnp.int32, logits.shape, 1)
            target = column(label.astype(F32), logits.shape[1])
            hit = lane.astype(F32) == target
            picked = jnp.sum(jnp.where(hit, logits, 0.0), axis=1, keepdims=True)
            w = weight[:, :1] * live
            rest = jnp.sum(jnp.where(hit, 0.0, expo), axis=1, keepdims=True)
            grad = jnp.where(hit, -rest, expo) * (w / total)
            return jnp.sum(w * (top + jnp.log(total) - picked)), grad.astype(BF)

        label = labels[...]
        spot = lax.broadcasted_iota(jnp.int32, (LANES, width), 0)
        two = w_delete[...].astype(F32)
        both_rows = jnp.where(spot == 0, two[0:1], jnp.where(spot == 1, two[1:2], 0.0)).astype(BF)
        logits = nt(h, both_rows)
        lane = lax.broadcasted_iota(jnp.int32, logits.shape, 1)
        logits = jnp.where(lane < 2, logits, -1e30)
        loss_d, grad_d = entropy(logits, lax.rem(label, 2), (section == 0).astype(F32))
        logits = nn(h, w_insert[:width]) + nn(after, w_insert[width:])
        loss_i, grad_i = entropy(logits, lax.rem(label, INS), (section == 1).astype(F32))
        loss[...] = jnp.full(loss.shape, loss_d + loss_i)
        d_after = nt(grad_i, w_insert[width:]) * linked
        dfinal[...] = nn(grad_d, both_rows) + nt(grad_i, w_insert[:width]) + pltpu.roll(d_after, 1, 0)
        d_delete[...] = nn(flip(grad_d)[:EXTRA], h)[: d_delete.shape[0]]
        both_t = turn_rows(jnp.concatenate([h, after], axis=1), turned, ordered, owners())
        grad = nn(both_t, grad_i).astype(keep.dtype)
        block = both_t.shape[0] // n_dp
        half = block // 2
        for slot in range(n_dp):
            ref, index = (keep, slot) if slot < n_half else (send, slot - n_half)
            ref[index, :, :INS] = grad[slot * block : slot * block + half]
            ref[index, :, INS:] = grad[slot * block + half : (slot + 1) * block]


    def shard_base(chunk, shard):
        section, me = lax.axis_index("pass"), lax.axis_index("dp")
        return ((section ^ (chunk >> 1)) * n_dp + (me ^ (chunk & 1))) * shard

    def hits(base, start, shape, label):
        ids = lax.broadcasted_iota(jnp.int32, shape, 0) + (base + start)
        return ids == label

    def slots_of(refs):
        return [(ref, (i, half)) for half in range(2) for ref in refs for i in range(ref.shape[0])]

    def logit_kernel(n_prev, turn, n_tokens, spots, *refs):
        slots = [slots_of(refs[:n_tokens])[i] for i in spots]
        vocab, refs = refs[n_tokens : n_tokens + 4], refs[n_tokens + 4 :]
        if n_prev:
            prev, refs = refs[0], refs[1:]
        n = len(slots) // 2
        stats, expos = refs[0], refs[1 : 1 + n]
        turned = refs[1 + n] if turn else None
        h, logits = refs[-2:]
        size = (slots[0][0].shape[1] - EXTRA) // 2
        count = 2 * size
        shard = vocab[0].shape[0]
        if n_prev:
            stats[:, : n_prev * count] = prev[...]
        for tile in range(n):
            both = slots[2 * tile : 2 * tile + 2]
            for index, (ref, (i, half)) in enumerate(both):
                h[index * size : (index + 1) * size] = ref[i, half * size : (half + 1) * size]
            marks = jnp.concatenate(
                [ref[i, count:, half * size : (half + 1) * size].astype(F32) for ref, (i, half) in both], axis=1
            )
            label_f = marks[0:1] * 256.0 + marks[1:2]
            label = label_f.astype(jnp.int32)
            weight = marks[2:3]
            peak = jnp.full((8, count), -jnp.inf, F32)
            for chunk, ref in enumerate(vocab):
                for start in range(0, shard, 1024):
                    step = min(1024, shard - start)
                    value = nt(ref[start : start + step], h[...])
                    at = chunk * shard + start
                    logits[at : at + step] = value
                    peak = jnp.maximum(peak, jnp.max(value.reshape(step // 8, 8, count), axis=0))
                if turn and not tile:
                    turned[:, chunk * shard : (chunk + 1) * shard] = flip(ref[...])
            peak = jnp.max(peak, axis=0, keepdims=True)
            total = jnp.zeros((8, count), F32)
            chosen = jnp.zeros((8, count), F32)
            sub = min(shard, 128)
            expo = expos[tile]
            for chunk in range(4):
                base = shard_base(chunk, shard)

                def part(i, carry, chunk=chunk, base=base, expo=expo, peak=peak, label=label):
                    total, chosen = carry
                    at = pl.multiple_of(chunk * shard + i * sub, sub)
                    value = logits[pl.ds(at, sub)]
                    hit = hits(base, i * sub, (sub, count), label)
                    weight_of = jnp.where(hit, 0.0, jnp.exp(value - peak))
                    expo[pl.ds(at, sub)] = weight_of.astype(BF)
                    total = total + jnp.sum(weight_of.reshape(sub // 8, 8, count), axis=0)
                    picked = jnp.where(hit, value, 0.0)
                    return total, chosen + jnp.sum(picked.reshape(sub // 8, 8, count), axis=0)

                total, chosen = lax.fori_loop(0, shard // sub, part, (total, chosen), unroll=True)
            total = jnp.sum(total, axis=0, keepdims=True)
            chosen = jnp.sum(chosen, axis=0, keepdims=True)
            line = lax.broadcasted_iota(jnp.int32, (8, count), 0)
            block = jnp.zeros((8, count), F32)
            for at, value in enumerate((peak, total, chosen, label_f, weight)):
                block = jnp.where(line == at, value, block)
            at = (n_prev + tile) * count
            stats[:, at : at + count] = block

    def logit_call(tokens, vocab, prev, turn, spots):
        height, width = tokens[0].shape[1:]
        count = height - EXTRA
        n = len(spots) // 2
        shard = vocab[0].shape[0]
        n_prev = prev[0].shape[1] // count if prev else 0
        outs = [like((8, (n_prev + n) * count), F32)] + [like((4 * shard, count), BF)] * n
        stats, *rest = run(
            functools.partial(logit_kernel, n_prev, turn, len(tokens), spots),
            outs + ([like((width, 4 * shard), BF)] if turn else []),
            [*tokens, *vocab, *prev],
            2.8 * n,
            12,
            [pltpu.VMEM((count, width), BF), pltpu.VMEM((4 * shard, count), F32)],
            "token_logits",
        )
        return stats, rest[:n], rest[n:]

    def merged(own, other):
        peak = jnp.maximum(own[0:1], other[0:1])
        total = own[1:2] * jnp.exp(own[0:1] - peak) + other[1:2] * jnp.exp(other[0:1] - peak)
        return peak, total, own[2:3] + other[2:3]

    def merge_kernel(step, order, own, other, out):
        size = own.shape[1] // len(order)
        blocks = [other[:, i * size : (i + 1) * size] for i in range(len(order))]
        bit = len(order) >> (step + 2)
        swapped = jnp.concatenate([blocks[order.index((half, slot ^ bit))] for half, slot in order], axis=1)
        mine = own[...]
        peak, total, chosen = merged(mine, swapped)
        line = lax.broadcasted_iota(jnp.int32, mine.shape, 0)
        out[...] = jnp.where(
            line == 0, peak, jnp.where(line == 1, total, jnp.where(line == 2, chosen, mine))
        )

    def merge_all_kernel(order, own, near, next_, far, out):
        size = own.shape[1] // len(order)
        result = None
        for ref, bit in ((own, 0), (near, 1), (next_, 2), (far, 3)):
            blocks = [ref[:, i * size : (i + 1) * size] for i in range(len(order))]
            mine = jnp.concatenate([blocks[order.index((half, slot ^ bit))] for half, slot in order], axis=1)
            result = (mine[0:1], mine[1:2], mine[2:3]) if result is None else merged(jnp.concatenate(result, axis=0), mine)
        line = lax.broadcasted_iota(jnp.int32, own.shape, 0)
        peak, total, chosen = result
        out[...] = jnp.where(
            line == 0, peak, jnp.where(line == 1, total, jnp.where(line == 2, chosen, own[...]))
        )

    def closing(local, merged_ref, other):
        peak, total, chosen = merged(merged_ref, other)
        hit = jnp.exp(chosen - peak)
        full = total + hit
        lse = peak + jnp.log(full)
        weight = local[4:5]
        factor = weight * jnp.exp(local[0:1] - lse)
        return lse, chosen, factor, -weight * (total / full)

    def dlogits_into(ref, at, cols, expo, start, base, shape, label, factor, at_label):
        sub = min(shape[0], 128)

        def part(i, _):
            row = pl.multiple_of(i * sub, sub)
            hit = hits(base, i * sub, (sub, shape[1]), label)
            value = expo[pl.ds(pl.multiple_of(start + row, sub), sub)].astype(F32) * factor
            ref[pl.ds(pl.multiple_of(at + row, sub), sub), cols] = jnp.where(hit, at_label, value).astype(BF)
            return 0

        lax.fori_loop(0, shape[0] // sub, part, 0, unroll=True)

    def dtoken_kernel(tile, expo, vocab_t, local, merged_ref, other, out, dlogits):
        rows, count = expo.shape
        shard = rows // 4
        span = slice(tile * count, (tile + 1) * count)
        _, _, factor, at_label = closing(local[:, span], merged_ref[:, span], other[:, span])
        label = local[3:4, span].astype(jnp.int32)
        for chunk in range(4):
            dlogits_into(
                dlogits, chunk * shard, slice(None), expo, chunk * shard, shard_base(chunk, shard),
                (shard, count), label, factor, at_label,
            )
        total = nn(vocab_t[...], dlogits[...]).T.astype(out.dtype)
        out[0] = total[: count // 2]
        out[1] = total[count // 2 :]

    def dtoken_call(expo, tile, local, merged_ref, other, vocab_t, dtype):
        rows, count = expo.shape
        return run(
            functools.partial(dtoken_kernel, tile),
            [like((2, count // 2, vocab_t.shape[0]), dtype)],
            [expo, vocab_t, local, merged_ref, other],
            2.2,
            8,
            [pltpu.VMEM((rows, count), BF)],
            "token_dfinal",
        )[0]

    def dvocab_kernel(shard, parity, n_tiles, *refs):
        expos, tokens = refs[:n_tiles], refs[n_tiles:-6]
        local, merged_ref, other, out, dlogits, held = refs[-6:]
        index = pl.program_id(0)
        _, _, factor, at_label = closing(local[...], merged_ref[...], other[...])
        label = local[3:4].astype(jnp.int32)
        size = (tokens[0].shape[1] - EXTRA) // 2
        count = 2 * size
        section, me = lax.axis_index("pass"), lax.axis_index("dp")
        chunk = 2 * index + parity
        base = ((section ^ (chunk >> 1)) * n_dp + (me ^ (chunk & 1))) * shard
        slots = slots_of(tokens[:2]) + [slot for token in tokens[2:] for slot in slots_of([token])]
        for at, (token, (i, half)) in enumerate(slots):
            held[at * size : (at + 1) * size] = token[i, half * size : (half + 1) * size]
        for at, expo in enumerate(expos):
            cols = slice(at * count, (at + 1) * count)
            dlogits_into(
                dlogits, 0, cols, expo, 0, base, (shard, count), label[:, cols], factor[:, cols], at_label[:, cols]
            )
        out[...] = nn(dlogits[...], held[...]).astype(out.dtype)

    def dvocab_call(expos, tokens, local, merged_ref, other, parity, dtype):
        shard, count = expos[0].shape[0] // 4, expos[0].shape[1]
        width = tokens[0].shape[2]
        total = local.shape[1]
        fixed2 = pl.BlockSpec(local.shape, lambda c: (0, 0))
        return pl.pallas_call(
            functools.partial(dvocab_kernel, shard, parity, len(expos)),
            grid=(2,),
            in_specs=[pl.BlockSpec((shard, count), lambda c: (2 * c + parity, 0))] * len(expos)
            + [pl.BlockSpec(t.shape, lambda c: (0, 0, 0)) for t in tokens]
            + [fixed2] * 3,
            out_specs=pl.BlockSpec((shard, width), lambda c: (c, 0)),
            out_shape=like((2 * shard, width), dtype),
            scratch_shapes=[pltpu.VMEM((shard, total), BF), pltpu.VMEM((total, width), BF)],
            compiler_params=pltpu.CompilerParams(vmem_limit_bytes=20 * MIB),
            cost_estimate=cost(0.1),
            name="token_dvocab",
        )(*expos, *tokens, local, merged_ref, other)


    def ffn_back_kernel(
        hidden, third, gain, w_ffn, slope, second, shift, w_in,
        kept0, kept1, moved0, moved1, dhead, head_loss, local, merged_ref, other, ins_keep, ins_send,
        dsecond, keep, send, vecs, loss, wide_t, wide_s, thin_t, thin_s, dinner,
    ):
        width = third.shape[1]
        count = third.shape[0]
        live = (lax.axis_index("pass") >= 2).astype(F32)
        hidden_t = turn_rows(hidden[...], wide_t, wide_s, owners())
        parts = [kept[...] + moved[...].astype(F32) for kept, moved in ((kept0, moved0), (kept1, moved1))]
        dfinal = dhead[...] + live * jnp.concatenate(parts, axis=0)
        unit3, rstd3 = norm_parts(third[...])
        gains = gain[...].astype(F32)
        dthird, g_gain3, g_bias3 = norm_bwd(dfinal, unit3, rstd3, gains[3:4])
        low = dthird.astype(BF)
        pack(keep, send, 0, 0, hidden_t, low)
        for col in range(w_ffn.shape[0] // width):
            span = slice(col * width, (col + 1) * width)
            part = nt(low, w_ffn[span]).astype(BF).astype(F32) * slope[:, span].astype(F32)
            dinner[:, span] = part.astype(BF)
        unit2, rstd2 = norm_parts(second[...])
        normed_t = turn_rows(norm_out(unit2, gains, shift[...].astype(F32), 2), thin_t, thin_s, owners())
        pack(keep, send, 4 * (width // n_dp), 0, normed_t, dinner[...])
        extra = ins_keep.shape[1]
        keep[:, keep.shape[1] - extra :] = ins_keep[...]
        send[:, keep.shape[1] - extra :] = ins_send[...]
        dnormed = nt(dinner[...], w_in[...])
        back, g_gain2, g_bias2 = norm_bwd(dnormed, unit2, rstd2, gains[2:3])
        dsecond[...] = dthird + back
        token_loss = 0.0
        for start in (0, count):
            span = slice(start, start + count // 2)
            lse, chosen, _, _ = closing(local[:, span], merged_ref[:, span], other[:, span])
            token_loss = token_loss + jnp.sum(local[4:5, span] * (lse - chosen))
        loss[...] = head_loss[...] + token_loss * live
        line = lax.broadcasted_iota(jnp.int32, (8, width), 0)
        block = jnp.zeros((8, width), F32)
        for at, value in enumerate((g_gain3, g_gain2, g_bias3, g_bias2)):
            block = jnp.where(line == at, value, block)
        vecs[...] = block

    def cross_back_kernel(
        dsecond, w_out, ctx, keyval, probs, query, part0, part1, part2, part3, w_kv, first, gain, shift, w_query,
        dfirst, keep, send, vecs, dsrc0, dsrc2, dsrc13, thin_t, thin_s, src_t, src_s, dquery, dkeyval, dctx,
    ):
        width = first.shape[1]
        owner_list = owners()
        low = dsecond[...].astype(BF)
        dctx[...] = nt(low, w_out[...]).astype(BF)
        at = pack(keep, send, 0, 0, turn_rows(ctx[...], thin_t, thin_s, owner_list), low)
        attend_bwd(
            tile_of(dctx, 0), tile_of(query, 0), tile_of(keyval, 0), tile_of(keyval, width), probs,
            put_in(dquery, 0), put_in(dkeyval, 0), put_in(dkeyval, width), (width // HEADS) ** -0.5, width // LANES,
        )
        size = part0.shape[0] - EXTRA
        source = jnp.concatenate([p[:size] for p in (part0, part1, part2, part3)], axis=0)
        at = pack(keep, send, 0, at, turn_rows(source, src_t, src_s, owner_list), dkeyval[...])
        for index, (ref, row) in enumerate(((dsrc0, 0), (dsrc13, 0), (dsrc2, 0), (dsrc13, size))):
            part = nt(dkeyval[index * size : (index + 1) * size], w_kv[...])
            ref[row : row + size] = part.astype(ref.dtype)
        gains, shifts = gain[...].astype(F32), shift[...].astype(F32)
        unit, rstd = norm_parts(first[...])
        normed_t = turn_rows(norm_out(unit, gains, shifts, 1), thin_t, thin_s, owner_list)
        pack(keep, send, 0, at, normed_t, dquery[...])
        back, g_gain, g_bias = norm_bwd(nt(dquery[...], w_query[...]), unit, rstd, gains[1:2])
        dfirst[...] = dsecond[...] + back
        line = lax.broadcasted_iota(jnp.int32, (8, width), 0)
        vecs[...] = jnp.where(line == 0, g_gain, jnp.where(line == 1, g_bias, 0.0))

    def self_back_kernel(
        dfirst, w_out, ctx, qkv, probs, x, gain, shift, w_qkv, vec_ffn, vec_cross, d_delete,
        dx, keep, send, thin_t, thin_s, dqkv, dctx,
    ):
        width = x.shape[1]
        owner_list = owners()
        low = dfirst[...].astype(BF)
        dctx[...] = nt(low, w_out[...]).astype(BF)
        at = pack(keep, send, 0, 0, turn_rows(ctx[...], thin_t, thin_s, owner_list), low)
        attend_bwd(
            tile_of(dctx, 0), tile_of(qkv, 0), tile_of(qkv, width), tile_of(qkv, 2 * width), probs,
            put_in(dqkv, 0), put_in(dqkv, width), put_in(dqkv, 2 * width), (width // HEADS) ** -0.5, width // LANES,
        )
        gains, shifts = gain[...].astype(F32), shift[...].astype(F32)
        unit, rstd = norm_parts(x[...].astype(F32))
        normed_t = turn_rows(norm_out(unit, gains, shifts, 0), thin_t, thin_s, owner_list)
        at = pack(keep, send, 0, at, normed_t, dqkv[...])
        back, g_gain, g_bias = norm_bwd(nt(dqkv[...], w_qkv[...]), unit, rstd, gains[0:1])
        dx[...] = dfirst[...] + back
        line = lax.broadcasted_iota(jnp.int32, (EXTRA, width), 0)
        block = jnp.zeros((EXTRA, width), F32)
        lines = (
            (0, d_delete[0:1]), (1, d_delete[1:2]),
            (8, g_gain), (9, vec_cross[0:1]), (10, vec_ffn[1:2]), (11, vec_ffn[0:1]),
            (12, g_bias), (13, vec_cross[1:2]), (14, vec_ffn[3:4]), (15, vec_ffn[2:3]),
        )
        for row, value in lines:
            block = jnp.where(line == row, value, block)
        block = block.astype(keep.dtype)
        at = at * (width // n_dp)
        for slot in range(n_half):
            keep[slot, at:] = block
            send[slot, at:] = block


    def add_kernel(pairs, *refs):
        ins, outs = refs[: 2 * pairs], refs[2 * pairs :]
        at = 0
        for keep, got in zip(ins[::2], ins[1::2]):
            rows = keep.shape[1]
            slot = 0
            for ref in outs:
                for i in range(ref.shape[0]):
                    value = keep[slot].astype(F32) + got[slot].astype(F32)
                    ref[i, at : at + rows] = value.astype(ref.dtype)
                    slot += 1
            at += rows

    def add_call(blocks, *counts):
        rows, width = sum(b.shape[1] for b in blocks[::2]), blocks[0].shape[2]
        outs = [like((count, rows, width), wire_of(width)) for count in counts]
        return run(functools.partial(add_kernel, len(blocks) // 2), outs, blocks, 0.8, 8, name="sum_slots")

    def wire_of(width):
        return small_dtype(width // n_dp)

    def regroup_kernel(plan, n_terms, *refs):
        value = refs[0][...].astype(F32)
        for ref in refs[1:n_terms]:
            value = value + ref[...].astype(F32)
        for spans, ref in zip(plan, refs[n_terms:]):
            at = 0
            for start, stop in spans:
                ref[at : at + stop - start] = value[start:stop].astype(ref.dtype)
                at += stop - start

    def pair_kernel(plan, n_terms, *refs):
        first = refs[0][...].astype(F32) + refs[1][...].astype(F32)
        value = first + (refs[2][...].astype(F32) + refs[3][...].astype(F32))
        for spans, ref in zip(plan, refs[n_terms:]):
            at = 0
            for start, stop in spans:
                ref[at : at + stop - start] = value[start:stop].astype(ref.dtype)
                at += stop - start

    def regroup(terms, plan, kernel=regroup_kernel, name="sum_rows"):
        width = terms[0].shape[-1]
        outs = [like((sum(b - a for a, b in spans), width), wire_of(width)) for spans in plan]
        terms = [t.reshape(t.shape[-2:]) for t in terms]
        return run(functools.partial(kernel, plan, len(terms)), outs, terms, 0.7, 8, name=name)

    def picked(pieces):
        section = lax.axis_index("pass")
        values = [p.astype(F32) for p in pieces]
        result = []
        for j in range(4):
            value = values[0]
            for b in (1, 2, 3):
                value = jnp.where((section ^ b) == j, values[b], value)
            result.append(value)
        return result

    def halves(refs):
        rows = refs[0].shape[0] // 2
        return [r[:rows] for r in refs], [r[rows:] for r in refs]

    def ffn_end_kernel(own, near, third, far, extra, p_out, p_in, p_insert):
        outs, ins = halves((own, near, third, far))
        rows, width = outs[0].shape
        for j, value in enumerate(picked(outs)):
            p_out[j * rows : (j + 1) * rows] = value
        for j, value in enumerate(picked(ins)):
            p_in[:, j * width : (j + 1) * width] = value
        half = p_insert.shape[0] // 2
        value = extra[...].astype(F32)
        p_insert[:half] = value[:, :INS]
        p_insert[half:] = value[:, INS:]

    def attention_end_kernel(
        own, near, third, far, extra, p_cross, p_kv, p_query, p_out, p_qkv, p_gain, p_bias, p_delete
    ):
        cross, own_part = halves((own, near, third, far))
        width = extra.shape[1]
        values = picked(cross)
        p_cross[...] = values[0]
        p_kv[:, :width] = values[1]
        p_kv[:, width:] = values[2]
        p_query[...] = values[3]
        values = picked(own_part)
        p_out[...] = values[0]
        for j in range(3):
            p_qkv[:, j * width : (j + 1) * width] = values[j + 1]
        size = p_gain.shape[1]
        me = lax.axis_index("dp")
        mine = pltpu.roll(extra[...].astype(F32), lax.rem(width - me * size, width), 1)
        p_gain[...] = mine[8:12, :size]
        p_bias[...] = mine[12:16, :size]
        p_delete[...] = mine[:2, :size]

    def body(
        decoder_in,
        decoder_segments,
        edit_target,
        loss_mask,
        source_out,
        source_segments,
        norm_gain,
        norm_bias,
        self_qkv,
        self_out,
        cross_query,
        cross_kv,
        cross_out,
        ffn_in,
        ffn_out,
        delete_head,
        insert_head,
        token_head,
    ):
        section = lax.axis_index("pass")
        segs, labels, mask = decoder_segments[0], edit_target[0], loss_mask[0]
        rows = decoder_in[0, 0]
        count, width = rows.shape
        shard = token_head.shape[0]
        part = source_out.shape[1]
        src = n_pass * part
        hid = ffn_in.shape[1]
        unit = width // n_dp
        wire = small_dtype(unit)

        note = jnp.pad(source_segments.astype(BF), ((0, EXTRA - 1), (0, width - part)))
        mine = jnp.concatenate([source_out[0], note], axis=0)
        parts = [mine] + [swap_pass(mine, bit) for bit in (1, 2, 3)]

        gain, shift = Far(norm_gain), Far(norm_bias)
        first, query, w_kv, first_far, query_far, qkv, probs1, ctx1 = run(
            self_kernel,
            [
                like((count, width), F32),
                like((count, width), BF),
                like(cross_kv.shape, BF),
                Far(like((count, width), F32)),
                Far(like((count, width), BF)),
                Far(like((count, 3 * width), BF)),
                Far(like((HEADS, count, count), BF)),
                Far(like((count, width), BF)),
            ],
            [Far(rows), gain, shift, Far(self_qkv), Far(segs), Far(self_out), Far(cross_query), Raw(cross_kv)],
            4.2,
            10,
            [pltpu.VMEM((count, count), F32), pltpu.SemaphoreType.DMA],
            "self_forward",
        )
        second, keyval, probs2, ctx2, hidden, slope, third, layer, final = run(
            cross_kernel,
            [
                Far(like((count, width), F32)),
                Far(like((src, 2 * width), BF)),
                Far(like((HEADS, src, count), BF)),
                Far(like((count, width), BF)),
                Far(like((count, hid), BF)),
                Far(like((count, hid), BF)),
                Far(like((count, width), F32)),
                Far(like((count, width), BF)),
                like((count + EXTRA, width), BF),
            ],
            [first, query, w_kv, Far(segs), *parts, Pin(cross_out), gain, shift]
            + [Pin(ffn_in), Pin(ffn_out), Far(labels), Far(mask)],
            7.6,
            20,
            [pltpu.VMEM((src, count), F32)],
            "cross_forward",
        )

        near = swap_pass(after(token_head, parts[1]), 1)
        moved = lax.ppermute(final, "pass", [(2, 0), (3, 1)])
        group = jnp.where(section >= 2, final, moved)[None]
        tokens = [group]
        for step in reversed(range(n_steps)):
            tokens.append(swap_chip(group, step))
            if step:
                group = jnp.concatenate([group, tokens[-1]], axis=0)
        near = after(near, tokens[1])
        vocab = (token_head, swap_core(token_head), near, swap_core(near))
        expos, stats, vocab_t, order = [[], []], (), None, []
        for pieces in [tokens[:2]] + [[t] for t in tokens[2:]]:
            made = []
            for tile in range(sum(p.shape[0] for p in pieces)):
                stats, new, turned = logit_call(pieces, vocab, stats, not vocab_t, (2 * tile, 2 * tile + 1))
                stats = (stats,)
                vocab_t = vocab_t or turned
                made += new
            first_slot, n_slots = len(order) // 2, sum(p.shape[0] for p in pieces)
            for half in range(2):
                spot = half * len(made) // 2
                expos[half] += [(e, len(order) // 2 + i) for i, e in enumerate(made[spot : spot + len(made) // 2])]
                order += [(half, first_slot + i) for i in range(n_slots)]
        (vocab_t,) = vocab_t
        local = stats[0]
        whole = local
        if n_steps == 2:
            both = lax.ppermute(local, "dp", [(i, i ^ chip_bits[0] ^ chip_bits[1]) for i in range(n_dp)])
            (whole,) = run(
                functools.partial(merge_all_kernel, order), [like(local.shape, F32)],
                [local, swap_chip(local, 1), swap_chip(local, 0), both], 1.0, 8, name="stats_merge",
            )
        else:
            for step in range(n_steps):
                (whole,) = run(
                    functools.partial(merge_kernel, step, order), [like(local.shape, F32)],
                    [whole, swap_chip(whole, step)], 1.0, 8, name="stats_merge",
                )
        other = swap_pass(whole, 2)

        ins_rows = 2 * width // n_dp // 2
        dhead, ins_keep, ins_send, d_delete, head_loss = run(
            head_kernel,
            [
                like((count, width), F32),
                like((n_half, ins_rows, 2 * INS), wire),
                like((n_half, ins_rows, 2 * INS), wire),
                like((8, width), F32),
                like((8, LANES), F32),
            ],
            [after(final, whole), Far(segs), Far(labels), Far(mask), Far(delete_head.T), Pin(insert_head)],
            1.4,
            10,
            turn_scratch(2 * width, count),
            "small_heads",
        )
        other = after(other, dhead)

        n_tiles = len(expos[0])
        made = [[None] * n_tiles for _ in expos]
        for tile in reversed(range(n_tiles)):
            for half in range(2):
                dtype = BF if tile >= n_tiles // 2 and n_tiles > 1 else F32
                expo, spot = expos[half][tile]
                made[half][tile] = dtoken_call(expo, spot, local, whole, other, vocab_t, dtype)
        kept = []
        for half in range(2):
            tiles = made[half]
            for step in range(n_steps):
                if len(tiles) > 1:
                    middle = len(tiles) // 2
                    sending = tiles[middle:]
                    sending = jnp.concatenate(sending, axis=0) if len(sending) > 1 else sending[0]
                    got = swap_chip(sending.astype(BF), step)
                    tiles = [t + got[2 * i : 2 * i + 2].astype(F32) for i, t in enumerate(tiles[:middle])]
                else:
                    got = swap_chip(tiles[0][1].astype(BF), step)
                    kept.append(tiles[0][0] + got.astype(F32))
        backs = [lax.ppermute(k.astype(BF), "pass", [(0, 2), (1, 3)]) for k in kept]

        flat = [e for e, _ in sorted(sum(expos, []), key=lambda pair: pair[1])]
        dvocab_send = dvocab_call(flat, tokens, after(local, *kept), whole, other, 1, BF)
        dvocab_keep = dvocab_call(flat, tokens, after(local, dvocab_send), whole, other, 0, BF)
        backs = after_all(backs, dvocab_send, dvocab_keep)
        vocab_got = swap_core(after(dvocab_send, *backs))

        def packed(rows):
            return like((n_half, rows, width), wire)

        def sent(x):
            return x.astype(BF)

        def reduce_chips(blocks, step):
            while step < n_steps:
                half = n_half >> (step + 1)
                keep, send = add_call(blocks, half, half)
                blocks = [keep, swap_chip(sent(send), step)]
                step += 1
            return blocks

        rows_ffn = 8 * unit + ins_rows
        dsecond, keep_ffn, send_ffn, vec_ffn, loss = run(
            ffn_back_kernel,
            [like((count, width), F32), packed(rows_ffn), packed(rows_ffn), like((8, width), F32), like((8, LANES), F32)],
            [Pin(hidden), Pin(third), gain, Pin(ffn_out), Pin(slope), Pin(second), shift, Pin(ffn_in)]
            + [*kept, *backs, dhead, head_loss, local, whole, other, ins_keep, ins_send],
            0.1,
            16,
            turn_scratch(hid, count) + turn_scratch(width, count) + [pltpu.VMEM((count, hid), BF)],
            "ffn_backward",
        )
        dsecond, keep_ffn, send_ffn, vec_ffn, loss = after_all(
            [dsecond, keep_ffn, send_ffn, vec_ffn, loss], vocab_got
        )
        vocab_keep = dvocab_keep[:shard].astype(F32) + vocab_got[:shard].astype(F32)
        vocab_send = (dvocab_keep[shard:].astype(F32) + vocab_got[shard:].astype(F32)).astype(BF)
        cuts = [shard * i // 64 for i in (0, 30, 42, 64)]
        vocab_parts = [vocab_send[a:b] for a, b in zip(cuts, cuts[1:])]
        vocab_parts[0] = swap_pass(vocab_parts[0], 1)
        keep_ffn, send_ffn = add_call([keep_ffn, swap_core(sent(send_ffn))], n_half // 2, n_half // 2)
        dsecond = after(dsecond, send_ffn)
        dfirst, *chunk_cross, vec_cross, src0, src2, src13 = run(
            cross_back_kernel,
            [
                like((count, width), F32),
                packed(4 * unit),
                packed(4 * unit),
                like((8, width), F32),
                like((part, width), F32),
                like((part, width), F32),
                like((2 * part, width), BF),
            ],
            [dsecond, Pin(cross_out), Pin(ctx2), Pin(keyval), Pin(probs2), Pin(query_far), *parts]
            + [Pin(cross_kv), Pin(first_far), gain, shift, Pin(cross_query)],
            0.1,
            15,
            turn_scratch(width, count)
            + turn_scratch(width, src)
            + [pltpu.VMEM((count, width), BF), pltpu.VMEM((src, 2 * width), BF), pltpu.VMEM((count, width), BF)],
            "cross_backward",
        )
        blocks_ffn = [keep_ffn, swap_chip(sent(send_ffn), 0)]
        dfirst, *chunk_cross, vec_cross, src0, src2, src13 = after_all(
            [dfirst, *chunk_cross, vec_cross, src0, src2, src13], vocab_parts[0]
        )
        vocab_parts[1] = swap_pass(after(vocab_parts[1], dfirst), 1)
        input_grad, *chunk_self = run(
            self_back_kernel,
            [Far(like((count, width), F32)), packed(4 * unit + EXTRA), packed(4 * unit + EXTRA)],
            [dfirst, Pin(self_out), Pin(ctx1), Pin(qkv), Pin(probs1), Pin(rows), gain, shift, Pin(self_qkv)]
            + [vec_ffn, vec_cross, d_delete],
            0.1,
            12,
            turn_scratch(width, count) + [pltpu.VMEM((count, 3 * width), BF), pltpu.VMEM((count, width), BF)],
            "self_backward",
        )
        def rows_at(*spots, extra=0, start=8):
            spans = [(i * unit, (i + 1) * unit) for i in spots]
            return spans + ([(start * unit, start * unit + extra)] if extra else [])

        input_grad, *chunk_self = after_all([input_grad, *chunk_self], blocks_ffn[1], vocab_parts[1])
        blocks_ffn = reduce_chips(blocks_ffn, 1)

        got_cross = swap_core(sent(chunk_cross[1]))
        keep_self, send_self = chunk_self
        send_self = after(send_self, got_cross)
        got_self = swap_core(sent(send_self))
        keep_att, send_att = add_call([chunk_cross[0], got_cross, keep_self, got_self], n_half // 2, n_half // 2)
        source_got = swap_pass(src13, 1)
        source_half = swap_pass((src2 + source_got[part:].astype(F32)).astype(BF), 2)
        source_grad = (src0 + source_got[:part].astype(F32)) + source_half.astype(F32)
        blocks_att = [keep_att, swap_chip(after(sent(send_att), blocks_ffn[1], source_got), 0)]

        keep, send = regroup(
            blocks_ffn,
            [rows_at(0, 2, 4, 6, extra=ins_rows), rows_at(1, 3, 5, 7, extra=ins_rows)],
        )
        got = swap_pass(sent(send), 1)
        got = after(got, source_half)
        blocks_att[1] = after(blocks_att[1], got)
        blocks_att = reduce_chips(blocks_att, 1)
        keep, send = regroup(
            [keep, got],
            [rows_at(0, 2, extra=ins_rows, start=4), rows_at(1, 3, extra=ins_rows, start=4)],
        )
        got = swap_pass(sent(send), 2)
        vocab_parts[2] = swap_pass(after(vocab_parts[2], send), 1)
        token_grad = vocab_keep + jnp.concatenate(vocab_parts, axis=0).astype(F32)
        blocks_att[1] = after(blocks_att[1], got)
        pieces_by_place = regroup(blocks_att, [rows_at(i, 4 + i, extra=EXTRA) for i in range(4)])
        own, ins_sum = regroup([keep, got], [rows_at(0, 1), rows_at(extra=ins_rows, start=2)])
        near, third_part = swap_pass(sent(own), 1), swap_pass(sent(own), 2)
        ffn_parts = [own, near, third_part, swap_pass(third_part, 1), ins_sum]

        gots = [swap_pass(sent(pieces_by_place[b]), b) for b in (1, 2, 3)]
        own, extra_sum = regroup(
            [pieces_by_place[0], *gots], [rows_at(0, 1), rows_at(extra=EXTRA, start=2)], pair_kernel, "sum_pass"
        )
        attention_parts = [own] + [swap_pass(sent(own), b) for b in (1, 2, 3)] + [extra_sum]

        def out(*shape):
            return Far(like(shape, F32))

        p_out, p_in, p_insert = run(
            ffn_end_kernel, [out(hid // n_dp, width), out(unit, hid), out(2 * unit, INS)], ffn_parts, 1.0, 8,
            name="ffn_sums",
        )
        p_cross, p_kv, p_query, p_self, p_qkv, p_gain, p_bias, p_delete = run(
            attention_end_kernel,
            [out(unit, width), out(unit, 2 * width), out(unit, width), out(unit, width), out(unit, 3 * width)]
            + [out(4, unit), out(4, unit), out(2, unit)],
            attention_parts,
            1.0,
            8,
            name="attention_sums",
        )
        return (
            layer[None, None],
            loss[:1, :1],
            input_grad[None, None],
            source_grad[None],
            p_gain,
            p_bias,
            p_qkv,
            p_self,
            p_query,
            p_kv,
            p_cross,
            p_in,
            p_out,
            p_delete.T,
            p_insert,
            token_grad,
        )

    full = ("pass", "dp")
    rows_at, row_at = P("pass", "dp", None, None), P("pass", "dp", None)
    weight_at = P("dp", None)
    return jax.shard_map(
        body,
        mesh=mesh,
        in_specs=(rows_at, row_at, row_at, row_at, P("dp", "pass", None), P("dp", "pass"))
        + (P(),) * 11
        + (P(full, None),),
        out_specs=(rows_at, P("pass", "dp"), rows_at, P("dp", "pass", None), P(None, "dp"), P(None, "dp"))
        + (weight_at,) * 9
        + (P(full, None),),
        check_vma=False,
    )
```

```python
import functools

import jax
import jax.numpy as jnp
from jax import lax
from jax.experimental import pallas as pl
from jax.experimental.pallas import tpu as pltpu
from jax.sharding import PartitionSpec as P

HEADS = 8
INS = 256
EPS = 1e-05
LANES = 128
EXTRA = 16
BF = jnp.bfloat16
F32 = jnp.float32
MIB = 1 << 20


def cost(us):
    return pl.CostEstimate(flops=int(us * 0.3e9), bytes_accessed=1, transcendentals=0)


def dot(left, right, dims):
    return lax.dot_general(left, right, (dims, ((), ())), preferred_element_type=F32)


def nn(left, right):
    return dot(left, right, ((1,), (0,)))


def nt(left, right):
    return dot(left, right, ((1,), (1,)))


def flip(values):
    return values.astype(F32).T.astype(BF)


class Far:
    def __init__(self, value):
        self.value = value


class Raw(Far):
    pass


class Pin(Far):
    pass


class Fetched:
    def __init__(self, source, buffer, sem):
        self.buffer, self.shape, self.dtype = buffer, buffer.shape, buffer.dtype
        self.copy = pltpu.make_async_copy(source, buffer, sem)
        self.copy.start()
        self.waiting = True

    def wait(self):
        if self.waiting:
            self.copy.wait()
            self.waiting = False

    def __getitem__(self, index):
        self.wait()
        return self.buffer[index]


class Stored:
    def __init__(self, target, buffer, sem):
        self.buffer, self.shape, self.dtype = buffer, buffer.shape, buffer.dtype
        self.copy = pltpu.make_async_copy(buffer, target, sem)
        self.target, self.sem = target, sem
        self.sent = False

    def __getitem__(self, index):
        return self.buffer[index]

    def __setitem__(self, index, value):
        self.buffer[index] = value

    def send(self):
        self.copy.start()
        self.sent = True

    def send_part(self, index):
        pltpu.make_async_copy(self.buffer.at[index], self.target.at[index], self.sem).start()
        self.sent = True


def run(kernel, outs, ins, us, limit, scratch=(), name=None):
    far_in, far_out = [type(x) is Far for x in ins], [type(x) is Far for x in outs]
    marks_in, marks_out = [type(x) for x in ins], [type(x) for x in outs]
    ins = [x.value if isinstance(x, Far) else x for x in ins]
    outs = [x.value if isinstance(x, Far) else x for x in outs]
    buffers = [pltpu.VMEM(x.shape, x.dtype) for x, f in zip(ins + outs, far_in + far_out) if f]
    spaces = {Far: pltpu.HBM, Raw: pltpu.HBM, Pin: pltpu.VMEM}
    ins = [pltpu.with_memory_space_constraint(x, spaces[m]) if m in spaces else x for x, m in zip(ins, marks_in)]
    outs = [spaces[m](x.shape, x.dtype) if m in spaces else x for x, m in zip(outs, marks_out)]
    n_in, n_out = len(ins), len(outs)

    def wrapped(*refs):
        if buffers:
            sems = refs[-1]
            held = list(refs[-1 - len(buffers) : -1])
            rest = refs[n_in + n_out : len(refs) - 1 - len(buffers)]
        else:
            held, rest = [], refs[n_in + n_out :]
        given, made, count = [], [], 0
        for ref, far in zip(refs[:n_in], far_in):
            given.append(Fetched(ref, held[count], sems.at[count]) if far else ref)
            count += far
        for ref, far in zip(refs[n_in : n_in + n_out], far_out):
            made.append(Stored(ref, held[count], sems.at[count]) if far else ref)
            count += far
        kernel(*given, *made, *rest)
        for x in given:
            if isinstance(x, Fetched):
                x.wait()
        for x in made:
            if isinstance(x, Stored) and not x.sent:
                x.send()
        for x in made:
            if isinstance(x, Stored):
                x.copy.wait()

    def place(mark):
        return pl.BlockSpec(memory_space=spaces.get(mark, pltpu.VMEM))

    return pl.pallas_call(
        wrapped,
        out_shape=outs,
        in_specs=[place(m) for m in marks_in],
        out_specs=[place(m) for m in marks_out],
        scratch_shapes=list(scratch) + buffers + ([pltpu.SemaphoreType.DMA((len(buffers),))] if buffers else []),
        compiler_params=pltpu.CompilerParams(vmem_limit_bytes=limit * MIB),
        cost_estimate=cost(us),
        name=name,
    )(*ins)


def after(value, *done):
    return lax.optimization_barrier((value, *done))[0]


def after_all(values, *done):
    return list(lax.optimization_barrier((*values, *done))[: len(values)])


def like(shape, dtype):
    return jax.ShapeDtypeStruct(shape, dtype)


def norm_parts(values):
    center = values - jnp.mean(values, axis=-1, keepdims=True)
    rstd = lax.rsqrt(jnp.mean(center * center, axis=-1, keepdims=True) + EPS)
    return center * rstd, rstd


def norm_out(unit, gain, shift, index):
    return (unit * gain[index : index + 1] + shift[index : index + 1]).astype(BF)


def norm_bwd(grad, unit, rstd, gain):
    scaled = grad * gain
    back = rstd * (
        scaled
        - jnp.mean(scaled, axis=-1, keepdims=True)
        - unit * jnp.mean(scaled * unit, axis=-1, keepdims=True)
    )
    return back, jnp.sum(grad * unit, axis=0, keepdims=True), jnp.sum(grad, axis=0, keepdims=True)


def column(row, count):
    return jnp.broadcast_to(row, (count, row.shape[1])).T


def lane_half(values, half):
    lane = lax.broadcasted_iota(jnp.int32, values.shape, 1)
    picked = (lane >= LANES // 2) if half else (lane < LANES // 2)
    return jnp.where(picked, values, jnp.zeros_like(values))


def attend(query, keys, values, bias_ref, probs_ref, out_ref, scale, finished=None):
    half_size = LANES // 2
    for tile in range(out_ref.shape[1] // LANES):
        q = query(tile).astype(F32) * scale
        k, v_t = keys(tile), flip(values(tile))
        parts = []
        for half in range(2):
            scores = nt(k, lane_half(q, half).astype(BF)) + bias_ref[...]
            expo = jnp.exp(scores - jnp.max(scores, axis=0, keepdims=True))
            probs = (expo * (1.0 / jnp.sum(expo, axis=0, keepdims=True))).astype(BF)
            probs_ref[2 * tile + half] = probs
            parts.append(nn(v_t[half * half_size : (half + 1) * half_size], probs))
        out_ref[:, tile * LANES : (tile + 1) * LANES] = jnp.concatenate(parts, axis=0).T.astype(BF)
        if finished:
            finished(tile)


def attend_bwd(grad, query, keys, values, probs_ref, put_query, put_keys, put_values, scale, tiles):
    half_size = LANES // 2
    for tile in range(tiles):
        g, q, k, v = grad(tile), query(tile), keys(tile), values(tile)
        k_t = flip(k)
        dq, dk, dv = [], [], []
        for half in range(2):
            probs = probs_ref[2 * tile + half]
            full = probs.astype(F32)
            dprobs = nt(v, lane_half(g, half))
            delta = jnp.sum(dprobs * full, axis=0, keepdims=True)
            dscores = (full * ((dprobs - delta) * scale)).astype(BF)
            dv.append(nn(probs, g))
            dk.append(nn(dscores, q))
            dq.append(nn(k_t[half * half_size : (half + 1) * half_size], dscores))
        lane = lax.broadcasted_iota(jnp.int32, dk[0].shape, 1) < half_size
        put_query(tile, jnp.concatenate(dq, axis=0).T.astype(BF))
        put_keys(tile, jnp.where(lane, dk[0], dk[1]).astype(BF))
        put_values(tile, jnp.where(lane, dv[0], dv[1]).astype(BF))


def tile_of(ref, start):
    return lambda tile: ref[:, start + tile * LANES : start + (tile + 1) * LANES]


def put_in(ref, start):
    def put(tile, value):
        ref[:, start + tile * LANES : start + (tile + 1) * LANES] = value

    return put


def solution(mesh):
    n_pass, n_dp = mesh.shape["pass"], mesh.shape["dp"]
    bits = [1 << i for i in range(n_dp.bit_length() - 1)]
    core_bit, chip_bits = bits[0], bits[1:]
    orders = (chip_bits, chip_bits[1::-1] + chip_bits[2:])
    n_steps = len(chip_bits)
    n_half = n_dp // 2

    def swap_core(x):
        return lax.ppermute(x, "dp", [(i, i ^ core_bit) for i in range(n_dp)])

    def swap_chip(x, step):
        return lax.ppermute(x, "dp", [(i, i ^ orders[i & 1][step]) for i in range(n_dp)])

    def swap_pass(x, bit):
        return lax.ppermute(x, "pass", [(i, i ^ bit) for i in range(n_pass)])

    def owners():
        me = lax.axis_index("dp")
        core = me & 1
        result = []
        for slot in range(n_dp):
            own_half = slot < n_half
            turn = core if own_half else 1 - core
            owner = me if own_half else me ^ 1
            for step in range(n_steps):
                if (slot >> (n_steps - 1 - step)) & 1:
                    owner = owner ^ jnp.where(turn == 0, orders[0][step], orders[1][step])
            result.append(owner)
        return result

    def small_dtype(rows):
        return BF if rows % 16 == 0 else F32

    def in_quarters(rows):
        return rows % 64 == 0

    def turn_rows(values, turned_ref, sorted_ref, owner_list):
        block = values.shape[1] // n_dp
        turned_ref[...] = values.astype(F32).T.astype(turned_ref.dtype)
        for slot, owner in enumerate(owner_list):
            start = pl.multiple_of(owner * block, block)
            sorted_ref[slot * block : (slot + 1) * block] = turned_ref[pl.ds(start, block)]
        return sorted_ref[...].astype(BF)

    def turn_scratch(features, count):
        dtype = small_dtype(features // n_dp)
        return [pltpu.VMEM((features, count), dtype)] * 2

    def pack(keep_ref, send_ref, base, first, left_t, right):
        width = keep_ref.shape[2]
        section = lax.axis_index("pass")
        unit = width // n_dp
        block = left_t.shape[0] // n_dp
        quarter = first
        for col in range(right.shape[1] // width):
            grad = nn(left_t, right[:, col * width : (col + 1) * width]).astype(keep_ref.dtype)
            for piece in range(block // unit):
                place = pl.ds(pl.multiple_of(base + (quarter ^ section) * unit, unit), unit)
                for slot in range(n_dp):
                    ref, index = (keep_ref, slot) if slot < n_half else (send_ref, slot - n_half)
                    start = slot * block + piece * unit
                    ref[index, place] = grad[start : start + unit]
                quarter += 1
        return quarter


    def self_kernel(
        x, gain, shift, w_qkv, seg, w_out, w_query, w_next, first, query, held, first_far, query_far, qkv, probs, ctx,
        bias, sem,
    ):
        copy = pltpu.make_async_copy(w_next, held, sem)
        copy.start()
        width = x.shape[1]
        gains, shifts = gain[...].astype(F32), shift[...].astype(F32)
        rows = x[...].astype(F32)
        unit, _ = norm_parts(rows)
        qkv[...] = nn(norm_out(unit, gains, shifts, 0), w_qkv[...]).astype(BF)
        seg_row = seg[...].astype(F32)
        bias[...] = jnp.where(column(seg_row, seg_row.shape[1]) == seg_row, 0.0, -1000000000.0)
        attend(
            tile_of(qkv, 0), tile_of(qkv, width), tile_of(qkv, 2 * width), bias, probs, ctx, (width // HEADS) ** -0.5
        )
        for ref in (qkv, probs, ctx):
            ref.send()
        added = rows + nn(ctx[...], w_out[...])
        first[...] = added
        first_far[...] = added
        first_far.send()
        unit, _ = norm_parts(added)
        value = nn(norm_out(unit, gains, shifts, 1), w_query[...]).astype(BF)
        query[...] = value
        query_far[...] = value
        copy.wait()

    def cross_kernel(
        first, query, w_kv, seg, part0, part1, part2, part3, w_out, gain, shift, w_in, w_ffn, labels, mask,
        second, keyval, probs, ctx, hidden, slope, third, layer, final, bias,
    ):
        width = first.shape[1]
        count = first.shape[0]
        seg_row = seg[...].astype(F32)
        size = part0.shape[0] - EXTRA
        for index, part in enumerate((part0, part1, part2, part3)):
            span = slice(index * size, (index + 1) * size)
            keyval[span] = nn(part[:size], w_kv[...]).astype(BF)
            source_seg = part[size : size + EXTRA, :size].astype(F32)[0:1]
            bias[span] = jnp.where(column(source_seg, count) == seg_row, 0.0, -1000000000.0)
        keyval.send()
        attend(
            tile_of(query, 0), tile_of(keyval, 0), tile_of(keyval, width), bias, probs, ctx, (width // HEADS) ** -0.5,
            lambda tile: probs.send_part(pl.ds(2 * tile, 2)),
        )
        ctx.send()
        added = first[...] + nn(ctx[...], w_out[...])
        second[...] = added
        second.send()
        gains, shifts = gain[...].astype(F32), shift[...].astype(F32)
        unit, _ = norm_parts(added)
        normed = norm_out(unit, gains, shifts, 2)
        for col in range(w_in.shape[1] // width):
            span = slice(col * width, (col + 1) * width)
            inner = nn(normed, w_in[:, span])
            cdf = 0.5 * (1.0 + lax.erf(inner * 0.7071067811865476))
            hidden[:, span] = (inner * cdf).astype(BF)
            hidden.send_part((slice(None), span))
            slope[:, span] = (cdf + inner * jnp.exp(-0.5 * inner * inner) * 0.3989422804014327).astype(BF)
            slope.send_part((slice(None), span))
        added = added + nn(hidden[...], w_ffn[...])
        third[...] = added
        layer[...] = added.astype(BF)
        third.send()
        layer.send()
        unit, _ = norm_parts(added)
        normed = norm_out(unit, gains, shifts, 3)
        final[:count] = normed
        label = labels[...]
        line = lax.broadcasted_iota(jnp.int32, (EXTRA, count), 0)
        high = lax.shift_right_logical(label, 8).astype(F32)
        marks = jnp.where(line == 0, high, 0.0)
        marks = jnp.where(line == 1, (label & 255).astype(F32), marks)
        marks = jnp.where(line == 2, mask[...].astype(F32), marks)
        final[count:] = jnp.concatenate([marks, jnp.zeros((EXTRA, width - count), F32)], axis=1).astype(BF)

    def head_kernel(
        final, seg, labels, mask, w_delete, w_insert,
        dfinal, keep, send, d_delete, loss, turned, ordered,
    ):
        section = lax.axis_index("pass")
        count = seg.shape[1]
        width = final.shape[1]
        h = final[:count]
        h32 = h.astype(F32)
        seg_col = column(seg[...].astype(F32), LANES)
        row_id = lax.broadcasted_iota(jnp.int32, (count, LANES), 0)
        linked = (pltpu.roll(seg_col, count - 1, 0) == seg_col) & (row_id < count - 1)
        linked = jnp.concatenate([linked.astype(F32)] * (width // LANES), axis=1)
        after = (pltpu.roll(h32, count - 1, 0) * linked).astype(BF)
        weight = column(mask[...].astype(F32), LANES)

        def entropy(logits, label, live):
            top = jnp.max(logits, axis=-1, keepdims=True)
            expo = jnp.exp(logits - top)
            total = jnp.sum(expo, axis=-1, keepdims=True)
            lane = lax.broadcasted_iota(jnp.int32, logits.shape, 1)
            target = column(label.astype(F32), logits.shape[1])
            hit = lane.astype(F32) == target
            picked = jnp.sum(jnp.where(hit, logits, 0.0), axis=1, keepdims=True)
            w = weight[:, :1] * live
            rest = jnp.sum(jnp.where(hit, 0.0, expo), axis=1, keepdims=True)
            grad = jnp.where(hit, -rest, expo) * (w / total)
            return jnp.sum(w * (top + jnp.log(total) - picked)), grad.astype(BF)

        label = labels[...]
        spot = lax.broadcasted_iota(jnp.int32, (LANES, width), 0)
        two = w_delete[...].astype(F32)
        both_rows = jnp.where(spot == 0, two[0:1], jnp.where(spot == 1, two[1:2], 0.0)).astype(BF)
        logits = nt(h, both_rows)
        lane = lax.broadcasted_iota(jnp.int32, logits.shape, 1)
        logits = jnp.where(lane < 2, logits, -1e30)
        loss_d, grad_d = entropy(logits, lax.rem(label, 2), (section == 0).astype(F32))
        logits = nn(h, w_insert[:width]) + nn(after, w_insert[width:])
        loss_i, grad_i = entropy(logits, lax.rem(label, INS), (section == 1).astype(F32))
        loss[...] = jnp.full(loss.shape, loss_d + loss_i)
        d_after = nt(grad_i, w_insert[width:]) * linked
        dfinal[...] = nn(grad_d, both_rows) + nt(grad_i, w_insert[:width]) + pltpu.roll(d_after, 1, 0)
        d_delete[...] = nn(flip(grad_d)[:EXTRA], h)[: d_delete.shape[0]]
        both_t = turn_rows(jnp.concatenate([h, after], axis=1), turned, ordered, owners())
        grad = nn(both_t, grad_i).astype(keep.dtype)
        block = both_t.shape[0] // n_dp
        half = block // 2
        for slot in range(n_dp):
            ref, index = (keep, slot) if slot < n_half else (send, slot - n_half)
            ref[index, :, :INS] = grad[slot * block : slot * block + half]
            ref[index, :, INS:] = grad[slot * block + half : (slot + 1) * block]


    def shard_base(chunk, shard):
        section, me = lax.axis_index("pass"), lax.axis_index("dp")
        return ((section ^ (chunk >> 1)) * n_dp + (me ^ (chunk & 1))) * shard

    def hits(base, start, shape, label):
        ids = lax.broadcasted_iota(jnp.int32, shape, 0) + (base + start)
        return ids == label

    def slots_of(refs):
        return [(ref, (i, half)) for half in range(2) for ref in refs for i in range(ref.shape[0])]

    def logit_kernel(n_prev, turn, n_tokens, spots, *refs):
        slots = [slots_of(refs[:n_tokens])[i] for i in spots]
        vocab, refs = refs[n_tokens : n_tokens + 4], refs[n_tokens + 4 :]
        if n_prev:
            prev, refs = refs[0], refs[1:]
        n = len(slots) // 2
        stats, expos = refs[0], refs[1 : 1 + n]
        turned = refs[1 + n] if turn else None
        h, logits = refs[-2:]
        size = (slots[0][0].shape[1] - EXTRA) // 2
        count = 2 * size
        shard = vocab[0].shape[0]
        if n_prev:
            stats[:, : n_prev * count] = prev[...]
        for tile in range(n):
            both = slots[2 * tile : 2 * tile + 2]
            for index, (ref, (i, half)) in enumerate(both):
                h[index * size : (index + 1) * size] = ref[i, half * size : (half + 1) * size]
            marks = jnp.concatenate(
                [ref[i, count:, half * size : (half + 1) * size].astype(F32) for ref, (i, half) in both], axis=1
            )
            label_f = marks[0:1] * 256.0 + marks[1:2]
            label = label_f.astype(jnp.int32)
            weight = marks[2:3]
            peak = jnp.full((8, count), -jnp.inf, F32)
            for chunk, ref in enumerate(vocab):
                for start in range(0, shard, 1024):
                    step = min(1024, shard - start)
                    value = nt(ref[start : start + step], h[...])
                    at = chunk * shard + start
                    logits[at : at + step] = value
                    peak = jnp.maximum(peak, jnp.max(value.reshape(step // 8, 8, count), axis=0))
                if turn and not tile:
                    turned[:, chunk * shard : (chunk + 1) * shard] = flip(ref[...])
            peak = jnp.max(peak, axis=0, keepdims=True)
            total = jnp.zeros((8, count), F32)
            chosen = jnp.zeros((8, count), F32)
            sub = min(shard, 128)
            expo = expos[tile]
            for chunk in range(4):
                base = shard_base(chunk, shard)

                def part(i, carry, chunk=chunk, base=base, expo=expo, peak=peak, label=label):
                    total, chosen = carry
                    at = pl.multiple_of(chunk * shard + i * sub, sub)
                    value = logits[pl.ds(at, sub)]
                    hit = hits(base, i * sub, (sub, count), label)
                    weight_of = jnp.where(hit, 0.0, jnp.exp(value - peak))
                    expo[pl.ds(at, sub)] = weight_of.astype(BF)
                    total = total + jnp.sum(weight_of.reshape(sub // 8, 8, count), axis=0)
                    picked = jnp.where(hit, value, 0.0)
                    return total, chosen + jnp.sum(picked.reshape(sub // 8, 8, count), axis=0)

                total, chosen = lax.fori_loop(0, shard // sub, part, (total, chosen), unroll=True)
            total = jnp.sum(total, axis=0, keepdims=True)
            chosen = jnp.sum(chosen, axis=0, keepdims=True)
            line = lax.broadcasted_iota(jnp.int32, (8, count), 0)
            block = jnp.zeros((8, count), F32)
            for at, value in enumerate((peak, total, chosen, label_f, weight)):
                block = jnp.where(line == at, value, block)
            at = (n_prev + tile) * count
            stats[:, at : at + count] = block

    def logit_call(tokens, vocab, prev, turn, spots):
        height, width = tokens[0].shape[1:]
        count = height - EXTRA
        n = len(spots) // 2
        shard = vocab[0].shape[0]
        n_prev = prev[0].shape[1] // count if prev else 0
        outs = [like((8, (n_prev + n) * count), F32)] + [like((4 * shard, count), BF)] * n
        stats, *rest = run(
            functools.partial(logit_kernel, n_prev, turn, len(tokens), spots),
            outs + ([like((width, 4 * shard), BF)] if turn else []),
            [*tokens, *vocab, *prev],
            2.8 * n,
            12,
            [pltpu.VMEM((count, width), BF), pltpu.VMEM((4 * shard, count), F32)],
            "token_logits",
        )
        return stats, rest[:n], rest[n:]

    def merged(own, other):
        peak = jnp.maximum(own[0:1], other[0:1])
        total = own[1:2] * jnp.exp(own[0:1] - peak) + other[1:2] * jnp.exp(other[0:1] - peak)
        return peak, total, own[2:3] + other[2:3]

    def merge_kernel(step, order, own, other, out):
        size = own.shape[1] // len(order)
        blocks = [other[:, i * size : (i + 1) * size] for i in range(len(order))]
        bit = len(order) >> (step + 2)
        swapped = jnp.concatenate([blocks[order.index((half, slot ^ bit))] for half, slot in order], axis=1)
        mine = own[...]
        peak, total, chosen = merged(mine, swapped)
        line = lax.broadcasted_iota(jnp.int32, mine.shape, 0)
        out[...] = jnp.where(
            line == 0, peak, jnp.where(line == 1, total, jnp.where(line == 2, chosen, mine))
        )

    def merge_all_kernel(order, own, near, next_, far, out):
        size = own.shape[1] // len(order)
        result = None
        for ref, bit in ((own, 0), (near, 1), (next_, 2), (far, 3)):
            blocks = [ref[:, i * size : (i + 1) * size] for i in range(len(order))]
            mine = jnp.concatenate([blocks[order.index((half, slot ^ bit))] for half, slot in order], axis=1)
            result = (mine[0:1], mine[1:2], mine[2:3]) if result is None else merged(jnp.concatenate(result, axis=0), mine)
        line = lax.broadcasted_iota(jnp.int32, own.shape, 0)
        peak, total, chosen = result
        out[...] = jnp.where(
            line == 0, peak, jnp.where(line == 1, total, jnp.where(line == 2, chosen, own[...]))
        )

    def closing(local, merged_ref, other):
        peak, total, chosen = merged(merged_ref, other)
        hit = jnp.exp(chosen - peak)
        full = total + hit
        lse = peak + jnp.log(full)
        weight = local[4:5]
        factor = weight * jnp.exp(local[0:1] - lse)
        return lse, chosen, factor, -weight * (total / full)

    def dlogits_into(ref, at, cols, expo, start, base, shape, label, factor, at_label):
        sub = min(shape[0], 128)

        def part(i, _):
            row = pl.multiple_of(i * sub, sub)
            hit = hits(base, i * sub, (sub, shape[1]), label)
            value = expo[pl.ds(pl.multiple_of(start + row, sub), sub)].astype(F32) * factor
            ref[pl.ds(pl.multiple_of(at + row, sub), sub), cols] = jnp.where(hit, at_label, value).astype(BF)
            return 0

        lax.fori_loop(0, shape[0] // sub, part, 0, unroll=True)

    def dtoken_kernel(tile, expo, vocab_t, local, merged_ref, other, out, dlogits):
        rows, count = expo.shape
        shard = rows // 4
        span = slice(tile * count, (tile + 1) * count)
        _, _, factor, at_label = closing(local[:, span], merged_ref[:, span], other[:, span])
        label = local[3:4, span].astype(jnp.int32)
        for chunk in range(4):
            dlogits_into(
                dlogits, chunk * shard, slice(None), expo, chunk * shard, shard_base(chunk, shard),
                (shard, count), label, factor, at_label,
            )
        total = nn(vocab_t[...], dlogits[...]).T.astype(out.dtype)
        out[0] = total[: count // 2]
        out[1] = total[count // 2 :]

    def dtoken_call(expo, tile, local, merged_ref, other, vocab_t, dtype):
        rows, count = expo.shape
        return run(
            functools.partial(dtoken_kernel, tile),
            [like((2, count // 2, vocab_t.shape[0]), dtype)],
            [expo, vocab_t, local, merged_ref, other],
            2.2,
            8,
            [pltpu.VMEM((rows, count), BF)],
            "token_dfinal",
        )[0]

    def dvocab_kernel(shard, parity, n_tiles, *refs):
        expos, tokens = refs[:n_tiles], refs[n_tiles:-6]
        local, merged_ref, other, out, dlogits, held = refs[-6:]
        index = pl.program_id(0)
        _, _, factor, at_label = closing(local[...], merged_ref[...], other[...])
        label = local[3:4].astype(jnp.int32)
        size = (tokens[0].shape[1] - EXTRA) // 2
        count = 2 * size
        section, me = lax.axis_index("pass"), lax.axis_index("dp")
        chunk = 2 * index + parity
        base = ((section ^ (chunk >> 1)) * n_dp + (me ^ (chunk & 1))) * shard
        slots = slots_of(tokens[:2]) + [slot for token in tokens[2:] for slot in slots_of([token])]
        for at, (token, (i, half)) in enumerate(slots):
            held[at * size : (at + 1) * size] = token[i, half * size : (half + 1) * size]
        for at, expo in enumerate(expos):
            cols = slice(at * count, (at + 1) * count)
            dlogits_into(
                dlogits, 0, cols, expo, 0, base, (shard, count), label[:, cols], factor[:, cols], at_label[:, cols]
            )
        out[...] = nn(dlogits[...], held[...]).astype(out.dtype)

    def dvocab_call(expos, tokens, local, merged_ref, other, parity, dtype):
        shard, count = expos[0].shape[0] // 4, expos[0].shape[1]
        width = tokens[0].shape[2]
        total = local.shape[1]
        fixed2 = pl.BlockSpec(local.shape, lambda c: (0, 0))
        return pl.pallas_call(
            functools.partial(dvocab_kernel, shard, parity, len(expos)),
            grid=(2,),
            in_specs=[pl.BlockSpec((shard, count), lambda c: (2 * c + parity, 0))] * len(expos)
            + [pl.BlockSpec(t.shape, lambda c: (0, 0, 0)) for t in tokens]
            + [fixed2] * 3,
            out_specs=pl.BlockSpec((shard, width), lambda c: (c, 0)),
            out_shape=like((2 * shard, width), dtype),
            scratch_shapes=[pltpu.VMEM((shard, total), BF), pltpu.VMEM((total, width), BF)],
            compiler_params=pltpu.CompilerParams(vmem_limit_bytes=20 * MIB),
            cost_estimate=cost(0.1),
            name="token_dvocab",
        )(*expos, *tokens, local, merged_ref, other)


    def ffn_back_kernel(
        hidden, third, gain, w_ffn, slope, second, shift, w_in,
        kept0, kept1, moved0, moved1, dhead, head_loss, local, merged_ref, other, ins_keep, ins_send,
        dsecond, keep, send, vecs, loss, wide_t, wide_s, thin_t, thin_s, dinner,
    ):
        width = third.shape[1]
        count = third.shape[0]
        live = (lax.axis_index("pass") >= 2).astype(F32)
        hidden_t = turn_rows(hidden[...], wide_t, wide_s, owners())
        parts = [kept[...] + moved[...].astype(F32) for kept, moved in ((kept0, moved0), (kept1, moved1))]
        dfinal = dhead[...] + live * jnp.concatenate(parts, axis=0)
        unit3, rstd3 = norm_parts(third[...])
        gains = gain[...].astype(F32)
        dthird, g_gain3, g_bias3 = norm_bwd(dfinal, unit3, rstd3, gains[3:4])
        low = dthird.astype(BF)
        pack(keep, send, 0, 0, hidden_t, low)
        for col in range(w_ffn.shape[0] // width):
            span = slice(col * width, (col + 1) * width)
            part = nt(low, w_ffn[span]).astype(BF).astype(F32) * slope[:, span].astype(F32)
            dinner[:, span] = part.astype(BF)
        unit2, rstd2 = norm_parts(second[...])
        normed_t = turn_rows(norm_out(unit2, gains, shift[...].astype(F32), 2), thin_t, thin_s, owners())
        pack(keep, send, 4 * (width // n_dp), 0, normed_t, dinner[...])
        extra = ins_keep.shape[1]
        base, section = keep.shape[1] - extra, lax.axis_index("pass")
        if in_quarters(extra):
            size = extra // 4
            for quarter in range(4):
                span = slice(quarter * size, (quarter + 1) * size)
                place = pl.ds(pl.multiple_of(base + (quarter ^ section) * size, size), size)
                keep[:, place] = ins_keep[:, span]
                send[:, place] = ins_send[:, span]
        else:
            keep[:, base:] = ins_keep[...]
            send[:, base:] = ins_send[...]
        dnormed = nt(dinner[...], w_in[...])
        back, g_gain2, g_bias2 = norm_bwd(dnormed, unit2, rstd2, gains[2:3])
        dsecond[...] = dthird + back
        token_loss = 0.0
        for start in (0, count):
            span = slice(start, start + count // 2)
            lse, chosen, _, _ = closing(local[:, span], merged_ref[:, span], other[:, span])
            token_loss = token_loss + jnp.sum(local[4:5, span] * (lse - chosen))
        loss[...] = head_loss[...] + token_loss * live
        line = lax.broadcasted_iota(jnp.int32, (8, width), 0)
        block = jnp.zeros((8, width), F32)
        for at, value in enumerate((g_gain3, g_gain2, g_bias3, g_bias2)):
            block = jnp.where(line == at, value, block)
        vecs[...] = block

    def cross_back_kernel(
        dsecond, w_out, ctx, keyval, probs, query, part0, part1, part2, part3, w_kv, first, gain, shift, w_query,
        dfirst, keep, send, vecs, dsrc0, dsrc2, dsrc13, thin_t, thin_s, src_t, src_s, dquery, dkeyval, dctx,
    ):
        width = first.shape[1]
        owner_list = owners()
        low = dsecond[...].astype(BF)
        dctx[...] = nt(low, w_out[...]).astype(BF)
        at = pack(keep, send, 0, 0, turn_rows(ctx[...], thin_t, thin_s, owner_list), low)
        attend_bwd(
            tile_of(dctx, 0), tile_of(query, 0), tile_of(keyval, 0), tile_of(keyval, width), probs,
            put_in(dquery, 0), put_in(dkeyval, 0), put_in(dkeyval, width), (width // HEADS) ** -0.5, width // LANES,
        )
        size = part0.shape[0] - EXTRA
        source = jnp.concatenate([p[:size] for p in (part0, part1, part2, part3)], axis=0)
        at = pack(keep, send, 0, at, turn_rows(source, src_t, src_s, owner_list), dkeyval[...])
        for index, (ref, row) in enumerate(((dsrc0, 0), (dsrc13, 0), (dsrc2, 0), (dsrc13, size))):
            part = nt(dkeyval[index * size : (index + 1) * size], w_kv[...])
            ref[row : row + size] = part.astype(ref.dtype)
        gains, shifts = gain[...].astype(F32), shift[...].astype(F32)
        unit, rstd = norm_parts(first[...])
        normed_t = turn_rows(norm_out(unit, gains, shifts, 1), thin_t, thin_s, owner_list)
        pack(keep, send, 0, at, normed_t, dquery[...])
        back, g_gain, g_bias = norm_bwd(nt(dquery[...], w_query[...]), unit, rstd, gains[1:2])
        dfirst[...] = dsecond[...] + back
        line = lax.broadcasted_iota(jnp.int32, (8, width), 0)
        vecs[...] = jnp.where(line == 0, g_gain, jnp.where(line == 1, g_bias, 0.0))

    def self_back_kernel(
        dfirst, w_out, ctx, qkv, probs, x, gain, shift, w_qkv, vec_ffn, vec_cross, d_delete,
        dx, keep, send, thin_t, thin_s, dqkv, dctx,
    ):
        width = x.shape[1]
        owner_list = owners()
        low = dfirst[...].astype(BF)
        dctx[...] = nt(low, w_out[...]).astype(BF)
        at = pack(keep, send, 0, 0, turn_rows(ctx[...], thin_t, thin_s, owner_list), low)
        attend_bwd(
            tile_of(dctx, 0), tile_of(qkv, 0), tile_of(qkv, width), tile_of(qkv, 2 * width), probs,
            put_in(dqkv, 0), put_in(dqkv, width), put_in(dqkv, 2 * width), (width // HEADS) ** -0.5, width // LANES,
        )
        gains, shifts = gain[...].astype(F32), shift[...].astype(F32)
        unit, rstd = norm_parts(x[...].astype(F32))
        normed_t = turn_rows(norm_out(unit, gains, shifts, 0), thin_t, thin_s, owner_list)
        at = pack(keep, send, 0, at, normed_t, dqkv[...])
        back, g_gain, g_bias = norm_bwd(nt(dqkv[...], w_qkv[...]), unit, rstd, gains[0:1])
        dx[...] = dfirst[...] + back
        line = lax.broadcasted_iota(jnp.int32, (EXTRA, width), 0)
        block = jnp.zeros((EXTRA, width), F32)
        lines = (
            (0, d_delete[0:1]), (1, d_delete[1:2]),
            (8, g_gain), (9, vec_cross[0:1]), (10, vec_ffn[1:2]), (11, vec_ffn[0:1]),
            (12, g_bias), (13, vec_cross[1:2]), (14, vec_ffn[3:4]), (15, vec_ffn[2:3]),
        )
        for row, value in lines:
            block = jnp.where(line == row, value, block)
        block = block.astype(keep.dtype)
        at = at * (width // n_dp)
        for slot in range(n_half):
            keep[slot, at:] = block
            send[slot, at:] = block


    def add_kernel(pairs, *refs):
        ins, outs = refs[: 2 * pairs], refs[2 * pairs :]
        at = 0
        for keep, got in zip(ins[::2], ins[1::2]):
            rows = keep.shape[1]
            slot = 0
            for ref in outs:
                for i in range(ref.shape[0]):
                    value = keep[slot].astype(F32) + got[slot].astype(F32)
                    ref[i, at : at + rows] = value.astype(ref.dtype)
                    slot += 1
            at += rows

    def add_call(blocks, *counts):
        rows, width = sum(b.shape[1] for b in blocks[::2]), blocks[0].shape[2]
        outs = [like((count, rows, width), wire_of(width)) for count in counts]
        return run(functools.partial(add_kernel, len(blocks) // 2), outs, blocks, 0.8, 8, name="sum_slots")

    def wire_of(width):
        return small_dtype(width // n_dp)

    def regroup_kernel(plan, n_terms, *refs):
        value = refs[0][...].astype(F32)
        for ref in refs[1:n_terms]:
            value = value + ref[...].astype(F32)
        for spans, ref in zip(plan, refs[n_terms:]):
            at = 0
            for start, stop in spans:
                ref[at : at + stop - start] = value[start:stop].astype(ref.dtype)
                at += stop - start

    def pair_kernel(plan, n_terms, *refs):
        first = refs[0][...].astype(F32) + refs[1][...].astype(F32)
        value = first + (refs[2][...].astype(F32) + refs[3][...].astype(F32))
        for spans, ref in zip(plan, refs[n_terms:]):
            at = 0
            for start, stop in spans:
                ref[at : at + stop - start] = value[start:stop].astype(ref.dtype)
                at += stop - start

    def regroup(terms, plan, kernel=regroup_kernel, name="sum_rows"):
        width = terms[0].shape[-1]
        outs = [like((sum(b - a for a, b in spans), width), wire_of(width)) for spans in plan]
        terms = [t.reshape(t.shape[-2:]) for t in terms]
        return run(functools.partial(kernel, plan, len(terms)), outs, terms, 0.7, 8, name=name)

    def picked(pieces):
        section = lax.axis_index("pass")
        values = [p.astype(F32) for p in pieces]
        result = []
        for j in range(4):
            value = values[0]
            for b in (1, 2, 3):
                value = jnp.where((section ^ b) == j, values[b], value)
            result.append(value)
        return result

    def halves(refs):
        rows = refs[0].shape[0] // 2
        return [r[:rows] for r in refs], [r[rows:] for r in refs]

    def ffn_end_kernel(own, near, third, far, *rest):
        extra, (p_out, p_in, p_insert) = rest[:-3], rest[-3:]
        refs = (own, near, third, far)
        rows, width = p_in.shape[0], own.shape[1]
        for j, value in enumerate(picked([r[:rows] for r in refs])):
            p_out[j * rows : (j + 1) * rows] = value
        for j, value in enumerate(picked([r[rows : 2 * rows] for r in refs])):
            p_in[:, j * width : (j + 1) * width] = value
        half = p_insert.shape[0] // 2
        if extra:
            values = [extra[0][...].astype(F32)]
        else:
            values = picked([r[2 * rows :] for r in refs])
        size = half // len(values)
        for j, value in enumerate(values):
            p_insert[j * size : (j + 1) * size] = value[:, :INS]
            p_insert[half + j * size : half + (j + 1) * size] = value[:, INS:]

    def attention_end_kernel(
        own, near, third, far, extra, p_cross, p_kv, p_query, p_out, p_qkv, p_gain, p_bias, p_delete
    ):
        cross, own_part = halves((own, near, third, far))
        width = extra.shape[1]
        values = picked(cross)
        p_cross[...] = values[0]
        p_kv[:, :width] = values[1]
        p_kv[:, width:] = values[2]
        p_query[...] = values[3]
        values = picked(own_part)
        p_out[...] = values[0]
        for j in range(3):
            p_qkv[:, j * width : (j + 1) * width] = values[j + 1]
        size = p_gain.shape[1]
        me = lax.axis_index("dp")
        mine = pltpu.roll(extra[...].astype(F32), lax.rem(width - me * size, width), 1)
        p_gain[...] = mine[8:12, :size]
        p_bias[...] = mine[12:16, :size]
        p_delete[...] = mine[:2, :size]

    def body(
        decoder_in,
        decoder_segments,
        edit_target,
        loss_mask,
        source_out,
        source_segments,
        norm_gain,
        norm_bias,
        self_qkv,
        self_out,
        cross_query,
        cross_kv,
        cross_out,
        ffn_in,
        ffn_out,
        delete_head,
        insert_head,
        token_head,
    ):
        section = lax.axis_index("pass")
        segs, labels, mask = decoder_segments[0], edit_target[0], loss_mask[0]
        rows = decoder_in[0, 0]
        count, width = rows.shape
        shard = token_head.shape[0]
        part = source_out.shape[1]
        src = n_pass * part
        hid = ffn_in.shape[1]
        unit = width // n_dp
        wire = small_dtype(unit)

        note = jnp.pad(source_segments.astype(BF), ((0, EXTRA - 1), (0, width - part)))
        mine = jnp.concatenate([source_out[0], note], axis=0)
        parts = [mine] + [swap_pass(mine, bit) for bit in (1, 2, 3)]

        gain, shift = Far(norm_gain), Far(norm_bias)
        first, query, w_kv, first_far, query_far, qkv, probs1, ctx1 = run(
            self_kernel,
            [
                like((count, width), F32),
                like((count, width), BF),
                like(cross_kv.shape, BF),
                Far(like((count, width), F32)),
                Far(like((count, width), BF)),
                Far(like((count, 3 * width), BF)),
                Far(like((HEADS, count, count), BF)),
                Far(like((count, width), BF)),
            ],
            [Far(rows), gain, shift, Far(self_qkv), Far(segs), Far(self_out), Far(cross_query), Raw(cross_kv)],
            4.2,
            10,
            [pltpu.VMEM((count, count), F32), pltpu.SemaphoreType.DMA],
            "self_forward",
        )
        second, keyval, probs2, ctx2, hidden, slope, third, layer, final = run(
            cross_kernel,
            [
                Far(like((count, width), F32)),
                Far(like((src, 2 * width), BF)),
                Far(like((HEADS, src, count), BF)),
                Far(like((count, width), BF)),
                Far(like((count, hid), BF)),
                Far(like((count, hid), BF)),
                Far(like((count, width), F32)),
                Far(like((count, width), BF)),
                like((count + EXTRA, width), BF),
            ],
            [first, query, w_kv, Far(segs), *parts, Pin(cross_out), gain, shift]
            + [Pin(ffn_in), Pin(ffn_out), Far(labels), Far(mask)],
            7.6,
            20,
            [pltpu.VMEM((src, count), F32)],
            "cross_forward",
        )

        near = swap_pass(after(token_head, parts[1]), 1)
        moved = lax.ppermute(final, "pass", [(2, 0), (3, 1)])

        ins_rows = 2 * width // n_dp // 2
        dhead, ins_keep, ins_send, d_delete, head_loss = run(
            head_kernel,
            [
                like((count, width), F32),
                like((n_half, ins_rows, 2 * INS), wire),
                like((n_half, ins_rows, 2 * INS), wire),
                like((8, width), F32),
                like((8, LANES), F32),
            ],
            [final, Far(segs), Far(labels), Far(mask), Far(delete_head.T), Pin(insert_head)],
            1.4,
            10,
            turn_scratch(2 * width, count),
            "small_heads",
        )
        moved = after(moved, dhead)
        group = jnp.where(section >= 2, final, moved)[None]
        tokens = [group]
        for step in reversed(range(n_steps)):
            tokens.append(swap_chip(group, step))
            if step:
                group = jnp.concatenate([group, tokens[-1]], axis=0)
        near = after(near, tokens[1])
        vocab = (token_head, swap_core(token_head), near, swap_core(near))
        expos, stats, vocab_t, order = [[], []], (), None, []
        for pieces in [tokens[:2]] + [[t] for t in tokens[2:]]:
            made = []
            for tile in range(sum(p.shape[0] for p in pieces)):
                stats, new, turned = logit_call(pieces, vocab, stats, not vocab_t, (2 * tile, 2 * tile + 1))
                stats = (stats,)
                vocab_t = vocab_t or turned
                made += new
            first_slot, n_slots = len(order) // 2, sum(p.shape[0] for p in pieces)
            for half in range(2):
                spot = half * len(made) // 2
                expos[half] += [(e, len(order) // 2 + i) for i, e in enumerate(made[spot : spot + len(made) // 2])]
                order += [(half, first_slot + i) for i in range(n_slots)]
        (vocab_t,) = vocab_t
        local = stats[0]
        whole = local
        if n_steps == 2:
            both = lax.ppermute(local, "dp", [(i, i ^ chip_bits[0] ^ chip_bits[1]) for i in range(n_dp)])
            (whole,) = run(
                functools.partial(merge_all_kernel, order), [like(local.shape, F32)],
                [local, swap_chip(local, 1), swap_chip(local, 0), both], 1.0, 8, name="stats_merge",
            )
        else:
            for step in range(n_steps):
                (whole,) = run(
                    functools.partial(merge_kernel, step, order), [like(local.shape, F32)],
                    [whole, swap_chip(whole, step)], 1.0, 8, name="stats_merge",
                )
        other = swap_pass(whole, 2)

        n_tiles = len(expos[0])
        made = [[None] * n_tiles for _ in expos]
        for tile in reversed(range(n_tiles)):
            for half in range(2):
                dtype = BF if tile >= n_tiles // 2 and n_tiles > 1 else F32
                expo, spot = expos[half][tile]
                made[half][tile] = dtoken_call(expo, spot, local, whole, other, vocab_t, dtype)
        kept = []
        for half in range(2):
            tiles = made[half]
            for step in range(n_steps):
                if len(tiles) > 1:
                    middle = len(tiles) // 2
                    sending = tiles[middle:]
                    sending = jnp.concatenate(sending, axis=0) if len(sending) > 1 else sending[0]
                    got = swap_chip(sending.astype(BF), step)
                    tiles = [t + got[2 * i : 2 * i + 2].astype(F32) for i, t in enumerate(tiles[:middle])]
                else:
                    got = swap_chip(tiles[0][1].astype(BF), step)
                    kept.append(tiles[0][0] + got.astype(F32))
        backs = [lax.ppermute(k.astype(BF), "pass", [(0, 2), (1, 3)]) for k in kept]

        flat = [e for e, _ in sorted(sum(expos, []), key=lambda pair: pair[1])]
        dvocab_send = dvocab_call(flat, tokens, after(local, *kept), whole, other, 1, BF)
        dvocab_keep = dvocab_call(flat, tokens, after(local, dvocab_send), whole, other, 0, BF)
        backs = after_all(backs, dvocab_send, dvocab_keep)
        vocab_got = swap_core(after(dvocab_send, *backs))

        def packed(rows):
            return like((n_half, rows, width), wire)

        def sent(x):
            return x.astype(BF)

        def reduce_chips(blocks, step):
            while step < n_steps:
                half = n_half >> (step + 1)
                keep, send = add_call(blocks, half, half)
                blocks = [keep, swap_chip(sent(send), step)]
                step += 1
            return blocks

        rows_ffn = 8 * unit + ins_rows
        dsecond, keep_ffn, send_ffn, vec_ffn, loss = run(
            ffn_back_kernel,
            [like((count, width), F32), packed(rows_ffn), packed(rows_ffn), like((8, width), F32), like((8, LANES), F32)],
            [Pin(hidden), Pin(third), gain, Pin(ffn_out), Pin(slope), Pin(second), shift, Pin(ffn_in)]
            + [*kept, *backs, dhead, head_loss, local, whole, other, ins_keep, ins_send],
            0.1,
            16,
            turn_scratch(hid, count) + turn_scratch(width, count) + [pltpu.VMEM((count, hid), BF)],
            "ffn_backward",
        )
        dsecond, keep_ffn, send_ffn, vec_ffn, loss = after_all(
            [dsecond, keep_ffn, send_ffn, vec_ffn, loss], vocab_got
        )
        vocab_keep = dvocab_keep[:shard].astype(F32) + vocab_got[:shard].astype(F32)
        vocab_send = (dvocab_keep[shard:].astype(F32) + vocab_got[shard:].astype(F32)).astype(BF)
        cuts = [shard * i // 64 for i in (0, 30, 42, 64)]
        vocab_parts = [vocab_send[a:b] for a, b in zip(cuts, cuts[1:])]
        vocab_parts[0] = swap_pass(vocab_parts[0], 1)
        keep_ffn, send_ffn = add_call([keep_ffn, swap_core(sent(send_ffn))], n_half // 2, n_half // 2)
        dsecond = after(dsecond, send_ffn)
        dfirst, *chunk_cross, vec_cross, src0, src2, src13 = run(
            cross_back_kernel,
            [
                like((count, width), F32),
                packed(4 * unit),
                packed(4 * unit),
                like((8, width), F32),
                like((part, width), F32),
                like((part, width), F32),
                like((2 * part, width), BF),
            ],
            [dsecond, Pin(cross_out), Pin(ctx2), Pin(keyval), Pin(probs2), Pin(query_far), *parts]
            + [Pin(cross_kv), Pin(first_far), gain, shift, Pin(cross_query)],
            0.1,
            15,
            turn_scratch(width, count)
            + turn_scratch(width, src)
            + [pltpu.VMEM((count, width), BF), pltpu.VMEM((src, 2 * width), BF), pltpu.VMEM((count, width), BF)],
            "cross_backward",
        )
        blocks_ffn = [keep_ffn, swap_chip(sent(send_ffn), 0)]
        dfirst, *chunk_cross, vec_cross, src0, src2, src13 = after_all(
            [dfirst, *chunk_cross, vec_cross, src0, src2, src13], vocab_parts[0]
        )
        vocab_parts[1] = swap_pass(after(vocab_parts[1], dfirst), 1)
        input_grad, *chunk_self = run(
            self_back_kernel,
            [Far(like((count, width), F32)), packed(4 * unit + EXTRA), packed(4 * unit + EXTRA)],
            [dfirst, Pin(self_out), Pin(ctx1), Pin(qkv), Pin(probs1), Pin(rows), gain, shift, Pin(self_qkv)]
            + [vec_ffn, vec_cross, d_delete],
            0.1,
            12,
            turn_scratch(width, count) + [pltpu.VMEM((count, 3 * width), BF), pltpu.VMEM((count, width), BF)],
            "self_backward",
        )
        def rows_at(*spots, extra=0, start=8):
            spans = [(i * unit, (i + 1) * unit) for i in spots]
            return spans + ([(start * unit, start * unit + extra)] if extra else [])

        input_grad, *chunk_self = after_all([input_grad, *chunk_self], blocks_ffn[1], vocab_parts[1])
        blocks_ffn = reduce_chips(blocks_ffn, 1)

        got_cross = swap_core(sent(chunk_cross[1]))
        keep_self, send_self = chunk_self
        send_self = after(send_self, got_cross)
        got_self = swap_core(sent(send_self))
        keep_att, send_att = add_call([chunk_cross[0], got_cross, keep_self, got_self], n_half // 2, n_half // 2)
        source_got = swap_pass(src13, 1)
        source_half = swap_pass((src2 + source_got[part:].astype(F32)).astype(BF), 2)
        source_grad = (src0 + source_got[:part].astype(F32)) + source_half.astype(F32)
        blocks_att = [keep_att, swap_chip(after(sent(send_att), blocks_ffn[1], source_got), 0)]

        split = in_quarters(ins_rows)
        size = ins_rows // 4

        def ffn_rows(places, count):
            spans = [(k * count * unit + p * unit, k * count * unit + (p + 1) * unit) for k in range(2) for p in places]
            base = 2 * count * unit
            if split:
                return spans + [(base + p * size, base + (p + 1) * size) for p in places]
            return spans + [(base, base + ins_rows)]

        keep, send = regroup(blocks_ffn, [ffn_rows((0, 2), 4), ffn_rows((1, 3), 4)])
        got = swap_pass(sent(send), 1)
        got = after(got, source_half)
        blocks_att[1] = after(blocks_att[1], got)
        blocks_att = reduce_chips(blocks_att, 1)
        keep, send = regroup([keep, got], [ffn_rows((0,), 2), ffn_rows((1,), 2)])
        got = swap_pass(sent(send), 2)
        vocab_parts[2] = swap_pass(after(vocab_parts[2], send), 1)
        token_grad = vocab_keep + jnp.concatenate(vocab_parts, axis=0).astype(F32)
        blocks_att[1] = after(blocks_att[1], got)
        pieces_by_place = regroup(blocks_att, [rows_at(i, 4 + i, extra=EXTRA) for i in range(4)])
        if split:
            (own,) = regroup([keep, got], [[(0, 2 * unit + size)]])
            ins_sum = []
        else:
            own, *ins_sum = regroup([keep, got], [rows_at(0, 1), rows_at(extra=ins_rows, start=2)])
        near, third_part = swap_pass(sent(own), 1), swap_pass(sent(own), 2)
        ffn_parts = [own, near, third_part, swap_pass(third_part, 1), *ins_sum]

        gots = [swap_pass(sent(pieces_by_place[b]), b) for b in (1, 2, 3)]
        own, extra_sum = regroup(
            [pieces_by_place[0], *gots], [rows_at(0, 1), rows_at(extra=EXTRA, start=2)], pair_kernel, "sum_pass"
        )
        attention_parts = [own] + [swap_pass(sent(own), b) for b in (1, 2, 3)] + [extra_sum]

        def out(*shape):
            return Far(like(shape, F32))

        p_out, p_in, p_insert = run(
            ffn_end_kernel, [out(hid // n_dp, width), out(unit, hid), out(2 * unit, INS)], ffn_parts, 1.0, 8,
            name="ffn_sums",
        )
        p_cross, p_kv, p_query, p_self, p_qkv, p_gain, p_bias, p_delete = run(
            attention_end_kernel,
            [out(unit, width), out(unit, 2 * width), out(unit, width), out(unit, width), out(unit, 3 * width)]
            + [out(4, unit), out(4, unit), out(2, unit)],
            attention_parts,
            1.0,
            8,
            name="attention_sums",
        )
        return (
            layer[None, None],
            loss[:1, :1],
            input_grad[None, None],
            source_grad[None],
            p_gain,
            p_bias,
            p_qkv,
            p_self,
            p_query,
            p_kv,
            p_cross,
            p_in,
            p_out,
            p_delete.T,
            p_insert,
            token_grad,
        )

    full = ("pass", "dp")
    rows_at, row_at = P("pass", "dp", None, None), P("pass", "dp", None)
    weight_at = P("dp", None)
    return jax.shard_map(
        body,
        mesh=mesh,
        in_specs=(rows_at, row_at, row_at, row_at, P("dp", "pass", None), P("dp", "pass"))
        + (P(),) * 11
        + (P(full, None),),
        out_specs=(rows_at, P("pass", "dp"), rows_at, P("dp", "pass", None), P(None, "dp"), P(None, "dp"))
        + (weight_at,) * 9
        + (P(full, None),),
        check_vma=False,
    )
```

```python
import functools

import jax
import jax.numpy as jnp
from jax import lax
from jax.experimental import pallas as pl
from jax.experimental.pallas import tpu as pltpu
from jax.sharding import PartitionSpec as P

HEADS = 8
INS = 256
EPS = 1e-05
LANES = 128
EXTRA = 16
BF = jnp.bfloat16
F32 = jnp.float32
MIB = 1 << 20


def cost(us):
    return pl.CostEstimate(flops=int(us * 0.3e9), bytes_accessed=1, transcendentals=0)


def dot(left, right, dims):
    return lax.dot_general(left, right, (dims, ((), ())), preferred_element_type=F32)


def nn(left, right):
    return dot(left, right, ((1,), (0,)))


def nt(left, right):
    return dot(left, right, ((1,), (1,)))


def flip(values):
    return values.astype(F32).T.astype(BF)


class Far:
    def __init__(self, value):
        self.value = value


class Raw(Far):
    pass


class Pin(Far):
    pass


class Fetched:
    def __init__(self, source, buffer, sem):
        self.buffer, self.shape, self.dtype = buffer, buffer.shape, buffer.dtype
        self.copy = pltpu.make_async_copy(source, buffer, sem)
        self.copy.start()
        self.waiting = True

    def wait(self):
        if self.waiting:
            self.copy.wait()
            self.waiting = False

    def __getitem__(self, index):
        self.wait()
        return self.buffer[index]


class Stored:
    def __init__(self, target, buffer, sem):
        self.buffer, self.shape, self.dtype = buffer, buffer.shape, buffer.dtype
        self.copy = pltpu.make_async_copy(buffer, target, sem)
        self.target, self.sem = target, sem
        self.sent = False

    def __getitem__(self, index):
        return self.buffer[index]

    def __setitem__(self, index, value):
        self.buffer[index] = value

    def send(self):
        self.copy.start()
        self.sent = True

    def send_part(self, index):
        pltpu.make_async_copy(self.buffer.at[index], self.target.at[index], self.sem).start()
        self.sent = True


def run(kernel, outs, ins, us, limit, scratch=(), name=None):
    far_in, far_out = [type(x) is Far for x in ins], [type(x) is Far for x in outs]
    marks_in, marks_out = [type(x) for x in ins], [type(x) for x in outs]
    ins = [x.value if isinstance(x, Far) else x for x in ins]
    outs = [x.value if isinstance(x, Far) else x for x in outs]
    buffers = [pltpu.VMEM(x.shape, x.dtype) for x, f in zip(ins + outs, far_in + far_out) if f]
    spaces = {Far: pltpu.HBM, Raw: pltpu.HBM, Pin: pltpu.VMEM}
    ins = [pltpu.with_memory_space_constraint(x, spaces[m]) if m in spaces else x for x, m in zip(ins, marks_in)]
    outs = [spaces[m](x.shape, x.dtype) if m in spaces else x for x, m in zip(outs, marks_out)]
    n_in, n_out = len(ins), len(outs)

    def wrapped(*refs):
        if buffers:
            sems = refs[-1]
            held = list(refs[-1 - len(buffers) : -1])
            rest = refs[n_in + n_out : len(refs) - 1 - len(buffers)]
        else:
            held, rest = [], refs[n_in + n_out :]
        given, made, count = [], [], 0
        for ref, far in zip(refs[:n_in], far_in):
            given.append(Fetched(ref, held[count], sems.at[count]) if far else ref)
            count += far
        for ref, far in zip(refs[n_in : n_in + n_out], far_out):
            made.append(Stored(ref, held[count], sems.at[count]) if far else ref)
            count += far
        kernel(*given, *made, *rest)
        for x in given:
            if isinstance(x, Fetched):
                x.wait()
        for x in made:
            if isinstance(x, Stored) and not x.sent:
                x.send()
        for x in made:
            if isinstance(x, Stored):
                x.copy.wait()

    def place(mark):
        return pl.BlockSpec(memory_space=spaces.get(mark, pltpu.VMEM))

    return pl.pallas_call(
        wrapped,
        out_shape=outs,
        in_specs=[place(m) for m in marks_in],
        out_specs=[place(m) for m in marks_out],
        scratch_shapes=list(scratch) + buffers + ([pltpu.SemaphoreType.DMA((len(buffers),))] if buffers else []),
        compiler_params=pltpu.CompilerParams(vmem_limit_bytes=limit * MIB),
        cost_estimate=cost(us),
        name=name,
    )(*ins)


def after(value, *done):
    return lax.optimization_barrier((value, *done))[0]


def after_all(values, *done):
    return list(lax.optimization_barrier((*values, *done))[: len(values)])


def like(shape, dtype):
    return jax.ShapeDtypeStruct(shape, dtype)


def norm_parts(values):
    center = values - jnp.mean(values, axis=-1, keepdims=True)
    rstd = lax.rsqrt(jnp.mean(center * center, axis=-1, keepdims=True) + EPS)
    return center * rstd, rstd


def norm_out(unit, gain, shift, index):
    return (unit * gain[index : index + 1] + shift[index : index + 1]).astype(BF)


def norm_bwd(grad, unit, rstd, gain):
    scaled = grad * gain
    back = rstd * (
        scaled
        - jnp.mean(scaled, axis=-1, keepdims=True)
        - unit * jnp.mean(scaled * unit, axis=-1, keepdims=True)
    )
    return back, jnp.sum(grad * unit, axis=0, keepdims=True), jnp.sum(grad, axis=0, keepdims=True)


def column(row, count):
    return jnp.broadcast_to(row, (count, row.shape[1])).T


def lane_half(values, half):
    lane = lax.broadcasted_iota(jnp.int32, values.shape, 1)
    picked = (lane >= LANES // 2) if half else (lane < LANES // 2)
    return jnp.where(picked, values, jnp.zeros_like(values))


def attend(query, keys, values, bias_ref, probs_ref, out_ref, scale, finished=None):
    half_size = LANES // 2
    for tile in range(out_ref.shape[1] // LANES):
        q = query(tile).astype(F32) * scale
        k, v_t = keys(tile), flip(values(tile))
        both = jnp.concatenate([lane_half(q, 0), lane_half(q, 1)], axis=0).astype(BF)
        count = q.shape[0]
        scores = nt(k, both)
        parts = []
        for half in range(2):
            mine = scores[:, half * count : (half + 1) * count] + bias_ref[...]
            expo = jnp.exp(mine - jnp.max(mine, axis=0, keepdims=True))
            probs = (expo * (1.0 / jnp.sum(expo, axis=0, keepdims=True))).astype(BF)
            probs_ref[2 * tile + half] = probs
            parts.append(nn(v_t[half * half_size : (half + 1) * half_size], probs))
        out_ref[:, tile * LANES : (tile + 1) * LANES] = jnp.concatenate(parts, axis=0).T.astype(BF)
        if finished:
            finished(tile)


def attend_bwd(grad, query, keys, values, probs_ref, put_query, put_keys, put_values, scale, tiles):
    half_size = LANES // 2
    for tile in range(tiles):
        g, q, k, v = grad(tile), query(tile), keys(tile), values(tile)
        k_t = flip(k)
        dq, dk, dv = [], [], []
        for half in range(2):
            probs = probs_ref[2 * tile + half]
            full = probs.astype(F32)
            dprobs = nt(v, lane_half(g, half))
            delta = jnp.sum(dprobs * full, axis=0, keepdims=True)
            dscores = (full * ((dprobs - delta) * scale)).astype(BF)
            dv.append(nn(probs, g))
            dk.append(nn(dscores, q))
            dq.append(nn(k_t[half * half_size : (half + 1) * half_size], dscores))
        lane = lax.broadcasted_iota(jnp.int32, dk[0].shape, 1) < half_size
        put_query(tile, jnp.concatenate(dq, axis=0).T.astype(BF))
        put_keys(tile, jnp.where(lane, dk[0], dk[1]).astype(BF))
        put_values(tile, jnp.where(lane, dv[0], dv[1]).astype(BF))


def tile_of(ref, start):
    return lambda tile: ref[:, start + tile * LANES : start + (tile + 1) * LANES]


def put_in(ref, start):
    def put(tile, value):
        ref[:, start + tile * LANES : start + (tile + 1) * LANES] = value

    return put


def solution(mesh):
    n_pass, n_dp = mesh.shape["pass"], mesh.shape["dp"]
    bits = [1 << i for i in range(n_dp.bit_length() - 1)]
    core_bit, chip_bits = bits[0], bits[1:]
    orders = (chip_bits, chip_bits[1::-1] + chip_bits[2:])
    n_steps = len(chip_bits)
    n_half = n_dp // 2

    def swap_core(x):
        return lax.ppermute(x, "dp", [(i, i ^ core_bit) for i in range(n_dp)])

    def swap_chip(x, step):
        return lax.ppermute(x, "dp", [(i, i ^ orders[i & 1][step]) for i in range(n_dp)])

    def swap_pass(x, bit):
        return lax.ppermute(x, "pass", [(i, i ^ bit) for i in range(n_pass)])

    def owners():
        me = lax.axis_index("dp")
        core = me & 1
        result = []
        for slot in range(n_dp):
            own_half = slot < n_half
            turn = core if own_half else 1 - core
            owner = me if own_half else me ^ 1
            for step in range(n_steps):
                if (slot >> (n_steps - 1 - step)) & 1:
                    owner = owner ^ jnp.where(turn == 0, orders[0][step], orders[1][step])
            result.append(owner)
        return result

    def small_dtype(rows):
        return BF if rows % 16 == 0 else F32

    def in_quarters(rows):
        return rows % 64 == 0

    def turn_rows(values, turned_ref, sorted_ref, owner_list):
        block = values.shape[1] // n_dp
        turned_ref[...] = values.astype(F32).T.astype(turned_ref.dtype)
        for slot, owner in enumerate(owner_list):
            start = pl.multiple_of(owner * block, block)
            sorted_ref[slot * block : (slot + 1) * block] = turned_ref[pl.ds(start, block)]
        return sorted_ref[...].astype(BF)

    def turn_scratch(features, count):
        dtype = small_dtype(features // n_dp)
        return [pltpu.VMEM((features, count), dtype)] * 2

    def pack(keep_ref, send_ref, base, first, left_t, right):
        width = keep_ref.shape[2]
        section = lax.axis_index("pass")
        unit = width // n_dp
        block = left_t.shape[0] // n_dp
        quarter = first
        for col in range(right.shape[1] // width):
            grad = nn(left_t, right[:, col * width : (col + 1) * width]).astype(keep_ref.dtype)
            for piece in range(block // unit):
                place = pl.ds(pl.multiple_of(base + (quarter ^ section) * unit, unit), unit)
                for slot in range(n_dp):
                    ref, index = (keep_ref, slot) if slot < n_half else (send_ref, slot - n_half)
                    start = slot * block + piece * unit
                    ref[index, place] = grad[start : start + unit]
                quarter += 1
        return quarter


    def self_kernel(
        x, gain, shift, w_qkv, seg, w_out, w_query, w_next, first, query, held, first_far, query_far, qkv, probs, ctx,
        bias, sem,
    ):
        copy = pltpu.make_async_copy(w_next, held, sem)
        copy.start()
        width = x.shape[1]
        gains, shifts = gain[...].astype(F32), shift[...].astype(F32)
        rows = x[...].astype(F32)
        unit, _ = norm_parts(rows)
        qkv[...] = nn(norm_out(unit, gains, shifts, 0), w_qkv[...]).astype(BF)
        seg_row = seg[...].astype(F32)
        bias[...] = jnp.where(column(seg_row, seg_row.shape[1]) == seg_row, 0.0, -1000000000.0)
        attend(
            tile_of(qkv, 0), tile_of(qkv, width), tile_of(qkv, 2 * width), bias, probs, ctx, (width // HEADS) ** -0.5
        )
        for ref in (qkv, probs, ctx):
            ref.send()
        added = rows + nn(ctx[...], w_out[...])
        first[...] = added
        first_far[...] = added
        first_far.send()
        unit, _ = norm_parts(added)
        value = nn(norm_out(unit, gains, shifts, 1), w_query[...]).astype(BF)
        query[...] = value
        query_far[...] = value
        copy.wait()

    def cross_kernel(
        first, query, w_kv, seg, part0, part1, part2, part3, w_out, gain, shift, w_in, w_ffn, labels, mask,
        second, keyval, probs, ctx, hidden, slope, third, layer, final, bias,
    ):
        width = first.shape[1]
        count = first.shape[0]
        seg_row = seg[...].astype(F32)
        size = part0.shape[0] - EXTRA
        for index, part in enumerate((part0, part1, part2, part3)):
            span = slice(index * size, (index + 1) * size)
            keyval[span] = nn(part[:size], w_kv[...]).astype(BF)
            source_seg = part[size : size + EXTRA, :size].astype(F32)[0:1]
            bias[span] = jnp.where(column(source_seg, count) == seg_row, 0.0, -1000000000.0)
        keyval.send()
        attend(
            tile_of(query, 0), tile_of(keyval, 0), tile_of(keyval, width), bias, probs, ctx, (width // HEADS) ** -0.5,
            lambda tile: probs.send_part(pl.ds(2 * tile, 2)),
        )
        ctx.send()
        added = first[...] + nn(ctx[...], w_out[...])
        second[...] = added
        second.send()
        gains, shifts = gain[...].astype(F32), shift[...].astype(F32)
        unit, _ = norm_parts(added)
        normed = norm_out(unit, gains, shifts, 2)
        for col in range(w_in.shape[1] // width):
            span = slice(col * width, (col + 1) * width)
            inner = nn(normed, w_in[:, span])
            cdf = 0.5 * (1.0 + lax.erf(inner * 0.7071067811865476))
            hidden[:, span] = (inner * cdf).astype(BF)
            hidden.send_part((slice(None), span))
            slope[:, span] = (cdf + inner * jnp.exp(-0.5 * inner * inner) * 0.3989422804014327).astype(BF)
            slope.send_part((slice(None), span))
        added = added + nn(hidden[...], w_ffn[...])
        third[...] = added
        layer[...] = added.astype(BF)
        third.send()
        layer.send()
        unit, _ = norm_parts(added)
        normed = norm_out(unit, gains, shifts, 3)
        final[:count] = normed
        label = labels[...]
        line = lax.broadcasted_iota(jnp.int32, (EXTRA, count), 0)
        high = lax.shift_right_logical(label, 8).astype(F32)
        marks = jnp.where(line == 0, high, 0.0)
        marks = jnp.where(line == 1, (label & 255).astype(F32), marks)
        marks = jnp.where(line == 2, mask[...].astype(F32), marks)
        final[count:] = jnp.concatenate([marks, jnp.zeros((EXTRA, width - count), F32)], axis=1).astype(BF)

    def head_kernel(
        final, seg, labels, mask, w_delete, w_insert,
        dfinal, keep, send, d_delete, loss, turned, ordered,
    ):
        section = lax.axis_index("pass")
        count = seg.shape[1]
        width = final.shape[1]
        h = final[:count]
        h32 = h.astype(F32)
        seg_col = column(seg[...].astype(F32), LANES)
        row_id = lax.broadcasted_iota(jnp.int32, (count, LANES), 0)
        linked = (pltpu.roll(seg_col, count - 1, 0) == seg_col) & (row_id < count - 1)
        linked = jnp.concatenate([linked.astype(F32)] * (width // LANES), axis=1)
        after = (pltpu.roll(h32, count - 1, 0) * linked).astype(BF)
        weight = column(mask[...].astype(F32), LANES)

        def entropy(logits, label, live):
            top = jnp.max(logits, axis=-1, keepdims=True)
            expo = jnp.exp(logits - top)
            total = jnp.sum(expo, axis=-1, keepdims=True)
            lane = lax.broadcasted_iota(jnp.int32, logits.shape, 1)
            target = column(label.astype(F32), logits.shape[1])
            hit = lane.astype(F32) == target
            picked = jnp.sum(jnp.where(hit, logits, 0.0), axis=1, keepdims=True)
            w = weight[:, :1] * live
            rest = jnp.sum(jnp.where(hit, 0.0, expo), axis=1, keepdims=True)
            grad = jnp.where(hit, -rest, expo) * (w / total)
            return jnp.sum(w * (top + jnp.log(total) - picked)), grad.astype(BF)

        label = labels[...]
        spot = lax.broadcasted_iota(jnp.int32, (LANES, width), 0)
        two = w_delete[...].astype(F32)
        both_rows = jnp.where(spot == 0, two[0:1], jnp.where(spot == 1, two[1:2], 0.0)).astype(BF)
        logits = nt(h, both_rows)
        lane = lax.broadcasted_iota(jnp.int32, logits.shape, 1)
        logits = jnp.where(lane < 2, logits, -1e30)
        loss_d, grad_d = entropy(logits, lax.rem(label, 2), (section == 0).astype(F32))
        logits = nn(h, w_insert[:width]) + nn(after, w_insert[width:])
        loss_i, grad_i = entropy(logits, lax.rem(label, INS), (section == 1).astype(F32))
        loss[...] = jnp.full(loss.shape, loss_d + loss_i)
        d_after = nt(grad_i, w_insert[width:]) * linked
        dfinal[...] = nn(grad_d, both_rows) + nt(grad_i, w_insert[:width]) + pltpu.roll(d_after, 1, 0)
        d_delete[...] = nn(flip(grad_d)[:EXTRA], h)[: d_delete.shape[0]]
        both_t = turn_rows(jnp.concatenate([h, after], axis=1), turned, ordered, owners())
        grad = nn(both_t, grad_i).astype(keep.dtype)
        block = both_t.shape[0] // n_dp
        half = block // 2
        for slot in range(n_dp):
            ref, index = (keep, slot) if slot < n_half else (send, slot - n_half)
            ref[index, :, :INS] = grad[slot * block : slot * block + half]
            ref[index, :, INS:] = grad[slot * block + half : (slot + 1) * block]


    def shard_base(chunk, shard):
        section, me = lax.axis_index("pass"), lax.axis_index("dp")
        return ((section ^ (chunk >> 1)) * n_dp + (me ^ (chunk & 1))) * shard

    def hits(base, start, shape, label):
        ids = lax.broadcasted_iota(jnp.int32, shape, 0) + (base + start)
        return ids == label

    def slots_of(refs):
        return [(ref, (i, half)) for half in range(2) for ref in refs for i in range(ref.shape[0])]

    def logit_kernel(n_prev, turn, n_tokens, spots, *refs):
        slots = [slots_of(refs[:n_tokens])[i] for i in spots]
        vocab, refs = refs[n_tokens : n_tokens + 6], refs[n_tokens + 6 :]
        if n_prev:
            prev, refs = refs[0], refs[1:]
        n = len(slots) // 2
        stats, expos = refs[0], refs[1 : 1 + n]
        turned = refs[1 + n] if turn else None
        h, logits = refs[-2:]
        size = (slots[0][0].shape[1] - EXTRA) // 2
        count = 2 * size
        shard = vocab[0].shape[0]
        if n_prev:
            stats[:, : n_prev * count] = prev[...]
        for tile in range(n):
            both = slots[2 * tile : 2 * tile + 2]
            for index, (ref, (i, half)) in enumerate(both):
                h[index * size : (index + 1) * size] = ref[i, half * size : (half + 1) * size]
            marks = jnp.concatenate(
                [ref[i, count:, half * size : (half + 1) * size].astype(F32) for ref, (i, half) in both], axis=1
            )
            label_f = marks[0:1] * 256.0 + marks[1:2]
            label = label_f.astype(jnp.int32)
            weight = marks[2:3]
            peak = jnp.full((8, count), -jnp.inf, F32)
            at = 0
            for ref in vocab:
                first_row = at
                for start in range(0, ref.shape[0], 1024):
                    step = min(1024, ref.shape[0] - start)
                    value = nt(ref[start : start + step], h[...])
                    logits[at : at + step] = value
                    peak = jnp.maximum(peak, jnp.max(value.reshape(step // 8, 8, count), axis=0))
                    at += step
                if turn and not tile:
                    turned[:, first_row:at] = flip(ref[...])
            peak = jnp.max(peak, axis=0, keepdims=True)
            total = jnp.zeros((8, count), F32)
            chosen = jnp.zeros((8, count), F32)
            sub = min(shard, 128)
            expo = expos[tile]
            for chunk in range(4):
                base = shard_base(chunk, shard)

                def part(i, carry, chunk=chunk, base=base, expo=expo, peak=peak, label=label):
                    total, chosen = carry
                    at = pl.multiple_of(chunk * shard + i * sub, sub)
                    value = logits[pl.ds(at, sub)]
                    hit = hits(base, i * sub, (sub, count), label)
                    weight_of = jnp.where(hit, 0.0, jnp.exp(value - peak))
                    expo[pl.ds(at, sub)] = weight_of.astype(BF)
                    total = total + jnp.sum(weight_of.reshape(sub // 8, 8, count), axis=0)
                    picked = jnp.where(hit, value, 0.0)
                    return total, chosen + jnp.sum(picked.reshape(sub // 8, 8, count), axis=0)

                total, chosen = lax.fori_loop(0, shard // sub, part, (total, chosen), unroll=True)
            total = jnp.sum(total, axis=0, keepdims=True)
            chosen = jnp.sum(chosen, axis=0, keepdims=True)
            line = lax.broadcasted_iota(jnp.int32, (8, count), 0)
            block = jnp.zeros((8, count), F32)
            for at, value in enumerate((peak, total, chosen, label_f, weight)):
                block = jnp.where(line == at, value, block)
            at = (n_prev + tile) * count
            stats[:, at : at + count] = block

    def logit_call(tokens, vocab, prev, turn, spots):
        height, width = tokens[0].shape[1:]
        count = height - EXTRA
        n = len(spots) // 2
        shard = vocab[0].shape[0]
        n_prev = prev[0].shape[1] // count if prev else 0
        outs = [like((8, (n_prev + n) * count), F32)] + [like((4 * shard, count), BF)] * n
        stats, *rest = run(
            functools.partial(logit_kernel, n_prev, turn, len(tokens), spots),
            outs + ([like((width, 4 * shard), BF)] if turn else []),
            [*tokens, *vocab, *prev],
            2.8 * n,
            12,
            [pltpu.VMEM((count, width), BF), pltpu.VMEM((4 * shard, count), F32)],
            "token_logits",
        )
        return stats, rest[:n], rest[n:]

    def merged(own, other):
        peak = jnp.maximum(own[0:1], other[0:1])
        total = own[1:2] * jnp.exp(own[0:1] - peak) + other[1:2] * jnp.exp(other[0:1] - peak)
        return peak, total, own[2:3] + other[2:3]

    def merge_kernel(step, order, own, other, out):
        size = own.shape[1] // len(order)
        blocks = [other[:, i * size : (i + 1) * size] for i in range(len(order))]
        bit = len(order) >> (step + 2)
        swapped = jnp.concatenate([blocks[order.index((half, slot ^ bit))] for half, slot in order], axis=1)
        mine = own[...]
        peak, total, chosen = merged(mine, swapped)
        line = lax.broadcasted_iota(jnp.int32, mine.shape, 0)
        out[...] = jnp.where(
            line == 0, peak, jnp.where(line == 1, total, jnp.where(line == 2, chosen, mine))
        )

    def merge_all_kernel(order, own, near, next_, far, out):
        size = own.shape[1] // len(order)
        result = None
        for ref, bit in ((own, 0), (near, 1), (next_, 2), (far, 3)):
            blocks = [ref[:, i * size : (i + 1) * size] for i in range(len(order))]
            mine = jnp.concatenate([blocks[order.index((half, slot ^ bit))] for half, slot in order], axis=1)
            result = (mine[0:1], mine[1:2], mine[2:3]) if result is None else merged(jnp.concatenate(result, axis=0), mine)
        line = lax.broadcasted_iota(jnp.int32, own.shape, 0)
        peak, total, chosen = result
        out[...] = jnp.where(
            line == 0, peak, jnp.where(line == 1, total, jnp.where(line == 2, chosen, own[...]))
        )

    def closing(local, merged_ref, other):
        peak, total, chosen = merged(merged_ref, other)
        hit = jnp.exp(chosen - peak)
        full = total + hit
        lse = peak + jnp.log(full)
        weight = local[4:5]
        factor = weight * jnp.exp(local[0:1] - lse)
        return lse, chosen, factor, -weight * (total / full)

    def dlogits_into(ref, at, cols, expo, start, base, shape, label, factor, at_label):
        sub = min(shape[0], 128)

        def part(i, _):
            row = pl.multiple_of(i * sub, sub)
            hit = hits(base, i * sub, (sub, shape[1]), label)
            value = expo[pl.ds(pl.multiple_of(start + row, sub), sub)].astype(F32) * factor
            ref[pl.ds(pl.multiple_of(at + row, sub), sub), cols] = jnp.where(hit, at_label, value).astype(BF)
            return 0

        lax.fori_loop(0, shape[0] // sub, part, 0, unroll=True)

    def dtoken_kernel(tile, expo, vocab_t, local, merged_ref, other, out, dlogits):
        rows, count = expo.shape
        shard = rows // 4
        span = slice(tile * count, (tile + 1) * count)
        _, _, factor, at_label = closing(local[:, span], merged_ref[:, span], other[:, span])
        label = local[3:4, span].astype(jnp.int32)
        for chunk in range(4):
            dlogits_into(
                dlogits, chunk * shard, slice(None), expo, chunk * shard, shard_base(chunk, shard),
                (shard, count), label, factor, at_label,
            )
        total = nn(vocab_t[...], dlogits[...]).T.astype(out.dtype)
        out[0] = total[: count // 2]
        out[1] = total[count // 2 :]

    def dtoken_call(expo, tile, local, merged_ref, other, vocab_t, dtype):
        rows, count = expo.shape
        return run(
            functools.partial(dtoken_kernel, tile),
            [like((2, count // 2, vocab_t.shape[0]), dtype)],
            [expo, vocab_t, local, merged_ref, other],
            2.2,
            8,
            [pltpu.VMEM((rows, count), BF)],
            "token_dfinal",
        )[0]

    def dvocab_kernel(shard, parity, n_tiles, *refs):
        expos, tokens = refs[:n_tiles], refs[n_tiles:-6]
        local, merged_ref, other, out, dlogits, held = refs[-6:]
        index = pl.program_id(0)
        _, _, factor, at_label = closing(local[...], merged_ref[...], other[...])
        label = local[3:4].astype(jnp.int32)
        size = (tokens[0].shape[1] - EXTRA) // 2
        count = 2 * size
        section, me = lax.axis_index("pass"), lax.axis_index("dp")
        chunk = 2 * index + parity
        base = ((section ^ (chunk >> 1)) * n_dp + (me ^ (chunk & 1))) * shard
        slots = slots_of(tokens[:2]) + [slot for token in tokens[2:] for slot in slots_of([token])]
        for at, (token, (i, half)) in enumerate(slots):
            held[at * size : (at + 1) * size] = token[i, half * size : (half + 1) * size]
        for at, expo in enumerate(expos):
            cols = slice(at * count, (at + 1) * count)
            dlogits_into(
                dlogits, 0, cols, expo, 0, base, (shard, count), label[:, cols], factor[:, cols], at_label[:, cols]
            )
        out[...] = nn(dlogits[...], held[...]).astype(out.dtype)

    def dvocab_call(expos, tokens, local, merged_ref, other, parity, dtype):
        shard, count = expos[0].shape[0] // 4, expos[0].shape[1]
        width = tokens[0].shape[2]
        total = local.shape[1]
        fixed2 = pl.BlockSpec(local.shape, lambda c: (0, 0))
        return pl.pallas_call(
            functools.partial(dvocab_kernel, shard, parity, len(expos)),
            grid=(2,),
            in_specs=[pl.BlockSpec((shard, count), lambda c: (2 * c + parity, 0))] * len(expos)
            + [pl.BlockSpec(t.shape, lambda c: (0, 0, 0)) for t in tokens]
            + [fixed2] * 3,
            out_specs=pl.BlockSpec((shard, width), lambda c: (c, 0)),
            out_shape=like((2 * shard, width), dtype),
            scratch_shapes=[pltpu.VMEM((shard, total), BF), pltpu.VMEM((total, width), BF)],
            compiler_params=pltpu.CompilerParams(vmem_limit_bytes=20 * MIB),
            cost_estimate=cost(0.1),
            name="token_dvocab",
        )(*expos, *tokens, local, merged_ref, other)


    def ffn_back_kernel(
        hidden, third, gain, w_ffn, slope, second, shift, w_in,
        kept0, kept1, moved0, moved1, dhead, head_loss, local, merged_ref, other, ins_keep, ins_send,
        dsecond, keep, send, vecs, loss, wide_t, wide_s, thin_t, thin_s, dinner,
    ):
        width = third.shape[1]
        count = third.shape[0]
        live = (lax.axis_index("pass") >= 2).astype(F32)
        hidden_t = turn_rows(hidden[...], wide_t, wide_s, owners())
        parts = [kept[...] + moved[...].astype(F32) for kept, moved in ((kept0, moved0), (kept1, moved1))]
        dfinal = dhead[...] + live * jnp.concatenate(parts, axis=0)
        unit3, rstd3 = norm_parts(third[...])
        gains = gain[...].astype(F32)
        dthird, g_gain3, g_bias3 = norm_bwd(dfinal, unit3, rstd3, gains[3:4])
        low = dthird.astype(BF)
        pack(keep, send, 0, 0, hidden_t, low)
        for col in range(w_ffn.shape[0] // width):
            span = slice(col * width, (col + 1) * width)
            part = nt(low, w_ffn[span]).astype(BF).astype(F32) * slope[:, span].astype(F32)
            dinner[:, span] = part.astype(BF)
        unit2, rstd2 = norm_parts(second[...])
        normed_t = turn_rows(norm_out(unit2, gains, shift[...].astype(F32), 2), thin_t, thin_s, owners())
        pack(keep, send, 4 * (width // n_dp), 0, normed_t, dinner[...])
        extra = ins_keep.shape[1]
        base, section = keep.shape[1] - extra, lax.axis_index("pass")
        if in_quarters(extra):
            size = extra // 4
            for quarter in range(4):
                span = slice(quarter * size, (quarter + 1) * size)
                place = pl.ds(pl.multiple_of(base + (quarter ^ section) * size, size), size)
                keep[:, place] = ins_keep[:, span]
                send[:, place] = ins_send[:, span]
        else:
            keep[:, base:] = ins_keep[...]
            send[:, base:] = ins_send[...]
        dnormed = nt(dinner[...], w_in[...])
        back, g_gain2, g_bias2 = norm_bwd(dnormed, unit2, rstd2, gains[2:3])
        dsecond[...] = dthird + back
        token_loss = 0.0
        for start in (0, count):
            span = slice(start, start + count // 2)
            lse, chosen, _, _ = closing(local[:, span], merged_ref[:, span], other[:, span])
            token_loss = token_loss + jnp.sum(local[4:5, span] * (lse - chosen))
        loss[...] = head_loss[...] + token_loss * live
        line = lax.broadcasted_iota(jnp.int32, (8, width), 0)
        block = jnp.zeros((8, width), F32)
        for at, value in enumerate((g_gain3, g_gain2, g_bias3, g_bias2)):
            block = jnp.where(line == at, value, block)
        vecs[...] = block

    def cross_back_kernel(
        dsecond, w_out, ctx, keyval, probs, query, part0, part1, part2, part3, w_kv, first, gain, shift, w_query,
        dfirst, keep, send, vecs, dsrc0, dsrc2, dsrc13, thin_t, thin_s, src_t, src_s, dquery, dkeyval, dctx,
    ):
        width = first.shape[1]
        owner_list = owners()
        low = dsecond[...].astype(BF)
        dctx[...] = nt(low, w_out[...]).astype(BF)
        at = pack(keep, send, 0, 0, turn_rows(ctx[...], thin_t, thin_s, owner_list), low)
        attend_bwd(
            tile_of(dctx, 0), tile_of(query, 0), tile_of(keyval, 0), tile_of(keyval, width), probs,
            put_in(dquery, 0), put_in(dkeyval, 0), put_in(dkeyval, width), (width // HEADS) ** -0.5, width // LANES,
        )
        size = part0.shape[0] - EXTRA
        source = jnp.concatenate([p[:size] for p in (part0, part1, part2, part3)], axis=0)
        at = pack(keep, send, 0, at, turn_rows(source, src_t, src_s, owner_list), dkeyval[...])
        for index, (ref, row) in enumerate(((dsrc0, 0), (dsrc13, 0), (dsrc2, 0), (dsrc13, size))):
            part = nt(dkeyval[index * size : (index + 1) * size], w_kv[...])
            ref[row : row + size] = part.astype(ref.dtype)
        gains, shifts = gain[...].astype(F32), shift[...].astype(F32)
        unit, rstd = norm_parts(first[...])
        normed_t = turn_rows(norm_out(unit, gains, shifts, 1), thin_t, thin_s, owner_list)
        pack(keep, send, 0, at, normed_t, dquery[...])
        back, g_gain, g_bias = norm_bwd(nt(dquery[...], w_query[...]), unit, rstd, gains[1:2])
        dfirst[...] = dsecond[...] + back
        line = lax.broadcasted_iota(jnp.int32, (8, width), 0)
        vecs[...] = jnp.where(line == 0, g_gain, jnp.where(line == 1, g_bias, 0.0))

    def self_back_kernel(
        dfirst, w_out, ctx, qkv, probs, x, gain, shift, w_qkv, vec_ffn, vec_cross, d_delete,
        dx, keep, send, thin_t, thin_s, dqkv, dctx,
    ):
        width = x.shape[1]
        owner_list = owners()
        low = dfirst[...].astype(BF)
        dctx[...] = nt(low, w_out[...]).astype(BF)
        at = pack(keep, send, 0, 0, turn_rows(ctx[...], thin_t, thin_s, owner_list), low)
        attend_bwd(
            tile_of(dctx, 0), tile_of(qkv, 0), tile_of(qkv, width), tile_of(qkv, 2 * width), probs,
            put_in(dqkv, 0), put_in(dqkv, width), put_in(dqkv, 2 * width), (width // HEADS) ** -0.5, width // LANES,
        )
        gains, shifts = gain[...].astype(F32), shift[...].astype(F32)
        unit, rstd = norm_parts(x[...].astype(F32))
        normed_t = turn_rows(norm_out(unit, gains, shifts, 0), thin_t, thin_s, owner_list)
        at = pack(keep, send, 0, at, normed_t, dqkv[...])
        back, g_gain, g_bias = norm_bwd(nt(dqkv[...], w_qkv[...]), unit, rstd, gains[0:1])
        dx[...] = dfirst[...] + back
        line = lax.broadcasted_iota(jnp.int32, (EXTRA, width), 0)
        block = jnp.zeros((EXTRA, width), F32)
        lines = (
            (0, d_delete[0:1]), (1, d_delete[1:2]),
            (8, g_gain), (9, vec_cross[0:1]), (10, vec_ffn[1:2]), (11, vec_ffn[0:1]),
            (12, g_bias), (13, vec_cross[1:2]), (14, vec_ffn[3:4]), (15, vec_ffn[2:3]),
        )
        for row, value in lines:
            block = jnp.where(line == row, value, block)
        block = block.astype(keep.dtype)
        at = at * (width // n_dp)
        for slot in range(n_half):
            keep[slot, at:] = block
            send[slot, at:] = block


    def add_kernel(pairs, *refs):
        ins, outs = refs[: 2 * pairs], refs[2 * pairs :]
        at = 0
        for keep, got in zip(ins[::2], ins[1::2]):
            rows = keep.shape[1]
            slot = 0
            for ref in outs:
                for i in range(ref.shape[0]):
                    value = keep[slot].astype(F32) + got[slot].astype(F32)
                    ref[i, at : at + rows] = value.astype(ref.dtype)
                    slot += 1
            at += rows

    def add_call(blocks, *counts):
        rows, width = sum(b.shape[1] for b in blocks[::2]), blocks[0].shape[2]
        outs = [like((count, rows, width), wire_of(width)) for count in counts]
        return run(functools.partial(add_kernel, len(blocks) // 2), outs, blocks, 0.8, 8, name="sum_slots")

    def wire_of(width):
        return small_dtype(width // n_dp)

    def regroup_kernel(plan, n_terms, *refs):
        value = refs[0][...].astype(F32)
        for ref in refs[1:n_terms]:
            value = value + ref[...].astype(F32)
        for spans, ref in zip(plan, refs[n_terms:]):
            at = 0
            for start, stop in spans:
                ref[at : at + stop - start] = value[start:stop].astype(ref.dtype)
                at += stop - start

    def pair_kernel(plan, n_terms, *refs):
        first = refs[0][...].astype(F32) + refs[1][...].astype(F32)
        value = first + (refs[2][...].astype(F32) + refs[3][...].astype(F32))
        for spans, ref in zip(plan, refs[n_terms:]):
            at = 0
            for start, stop in spans:
                ref[at : at + stop - start] = value[start:stop].astype(ref.dtype)
                at += stop - start

    def regroup(terms, plan, kernel=regroup_kernel, name="sum_rows"):
        width = terms[0].shape[-1]
        outs = [like((sum(b - a for a, b in spans), width), wire_of(width)) for spans in plan]
        terms = [t.reshape(t.shape[-2:]) for t in terms]
        return run(functools.partial(kernel, plan, len(terms)), outs, terms, 0.7, 8, name=name)

    def picked(pieces):
        section = lax.axis_index("pass")
        values = [p.astype(F32) for p in pieces]
        result = []
        for j in range(4):
            value = values[0]
            for b in (1, 2, 3):
                value = jnp.where((section ^ b) == j, values[b], value)
            result.append(value)
        return result

    def halves(refs):
        rows = refs[0].shape[0] // 2
        return [r[:rows] for r in refs], [r[rows:] for r in refs]

    def ffn_end_kernel(own, near, third, far, *rest):
        extra, (p_out, p_in, p_insert) = rest[:-3], rest[-3:]
        refs = (own, near, third, far)
        rows, width = p_in.shape[0], own.shape[1]
        for j, value in enumerate(picked([r[:rows] for r in refs])):
            p_out[j * rows : (j + 1) * rows] = value
        for j, value in enumerate(picked([r[rows : 2 * rows] for r in refs])):
            p_in[:, j * width : (j + 1) * width] = value
        half = p_insert.shape[0] // 2
        if extra:
            values = [extra[0][...].astype(F32)]
        else:
            values = picked([r[2 * rows :] for r in refs])
        size = half // len(values)
        for j, value in enumerate(values):
            p_insert[j * size : (j + 1) * size] = value[:, :INS]
            p_insert[half + j * size : half + (j + 1) * size] = value[:, INS:]

    def attention_end_kernel(
        own, near, third, far, extra, p_cross, p_kv, p_query, p_out, p_qkv, p_gain, p_bias, p_delete
    ):
        cross, own_part = halves((own, near, third, far))
        width = extra.shape[1]
        values = picked(cross)
        p_cross[...] = values[0]
        p_kv[:, :width] = values[1]
        p_kv[:, width:] = values[2]
        p_query[...] = values[3]
        values = picked(own_part)
        p_out[...] = values[0]
        for j in range(3):
            p_qkv[:, j * width : (j + 1) * width] = values[j + 1]
        size = p_gain.shape[1]
        me = lax.axis_index("dp")
        mine = pltpu.roll(extra[...].astype(F32), lax.rem(width - me * size, width), 1)
        p_gain[...] = mine[8:12, :size]
        p_bias[...] = mine[12:16, :size]
        p_delete[...] = mine[:2, :size]

    def body(
        decoder_in,
        decoder_segments,
        edit_target,
        loss_mask,
        source_out,
        source_segments,
        norm_gain,
        norm_bias,
        self_qkv,
        self_out,
        cross_query,
        cross_kv,
        cross_out,
        ffn_in,
        ffn_out,
        delete_head,
        insert_head,
        token_head,
    ):
        section = lax.axis_index("pass")
        segs, labels, mask = decoder_segments[0], edit_target[0], loss_mask[0]
        rows = decoder_in[0, 0]
        count, width = rows.shape
        shard = token_head.shape[0]
        part = source_out.shape[1]
        src = n_pass * part
        hid = ffn_in.shape[1]
        unit = width // n_dp
        wire = small_dtype(unit)

        note = jnp.pad(source_segments.astype(BF), ((0, EXTRA - 1), (0, width - part)))
        mine = jnp.concatenate([source_out[0], note], axis=0)
        parts = [mine] + [swap_pass(mine, bit) for bit in (1, 2, 3)]

        gain, shift = Far(norm_gain), Far(norm_bias)
        first, query, w_kv, first_far, query_far, qkv, probs1, ctx1 = run(
            self_kernel,
            [
                like((count, width), F32),
                like((count, width), BF),
                like(cross_kv.shape, BF),
                Far(like((count, width), F32)),
                Far(like((count, width), BF)),
                Far(like((count, 3 * width), BF)),
                Far(like((HEADS, count, count), BF)),
                Far(like((count, width), BF)),
            ],
            [Far(rows), gain, shift, Far(self_qkv), Far(segs), Far(self_out), Far(cross_query), Raw(cross_kv)],
            4.2,
            10,
            [pltpu.VMEM((count, count), F32), pltpu.SemaphoreType.DMA],
            "self_forward",
        )
        second, keyval, probs2, ctx2, hidden, slope, third, layer, final = run(
            cross_kernel,
            [
                Far(like((count, width), F32)),
                Far(like((src, 2 * width), BF)),
                Far(like((HEADS, src, count), BF)),
                Far(like((count, width), BF)),
                Far(like((count, hid), BF)),
                Far(like((count, hid), BF)),
                Far(like((count, width), F32)),
                Far(like((count, width), BF)),
                like((count + EXTRA, width), BF),
            ],
            [first, query, w_kv, Far(segs), *parts, Pin(cross_out), gain, shift]
            + [Pin(ffn_in), Pin(ffn_out), Far(labels), Far(mask)],
            7.6,
            20,
            [pltpu.VMEM((src, count), F32)],
            "cross_forward",
        )

        cut = shard * 6 // 8
        near0 = swap_pass(after(token_head, parts[1])[:cut], 1)
        moved = lax.ppermute(final, "pass", [(2, 0), (3, 1)])

        ins_rows = 2 * width // n_dp // 2
        dhead, ins_keep, ins_send, d_delete, head_loss = run(
            head_kernel,
            [
                like((count, width), F32),
                like((n_half, ins_rows, 2 * INS), wire),
                like((n_half, ins_rows, 2 * INS), wire),
                like((8, width), F32),
                like((8, LANES), F32),
            ],
            [final, Far(segs), Far(labels), Far(mask), Far(delete_head.T), Pin(insert_head)],
            1.4,
            10,
            turn_scratch(2 * width, count),
            "small_heads",
        )
        moved = after(moved, dhead)
        near1 = swap_pass(after(token_head[cut:], moved), 1)
        group = jnp.where(section >= 2, final, moved)[None]
        tokens = [group]
        for step in reversed(range(n_steps)):
            tokens.append(swap_chip(group, step))
            if step:
                group = jnp.concatenate([group, tokens[-1]], axis=0)
        near0 = after(near0, moved)
        vocab = (token_head, swap_core(token_head), near0, near1, swap_core(near0), swap_core(near1))
        expos, stats, vocab_t, order = [[], []], (), None, []
        for pieces in [tokens[:2]] + [[t] for t in tokens[2:]]:
            made = []
            for tile in range(sum(p.shape[0] for p in pieces)):
                stats, new, turned = logit_call(pieces, vocab, stats, not vocab_t, (2 * tile, 2 * tile + 1))
                stats = (stats,)
                vocab_t = vocab_t or turned
                made += new
            first_slot, n_slots = len(order) // 2, sum(p.shape[0] for p in pieces)
            for half in range(2):
                spot = half * len(made) // 2
                expos[half] += [(e, len(order) // 2 + i) for i, e in enumerate(made[spot : spot + len(made) // 2])]
                order += [(half, first_slot + i) for i in range(n_slots)]
        (vocab_t,) = vocab_t
        local = stats[0]
        whole = local
        if n_steps == 2:
            both = lax.ppermute(local, "dp", [(i, i ^ chip_bits[0] ^ chip_bits[1]) for i in range(n_dp)])
            (whole,) = run(
                functools.partial(merge_all_kernel, order), [like(local.shape, F32)],
                [local, swap_chip(local, 1), swap_chip(local, 0), both], 1.0, 8, name="stats_merge",
            )
        else:
            for step in range(n_steps):
                (whole,) = run(
                    functools.partial(merge_kernel, step, order), [like(local.shape, F32)],
                    [whole, swap_chip(whole, step)], 1.0, 8, name="stats_merge",
                )
        other = swap_pass(whole, 2)

        n_tiles = len(expos[0])
        made = [[None] * n_tiles for _ in expos]
        for tile in reversed(range(n_tiles)):
            for half in range(2):
                dtype = BF if tile >= n_tiles // 2 and n_tiles > 1 else F32
                expo, spot = expos[half][tile]
                made[half][tile] = dtoken_call(expo, spot, local, whole, other, vocab_t, dtype)
        kept = []
        for half in range(2):
            tiles = made[half]
            for step in range(n_steps):
                if len(tiles) > 1:
                    middle = len(tiles) // 2
                    sending = tiles[middle:]
                    sending = jnp.concatenate(sending, axis=0) if len(sending) > 1 else sending[0]
                    got = swap_chip(sending.astype(BF), step)
                    tiles = [t + got[2 * i : 2 * i + 2].astype(F32) for i, t in enumerate(tiles[:middle])]
                else:
                    got = swap_chip(tiles[0][1].astype(BF), step)
                    kept.append(tiles[0][0] + got.astype(F32))
        backs = [lax.ppermute(k.astype(BF), "pass", [(0, 2), (1, 3)]) for k in kept]

        flat = [e for e, _ in sorted(sum(expos, []), key=lambda pair: pair[1])]
        dvocab_send = dvocab_call(flat, tokens, after(local, *kept), whole, other, 1, BF)
        dvocab_keep = dvocab_call(flat, tokens, after(local, dvocab_send), whole, other, 0, BF)
        backs = after_all(backs, dvocab_send, dvocab_keep)
        vocab_got = swap_core(after(dvocab_send, *backs))

        def packed(rows):
            return like((n_half, rows, width), wire)

        def sent(x):
            return x.astype(BF)

        def reduce_chips(blocks, step):
            while step < n_steps:
                half = n_half >> (step + 1)
                keep, send = add_call(blocks, half, half)
                blocks = [keep, swap_chip(sent(send), step)]
                step += 1
            return blocks

        rows_ffn = 8 * unit + ins_rows
        dsecond, keep_ffn, send_ffn, vec_ffn, loss = run(
            ffn_back_kernel,
            [like((count, width), F32), packed(rows_ffn), packed(rows_ffn), like((8, width), F32), like((8, LANES), F32)],
            [Pin(hidden), Pin(third), gain, Pin(ffn_out), Pin(slope), Pin(second), shift, Pin(ffn_in)]
            + [*kept, *backs, dhead, head_loss, local, whole, other, ins_keep, ins_send],
            0.1,
            16,
            turn_scratch(hid, count) + turn_scratch(width, count) + [pltpu.VMEM((count, hid), BF)],
            "ffn_backward",
        )
        dsecond, keep_ffn, send_ffn, vec_ffn, loss = after_all(
            [dsecond, keep_ffn, send_ffn, vec_ffn, loss], vocab_got
        )
        vocab_keep = dvocab_keep[:shard].astype(F32) + vocab_got[:shard].astype(F32)
        vocab_send = (dvocab_keep[shard:].astype(F32) + vocab_got[shard:].astype(F32)).astype(BF)
        cuts = [shard * i // 64 for i in (0, 30, 42, 64)]
        vocab_parts = [vocab_send[a:b] for a, b in zip(cuts, cuts[1:])]
        vocab_parts[0] = swap_pass(vocab_parts[0], 1)
        keep_ffn, send_ffn = add_call([keep_ffn, swap_core(sent(send_ffn))], n_half // 2, n_half // 2)
        dsecond = after(dsecond, send_ffn)
        dfirst, *chunk_cross, vec_cross, src0, src2, src13 = run(
            cross_back_kernel,
            [
                like((count, width), F32),
                packed(4 * unit),
                packed(4 * unit),
                like((8, width), F32),
                like((part, width), F32),
                like((part, width), F32),
                like((2 * part, width), BF),
            ],
            [dsecond, Pin(cross_out), Pin(ctx2), Pin(keyval), Pin(probs2), Pin(query_far), *parts]
            + [Pin(cross_kv), Pin(first_far), gain, shift, Pin(cross_query)],
            0.1,
            15,
            turn_scratch(width, count)
            + turn_scratch(width, src)
            + [pltpu.VMEM((count, width), BF), pltpu.VMEM((src, 2 * width), BF), pltpu.VMEM((count, width), BF)],
            "cross_backward",
        )
        blocks_ffn = [keep_ffn, swap_chip(sent(send_ffn), 0)]
        dfirst, *chunk_cross, vec_cross, src0, src2, src13 = after_all(
            [dfirst, *chunk_cross, vec_cross, src0, src2, src13], vocab_parts[0]
        )
        vocab_parts[1] = swap_pass(after(vocab_parts[1], dfirst), 1)
        input_grad, *chunk_self = run(
            self_back_kernel,
            [Far(like((count, width), F32)), packed(4 * unit + EXTRA), packed(4 * unit + EXTRA)],
            [dfirst, Pin(self_out), Pin(ctx1), Pin(qkv), Pin(probs1), Pin(rows), gain, shift, Pin(self_qkv)]
            + [vec_ffn, vec_cross, d_delete],
            0.1,
            12,
            turn_scratch(width, count) + [pltpu.VMEM((count, 3 * width), BF), pltpu.VMEM((count, width), BF)],
            "self_backward",
        )
        def rows_at(*spots, extra=0, start=8):
            spans = [(i * unit, (i + 1) * unit) for i in spots]
            return spans + ([(start * unit, start * unit + extra)] if extra else [])

        input_grad, *chunk_self = after_all([input_grad, *chunk_self], blocks_ffn[1], vocab_parts[1])
        blocks_ffn = reduce_chips(blocks_ffn, 1)

        got_cross = swap_core(sent(chunk_cross[1]))
        keep_self, send_self = chunk_self
        send_self = after(send_self, got_cross)
        got_self = swap_core(sent(send_self))
        keep_att, send_att = add_call([chunk_cross[0], got_cross, keep_self, got_self], n_half // 2, n_half // 2)
        source_got = swap_pass(src13, 1)
        source_half = swap_pass((src2 + source_got[part:].astype(F32)).astype(BF), 2)
        source_grad = (src0 + source_got[:part].astype(F32)) + source_half.astype(F32)
        blocks_att = [keep_att, swap_chip(after(sent(send_att), blocks_ffn[1], source_got), 0)]

        split = in_quarters(ins_rows)
        size = ins_rows // 4

        def ffn_rows(places, count):
            spans = [(k * count * unit + p * unit, k * count * unit + (p + 1) * unit) for k in range(2) for p in places]
            base = 2 * count * unit
            if split:
                return spans + [(base + p * size, base + (p + 1) * size) for p in places]
            return spans + [(base, base + ins_rows)]

        keep, send = regroup(blocks_ffn, [ffn_rows((0, 2), 4), ffn_rows((1, 3), 4)])
        got = swap_pass(sent(send), 1)
        got = after(got, source_half)
        blocks_att[1] = after(blocks_att[1], got)
        blocks_att = reduce_chips(blocks_att, 1)
        keep, send = regroup([keep, got], [ffn_rows((0,), 2), ffn_rows((1,), 2)])
        got = swap_pass(sent(send), 2)
        vocab_parts[2] = swap_pass(after(vocab_parts[2], send), 1)
        token_grad = vocab_keep + jnp.concatenate(vocab_parts, axis=0).astype(F32)
        blocks_att[1] = after(blocks_att[1], got)
        pieces_by_place = regroup(blocks_att, [rows_at(i, 4 + i, extra=EXTRA) for i in range(4)])
        if split:
            (own,) = regroup([keep, got], [[(0, 2 * unit + size)]])
            ins_sum = []
        else:
            own, *ins_sum = regroup([keep, got], [rows_at(0, 1), rows_at(extra=ins_rows, start=2)])
        near, third_part = swap_pass(sent(own), 1), swap_pass(sent(own), 2)
        ffn_parts = [own, near, third_part, swap_pass(third_part, 1), *ins_sum]

        gots = [swap_pass(sent(pieces_by_place[b]), b) for b in (1, 2, 3)]
        own, extra_sum = regroup(
            [pieces_by_place[0], *gots], [rows_at(0, 1), rows_at(extra=EXTRA, start=2)], pair_kernel, "sum_pass"
        )
        attention_parts = [own] + [swap_pass(sent(own), b) for b in (1, 2, 3)] + [extra_sum]

        def out(*shape):
            return Far(like(shape, F32))

        p_out, p_in, p_insert = run(
            ffn_end_kernel, [out(hid // n_dp, width), out(unit, hid), out(2 * unit, INS)], ffn_parts, 1.0, 8,
            name="ffn_sums",
        )
        p_cross, p_kv, p_query, p_self, p_qkv, p_gain, p_bias, p_delete = run(
            attention_end_kernel,
            [out(unit, width), out(unit, 2 * width), out(unit, width), out(unit, width), out(unit, 3 * width)]
            + [out(4, unit), out(4, unit), out(2, unit)],
            attention_parts,
            1.0,
            8,
            name="attention_sums",
        )
        return (
            layer[None, None],
            loss[:1, :1],
            input_grad[None, None],
            source_grad[None],
            p_gain,
            p_bias,
            p_qkv,
            p_self,
            p_query,
            p_kv,
            p_cross,
            p_in,
            p_out,
            p_delete.T,
            p_insert,
            token_grad,
        )

    full = ("pass", "dp")
    rows_at, row_at = P("pass", "dp", None, None), P("pass", "dp", None)
    weight_at = P("dp", None)
    return jax.shard_map(
        body,
        mesh=mesh,
        in_specs=(rows_at, row_at, row_at, row_at, P("dp", "pass", None), P("dp", "pass"))
        + (P(),) * 11
        + (P(full, None),),
        out_specs=(rows_at, P("pass", "dp"), rows_at, P("dp", "pass", None), P(None, "dp"), P(None, "dp"))
        + (weight_at,) * 9
        + (P(full, None),),
        check_vma=False,
    )
```

```python
import functools

import jax
import jax.numpy as jnp
from jax import lax
from jax.experimental import pallas as pl
from jax.experimental.pallas import tpu as pltpu
from jax.sharding import PartitionSpec as P

HEADS = 8
INS = 256
EPS = 1e-05
LANES = 128
EXTRA = 16
BF = jnp.bfloat16
F32 = jnp.float32
MIB = 1 << 20


def cost(us):
    return pl.CostEstimate(flops=int(us * 0.3e9), bytes_accessed=1, transcendentals=0)


def dot(left, right, dims):
    return lax.dot_general(left, right, (dims, ((), ())), preferred_element_type=F32)


def nn(left, right):
    return dot(left, right, ((1,), (0,)))


def nt(left, right):
    return dot(left, right, ((1,), (1,)))


def flip(values):
    return values.astype(F32).T.astype(BF)


class Far:
    def __init__(self, value):
        self.value = value


class Raw(Far):
    pass


class Pin(Far):
    pass


class Fetched:
    def __init__(self, source, buffer, sem):
        self.buffer, self.shape, self.dtype = buffer, buffer.shape, buffer.dtype
        self.copy = pltpu.make_async_copy(source, buffer, sem)
        self.copy.start()
        self.waiting = True

    def wait(self):
        if self.waiting:
            self.copy.wait()
            self.waiting = False

    def __getitem__(self, index):
        self.wait()
        return self.buffer[index]


class Stored:
    def __init__(self, target, buffer, sem):
        self.buffer, self.shape, self.dtype = buffer, buffer.shape, buffer.dtype
        self.copy = pltpu.make_async_copy(buffer, target, sem)
        self.target, self.sem = target, sem
        self.sent = False

    def __getitem__(self, index):
        return self.buffer[index]

    def __setitem__(self, index, value):
        self.buffer[index] = value

    def send(self):
        self.copy.start()
        self.sent = True

    def send_part(self, index):
        pltpu.make_async_copy(self.buffer.at[index], self.target.at[index], self.sem).start()
        self.sent = True


def run(kernel, outs, ins, us, limit, scratch=(), name=None):
    far_in, far_out = [type(x) is Far for x in ins], [type(x) is Far for x in outs]
    marks_in, marks_out = [type(x) for x in ins], [type(x) for x in outs]
    ins = [x.value if isinstance(x, Far) else x for x in ins]
    outs = [x.value if isinstance(x, Far) else x for x in outs]
    buffers = [pltpu.VMEM(x.shape, x.dtype) for x, f in zip(ins + outs, far_in + far_out) if f]
    spaces = {Far: pltpu.HBM, Raw: pltpu.HBM, Pin: pltpu.VMEM}
    ins = [pltpu.with_memory_space_constraint(x, spaces[m]) if m in spaces else x for x, m in zip(ins, marks_in)]
    outs = [spaces[m](x.shape, x.dtype) if m in spaces else x for x, m in zip(outs, marks_out)]
    n_in, n_out = len(ins), len(outs)

    def wrapped(*refs):
        if buffers:
            sems = refs[-1]
            held = list(refs[-1 - len(buffers) : -1])
            rest = refs[n_in + n_out : len(refs) - 1 - len(buffers)]
        else:
            held, rest = [], refs[n_in + n_out :]
        given, made, count = [], [], 0
        for ref, far in zip(refs[:n_in], far_in):
            given.append(Fetched(ref, held[count], sems.at[count]) if far else ref)
            count += far
        for ref, far in zip(refs[n_in : n_in + n_out], far_out):
            made.append(Stored(ref, held[count], sems.at[count]) if far else ref)
            count += far
        kernel(*given, *made, *rest)
        for x in given:
            if isinstance(x, Fetched):
                x.wait()
        for x in made:
            if isinstance(x, Stored) and not x.sent:
                x.send()
        for x in made:
            if isinstance(x, Stored):
                x.copy.wait()

    def place(mark):
        return pl.BlockSpec(memory_space=spaces.get(mark, pltpu.VMEM))

    return pl.pallas_call(
        wrapped,
        out_shape=outs,
        in_specs=[place(m) for m in marks_in],
        out_specs=[place(m) for m in marks_out],
        scratch_shapes=list(scratch) + buffers + ([pltpu.SemaphoreType.DMA((len(buffers),))] if buffers else []),
        compiler_params=pltpu.CompilerParams(vmem_limit_bytes=limit * MIB),
        cost_estimate=cost(us),
        name=name,
    )(*ins)


def after(value, *done):
    return lax.optimization_barrier((value, *done))[0]


def after_all(values, *done):
    return list(lax.optimization_barrier((*values, *done))[: len(values)])


def like(shape, dtype):
    return jax.ShapeDtypeStruct(shape, dtype)


def norm_parts(values):
    center = values - jnp.mean(values, axis=-1, keepdims=True)
    rstd = lax.rsqrt(jnp.mean(center * center, axis=-1, keepdims=True) + EPS)
    return center * rstd, rstd


def norm_out(unit, gain, shift, index):
    return (unit * gain[index : index + 1] + shift[index : index + 1]).astype(BF)


def norm_bwd(grad, unit, rstd, gain):
    scaled = grad * gain
    back = rstd * (
        scaled
        - jnp.mean(scaled, axis=-1, keepdims=True)
        - unit * jnp.mean(scaled * unit, axis=-1, keepdims=True)
    )
    return back, jnp.sum(grad * unit, axis=0, keepdims=True), jnp.sum(grad, axis=0, keepdims=True)


def column(row, count):
    return jnp.broadcast_to(row, (count, row.shape[1])).T


def lane_half(values, half):
    lane = lax.broadcasted_iota(jnp.int32, values.shape, 1)
    picked = (lane >= LANES // 2) if half else (lane < LANES // 2)
    return jnp.where(picked, values, jnp.zeros_like(values))


def attend(query, keys, values, bias_ref, probs_ref, out_ref, scale, finished=None):
    half_size = LANES // 2
    for tile in range(out_ref.shape[1] // LANES):
        q = query(tile).astype(F32) * scale
        k, v_t = keys(tile), flip(values(tile))
        both = jnp.concatenate([lane_half(q, 0), lane_half(q, 1)], axis=0).astype(BF)
        count = q.shape[0]
        scores = nt(k, both)
        parts = []
        for half in range(2):
            mine = scores[:, half * count : (half + 1) * count] + bias_ref[...]
            expo = jnp.exp(mine - jnp.max(mine, axis=0, keepdims=True))
            probs = (expo * (1.0 / jnp.sum(expo, axis=0, keepdims=True))).astype(BF)
            probs_ref[2 * tile + half] = probs
            parts.append(nn(v_t[half * half_size : (half + 1) * half_size], probs))
        out_ref[:, tile * LANES : (tile + 1) * LANES] = jnp.concatenate(parts, axis=0).T.astype(BF)
        if finished:
            finished(tile)


def attend_bwd(grad, query, keys, values, probs_ref, put_query, put_keys, put_values, scale, tiles):
    half_size = LANES // 2
    for tile in range(tiles):
        g, q, k, v = grad(tile), query(tile), keys(tile), values(tile)
        k_t = flip(k)
        dq, dk, dv = [], [], []
        for half in range(2):
            probs = probs_ref[2 * tile + half]
            full = probs.astype(F32)
            dprobs = nt(v, lane_half(g, half))
            delta = jnp.sum(dprobs * full, axis=0, keepdims=True)
            dscores = (full * ((dprobs - delta) * scale)).astype(BF)
            dv.append(nn(probs, g))
            dk.append(nn(dscores, q))
            dq.append(nn(k_t[half * half_size : (half + 1) * half_size], dscores))
        lane = lax.broadcasted_iota(jnp.int32, dk[0].shape, 1) < half_size
        put_query(tile, jnp.concatenate(dq, axis=0).T.astype(BF))
        put_keys(tile, jnp.where(lane, dk[0], dk[1]).astype(BF))
        put_values(tile, jnp.where(lane, dv[0], dv[1]).astype(BF))


def tile_of(ref, start):
    return lambda tile: ref[:, start + tile * LANES : start + (tile + 1) * LANES]


def put_in(ref, start):
    def put(tile, value):
        ref[:, start + tile * LANES : start + (tile + 1) * LANES] = value

    return put


def solution(mesh):
    n_pass, n_dp = mesh.shape["pass"], mesh.shape["dp"]
    bits = [1 << i for i in range(n_dp.bit_length() - 1)]
    core_bit, chip_bits = bits[0], bits[1:]
    orders = (chip_bits, chip_bits[1::-1] + chip_bits[2:])
    n_steps = len(chip_bits)
    n_half = n_dp // 2

    def swap_core(x):
        return lax.ppermute(x, "dp", [(i, i ^ core_bit) for i in range(n_dp)])

    def swap_chip(x, step):
        return lax.ppermute(x, "dp", [(i, i ^ orders[i & 1][step]) for i in range(n_dp)])

    def swap_pass(x, bit):
        return lax.ppermute(x, "pass", [(i, i ^ bit) for i in range(n_pass)])

    def owners():
        me = lax.axis_index("dp")
        core = me & 1
        result = []
        for slot in range(n_dp):
            own_half = slot < n_half
            turn = core if own_half else 1 - core
            owner = me if own_half else me ^ 1
            for step in range(n_steps):
                if (slot >> (n_steps - 1 - step)) & 1:
                    owner = owner ^ jnp.where(turn == 0, orders[0][step], orders[1][step])
            result.append(owner)
        return result

    def small_dtype(rows):
        return BF if rows % 16 == 0 else F32

    def in_quarters(rows):
        return rows % 64 == 0

    def turn_rows(values, turned_ref, sorted_ref, owner_list):
        block = values.shape[1] // n_dp
        turned_ref[...] = values.astype(F32).T.astype(turned_ref.dtype)
        for slot, owner in enumerate(owner_list):
            start = pl.multiple_of(owner * block, block)
            sorted_ref[slot * block : (slot + 1) * block] = turned_ref[pl.ds(start, block)]
        return sorted_ref[...].astype(BF)

    def turn_scratch(features, count):
        dtype = small_dtype(features // n_dp)
        return [pltpu.VMEM((features, count), dtype)] * 2

    def pack(keep_ref, send_ref, base, first, left_t, right):
        width = keep_ref.shape[2]
        section = lax.axis_index("pass")
        unit = width // n_dp
        block = left_t.shape[0] // n_dp
        quarter = first
        for col in range(right.shape[1] // width):
            grad = nn(left_t, right[:, col * width : (col + 1) * width]).astype(keep_ref.dtype)
            for piece in range(block // unit):
                place = pl.ds(pl.multiple_of(base + (quarter ^ section) * unit, unit), unit)
                for slot in range(n_dp):
                    ref, index = (keep_ref, slot) if slot < n_half else (send_ref, slot - n_half)
                    start = slot * block + piece * unit
                    ref[index, place] = grad[start : start + unit]
                quarter += 1
        return quarter


    def self_kernel(
        x, gain, shift, w_qkv, seg, w_out, w_query, w_next, first, query, held, first_far, query_far, qkv, probs, ctx,
        bias, sem,
    ):
        copy = pltpu.make_async_copy(w_next, held, sem)
        copy.start()
        width = x.shape[1]
        gains, shifts = gain[...].astype(F32), shift[...].astype(F32)
        rows = x[...].astype(F32)
        unit, _ = norm_parts(rows)
        qkv[...] = nn(norm_out(unit, gains, shifts, 0), w_qkv[...]).astype(BF)
        seg_row = seg[...].astype(F32)
        bias[...] = jnp.where(column(seg_row, seg_row.shape[1]) == seg_row, 0.0, -1000000000.0)
        attend(
            tile_of(qkv, 0), tile_of(qkv, width), tile_of(qkv, 2 * width), bias, probs, ctx, (width // HEADS) ** -0.5
        )
        for ref in (qkv, probs, ctx):
            ref.send()
        added = rows + nn(ctx[...], w_out[...])
        first[...] = added
        first_far[...] = added
        first_far.send()
        unit, _ = norm_parts(added)
        value = nn(norm_out(unit, gains, shifts, 1), w_query[...]).astype(BF)
        query[...] = value
        query_far[...] = value
        copy.wait()

    def cross_kernel(
        first, query, w_kv, seg, part0, part1, part2, part3, w_out, gain, shift, w_in, w_ffn, labels, mask,
        second, keyval, probs, ctx, hidden, slope, third, layer, final, bias,
    ):
        width = first.shape[1]
        count = first.shape[0]
        seg_row = seg[...].astype(F32)
        size = part0.shape[0] - EXTRA
        for index, part in enumerate((part0, part1, part2, part3)):
            span = slice(index * size, (index + 1) * size)
            keyval[span] = nn(part[:size], w_kv[...]).astype(BF)
            source_seg = part[size : size + EXTRA, :size].astype(F32)[0:1]
            bias[span] = jnp.where(column(source_seg, count) == seg_row, 0.0, -1000000000.0)
        keyval.send()
        attend(
            tile_of(query, 0), tile_of(keyval, 0), tile_of(keyval, width), bias, probs, ctx, (width // HEADS) ** -0.5,
            lambda tile: probs.send_part(pl.ds(2 * tile, 2)),
        )
        ctx.send()
        added = first[...] + nn(ctx[...], w_out[...])
        second[...] = added
        second.send()
        gains, shifts = gain[...].astype(F32), shift[...].astype(F32)
        unit, _ = norm_parts(added)
        normed = norm_out(unit, gains, shifts, 2)
        for col in range(w_in.shape[1] // width):
            span = slice(col * width, (col + 1) * width)
            inner = nn(normed, w_in[:, span])
            cdf = 0.5 * (1.0 + lax.erf(inner * 0.7071067811865476))
            hidden[:, span] = (inner * cdf).astype(BF)
            hidden.send_part((slice(None), span))
            slope[:, span] = (cdf + inner * jnp.exp(-0.5 * inner * inner) * 0.3989422804014327).astype(BF)
            slope.send_part((slice(None), span))
        added = added + nn(hidden[...], w_ffn[...])
        third[...] = added
        layer[...] = added.astype(BF)
        third.send()
        layer.send()
        unit, _ = norm_parts(added)
        normed = norm_out(unit, gains, shifts, 3)
        final[:count] = normed
        label = labels[...]
        line = lax.broadcasted_iota(jnp.int32, (EXTRA, count), 0)
        high = lax.shift_right_logical(label, 8).astype(F32)
        marks = jnp.where(line == 0, high, 0.0)
        marks = jnp.where(line == 1, (label & 255).astype(F32), marks)
        marks = jnp.where(line == 2, mask[...].astype(F32), marks)
        final[count:] = jnp.concatenate([marks, jnp.zeros((EXTRA, width - count), F32)], axis=1).astype(BF)

    def head_kernel(
        final, seg, labels, mask, w_delete, w_insert,
        dfinal, keep, send, d_delete, loss, turned, ordered,
    ):
        section = lax.axis_index("pass")
        count = seg.shape[1]
        width = final.shape[1]
        h = final[:count]
        h32 = h.astype(F32)
        seg_col = column(seg[...].astype(F32), LANES)
        row_id = lax.broadcasted_iota(jnp.int32, (count, LANES), 0)
        linked = (pltpu.roll(seg_col, count - 1, 0) == seg_col) & (row_id < count - 1)
        linked = jnp.concatenate([linked.astype(F32)] * (width // LANES), axis=1)
        after = (pltpu.roll(h32, count - 1, 0) * linked).astype(BF)
        weight = column(mask[...].astype(F32), LANES)

        def entropy(logits, label, live):
            top = jnp.max(logits, axis=-1, keepdims=True)
            expo = jnp.exp(logits - top)
            total = jnp.sum(expo, axis=-1, keepdims=True)
            lane = lax.broadcasted_iota(jnp.int32, logits.shape, 1)
            target = column(label.astype(F32), logits.shape[1])
            hit = lane.astype(F32) == target
            picked = jnp.sum(jnp.where(hit, logits, 0.0), axis=1, keepdims=True)
            w = weight[:, :1] * live
            rest = jnp.sum(jnp.where(hit, 0.0, expo), axis=1, keepdims=True)
            grad = jnp.where(hit, -rest, expo) * (w / total)
            return jnp.sum(w * (top + jnp.log(total) - picked)), grad.astype(BF)

        label = labels[...]
        spot = lax.broadcasted_iota(jnp.int32, (LANES, width), 0)
        two = w_delete[...].astype(F32)
        both_rows = jnp.where(spot == 0, two[0:1], jnp.where(spot == 1, two[1:2], 0.0)).astype(BF)
        logits = nt(h, both_rows)
        lane = lax.broadcasted_iota(jnp.int32, logits.shape, 1)
        logits = jnp.where(lane < 2, logits, -1e30)
        loss_d, grad_d = entropy(logits, lax.rem(label, 2), (section == 0).astype(F32))
        logits = nn(h, w_insert[:width]) + nn(after, w_insert[width:])
        loss_i, grad_i = entropy(logits, lax.rem(label, INS), (section == 1).astype(F32))
        loss[...] = jnp.full(loss.shape, loss_d + loss_i)
        d_after = nt(grad_i, w_insert[width:]) * linked
        dfinal[...] = nn(grad_d, both_rows) + nt(grad_i, w_insert[:width]) + pltpu.roll(d_after, 1, 0)
        d_delete[...] = nn(flip(grad_d)[:EXTRA], h)[: d_delete.shape[0]]
        both_t = turn_rows(jnp.concatenate([h, after], axis=1), turned, ordered, owners())
        grad = nn(both_t, grad_i).astype(keep.dtype)
        block = both_t.shape[0] // n_dp
        half = block // 2
        for slot in range(n_dp):
            ref, index = (keep, slot) if slot < n_half else (send, slot - n_half)
            ref[index, :, :INS] = grad[slot * block : slot * block + half]
            ref[index, :, INS:] = grad[slot * block + half : (slot + 1) * block]


    def shard_base(chunk, shard):
        section, me = lax.axis_index("pass"), lax.axis_index("dp")
        return ((section ^ (chunk >> 1)) * n_dp + (me ^ (chunk & 1))) * shard

    def hits(base, start, shape, label):
        ids = lax.broadcasted_iota(jnp.int32, shape, 0) + (base + start)
        return ids == label

    def slots_of(refs):
        return [(ref, (i, half)) for half in range(2) for ref in refs for i in range(ref.shape[0])]

    def logit_kernel(n_prev, turn, n_tokens, spots, *refs):
        slots = [slots_of(refs[:n_tokens])[i] for i in spots]
        vocab, refs = refs[n_tokens : n_tokens + 6], refs[n_tokens + 6 :]
        if n_prev:
            prev, refs = refs[0], refs[1:]
        n = len(slots) // 2
        stats, expos = refs[0], refs[1 : 1 + n]
        turned = refs[1 + n] if turn else None
        h, logits = refs[-2:]
        size = (slots[0][0].shape[1] - EXTRA) // 2
        count = 2 * size
        shard = vocab[0].shape[0]
        if n_prev:
            stats[:, : n_prev * count] = prev[...]
        for tile in range(n):
            both = slots[2 * tile : 2 * tile + 2]
            for index, (ref, (i, half)) in enumerate(both):
                h[index * size : (index + 1) * size] = ref[i, half * size : (half + 1) * size]
            marks = jnp.concatenate(
                [ref[i, count:, half * size : (half + 1) * size].astype(F32) for ref, (i, half) in both], axis=1
            )
            label_f = marks[0:1] * 256.0 + marks[1:2]
            label = label_f.astype(jnp.int32)
            weight = marks[2:3]
            peak = jnp.full((8, count), -jnp.inf, F32)
            at = 0
            for ref in vocab:
                first_row = at
                for start in range(0, ref.shape[0], 1024):
                    step = min(1024, ref.shape[0] - start)
                    value = nt(ref[start : start + step], h[...])
                    logits[at : at + step] = value
                    peak = jnp.maximum(peak, jnp.max(value.reshape(step // 8, 8, count), axis=0))
                    at += step
                if turn and not tile:
                    turned[:, first_row:at] = flip(ref[...])
            peak = jnp.max(peak, axis=0, keepdims=True)
            total = jnp.zeros((8, count), F32)
            chosen = jnp.zeros((8, count), F32)
            sub = min(shard, 128)
            expo = expos[tile]
            for chunk in range(4):
                base = shard_base(chunk, shard)

                def part(i, carry, chunk=chunk, base=base, expo=expo, peak=peak, label=label):
                    total, chosen = carry
                    at = pl.multiple_of(chunk * shard + i * sub, sub)
                    value = logits[pl.ds(at, sub)]
                    hit = hits(base, i * sub, (sub, count), label)
                    weight_of = jnp.where(hit, 0.0, jnp.exp(value - peak))
                    expo[pl.ds(at, sub)] = weight_of.astype(BF)
                    total = total + jnp.sum(weight_of.reshape(sub // 8, 8, count), axis=0)
                    picked = jnp.where(hit, value, 0.0)
                    return total, chosen + jnp.sum(picked.reshape(sub // 8, 8, count), axis=0)

                total, chosen = lax.fori_loop(0, shard // sub, part, (total, chosen), unroll=True)
            total = jnp.sum(total, axis=0, keepdims=True)
            chosen = jnp.sum(chosen, axis=0, keepdims=True)
            line = lax.broadcasted_iota(jnp.int32, (8, count), 0)
            block = jnp.zeros((8, count), F32)
            for at, value in enumerate((peak, total, chosen, label_f, weight)):
                block = jnp.where(line == at, value, block)
            at = (n_prev + tile) * count
            stats[:, at : at + count] = block

    def logit_call(tokens, vocab, prev, turn, spots):
        height, width = tokens[0].shape[1:]
        count = height - EXTRA
        n = len(spots) // 2
        shard = vocab[0].shape[0]
        n_prev = prev[0].shape[1] // count if prev else 0
        outs = [like((8, (n_prev + n) * count), F32)] + [like((4 * shard, count), BF)] * n
        stats, *rest = run(
            functools.partial(logit_kernel, n_prev, turn, len(tokens), spots),
            outs + ([like((width, 4 * shard), BF)] if turn else []),
            [*tokens, *vocab, *prev],
            2.8 * n,
            12,
            [pltpu.VMEM((count, width), BF), pltpu.VMEM((4 * shard, count), F32)],
            "token_logits",
        )
        return stats, rest[:n], rest[n:]

    def merged(own, other):
        peak = jnp.maximum(own[0:1], other[0:1])
        total = own[1:2] * jnp.exp(own[0:1] - peak) + other[1:2] * jnp.exp(other[0:1] - peak)
        return peak, total, own[2:3] + other[2:3]

    def merge_kernel(step, order, own, other, out):
        size = own.shape[1] // len(order)
        blocks = [other[:, i * size : (i + 1) * size] for i in range(len(order))]
        bit = len(order) >> (step + 2)
        swapped = jnp.concatenate([blocks[order.index((half, slot ^ bit))] for half, slot in order], axis=1)
        mine = own[...]
        peak, total, chosen = merged(mine, swapped)
        line = lax.broadcasted_iota(jnp.int32, mine.shape, 0)
        out[...] = jnp.where(
            line == 0, peak, jnp.where(line == 1, total, jnp.where(line == 2, chosen, mine))
        )

    def merge_all_kernel(order, own, near, next_, far, out):
        size = own.shape[1] // len(order)
        result = None
        for ref, bit in ((own, 0), (near, 1), (next_, 2), (far, 3)):
            blocks = [ref[:, i * size : (i + 1) * size] for i in range(len(order))]
            mine = jnp.concatenate([blocks[order.index((half, slot ^ bit))] for half, slot in order], axis=1)
            result = (mine[0:1], mine[1:2], mine[2:3]) if result is None else merged(jnp.concatenate(result, axis=0), mine)
        line = lax.broadcasted_iota(jnp.int32, own.shape, 0)
        peak, total, chosen = result
        out[...] = jnp.where(
            line == 0, peak, jnp.where(line == 1, total, jnp.where(line == 2, chosen, own[...]))
        )

    def closing(local, merged_ref, other):
        peak, total, chosen = merged(merged_ref, other)
        hit = jnp.exp(chosen - peak)
        full = total + hit
        lse = peak + jnp.log(full)
        weight = local[4:5]
        factor = weight * jnp.exp(local[0:1] - lse)
        return lse, chosen, factor, -weight * (total / full)

    def dlogits_into(ref, at, cols, expo, start, base, shape, label, factor, at_label):
        sub = min(shape[0], 128)

        def part(i, _):
            row = pl.multiple_of(i * sub, sub)
            hit = hits(base, i * sub, (sub, shape[1]), label)
            value = expo[pl.ds(pl.multiple_of(start + row, sub), sub)].astype(F32) * factor
            ref[pl.ds(pl.multiple_of(at + row, sub), sub), cols] = jnp.where(hit, at_label, value).astype(BF)
            return 0

        lax.fori_loop(0, shape[0] // sub, part, 0, unroll=True)

    def dtoken_kernel(tile, expo, vocab_t, local, merged_ref, other, out, dlogits):
        rows, count = expo.shape
        shard = rows // 4
        span = slice(tile * count, (tile + 1) * count)
        _, _, factor, at_label = closing(local[:, span], merged_ref[:, span], other[:, span])
        label = local[3:4, span].astype(jnp.int32)
        for chunk in range(4):
            dlogits_into(
                dlogits, chunk * shard, slice(None), expo, chunk * shard, shard_base(chunk, shard),
                (shard, count), label, factor, at_label,
            )
        total = nn(vocab_t[...], dlogits[...]).T.astype(out.dtype)
        out[0] = total[: count // 2]
        out[1] = total[count // 2 :]

    def dtoken_call(expo, tile, local, merged_ref, other, vocab_t, dtype):
        rows, count = expo.shape
        return run(
            functools.partial(dtoken_kernel, tile),
            [like((2, count // 2, vocab_t.shape[0]), dtype)],
            [expo, vocab_t, local, merged_ref, other],
            2.2,
            8,
            [pltpu.VMEM((rows, count), BF)],
            "token_dfinal",
        )[0]

    def dvocab_kernel(shard, parity, n_tiles, *refs):
        expos, tokens = refs[:n_tiles], refs[n_tiles:-6]
        local, merged_ref, other, out, dlogits, held = refs[-6:]
        index = pl.program_id(0)
        _, _, factor, at_label = closing(local[...], merged_ref[...], other[...])
        label = local[3:4].astype(jnp.int32)
        size = (tokens[0].shape[1] - EXTRA) // 2
        count = 2 * size
        section, me = lax.axis_index("pass"), lax.axis_index("dp")
        chunk = 2 * index + parity
        base = ((section ^ (chunk >> 1)) * n_dp + (me ^ (chunk & 1))) * shard
        slots = slots_of(tokens[:2]) + [slot for token in tokens[2:] for slot in slots_of([token])]
        for at, (token, (i, half)) in enumerate(slots):
            held[at * size : (at + 1) * size] = token[i, half * size : (half + 1) * size]
        for at, expo in enumerate(expos):
            cols = slice(at * count, (at + 1) * count)
            dlogits_into(
                dlogits, 0, cols, expo, 0, base, (shard, count), label[:, cols], factor[:, cols], at_label[:, cols]
            )
        out[...] = nn(dlogits[...], held[...]).astype(out.dtype)

    def dvocab_call(expos, tokens, local, merged_ref, other, parity, dtype):
        shard, count = expos[0].shape[0] // 4, expos[0].shape[1]
        width = tokens[0].shape[2]
        total = local.shape[1]
        fixed2 = pl.BlockSpec(local.shape, lambda c: (0, 0))
        return pl.pallas_call(
            functools.partial(dvocab_kernel, shard, parity, len(expos)),
            grid=(2,),
            in_specs=[pl.BlockSpec((shard, count), lambda c: (2 * c + parity, 0))] * len(expos)
            + [pl.BlockSpec(t.shape, lambda c: (0, 0, 0)) for t in tokens]
            + [fixed2] * 3,
            out_specs=pl.BlockSpec((shard, width), lambda c: (c, 0)),
            out_shape=like((2 * shard, width), dtype),
            scratch_shapes=[pltpu.VMEM((shard, total), BF), pltpu.VMEM((total, width), BF)],
            compiler_params=pltpu.CompilerParams(vmem_limit_bytes=20 * MIB),
            cost_estimate=cost(0.1),
            name="token_dvocab",
        )(*expos, *tokens, local, merged_ref, other)


    def ffn_back_kernel(
        hidden, third, gain, w_ffn, slope, second, shift, w_in,
        kept0, kept1, moved0, moved1, dhead, head_loss, local, merged_ref, other, ins_keep, ins_send,
        dsecond, keep, send, vecs, loss, wide_t, wide_s, thin_t, thin_s, dinner,
    ):
        width = third.shape[1]
        count = third.shape[0]
        live = (lax.axis_index("pass") >= 2).astype(F32)
        hidden_t = turn_rows(hidden[...], wide_t, wide_s, owners())
        parts = [kept[...] + moved[...].astype(F32) for kept, moved in ((kept0, moved0), (kept1, moved1))]
        dfinal = dhead[...] + live * jnp.concatenate(parts, axis=0)
        unit3, rstd3 = norm_parts(third[...])
        gains = gain[...].astype(F32)
        dthird, g_gain3, g_bias3 = norm_bwd(dfinal, unit3, rstd3, gains[3:4])
        low = dthird.astype(BF)
        pack(keep, send, 0, 0, hidden_t, low)
        for col in range(w_ffn.shape[0] // width):
            span = slice(col * width, (col + 1) * width)
            part = nt(low, w_ffn[span]).astype(BF).astype(F32) * slope[:, span].astype(F32)
            dinner[:, span] = part.astype(BF)
        unit2, rstd2 = norm_parts(second[...])
        normed_t = turn_rows(norm_out(unit2, gains, shift[...].astype(F32), 2), thin_t, thin_s, owners())
        pack(keep, send, 4 * (width // n_dp), 0, normed_t, dinner[...])
        extra = ins_keep.shape[1]
        base, section = keep.shape[1] - extra, lax.axis_index("pass")
        if in_quarters(extra):
            size = extra // 4
            for quarter in range(4):
                span = slice(quarter * size, (quarter + 1) * size)
                place = pl.ds(pl.multiple_of(base + (quarter ^ section) * size, size), size)
                keep[:, place] = ins_keep[:, span]
                send[:, place] = ins_send[:, span]
        else:
            keep[:, base:] = ins_keep[...]
            send[:, base:] = ins_send[...]
        dnormed = nt(dinner[...], w_in[...])
        back, g_gain2, g_bias2 = norm_bwd(dnormed, unit2, rstd2, gains[2:3])
        dsecond[...] = dthird + back
        token_loss = 0.0
        for start in (0, count):
            span = slice(start, start + count // 2)
            lse, chosen, _, _ = closing(local[:, span], merged_ref[:, span], other[:, span])
            token_loss = token_loss + jnp.sum(local[4:5, span] * (lse - chosen))
        loss[...] = head_loss[...] + token_loss * live
        line = lax.broadcasted_iota(jnp.int32, (8, width), 0)
        block = jnp.zeros((8, width), F32)
        for at, value in enumerate((g_gain3, g_gain2, g_bias3, g_bias2)):
            block = jnp.where(line == at, value, block)
        vecs[...] = block

    def cross_back_kernel(
        dsecond, w_out, ctx, keyval, probs, query, part0, part1, part2, part3, w_kv, first, gain, shift, w_query,
        dfirst, keep, send, vecs, dsrc0, dsrc2, dsrc13, thin_t, thin_s, src_t, src_s, dquery, dkeyval, dctx,
    ):
        width = first.shape[1]
        owner_list = owners()
        low = dsecond[...].astype(BF)
        dctx[...] = nt(low, w_out[...]).astype(BF)
        at = pack(keep, send, 0, 0, turn_rows(ctx[...], thin_t, thin_s, owner_list), low)
        attend_bwd(
            tile_of(dctx, 0), tile_of(query, 0), tile_of(keyval, 0), tile_of(keyval, width), probs,
            put_in(dquery, 0), put_in(dkeyval, 0), put_in(dkeyval, width), (width // HEADS) ** -0.5, width // LANES,
        )
        size = part0.shape[0] - EXTRA
        source = jnp.concatenate([p[:size] for p in (part0, part1, part2, part3)], axis=0)
        at = pack(keep, send, 0, at, turn_rows(source, src_t, src_s, owner_list), dkeyval[...])
        for index, (ref, row) in enumerate(((dsrc0, 0), (dsrc13, 0), (dsrc2, 0), (dsrc13, size))):
            part = nt(dkeyval[index * size : (index + 1) * size], w_kv[...])
            ref[row : row + size] = part.astype(ref.dtype)
        gains, shifts = gain[...].astype(F32), shift[...].astype(F32)
        unit, rstd = norm_parts(first[...])
        normed_t = turn_rows(norm_out(unit, gains, shifts, 1), thin_t, thin_s, owner_list)
        pack(keep, send, 0, at, normed_t, dquery[...])
        back, g_gain, g_bias = norm_bwd(nt(dquery[...], w_query[...]), unit, rstd, gains[1:2])
        dfirst[...] = dsecond[...] + back
        line = lax.broadcasted_iota(jnp.int32, (8, width), 0)
        vecs[...] = jnp.where(line == 0, g_gain, jnp.where(line == 1, g_bias, 0.0))

    def self_back_kernel(
        dfirst, w_out, ctx, qkv, probs, x, gain, shift, w_qkv, vec_ffn, vec_cross, d_delete,
        dx, keep, send, thin_t, thin_s, dqkv, dctx,
    ):
        width = x.shape[1]
        owner_list = owners()
        low = dfirst[...].astype(BF)
        dctx[...] = nt(low, w_out[...]).astype(BF)
        at = pack(keep, send, 0, 0, turn_rows(ctx[...], thin_t, thin_s, owner_list), low)
        attend_bwd(
            tile_of(dctx, 0), tile_of(qkv, 0), tile_of(qkv, width), tile_of(qkv, 2 * width), probs,
            put_in(dqkv, 0), put_in(dqkv, width), put_in(dqkv, 2 * width), (width // HEADS) ** -0.5, width // LANES,
        )
        gains, shifts = gain[...].astype(F32), shift[...].astype(F32)
        unit, rstd = norm_parts(x[...].astype(F32))
        normed_t = turn_rows(norm_out(unit, gains, shifts, 0), thin_t, thin_s, owner_list)
        at = pack(keep, send, 0, at, normed_t, dqkv[...])
        back, g_gain, g_bias = norm_bwd(nt(dqkv[...], w_qkv[...]), unit, rstd, gains[0:1])
        dx[...] = dfirst[...] + back
        line = lax.broadcasted_iota(jnp.int32, (EXTRA, width), 0)
        block = jnp.zeros((EXTRA, width), F32)
        lines = (
            (0, d_delete[0:1]), (1, d_delete[1:2]),
            (8, g_gain), (9, vec_cross[0:1]), (10, vec_ffn[1:2]), (11, vec_ffn[0:1]),
            (12, g_bias), (13, vec_cross[1:2]), (14, vec_ffn[3:4]), (15, vec_ffn[2:3]),
        )
        for row, value in lines:
            block = jnp.where(line == row, value, block)
        block = block.astype(keep.dtype)
        at = at * (width // n_dp)
        for slot in range(n_half):
            keep[slot, at:] = block
            send[slot, at:] = block


    def add_kernel(pairs, *refs):
        ins, outs = refs[: 2 * pairs], refs[2 * pairs :]
        at = 0
        for keep, got in zip(ins[::2], ins[1::2]):
            rows = keep.shape[1]
            slot = 0
            for ref in outs:
                for i in range(ref.shape[0]):
                    value = keep[slot].astype(F32) + got[slot].astype(F32)
                    ref[i, at : at + rows] = value.astype(ref.dtype)
                    slot += 1
            at += rows

    def add_call(blocks, *counts):
        rows, width = sum(b.shape[1] for b in blocks[::2]), blocks[0].shape[2]
        outs = [like((count, rows, width), wire_of(width)) for count in counts]
        return run(functools.partial(add_kernel, len(blocks) // 2), outs, blocks, 0.8, 8, name="sum_slots")

    def wire_of(width):
        return small_dtype(width // n_dp)

    def regroup_kernel(plan, n_terms, *refs):
        value = refs[0][...].astype(F32)
        for ref in refs[1:n_terms]:
            value = value + ref[...].astype(F32)
        for spans, ref in zip(plan, refs[n_terms:]):
            at = 0
            for start, stop in spans:
                ref[at : at + stop - start] = value[start:stop].astype(ref.dtype)
                at += stop - start

    def pair_kernel(plan, n_terms, *refs):
        first = refs[0][...].astype(F32) + refs[1][...].astype(F32)
        value = first + (refs[2][...].astype(F32) + refs[3][...].astype(F32))
        for spans, ref in zip(plan, refs[n_terms:]):
            at = 0
            for start, stop in spans:
                ref[at : at + stop - start] = value[start:stop].astype(ref.dtype)
                at += stop - start

    def regroup(terms, plan, kernel=regroup_kernel, name="sum_rows"):
        width = terms[0].shape[-1]
        outs = [like((sum(b - a for a, b in spans), width), wire_of(width)) for spans in plan]
        terms = [t.reshape(t.shape[-2:]) for t in terms]
        return run(functools.partial(kernel, plan, len(terms)), outs, terms, 0.7, 8, name=name)

    def picked(pieces):
        section = lax.axis_index("pass")
        values = [p.astype(F32) for p in pieces]
        result = []
        for j in range(4):
            value = values[0]
            for b in (1, 2, 3):
                value = jnp.where((section ^ b) == j, values[b], value)
            result.append(value)
        return result

    def halves(refs):
        rows = refs[0].shape[0] // 2
        return [r[:rows] for r in refs], [r[rows:] for r in refs]

    def ffn_end_kernel(own, near, third, far, *rest):
        extra, (p_out, p_in, p_insert) = rest[:-3], rest[-3:]
        refs = (own, near, third, far)
        rows, width = p_in.shape[0], own.shape[1]
        for j, value in enumerate(picked([r[:rows] for r in refs])):
            p_out[j * rows : (j + 1) * rows] = value
        for j, value in enumerate(picked([r[rows : 2 * rows] for r in refs])):
            p_in[:, j * width : (j + 1) * width] = value
        half = p_insert.shape[0] // 2
        if extra:
            values = [extra[0][...].astype(F32)]
        else:
            values = picked([r[2 * rows :] for r in refs])
        size = half // len(values)
        for j, value in enumerate(values):
            p_insert[j * size : (j + 1) * size] = value[:, :INS]
            p_insert[half + j * size : half + (j + 1) * size] = value[:, INS:]

    def attention_end_kernel(
        own, near, third, far, extra, p_cross, p_kv, p_query, p_out, p_qkv, p_gain, p_bias, p_delete
    ):
        cross, own_part = halves((own, near, third, far))
        width = extra.shape[1]
        values = picked(cross)
        p_cross[...] = values[0]
        p_kv[:, :width] = values[1]
        p_kv[:, width:] = values[2]
        p_query[...] = values[3]
        values = picked(own_part)
        p_out[...] = values[0]
        for j in range(3):
            p_qkv[:, j * width : (j + 1) * width] = values[j + 1]
        size = p_gain.shape[1]
        me = lax.axis_index("dp")
        mine = pltpu.roll(extra[...].astype(F32), lax.rem(width - me * size, width), 1)
        p_gain[...] = mine[8:12, :size]
        p_bias[...] = mine[12:16, :size]
        p_delete[...] = mine[:2, :size]

    def body(
        decoder_in,
        decoder_segments,
        edit_target,
        loss_mask,
        source_out,
        source_segments,
        norm_gain,
        norm_bias,
        self_qkv,
        self_out,
        cross_query,
        cross_kv,
        cross_out,
        ffn_in,
        ffn_out,
        delete_head,
        insert_head,
        token_head,
    ):
        section = lax.axis_index("pass")
        segs, labels, mask = decoder_segments[0], edit_target[0], loss_mask[0]
        rows = decoder_in[0, 0]
        count, width = rows.shape
        shard = token_head.shape[0]
        part = source_out.shape[1]
        src = n_pass * part
        hid = ffn_in.shape[1]
        unit = width // n_dp
        wire = small_dtype(unit)

        note = jnp.pad(source_segments.astype(BF), ((0, EXTRA - 1), (0, width - part)))
        mine = jnp.concatenate([source_out[0], note], axis=0)
        parts = [mine] + [swap_pass(mine, bit) for bit in (1, 2, 3)]

        gain, shift = Far(norm_gain), Far(norm_bias)
        first, query, w_kv, first_far, query_far, qkv, probs1, ctx1 = run(
            self_kernel,
            [
                like((count, width), F32),
                like((count, width), BF),
                like(cross_kv.shape, BF),
                Far(like((count, width), F32)),
                Far(like((count, width), BF)),
                Far(like((count, 3 * width), BF)),
                Far(like((HEADS, count, count), BF)),
                Far(like((count, width), BF)),
            ],
            [Far(rows), gain, shift, Far(self_qkv), Far(segs), Far(self_out), Far(cross_query), Raw(cross_kv)],
            4.2,
            10,
            [pltpu.VMEM((count, count), F32), pltpu.SemaphoreType.DMA],
            "self_forward",
        )
        second, keyval, probs2, ctx2, hidden, slope, third, layer, final = run(
            cross_kernel,
            [
                Far(like((count, width), F32)),
                Far(like((src, 2 * width), BF)),
                Far(like((HEADS, src, count), BF)),
                Far(like((count, width), BF)),
                Far(like((count, hid), BF)),
                Far(like((count, hid), BF)),
                Far(like((count, width), F32)),
                Far(like((count, width), BF)),
                like((count + EXTRA, width), BF),
            ],
            [first, query, w_kv, Far(segs), *parts, Pin(cross_out), gain, shift]
            + [Pin(ffn_in), Pin(ffn_out), Far(labels), Far(mask)],
            7.6,
            20,
            [pltpu.VMEM((src, count), F32)],
            "cross_forward",
        )

        cut = shard * 5 // 8
        near0 = swap_pass(after(token_head, parts[1])[:cut], 1)
        moved = lax.ppermute(final, "pass", [(2, 0), (3, 1)])

        ins_rows = 2 * width // n_dp // 2
        dhead, ins_keep, ins_send, d_delete, head_loss = run(
            head_kernel,
            [
                like((count, width), F32),
                like((n_half, ins_rows, 2 * INS), wire),
                like((n_half, ins_rows, 2 * INS), wire),
                like((8, width), F32),
                like((8, LANES), F32),
            ],
            [final, Far(segs), Far(labels), Far(mask), Far(delete_head.T), Pin(insert_head)],
            1.4,
            10,
            turn_scratch(2 * width, count),
            "small_heads",
        )
        moved = after(moved, dhead)
        near1 = swap_pass(after(token_head[cut:], moved), 1)
        group = jnp.where(section >= 2, final, moved)[None]
        tokens = [group]
        for step in reversed(range(n_steps)):
            tokens.append(swap_chip(group, step))
            if step:
                group = jnp.concatenate([group, tokens[-1]], axis=0)
        near0 = after(near0, moved)
        vocab = (token_head, swap_core(token_head), near0, near1, swap_core(near0), swap_core(near1))
        expos, stats, vocab_t, order = [[], []], (), None, []
        for pieces in [tokens[:2]] + [[t] for t in tokens[2:]]:
            made = []
            for tile in range(sum(p.shape[0] for p in pieces)):
                stats, new, turned = logit_call(pieces, vocab, stats, not vocab_t, (2 * tile, 2 * tile + 1))
                stats = (stats,)
                vocab_t = vocab_t or turned
                made += new
            first_slot, n_slots = len(order) // 2, sum(p.shape[0] for p in pieces)
            for half in range(2):
                spot = half * len(made) // 2
                expos[half] += [(e, len(order) // 2 + i) for i, e in enumerate(made[spot : spot + len(made) // 2])]
                order += [(half, first_slot + i) for i in range(n_slots)]
        (vocab_t,) = vocab_t
        local = stats[0]
        whole = local
        if n_steps == 2:
            both = lax.ppermute(local, "dp", [(i, i ^ chip_bits[0] ^ chip_bits[1]) for i in range(n_dp)])
            (whole,) = run(
                functools.partial(merge_all_kernel, order), [like(local.shape, F32)],
                [local, swap_chip(local, 1), swap_chip(local, 0), both], 1.0, 8, name="stats_merge",
            )
        else:
            for step in range(n_steps):
                (whole,) = run(
                    functools.partial(merge_kernel, step, order), [like(local.shape, F32)],
                    [whole, swap_chip(whole, step)], 1.0, 8, name="stats_merge",
                )
        other = swap_pass(whole, 2)

        n_tiles = len(expos[0])
        made = [[None] * n_tiles for _ in expos]
        for tile in reversed(range(n_tiles)):
            for half in range(2):
                dtype = BF if tile >= n_tiles // 2 and n_tiles > 1 else F32
                expo, spot = expos[half][tile]
                made[half][tile] = dtoken_call(expo, spot, local, whole, other, vocab_t, dtype)
        kept = []
        for half in range(2):
            tiles = made[half]
            for step in range(n_steps):
                if len(tiles) > 1:
                    middle = len(tiles) // 2
                    sending = tiles[middle:]
                    sending = jnp.concatenate(sending, axis=0) if len(sending) > 1 else sending[0]
                    got = swap_chip(sending.astype(BF), step)
                    tiles = [t + got[2 * i : 2 * i + 2].astype(F32) for i, t in enumerate(tiles[:middle])]
                else:
                    got = swap_chip(tiles[0][1].astype(BF), step)
                    kept.append(tiles[0][0] + got.astype(F32))
        backs = [lax.ppermute(k.astype(BF), "pass", [(0, 2), (1, 3)]) for k in kept]

        flat = [e for e, _ in sorted(sum(expos, []), key=lambda pair: pair[1])]
        dvocab_send = dvocab_call(flat, tokens, after(local, *kept), whole, other, 1, BF)
        dvocab_keep = dvocab_call(flat, tokens, after(local, dvocab_send), whole, other, 0, BF)
        backs = after_all(backs, dvocab_send, dvocab_keep)
        vocab_got = swap_core(after(dvocab_send, *backs))

        def packed(rows):
            return like((n_half, rows, width), wire)

        def sent(x):
            return x.astype(BF)

        def reduce_chips(blocks, step):
            while step < n_steps:
                half = n_half >> (step + 1)
                keep, send = add_call(blocks, half, half)
                blocks = [keep, swap_chip(sent(send), step)]
                step += 1
            return blocks

        rows_ffn = 8 * unit + ins_rows
        dsecond, keep_ffn, send_ffn, vec_ffn, loss = run(
            ffn_back_kernel,
            [like((count, width), F32), packed(rows_ffn), packed(rows_ffn), like((8, width), F32), like((8, LANES), F32)],
            [Pin(hidden), Pin(third), gain, Pin(ffn_out), Pin(slope), Pin(second), shift, Pin(ffn_in)]
            + [*kept, *backs, dhead, head_loss, local, whole, other, ins_keep, ins_send],
            0.1,
            16,
            turn_scratch(hid, count) + turn_scratch(width, count) + [pltpu.VMEM((count, hid), BF)],
            "ffn_backward",
        )
        dsecond, keep_ffn, send_ffn, vec_ffn, loss = after_all(
            [dsecond, keep_ffn, send_ffn, vec_ffn, loss], vocab_got
        )
        vocab_keep = dvocab_keep[:shard].astype(F32) + vocab_got[:shard].astype(F32)
        vocab_send = (dvocab_keep[shard:].astype(F32) + vocab_got[shard:].astype(F32)).astype(BF)
        cuts = [shard * i // 64 for i in (0, 30, 42, 64)]
        vocab_parts = [vocab_send[a:b] for a, b in zip(cuts, cuts[1:])]
        vocab_parts[0] = swap_pass(vocab_parts[0], 1)
        keep_ffn, send_ffn = add_call([keep_ffn, swap_core(sent(send_ffn))], n_half // 2, n_half // 2)
        dsecond = after(dsecond, send_ffn)
        dfirst, *chunk_cross, vec_cross, src0, src2, src13 = run(
            cross_back_kernel,
            [
                like((count, width), F32),
                packed(4 * unit),
                packed(4 * unit),
                like((8, width), F32),
                like((part, width), F32),
                like((part, width), F32),
                like((2 * part, width), BF),
            ],
            [dsecond, Pin(cross_out), Pin(ctx2), Pin(keyval), Pin(probs2), Pin(query_far), *parts]
            + [Pin(cross_kv), Pin(first_far), gain, shift, Pin(cross_query)],
            0.1,
            15,
            turn_scratch(width, count)
            + turn_scratch(width, src)
            + [pltpu.VMEM((count, width), BF), pltpu.VMEM((src, 2 * width), BF), pltpu.VMEM((count, width), BF)],
            "cross_backward",
        )
        blocks_ffn = [keep_ffn, swap_chip(sent(send_ffn), 0)]
        dfirst, *chunk_cross, vec_cross, src0, src2, src13 = after_all(
            [dfirst, *chunk_cross, vec_cross, src0, src2, src13], vocab_parts[0]
        )
        vocab_parts[1] = swap_pass(after(vocab_parts[1], dfirst), 1)
        input_grad, *chunk_self = run(
            self_back_kernel,
            [Far(like((count, width), F32)), packed(4 * unit + EXTRA), packed(4 * unit + EXTRA)],
            [dfirst, Pin(self_out), Pin(ctx1), Pin(qkv), Pin(probs1), Pin(rows), gain, shift, Pin(self_qkv)]
            + [vec_ffn, vec_cross, d_delete],
            0.1,
            12,
            turn_scratch(width, count) + [pltpu.VMEM((count, 3 * width), BF), pltpu.VMEM((count, width), BF)],
            "self_backward",
        )
        def rows_at(*spots, extra=0, start=8):
            spans = [(i * unit, (i + 1) * unit) for i in spots]
            return spans + ([(start * unit, start * unit + extra)] if extra else [])

        input_grad, *chunk_self = after_all([input_grad, *chunk_self], blocks_ffn[1], vocab_parts[1])
        blocks_ffn = reduce_chips(blocks_ffn, 1)

        got_cross = swap_core(sent(chunk_cross[1]))
        keep_self, send_self = chunk_self
        send_self = after(send_self, got_cross)
        got_self = swap_core(sent(send_self))
        keep_att, send_att = add_call([chunk_cross[0], got_cross, keep_self, got_self], n_half // 2, n_half // 2)
        source_got = swap_pass(src13, 1)
        source_half = swap_pass((src2 + source_got[part:].astype(F32)).astype(BF), 2)
        source_grad = (src0 + source_got[:part].astype(F32)) + source_half.astype(F32)
        blocks_att = [keep_att, swap_chip(after(sent(send_att), blocks_ffn[1], source_got), 0)]

        split = in_quarters(ins_rows)
        size = ins_rows // 4

        def ffn_rows(places, count):
            spans = [(k * count * unit + p * unit, k * count * unit + (p + 1) * unit) for k in range(2) for p in places]
            base = 2 * count * unit
            if split:
                return spans + [(base + p * size, base + (p + 1) * size) for p in places]
            return spans + [(base, base + ins_rows)]

        keep, send = regroup(blocks_ffn, [ffn_rows((0, 2), 4), ffn_rows((1, 3), 4)])
        got = swap_pass(sent(send), 1)
        got = after(got, source_half)
        blocks_att[1] = after(blocks_att[1], got)
        blocks_att = reduce_chips(blocks_att, 1)
        keep, send = regroup([keep, got], [ffn_rows((0,), 2), ffn_rows((1,), 2)])
        got = swap_pass(sent(send), 2)
        vocab_parts[2] = swap_pass(after(vocab_parts[2], send), 1)
        token_grad = vocab_keep + jnp.concatenate(vocab_parts, axis=0).astype(F32)
        blocks_att[1] = after(blocks_att[1], got)
        pieces_by_place = regroup(blocks_att, [rows_at(i, 4 + i, extra=EXTRA) for i in range(4)])
        if split:
            (own,) = regroup([keep, got], [[(0, 2 * unit + size)]])
            ins_sum = []
        else:
            own, *ins_sum = regroup([keep, got], [rows_at(0, 1), rows_at(extra=ins_rows, start=2)])
        near, third_part = swap_pass(sent(own), 1), swap_pass(sent(own), 2)
        ffn_parts = [own, near, third_part, swap_pass(third_part, 1), *ins_sum]

        gots = [swap_pass(sent(pieces_by_place[b]), b) for b in (1, 2, 3)]
        own, extra_sum = regroup(
            [pieces_by_place[0], *gots], [rows_at(0, 1), rows_at(extra=EXTRA, start=2)], pair_kernel, "sum_pass"
        )
        attention_parts = [own] + [swap_pass(sent(own), b) for b in (1, 2, 3)] + [extra_sum]

        def out(*shape):
            return Far(like(shape, F32))

        p_out, p_in, p_insert = run(
            ffn_end_kernel, [out(hid // n_dp, width), out(unit, hid), out(2 * unit, INS)], ffn_parts, 1.0, 8,
            name="ffn_sums",
        )
        p_cross, p_kv, p_query, p_self, p_qkv, p_gain, p_bias, p_delete = run(
            attention_end_kernel,
            [out(unit, width), out(unit, 2 * width), out(unit, width), out(unit, width), out(unit, 3 * width)]
            + [out(4, unit), out(4, unit), out(2, unit)],
            attention_parts,
            1.0,
            8,
            name="attention_sums",
        )
        return (
            layer[None, None],
            loss[:1, :1],
            input_grad[None, None],
            source_grad[None],
            p_gain,
            p_bias,
            p_qkv,
            p_self,
            p_query,
            p_kv,
            p_cross,
            p_in,
            p_out,
            p_delete.T,
            p_insert,
            token_grad,
        )

    full = ("pass", "dp")
    rows_at, row_at = P("pass", "dp", None, None), P("pass", "dp", None)
    weight_at = P("dp", None)
    return jax.shard_map(
        body,
        mesh=mesh,
        in_specs=(rows_at, row_at, row_at, row_at, P("dp", "pass", None), P("dp", "pass"))
        + (P(),) * 11
        + (P(full, None),),
        out_specs=(rows_at, P("pass", "dp"), rows_at, P("dp", "pass", None), P(None, "dp"), P(None, "dp"))
        + (weight_at,) * 9
        + (P(full, None),),
        check_vma=False,
    )
```
